32 devices in a mesh: section: 2 (over x), head: 4 (over y, core), ctx: 4 (over z).
Axes of the slice: x: 2, y: 2, z: 4, core: 2. Of those that a mesh axis runs over, the one named last changes fastest.
Arguments:
- tokens: bfloat16 [2, 1024, 1536], P(None, ('head', 'ctx')), may hold values from -6 to 6
- positions: int32 [2, 1024], replicated, may hold values from 0 to 1023, as said below
- norm1_gain: bfloat16 [2, 1536], P('section', ('head', 'ctx')), may hold values from 0.25 to 1.75
- qkv_bias: bfloat16 [2, 2048], P('section', ('head', 'ctx')), may hold values from -3 to 3
- qkv_weight: bfloat16 [2, 1536, 2048], P('section', ('head', 'ctx')), may hold values from -0.15625 to 0.15625
- out_weight: bfloat16 [2, 1536, 1536], P('section', ('head', 'ctx')), may hold values from -1.75 to 1.75
- norm2_gain: bfloat16 [2, 1536], P('section', ('head', 'ctx')), may hold values from 0.25 to 1.75
- gate_up_weight: bfloat16 [2, 1536, 17920], P('section', ('head', 'ctx')), may hold values from -0.15625 to 0.15625
- down_weight: bfloat16 [2, 1536, 8960], P('section', ('head', 'ctx')), may hold values from -0.0625 to 0.0625
- cotangent: bfloat16 [2, 1024, 1536], P(None, ('head', 'ctx')), may hold values from -6 to 6
Outputs:
- activations: bfloat16 [2, 2, 1024, 1536], P('section', None, ('head', 'ctx'))
- input_grads: bfloat16 [2, 2, 1024, 1536], P('section', None, ('head', 'ctx'))
- norm1_gain_grad: float32 [2, 1536], P('section', ('head', 'ctx'))
- query_key_bias_grad: float32 [2, 1792], P('section', ('head', 'ctx'))
- value_bias_grad: float32 [2, 256], P('section', ('head', 'ctx'))
- qkv_weight_grad: float32 [2, 1536, 2048], P('section', ('head', 'ctx'))
- out_weight_grad: float32 [2, 1536, 1536], P('section', ('head', 'ctx'))
- norm2_gain_grad: float32 [2, 1536], P('section', ('head', 'ctx'))
- gate_up_grad: float32 [2, 1536, 17920], P('section', ('head', 'ctx'))
- down_grad: float32 [2, 1536, 8960], P('section', ('head', 'ctx'))
The draws below stay inside these ranges and needn't reach their ends.
Inputs may be any that keep to these rules, and one draw needn't show every extreme that they name: Each micro-batch's positions are a permutation of 0 to 1023. The 256 tokens stored in the blocks h * 4 + c of 64 tokens, taken over all h in order, are two whole stretches of 128 consecutive positions in order: stretch i and stretch 2 * 4 - 1 - i, where which i belongs to which c is drawn for each micro-batch.
All inputs are finite; a program needn't handle non-finite values.
Results may differ from the reference program's by a relative error of at most 0.033.
Values may be sent and summed in bfloat16 or wider, within the bound.
A program may use at most 512 MiB of HBM per device.

```python
import math
import jax
import jax.numpy as jnp
from jax import lax

D = 1536
FF = 8960
QUERY_HEADS = 12
KEY_VALUE_HEADS = 2
HEAD_WIDTH_SIZE = 128
TOK_DEV = 64
MICRO_BATCHES = 2
SEQUENCE_TOKENS = 1024
GROUP = 256
QKV = 2048
QK_COLUMNS = 1792
SECTIONS = 2
N_HEAD = 4


def draw_positions(key, part):
    key = jax.random.fold_in(key, 11)
    rank_total = SEQUENCE_TOKENS // GROUP
    stretch_size = GROUP // 2
    stored = jnp.arange(SEQUENCE_TOKENS)
    head_slot = stored // (rank_total * TOK_DEV)
    rank_slot = stored // TOK_DEV % rank_total
    offset = head_slot * TOK_DEV + stored % TOK_DEV
    batches = []
    for number in range(MICRO_BATCHES):
        rank_order = jax.random.permutation(jax.random.fold_in(key, number), rank_total)
        paired = rank_order[rank_slot]
        stretch_id = jnp.where(offset < stretch_size, paired, 2 * rank_total - 1 - paired)
        batches.append(stretch_id * stretch_size + offset % stretch_size)
    return jnp.stack(batches).astype(jnp.int32)


def level_of(own_key, extent, split, smallest, high):
    loudness = 1.0
    for axis_at, shards_of in split:
        draws = jax.random.uniform(jax.random.fold_in(jax.random.fold_in(own_key, 6), axis_at), (shards_of,), jnp.float32, smallest / len(split), high / len(split))
        loudness = loudness * jnp.repeat(jnp.exp(draws), extent[axis_at] // shards_of).reshape((-1,) + (1,) * (len(extent) - 1 - axis_at))
    return loudness


def scatter_about(stream_key, shape, spread, limit, shards=(), kind=jnp.bfloat16):
    drawn = jax.random.normal(stream_key, shape, jnp.float32) * spread
    if len(shards) > 0:
        drawn = level_of(stream_key, shape, shards, -0.22, 0.18) * drawn
    return jnp.clip(drawn, min=-limit, max=limit).astype(kind)


def setup_inputs(seed: int = 0) -> dict:
    keys = jax.random.split(jax.random.key(seed), 11)
    tokens = scatter_about(keys[0], (MICRO_BATCHES, SEQUENCE_TOKENS, D), 1.0, 6.0, ((1, 16),))
    positions = draw_positions(jax.random.fold_in(keys[10], 71), 0)
    norm1_gain = jnp.clip(1.0 + 0.15 * jax.random.normal(keys[2], (SECTIONS, D), jnp.float32), 0.25, 1.75).astype(jnp.bfloat16)
    qkv_bias = scatter_about(keys[3], (SECTIONS, QKV), 0.5, 3.0, ((0, 2), (1, 16)))
    qkv_weight = scatter_about(keys[4], (SECTIONS, D, QKV), D ** -0.5, 0.15625, ((0, 2), (1, 16)))
    out_weight = scatter_about(keys[5], (SECTIONS, D, QUERY_HEADS * HEAD_WIDTH_SIZE), (max(QUERY_HEADS * HEAD_WIDTH_SIZE // 128, 4)) ** -0.5, 1.75, ((0, 2), (1, 16)))
    norm2_gain = jnp.clip(1.0 + 0.15 * jax.random.normal(keys[6], (SECTIONS, D), jnp.float32), 0.25, 1.75).astype(jnp.bfloat16)
    gate_up_weight = scatter_about(keys[7], (SECTIONS, D, 2 * FF), D ** -0.5, 0.15625, ((0, 2), (1, 16)))
    down_weight = scatter_about(keys[8], (SECTIONS, D, FF), FF ** -0.5, 0.0625, ((0, 2), (1, 16)))
    cotangent = scatter_about(keys[9], (MICRO_BATCHES, SEQUENCE_TOKENS, D), 1.0, 6.0, ((1, 16),))
    return {"tokens": tokens, "positions": positions, "norm1_gain": norm1_gain, "qkv_bias": qkv_bias, "qkv_weight": qkv_weight, "out_weight": out_weight, "norm2_gain": norm2_gain, "gate_up_weight": gate_up_weight, "down_weight": down_weight, "cotangent": cotangent}


EPSILON = 1e-06
THETA = 1000000.0

@jax.custom_vjp
def low(v):
    return lax.optimization_barrier(v.astype(jnp.bfloat16)).astype(jnp.float32)

@jax.custom_vjp
def low_back(v):
    return v

def low_keep(v):
    return (low(v), None)

def low_pass(kept, grad):
    return (grad,)

def back_keep(v):
    return (v, None)

def back_low(kept, grad):
    return (low(grad),)
low.defvjp(low_keep, low_pass)
low_back.defvjp(back_keep, back_low)

def highest_einsum(form, left_side, right_side):
    return jnp.einsum(form, left_side, right_side, precision=lax.Precision.HIGHEST)

def norm_rows(values, gain_row):
    return values * lax.rsqrt(lax.optimization_barrier(jnp.mean(values * values, axis=-1, keepdims=True)) + EPSILON) * gain_row

def rope_tables(position_ids):
    frequencies = THETA ** (-(jnp.arange(HEAD_WIDTH_SIZE // 2).astype(jnp.float32) * 2.0) / HEAD_WIDTH_SIZE)
    angles = position_ids.astype(jnp.float32)[..., None] * frequencies
    angles = jnp.concatenate([angles, angles], axis=-1)
    return (jnp.cos(angles)[..., None, :], jnp.sin(angles)[..., None, :])

def rotate(values, cosine_table, sine_table):
    half_width = values.shape[-1] // 2
    turned = jnp.concatenate([-values[..., half_width:], values[..., :half_width]], axis=-1)
    return values * cosine_table + turned * sine_table

def attend_block(query_block, query_positions, key_rows, value_rows, key_positions):
    score_scale = 1.0 / math.sqrt(HEAD_WIDTH_SIZE)
    scores = highest_einsum('qghd,kgd->qghk', query_block, key_rows) * score_scale
    scores = low_back(scores)
    allowed = (key_positions[None, :] <= query_positions[:, None])[:, None, None, :]
    scores = jnp.where(allowed, scores, -1e+30)
    highest = lax.optimization_barrier(jnp.max(scores, axis=-1, keepdims=True))
    exponents = jnp.exp(scores - highest)
    totals = lax.optimization_barrier(jnp.sum(exponents, axis=-1, keepdims=True))
    weighted = highest_einsum('qghk,kgd->qghd', low(exponents), value_rows)
    return weighted / totals

def attend(query_rows, key_rows, value_rows, position_ids):
    block_size = 512 if SEQUENCE_TOKENS % 512 == 0 else SEQUENCE_TOKENS
    block_total = SEQUENCE_TOKENS // block_size
    block_function = jax.checkpoint(attend_block)

    def one_sequence(inputs):
        queries_seq, keys_seq, values_seq, positions_seq = inputs
        query_blocks = queries_seq.reshape(block_total, block_size, N_HEAD, QUERY_HEADS // N_HEAD, HEAD_WIDTH_SIZE)
        position_blocks = positions_seq.reshape(block_total, block_size)

        def one_block(block_inputs):
            return block_function(block_inputs[0], block_inputs[1], keys_seq, values_seq, positions_seq)
        outcome = lax.map(one_block, (query_blocks, position_blocks))
        return outcome.reshape(SEQUENCE_TOKENS, QUERY_HEADS * HEAD_WIDTH_SIZE)
    return lax.map(one_sequence, (query_rows, key_rows, value_rows, position_ids))

def layer(inputs, position_ids, gain_one, bias_all, w_qkv, w_out, gain_two, w_gate_up, w_down):
    normed_one = low(norm_rows(inputs, gain_one))
    projected_rows = low_back(highest_einsum('msd,dc->msc', normed_one, w_qkv) + bias_all)
    query_columns = QUERY_HEADS * HEAD_WIDTH_SIZE
    key_columns = KEY_VALUE_HEADS * HEAD_WIDTH_SIZE
    queries = projected_rows[..., :query_columns].reshape(MICRO_BATCHES, SEQUENCE_TOKENS, QUERY_HEADS, HEAD_WIDTH_SIZE)
    key_row_block = projected_rows[..., query_columns:query_columns + key_columns].reshape(MICRO_BATCHES, SEQUENCE_TOKENS, KEY_VALUE_HEADS, HEAD_WIDTH_SIZE)
    value_row_block = projected_rows[..., query_columns + key_columns:].reshape(MICRO_BATCHES, SEQUENCE_TOKENS, KEY_VALUE_HEADS, HEAD_WIDTH_SIZE)
    cosine_table, sine_table = rope_tables(position_ids)
    copy_count = N_HEAD // KEY_VALUE_HEADS
    queries = low(low_back(rotate(queries, cosine_table, sine_table)))
    queries = queries.reshape(MICRO_BATCHES, SEQUENCE_TOKENS, N_HEAD, QUERY_HEADS // N_HEAD, HEAD_WIDTH_SIZE)
    keys_copied = low(low_back(jnp.repeat(rotate(key_row_block, cosine_table, sine_table), copy_count, axis=2)))
    values_copied = low(low_back(jnp.repeat(value_row_block, copy_count, axis=2)))
    attended = low(low_back(attend(queries, keys_copied, values_copied, position_ids)))
    middle = inputs + low_back(highest_einsum('msc,dc->msd', attended, w_out))
    normed_two = low(norm_rows(middle, gain_two))
    gate_up = low_back(highest_einsum('msd,dc->msc', normed_two, w_gate_up))
    hidden_low = low(jax.nn.silu(gate_up[..., :FF]) * gate_up[..., FF:])
    return middle + low_back(highest_einsum('msf,df->msd', hidden_low, w_down))

def reference(tokens, positions, norm1_gain, qkv_bias, qkv_weight, out_weight, norm2_gain, gate_up_weight, down_weight, cotangent):
    params = (norm1_gain, qkv_bias, qkv_weight, out_weight, norm2_gain, gate_up_weight, down_weight)
    first_set = tuple((weight_arg[0].astype(jnp.float32) for weight_arg in params))
    second_set = tuple((weight_arg[1].astype(jnp.float32) for weight_arg in params))

    def apply_layer(inputs, *weights):
        return layer(inputs, positions, *weights)
    first_out, first_back = jax.vjp(apply_layer, tokens.astype(jnp.float32), *first_set)
    middle_in = first_out.astype(jnp.bfloat16)
    second_out, second_back = jax.vjp(apply_layer, middle_in.astype(jnp.float32), *second_set)
    second_grads = second_back(cotangent.astype(jnp.float32))
    middle_grad = second_grads[0].astype(jnp.bfloat16)
    first_grads = first_back(middle_grad.astype(jnp.float32))
    activations = jnp.stack([middle_in, second_out.astype(jnp.bfloat16)])
    input_grads = jnp.stack([first_grads[0].astype(jnp.bfloat16), middle_grad])
    stacked = [jnp.stack([first_grads[slot_number], second_grads[slot_number]]) for slot_number in range(1, 8)]
    query_key_part = stacked[1][:, :QK_COLUMNS]
    value_part = stacked[1][:, QK_COLUMNS:]
    return (activations, input_grads, stacked[0], query_key_part, value_part, stacked[2], stacked[3], stacked[4], stacked[5], stacked[6])
```

```python
import functools
import math

import jax
import jax.numpy as jnp
from jax import lax
from jax.experimental import pallas as pl
from jax.experimental.pallas import tpu as pltpu
from jax.sharding import PartitionSpec as P

FF = 8960
QUERY_HEADS = 12
KEY_VALUE_HEADS = 2
HEAD_WIDTH_SIZE = 128


EPSILON = 1e-06
THETA = 1000000.0


def from_behind(value, axis, steps):
    count = lax.axis_size(axis)
    first, last = (max(0, -steps), min(count, count - steps))
    return lax.ppermute(value, axis, [(source, source + steps) for source in range(first, last)])


def rope_tables(position_ids, head_width):
    frequencies = THETA ** (-(jnp.arange(head_width // 2).astype(jnp.float32) * 2.0) / head_width)
    angles = position_ids.astype(jnp.float32)[..., None] * frequencies
    angles = jnp.concatenate([angles, angles], axis=-1)
    return (jnp.cos(angles)[..., None, :], jnp.sin(angles)[..., None, :])


def rotate(values, cosine_table, sine_table):
    half_width = values.shape[-1] // 2
    turned = jnp.concatenate([-values[..., half_width:], values[..., :half_width]], axis=-1)
    return values * cosine_table + turned * sine_table


def unrotate(grad_values, cosine_table, sine_table):
    half_width = grad_values.shape[-1] // 2
    scaled = grad_values * sine_table
    return grad_values * cosine_table + jnp.concatenate(
        [scaled[..., half_width:], -scaled[..., :half_width]], axis=-1
    )


def norm_rows(values, gain_row):
    inverse = lax.rsqrt(jnp.mean(values * values, axis=-1, keepdims=True) + EPSILON)
    return (values * inverse * gain_row, inverse)


def norm_back(values, inverse, gain_row, grad_values):
    weighted = grad_values * gain_row
    inner_mean = jnp.mean(weighted * values, axis=-1, keepdims=True)
    input_grad = inverse * weighted - values * inverse**3 * inner_mean
    gain_grad = jnp.sum((grad_values * values * inverse).reshape(-1, values.shape[-1]), axis=0)
    return (input_grad, gain_grad)


def pick(flag, first_tree, second_tree):
    return jax.tree.map(
        lambda left_side, right_side: jnp.where(flag, left_side, right_side),
        first_tree,
        second_tree,
    )


def masked_scores(queries, keys_now, query_pos, key_now):
    score_scale = 1.0 / math.sqrt(queries.shape[-1])
    allowed = (key_now[:, None, :] <= query_pos[:, :, None])[:, :, None, :]
    scores = (
        jnp.einsum("grhd,gkd->grhk", queries, keys_now, preferred_element_type=jnp.float32)
        * score_scale
    )
    return (jnp.where(allowed, scores, -1e30), allowed)


def attend_forward(queries, pair_group, query_pos, key_pos):
    head_width = queries.shape[-1]
    row_shape = queries.shape[:3]
    shard_piece = lax.all_gather(pair_group, "ctx", axis=1, tiled=True)
    running = jnp.full(row_shape, -1e30, jnp.float32)
    keys_now = shard_piece[:, :, 0, :head_width]
    values_now = shard_piece[:, :, 0, head_width:]
    scores, allowed = masked_scores(queries, keys_now, query_pos, key_pos)
    highest = jnp.maximum(running, jnp.max(scores, axis=-1))
    probs_now = jnp.where(allowed, jnp.exp(scores - highest[..., None]), 0.0)
    totals = jnp.sum(probs_now, axis=-1)
    accumulated = jnp.einsum(
        "grhk,gkd->grhd",
        probs_now.astype(jnp.bfloat16),
        values_now,
        preferred_element_type=jnp.float32,
    )
    running, totals, accumulated = (highest, totals, accumulated)
    return (accumulated / totals[..., None], running + jnp.log(totals))


def attend_backward(queries, pair_group, query_pos, key_pos, out_grads, lse_rows, delta_rows):
    head_width = queries.shape[-1]
    score_scale = 1.0 / math.sqrt(head_width)
    shard_piece = lax.all_gather(pair_group, "ctx", axis=1, tiled=True)
    keys_now = shard_piece[:, :, 0, :head_width]
    values_now = shard_piece[:, :, 0, head_width:]
    scores, allowed = masked_scores(queries, keys_now, query_pos, key_pos)
    probs_now = jnp.where(allowed, jnp.exp(scores - lse_rows[..., None]), 0.0)
    prob_grads = jnp.einsum(
        "grhd,gkd->grhk", out_grads, values_now, preferred_element_type=jnp.float32
    )
    score_grads = (probs_now * (prob_grads - delta_rows[..., None])).astype(jnp.bfloat16)
    query_grads = score_scale * jnp.einsum(
        "grhk,gkd->grhd", score_grads, keys_now, preferred_element_type=jnp.float32
    )
    key_part = score_scale * jnp.einsum(
        "grhk,grhd->gkd", score_grads, queries, preferred_element_type=jnp.float32
    )
    value_part = jnp.einsum(
        "grhk,grhd->gkd",
        probs_now.astype(jnp.bfloat16),
        out_grads,
        preferred_element_type=jnp.float32,
    )
    piece_term = jnp.concatenate([key_part, value_part], axis=-1)[:, :, None, :]
    return (query_grads, piece_term)


def layer_forward(inputs, own_pos, query_pos, key_pos, weights, heads_total):
    gain_one, bias_all, w_qkv, w_out, gain_two, w_gate_up, w_down = weights
    batch_length = inputs.shape[0]
    rows_total = inputs.shape[1]
    per_device = QUERY_HEADS // heads_total
    copy_count = heads_total // KEY_VALUE_HEADS
    query_columns = QUERY_HEADS * HEAD_WIDTH_SIZE
    key_columns = KEY_VALUE_HEADS * HEAD_WIDTH_SIZE
    residual = inputs.astype(jnp.float32)
    normed_one, inverse_one = norm_rows(residual, gain_one.astype(jnp.float32))
    normed_low = normed_one.astype(jnp.bfloat16)
    projected_rows = jnp.einsum(
        "grd,dc->grc", normed_low, w_qkv, preferred_element_type=jnp.float32
    ) + bias_all.astype(jnp.float32)
    cosine_table, sine_table = rope_tables(own_pos, HEAD_WIDTH_SIZE)
    queries = rotate(
        projected_rows[..., :query_columns].reshape(
            batch_length, rows_total, QUERY_HEADS, HEAD_WIDTH_SIZE
        ),
        cosine_table,
        sine_table,
    )
    key_row_block = rotate(
        projected_rows[..., query_columns : query_columns + key_columns].reshape(
            batch_length, rows_total, KEY_VALUE_HEADS, HEAD_WIDTH_SIZE
        ),
        cosine_table,
        sine_table,
    )
    value_row_block = projected_rows[..., query_columns + key_columns :].reshape(
        batch_length, rows_total, KEY_VALUE_HEADS, HEAD_WIDTH_SIZE
    )
    pair_rows = jnp.concatenate(
        [
            jnp.repeat(key_row_block, copy_count, axis=2),
            jnp.repeat(value_row_block, copy_count, axis=2),
        ],
        axis=-1,
    ).astype(jnp.bfloat16)
    query_send = queries.astype(jnp.bfloat16).reshape(
        batch_length, rows_total, heads_total, per_device * HEAD_WIDTH_SIZE
    )
    query_group, pair_group = (
        lax.all_to_all(query_send, "head", split_axis=2, concat_axis=1, tiled=True),
        lax.all_to_all(pair_rows, "head", split_axis=2, concat_axis=1, tiled=True),
    )
    group_rows = query_group.shape[1]
    query_group = query_group.reshape(batch_length, group_rows, per_device, HEAD_WIDTH_SIZE)
    attended, lse_rows = attend_forward(query_group, pair_group, query_pos, key_pos)
    out_send = attended.astype(jnp.bfloat16).reshape(
        batch_length, group_rows, 1, per_device * HEAD_WIDTH_SIZE
    )
    out_rows = lax.all_to_all(out_send, "head", split_axis=1, concat_axis=2, tiled=True).reshape(
        batch_length, rows_total, QUERY_HEADS * HEAD_WIDTH_SIZE
    )
    middle = residual + jnp.einsum(
        "grc,dc->grd", out_rows, w_out, preferred_element_type=jnp.float32
    )
    normed_two, inverse_two = norm_rows(middle, gain_two.astype(jnp.float32))
    normed_two_low = normed_two.astype(jnp.bfloat16)
    gate_up = jnp.einsum(
        "grd,dc->grc", normed_two_low, w_gate_up, preferred_element_type=jnp.float32
    )
    hidden_low = (jax.nn.silu(gate_up[..., :FF]) * gate_up[..., FF:]).astype(jnp.bfloat16)
    output = middle + jnp.einsum(
        "grf,df->grd", hidden_low, w_down, preferred_element_type=jnp.float32
    )
    kept_now = (
        residual,
        inverse_one,
        normed_low,
        query_group,
        pair_group,
        attended,
        lse_rows,
        out_rows,
        middle,
        inverse_two,
        normed_two_low,
        gate_up,
        hidden_low,
    )
    return (output, kept_now)


def layer_backward(out_grad, kept_now, own_pos, query_pos, key_pos, weights, heads_total):
    gain_one, bias_all, w_qkv, w_out, gain_two, w_gate_up, w_down = weights
    (
        residual,
        inverse_one,
        normed_low,
        query_group,
        pair_group,
        attended,
        lse_rows,
        out_rows,
        middle,
        inverse_two,
        normed_two_low,
        gate_up,
        hidden_low,
    ) = kept_now
    batch_length = out_grad.shape[0]
    rows_total = out_grad.shape[1]
    per_device = QUERY_HEADS // heads_total
    copy_count = heads_total // KEY_VALUE_HEADS
    branch_low = out_grad.astype(jnp.bfloat16)
    hidden_grad = jnp.einsum("grd,df->grf", branch_low, w_down, preferred_element_type=jnp.float32)
    gate_values = gate_up[..., :FF]
    up_values = gate_up[..., FF:]
    sigmoid_gate = jax.nn.sigmoid(gate_values)
    gate_grad = hidden_grad * up_values * sigmoid_gate * (1.0 + gate_values * (1.0 - sigmoid_gate))
    up_grad = hidden_grad * gate_values * sigmoid_gate
    gate_up_low = jnp.concatenate([gate_grad, up_grad], axis=-1).astype(jnp.bfloat16)
    normed_two_grad = jnp.einsum(
        "grc,dc->grd", gate_up_low, w_gate_up, preferred_element_type=jnp.float32
    )
    middle_part, gain_two_grad = norm_back(
        middle, inverse_two, gain_two.astype(jnp.float32), normed_two_grad
    )
    middle_grad = out_grad + middle_part
    middle_low = middle_grad.astype(jnp.bfloat16)
    out_grad_rows = jnp.einsum(
        "grd,dc->grc", middle_low, w_out, preferred_element_type=jnp.float32
    ).astype(jnp.bfloat16)
    out_grad_rows = out_grad_rows.reshape(
        batch_length, rows_total, heads_total, per_device * HEAD_WIDTH_SIZE
    )
    out_grad_group = lax.all_to_all(out_grad_rows, "head", split_axis=2, concat_axis=1, tiled=True)
    group_rows = out_grad_group.shape[1]
    out_grad_group = out_grad_group.reshape(batch_length, group_rows, per_device, HEAD_WIDTH_SIZE)
    delta_rows = jnp.sum(out_grad_group.astype(jnp.float32) * attended, axis=-1)
    query_grads, key_grads = attend_backward(
        query_group, pair_group, query_pos, key_pos, out_grad_group, lse_rows, delta_rows
    )
    pair_own = lax.psum_scatter(
        key_grads.astype(jnp.bfloat16), "ctx", scatter_dimension=1, tiled=True
    )
    query_send = query_grads.astype(jnp.bfloat16).reshape(
        batch_length, group_rows, 1, per_device * HEAD_WIDTH_SIZE
    )
    query_back, paired_backward = (
        lax.all_to_all(query_send, "head", split_axis=1, concat_axis=2, tiled=True),
        lax.all_to_all(pair_own, "head", split_axis=1, concat_axis=2, tiled=True),
    )
    query_rows = query_back.astype(jnp.float32).reshape(
        batch_length, rows_total, QUERY_HEADS, HEAD_WIDTH_SIZE
    )
    paired_sum = jnp.sum(
        paired_backward.astype(jnp.float32).reshape(
            batch_length, rows_total, KEY_VALUE_HEADS, copy_count, 2 * HEAD_WIDTH_SIZE
        ),
        axis=3,
    )
    cosine_table, sine_table = rope_tables(own_pos, HEAD_WIDTH_SIZE)
    query_pre = unrotate(query_rows, cosine_table, sine_table).reshape(
        batch_length, rows_total, QUERY_HEADS * HEAD_WIDTH_SIZE
    )
    key_pre = unrotate(paired_sum[..., :HEAD_WIDTH_SIZE], cosine_table, sine_table).reshape(
        batch_length, rows_total, KEY_VALUE_HEADS * HEAD_WIDTH_SIZE
    )
    value_before_rotation = paired_sum[..., HEAD_WIDTH_SIZE:].reshape(
        batch_length, rows_total, KEY_VALUE_HEADS * HEAD_WIDTH_SIZE
    )
    projected_low = jnp.concatenate([query_pre, key_pre, value_before_rotation], axis=-1).astype(
        jnp.bfloat16
    )
    bias_grad = jnp.sum(
        projected_low.astype(jnp.float32).reshape(-1, projected_low.shape[-1]), axis=0
    )
    normed_grad = jnp.einsum(
        "grc,dc->grd", projected_low, w_qkv, preferred_element_type=jnp.float32
    )
    input_part, gain_one_grad = norm_back(
        residual, inverse_one, gain_one.astype(jnp.float32), normed_grad
    )
    input_grad = middle_grad + input_part
    pieces = (
        normed_low,
        projected_low,
        middle_low,
        out_rows,
        normed_two_low,
        gate_up_low,
        branch_low,
        hidden_low,
    )
    return (input_grad, pieces, (gain_one_grad, bias_grad, gain_two_grad))


def reduce_block(left_side, columns):
    block_term = jnp.einsum("rd,rc->dc", left_side, columns, preferred_element_type=jnp.float32)
    return lax.psum_scatter(block_term, ("head", "ctx"), scatter_dimension=0, tiled=True)


def local(
    tokens,
    positions,
    norm1_gain,
    qkv_bias,
    qkv_weight,
    out_weight,
    norm2_gain,
    gate_up_weight,
    down_weight,
    cotangent,
):
    heads_total = lax.axis_size("head")
    rank_count = lax.axis_size("ctx")
    batch_count = tokens.shape[0]
    rows_total = tokens.shape[1]
    seq_total = positions.shape[1]
    group_rows = heads_total * rows_total
    section_index = lax.axis_index("section")
    rank_index = lax.axis_index("ctx")
    block_index = lax.axis_index("head") * rank_count + rank_index
    ordered = (
        positions.reshape(batch_count, heads_total, rank_count, rows_total)
        .transpose(0, 2, 1, 3)
        .reshape(batch_count, seq_total)
    )
    group_count = batch_count // batch_count
    tick_count = group_count + 1

    def positions_for(group_index):
        first_row = group_index * batch_count
        own_pos = lax.dynamic_slice(
            positions, (first_row, block_index * rows_total), (batch_count, rows_total)
        )
        query_pos = lax.dynamic_slice_in_dim(ordered, rank_index * group_rows, group_rows, 1)
        return (own_pos, query_pos, ordered)

    shards = (norm1_gain, qkv_bias, qkv_weight, out_weight, norm2_gain, gate_up_weight, down_weight)
    weights = tuple(
        (
            shard_value[0]
            for shard_value in (
                lax.all_gather(shards[0], ("head", "ctx"), axis=1, tiled=True),
                lax.all_gather(shards[1], ("head", "ctx"), axis=1, tiled=True),
                lax.all_gather(shards[2], ("head", "ctx"), axis=1, tiled=True),
                lax.all_gather(shards[3], ("head", "ctx"), axis=1, tiled=True),
                lax.all_gather(shards[4], ("head", "ctx"), axis=1, tiled=True),
                lax.all_gather(shards[5], ("head", "ctx"), axis=1, tiled=True),
                lax.all_gather(shards[6], ("head", "ctx"), axis=1, tiled=True),
            )
        )
    )
    received = jnp.zeros((batch_count, rows_total, tokens.shape[2]), jnp.bfloat16)
    outputs = []
    kept_list = []
    for tick_now in range(tick_count):
        first_row = min(tick_now, group_count - 1) * batch_count
        inputs = jnp.where(section_index == 0, tokens, received)
        own_pos, query_pos, key_pos = positions_for(
            jnp.clip(tick_now - section_index, 0, group_count - 1)
        )
        result, kept_now = layer_forward(inputs, own_pos, query_pos, key_pos, weights, heads_total)
        result_low = result.astype(jnp.bfloat16)
        outputs.append(result_low)
        kept_list.append(kept_now)
        if tick_now + 1 < tick_count:
            received = from_behind(result_low, "section", 1)
    received = jnp.zeros((batch_count, rows_total, tokens.shape[2]), jnp.bfloat16)
    grads_in = []
    piece_list = []
    small_sums = None
    for tick_now in range(tick_count):
        first_row = min(tick_now, group_count - 1) * batch_count
        incoming = jnp.where(section_index == 1, cotangent, received).astype(jnp.float32)
        kept_now = pick(
            section_index == 0,
            kept_list[max(tick_now - 1, 0)],
            kept_list[min(tick_now + 1, tick_count - 1)],
        )
        group_number = tick_now - 1 + section_index
        own_pos, query_pos, key_pos = positions_for(jnp.clip(group_number, 0, group_count - 1))
        input_grad, pieces, smalls = layer_backward(
            incoming, kept_now, own_pos, query_pos, key_pos, weights, heads_total
        )
        valid_flag = jnp.logical_and(group_number >= 0, group_number < group_count)
        smalls = tuple((jnp.where(valid_flag, entry_value, 0.0) for entry_value in smalls))
        if small_sums is None:
            small_sums = smalls
        else:
            small_sums = tuple(
                (left_side + right_side for left_side, right_side in zip(small_sums, smalls))
            )
        grad_low = input_grad.astype(jnp.bfloat16)
        grads_in.append(grad_low)
        piece_list.append(pieces)
        if tick_now + 1 < tick_count:
            received = from_behind(grad_low, "section", -1)
    activations = jnp.where(section_index == 0, outputs[0], outputs[1])[None]
    input_grads = jnp.where(section_index == 0, grads_in[1], grads_in[0])[None]
    chosen = [pick(section_index == 0, piece_list[1], piece_list[0])]
    merged = tuple(
        (
            jnp.concatenate([chosen_set[slot_number] for chosen_set in chosen], axis=0).reshape(
                batch_count * rows_total, -1
            )
            for slot_number in range(8)
        )
    )
    (
        normed_all,
        projected_all,
        middle_all,
        attn_all,
        normed_two_all,
        gate_up_all,
        branch_all,
        hidden_all,
    ) = merged
    pair_list = (
        (normed_all, projected_all),
        (middle_all, attn_all),
        (normed_two_all, gate_up_all),
        (branch_all, hidden_all),
    )
    share_list = []
    for left_side, right_side in pair_list:
        width_total = right_side.shape[1]
        piece_count = width_total // 4480 if width_total % 4480 == 0 else 1
        piece_width = width_total // piece_count
        piece_shares = []
        for piece_number in range(piece_count):
            columns = right_side[:, piece_number * piece_width : (piece_number + 1) * piece_width]
            piece_shares.append(reduce_block(left_side, columns))
        share_list.append(jnp.concatenate(piece_shares, axis=1)[None])
    qkv_weight_grad, out_weight_grad, gate_up_grad, down_grad = share_list
    split_width = (QUERY_HEADS + KEY_VALUE_HEADS) * HEAD_WIDTH_SIZE
    bias_sum = small_sums[1]
    gain_one_share, query_key_share, value_share, gain_two_share = (
        lax.psum_scatter(small_sums[0][None], ("head", "ctx"), scatter_dimension=1, tiled=True),
        lax.psum_scatter(
            bias_sum[None, :split_width], ("head", "ctx"), scatter_dimension=1, tiled=True
        ),
        lax.psum_scatter(
            bias_sum[None, split_width:], ("head", "ctx"), scatter_dimension=1, tiled=True
        ),
        lax.psum_scatter(small_sums[2][None], ("head", "ctx"), scatter_dimension=1, tiled=True),
    )
    return (
        activations,
        input_grads,
        gain_one_share,
        query_key_share,
        value_share,
        qkv_weight_grad,
        out_weight_grad,
        gain_two_share,
        gate_up_grad,
        down_grad,
    )


MESH_ID = pl.DeviceIdType.MESH
BF = jnp.bfloat16
F32 = jnp.float32
LANES = 128
HB = 128
VMEM_LIMIT = 60 * 1024 * 1024
DMA = pltpu.SemaphoreType.DMA
NT = (((1,), (1,)), ((), ()))
TN = (((0,), (0,)), ((), ()))
NN = (((1,), (0,)), ((), ()))


def mm(left_side, right_side, form=NN):
    return lax.dot_general(left_side, right_side, form, preferred_element_type=F32)


def where_am_i():
    head = lax.axis_index("head")
    return (lax.axis_index("section"), head // 2, lax.rem(head, 2), lax.axis_index("ctx"))


def at(x, y, k, z):
    return (x, y * 2 + k, z)


def remote(source, target, send_sem, recv_sem, device):
    return pltpu.make_async_remote_copy(
        src_ref=source,
        dst_ref=target,
        send_sem=send_sem,
        recv_sem=recv_sem,
        device_id=device,
        device_id_type=MESH_ID,
    )


def arrived(ref, sem):
    pltpu.make_async_copy(ref, ref, sem).wait()


def greet(devices):
    barrier = pltpu.get_barrier_semaphore()
    for device in devices:
        pl.semaphore_signal(barrier, inc=1, device_id=device, device_id_type=MESH_ID)
    pl.semaphore_wait(barrier, len(devices))


def greet_all(index, total, device_of):
    barrier = pltpu.get_barrier_semaphore()

    @pl.loop(1, total)
    def _(step):
        device = device_of(lax.rem(index + step, total))
        pl.semaphore_signal(barrier, inc=1, device_id=device, device_id_type=MESH_ID)

    pl.semaphore_wait(barrier, total - 1)


def params(collective_id):
    return pltpu.CompilerParams(
        collective_id=collective_id, has_side_effects=True, vmem_limit_bytes=VMEM_LIMIT
    )


def vmem():
    return pl.BlockSpec(memory_space=pltpu.VMEM)


def hbm():
    return pl.BlockSpec(memory_space=pl.ANY)


def row_norm(values):
    return lax.rsqrt(jnp.mean(values * values, axis=-1, keepdims=True) + EPSILON)


class Sizes:
    def __init__(self, mesh, tokens, qkv_weight, gate_up, down):
        self.ctx = mesh.shape["ctx"]
        self.group = 4 * self.ctx
        self.total = 2 * self.group
        self.batches, self.seq, self.width = tokens.shape
        self.rows = self.seq // self.group
        self.ff = down.shape[2]
        self.owned = self.width // self.group
        self.blocks = self.ff // HB
        self.most = -(-self.blocks // self.total)
        self.least = self.blocks // self.total
        self.extra = self.blocks % self.total
        self.hidden = self.most * HB
        self.per_group = QUERY_HEADS // 4
        self.qcols = self.per_group * HEAD_WIDTH_SIZE
        self.kcols = HEAD_WIDTH_SIZE
        self.acols = self.qcols + 2 * self.kcols
        self.atot = self.acols + self.qcols

    def fits(self):
        gathered = self.batches * self.seq * self.width * 2
        return (
            self.batches == 2
            and gathered * 3 < VMEM_LIMIT // 2
            and self.ff % HB == 0
            and self.least >= 1
            and self.owned % 16 == 0
            and self.rows % 32 == 0
        )


def flat_place(index, group, ctx):
    inside = lax.rem(index, group)
    return (index // group, inside // ctx, lax.rem(inside, ctx))


def first_column(sz, owner):
    return pl.multiple_of((owner * sz.least + jnp.minimum(owner, sz.extra)) * HB, HB)


def spread_kernel(
    sz,
    small,
    tokens,
    cotangent,
    qkv,
    out_w,
    gate_up,
    down,
    small_all,
    tok_own,
    cot_own,
    att_all,
    w_all,
    zeros,
    s_small,
    r_small,
    s_own,
    r_own,
    s_att,
    r_att,
    s_fwd,
    r_fwd,
    s_mlp,
    r_mlp,
    z_sem,
):
    n = sz.ctx
    x, y, k, z = where_am_i()
    me = x * sz.group + (y * 2 + k) * n + z
    row = pl.multiple_of(((y * 2 + k) * n + z) * sz.owned, 16)
    rows = pl.ds(row, sz.owned)
    place = lambda index: flat_place(index, sz.group, n)
    greet_all(me, sz.total, place)

    @pl.loop(1, sz.total)
    def _(step):
        remote(small, small_all.at[me], s_small, r_small, place(lax.rem(me + step, sz.total))).start()

    pltpu.make_async_copy(small, small_all.at[me], s_small).start()

    def owns(begin):
        @pl.when(x == y)
        def _():
            for batch in range(2):
                pairs = ((tokens, tok_own, 0), (cotangent, cot_own, 1))
                for source, target, slot in pairs:
                    own = jnp.logical_and(k == y, k == batch)

                    @pl.when(jnp.logical_not(own))
                    def _():
                        copy = remote(
                            source.at[batch],
                            target,
                            s_own.at[batch, slot],
                            r_own.at[slot],
                            at(x, k, batch, z),
                        )
                        copy.start() if begin else copy.wait_send()

                    if begin:

                        @pl.when(own)
                        def _():
                            pltpu.make_async_copy(source.at[batch], target, r_own.at[slot]).start()

    owns(True)

    mine = (2 * x + y) * n + z

    def att_parts(g):
        kv = g // (4 // KEY_VALUE_HEADS)
        q0 = pl.multiple_of(g * sz.qcols, HB)
        k0 = pl.multiple_of(QUERY_HEADS * HEAD_WIDTH_SIZE + kv * sz.kcols, HB)
        v0 = pl.multiple_of((QUERY_HEADS + KEY_VALUE_HEADS) * HEAD_WIDTH_SIZE + kv * sz.kcols, HB)
        return (
            (qkv.at[:, pl.ds(q0, sz.qcols)], att_all.at[x, rows, pl.ds(0, sz.qcols)]),
            (qkv.at[:, pl.ds(k0, sz.kcols)], att_all.at[x, rows, pl.ds(sz.qcols, sz.kcols)]),
            (
                qkv.at[:, pl.ds(v0, sz.kcols)],
                att_all.at[x, rows, pl.ds(sz.qcols + sz.kcols, sz.kcols)],
            ),
            (out_w.at[:, pl.ds(q0, sz.qcols)], att_all.at[x, rows, pl.ds(sz.acols, sz.qcols)]),
        )

    @pl.loop(1, sz.group)
    def _(step):
        index = lax.rem(mine + step, sz.group)
        g = index // n
        for source, target in att_parts(g):
            remote(
                source, target, s_att, r_att.at[x], at(g // 2, lax.rem(g, 2), k, lax.rem(index, n))
            ).start()

    for source, target in att_parts(2 * x + y):
        pltpu.make_async_copy(source, target, s_att).start()

    wide = sz.least * HB

    def moves(owner, offset, width):
        first = pl.multiple_of(first_column(sz, owner) + offset, HB)
        up_first = pl.multiple_of(sz.ff + first, HB)
        cols = pl.ds(offset, width)
        return (
            (gate_up.at[:, pl.ds(first, width)], w_all.at[x, 0, rows, cols]),
            (gate_up.at[:, pl.ds(up_first, width)], w_all.at[x, 1, rows, cols]),
            (down.at[:, pl.ds(first, width)], w_all.at[x, 2, rows, cols]),
        )

    @pl.loop(1, sz.total)
    def _(step):
        owner = lax.rem(me + step, sz.total)
        for source, target in moves(owner, 0, wide):
            remote(source, target, s_mlp.at[0], r_mlp.at[x, 0], place(owner)).start()
        if sz.extra:

            @pl.when(owner < sz.extra)
            def _():
                for source, target in moves(owner, wide, HB):
                    remote(source, target, s_mlp.at[1], r_mlp.at[x, 1], place(owner)).start()

    for source, target in moves(me, 0, wide):
        pltpu.make_async_copy(source, target, s_mlp.at[0]).start()
    if sz.extra:

        @pl.when(me < sz.extra)
        def _():
            for source, target in moves(me, wide, HB):
                pltpu.make_async_copy(source, target, s_mlp.at[1]).start()

        @pl.when(me >= sz.extra)
        def _():
            zeros[...] = jnp.zeros_like(zeros)
            empty = [
                pltpu.make_async_copy(
                    zeros, w_all.at[section, part, :, pl.ds(wide, HB)], z_sem.at[section, part]
                )
                for section in range(2)
                for part in range(3)
            ]
            for copy in empty:
                copy.start()
            for copy in empty:
                copy.wait()

    half = sz.width // 2
    stretch = sz.width // 4
    for section in range(2):
        for same in (True, False):

            @pl.when((x == section) == same)
            def _():
                count = half - sz.owned if same else half
                arrived(att_all.at[section, pl.ds(0, count)], r_att.at[section])

    arrived(att_all.at[0], s_att)
    for section in range(2):
        for part in range(2):
            span = att_all.at[
                section, pl.ds(pl.multiple_of((part * 2 + k) * stretch, 16), stretch)
            ]
            remote(span, span, s_fwd.at[section, part], r_fwd.at[section, part], at(x, y, 1 - k, z)).start()
    arrived(small_all.at[pl.ds(0, sz.total - 1)], r_small)
    arrived(small_all, s_small)
    arrived(tok_own, r_own.at[0])
    arrived(cot_own, r_own.at[1])
    for section in range(2):
        for part in range(2):
            span = att_all.at[
                section, pl.ds(pl.multiple_of((part * 2 + 1 - k) * stretch, 16), stretch)
            ]
            arrived(span, r_fwd.at[section, part])
            arrived(span, s_fwd.at[section, part])
    for section in range(2):
        for same in (True, False):

            @pl.when((x == section) == same)
            def _():
                count = sz.width - sz.owned if same else sz.width
                arrived(w_all.at[section, :, pl.ds(0, count), pl.ds(0, wide)], r_mlp.at[section, 0])
                if sz.extra:

                    @pl.when(me < sz.extra)
                    def _():
                        arrived(
                            w_all.at[section, :, pl.ds(0, count), pl.ds(0, HB)], r_mlp.at[section, 1]
                        )

    owns(False)
    arrived(w_all.at[:, :, :, pl.ds(0, wide)], s_mlp.at[0])
    if sz.extra:
        arrived(w_all.at[0, :, pl.ds(0, sz.extra * sz.owned), pl.ds(0, HB)], s_mlp.at[1])


def spread(sz, small, tokens, cotangent, qkv, out_w, gate_up, down):
    shapes = (
        jax.ShapeDtypeStruct((sz.total, 16, LANES), BF),
        jax.ShapeDtypeStruct((sz.rows, sz.width), BF),
        jax.ShapeDtypeStruct((sz.rows, sz.width), BF),
        jax.ShapeDtypeStruct((2, sz.width, sz.atot), BF),
        jax.ShapeDtypeStruct((2, 3, sz.width, sz.hidden), BF),
    )
    return pl.pallas_call(
        functools.partial(spread_kernel, sz),
        out_shape=shapes,
        in_specs=[hbm()] * 7,
        out_specs=[hbm()] * 5,
        scratch_shapes=[
            pltpu.VMEM((sz.width, HB), BF),
            DMA,
            DMA,
            DMA((2, 2)),
            DMA((2,)),
            DMA,
            DMA((2,)),
            DMA((2, 2)),
            DMA((2, 2)),
            DMA((2,)),
            DMA((2, 2)),
            DMA((2, 3)),
        ],
        compiler_params=params(1),
        name="spread_weights",
    )(small, tokens, cotangent, qkv, out_w, gate_up, down)


def collect_kernel(
    sz,
    dw0,
    dw1,
    da0,
    da1,
    small,
    act0,
    act1,
    grad0,
    grad1,
    w_in,
    att_in,
    small_in,
    act_out,
    grad_out,
    got,
    summed,
    s_core,
    r_core,
    s_mlp,
    r_mlp,
    s_att,
    r_att,
    s_small,
    r_small,
    s_out,
    r_out,
):
    n = sz.ctx
    x, y, k, z = where_am_i()
    me = x * sz.group + (y * 2 + k) * n + z
    place = lambda index: flat_place(index, sz.group, n)
    greet_all(me, sz.total, place)
    stretch = sz.width // 4
    wide = sz.least * HB

    def exchange(section, part):
        source = (da0, da1)[section]
        span = source.at[pl.ds(pl.multiple_of((part * 2 + 1 - k) * stretch, 16), stretch)]
        return remote(
            span,
            got.at[section, part],
            s_core.at[section, part],
            r_core.at[section, part],
            at(x, y, 1 - k, z),
        )

    for section in (1, 0):
        for part in range(2):
            exchange(section, part).start()

    def outs(begin):
        for section in range(2):
            for slot, (source, target) in enumerate(
                (((act0, act1)[section], act_out), ((grad0, grad1)[section], grad_out))
            ):
                own = jnp.logical_and(x == section, jnp.logical_and(x == y, y == k))

                @pl.when(jnp.logical_not(own))
                def _():
                    copy = remote(
                        source,
                        target.at[k],
                        s_out.at[section, slot],
                        r_out.at[slot, k],
                        at(section, x, y, z),
                    )
                    copy.start() if begin else copy.wait_send()

                if begin:

                    @pl.when(own)
                    def _():
                        pltpu.make_async_copy(source, target.at[k], r_out.at[slot, k]).start()

    outs(True)

    cols = pl.ds(first_column(sz, me), wide)
    more = pl.ds(pl.multiple_of(first_column(sz, me) + wide, HB), HB)

    def block(device, op):
        inside = lax.rem(device, sz.group)
        rows = pl.ds(pl.multiple_of(inside * sz.owned, 16), sz.owned)
        for section, source in enumerate((dw0, dw1)):

            @pl.when(device // sz.group == section)
            def _():
                op(source.at[:, rows, pl.ds(0, wide)], w_in.at[:, :, cols], 0)
                if sz.extra:

                    @pl.when(me < sz.extra)
                    def _():
                        op(source.at[:, rows, pl.ds(wide, HB)], w_in.at[:, :, more], 1)

    @pl.loop(1, sz.total)
    def _(step):
        device = lax.rem(me + step, sz.total)
        remote(
            small.at[device], small_in.at[me], s_small, r_small, place(device)
        ).start()
        block(
            device,
            lambda source, target, kind: remote(
                source, target, s_mlp.at[kind], r_mlp.at[kind], place(device)
            ).start(),
        )

    pltpu.make_async_copy(small.at[me], small_in.at[me], s_small).start()
    block(
        me,
        lambda source, target, kind: pltpu.make_async_copy(source, target, s_mlp.at[kind]).start(),
    )

    for section in (1, 0):
        for part in range(2):
            exchange(section, part).wait_recv()
            source = (da0, da1)[section]
            rows = pl.ds(pl.multiple_of((part * 2 + k) * stretch, 16), stretch)
            summed[section, part] = (
                source[rows].astype(F32) + got[section, part].astype(F32)
            ).astype(BF)

    mine = (2 * x + y) * n + z

    def att_pair(index):
        section, part, ctx = (index // (2 * n), lax.rem(index // n, 2), lax.rem(index, n))
        source = summed.at[
            section, part, pl.ds(pl.multiple_of(ctx * sz.owned, 16), sz.owned)
        ]
        return (source, att_in.at[mine], at(section, part, k, ctx))

    @pl.loop(1, sz.group)
    def _(step):
        source, target, device = att_pair(lax.rem(mine + step, sz.group))
        remote(source, target, s_att, r_att, device).start()

    source, target, _ = att_pair(mine)
    pltpu.make_async_copy(source, target, s_att).start()

    for section in range(2):
        for part in range(2):
            exchange(section, part).wait_send()
    outs(False)
    for slot, target in enumerate((act_out, grad_out)):
        for batch in range(2):
            arrived(target.at[batch], r_out.at[slot, batch])
    arrived(small_in.at[pl.ds(0, sz.total - 1)], r_small)
    arrived(small_in, s_small)
    arrived(att_in.at[pl.ds(0, sz.group - 1)], r_att)
    arrived(att_in, s_att)
    arrived(w_in.at[:, :, pl.ds(0, (sz.total - 1) * wide)], r_mlp.at[0])
    arrived(w_in.at[:, :, pl.ds(0, sz.total * wide)], s_mlp.at[0])
    if sz.extra:

        @pl.when(me < sz.extra)
        def _():
            if sz.extra > 1:
                arrived(w_in.at[:, :, pl.ds(0, (sz.extra - 1) * HB)], r_mlp.at[1])
            arrived(w_in.at[:, :, pl.ds(0, sz.total * HB)], s_mlp.at[1])

        @pl.when(me >= sz.extra)
        def _():
            arrived(w_in.at[:, :, pl.ds(0, sz.extra * HB)], r_mlp.at[1])


def collect(sz, dw, da, small, acts, grads):
    stretch = sz.width // 4
    shapes = (
        jax.ShapeDtypeStruct((3, sz.owned, sz.ff), BF),
        jax.ShapeDtypeStruct((sz.group, sz.owned, sz.atot), BF),
        jax.ShapeDtypeStruct((sz.total, 8, LANES), F32),
        jax.ShapeDtypeStruct((2, sz.rows, sz.width), BF),
        jax.ShapeDtypeStruct((2, sz.rows, sz.width), BF),
    )
    return pl.pallas_call(
        functools.partial(collect_kernel, sz),
        out_shape=shapes,
        in_specs=[hbm()] * 2 + [vmem()] * 2 + [hbm()] * 5,
        out_specs=[hbm()] * 5,
        scratch_shapes=[
            pltpu.VMEM((2, 2, stretch, sz.atot), BF),
            pltpu.VMEM((2, 2, stretch, sz.atot), BF),
            DMA((2, 2)),
            DMA((2, 2)),
            DMA((2,)),
            DMA((2,)),
            DMA,
            DMA,
            DMA,
            DMA,
            DMA((2, 2)),
            DMA((2, 2)),
        ],
        compiler_params=params(2),
        name="collect_gradients",
    )(dw[0], dw[1], da[0], da[1], small, *acts, *grads)


def half_turn(values):
    return pltpu.roll(values, HEAD_WIDTH_SIZE // 2, 1)


def pair_peers(x, y, k, z):
    return (at(1 - x, y, k, z), at(x, 1 - y, k, z), at(1 - x, 1 - y, k, z))


def pair_groups(x, y):
    return (2 * (1 - x) + y, 2 * x + 1 - y, 2 * (1 - x) + 1 - y)


def line_peers(n, x, y, k, z):
    return [at(x, y, k, lax.rem(z + step, n)) for step in range(1, n)]


def gather_pair(buffer, place, send, recv):
    x, y, k, z = place
    own = buffer.at[2 * x + y]
    copies = [
        remote(own, own, send.at[i], recv.at[i], device)
        for i, device in enumerate(pair_peers(x, y, k, z))
    ]
    for copy in copies:
        copy.start()
    return copies


def gathered_pair(buffer, place, copies, recv):
    x, y, k, z = place
    for i, group in enumerate(pair_groups(x, y)):
        arrived(buffer.at[group], recv.at[i])


def scatter_pair(parts, landed, place, send, recv):
    x, y, k, z = place
    groups = pair_groups(x, y)
    copies = [
        remote(parts.at[groups[i]], landed.at[i], send.at[i], recv.at[i], device)
        for i, device in enumerate(pair_peers(x, y, k, z))
    ]
    for copy in copies:
        copy.start()
    return copies


def attend_kernel(
    sz,
    section,
    x_ref,
    gain,
    bias,
    watt,
    cosine,
    sine,
    qpos,
    kpos,
    h1_out,
    n1_all,
    q_out,
    kv_all,
    o_out,
    lse_out,
    w,
    parts,
    landed,
    w_sem,
    s_in,
    r_in,
    s_kv,
    r_kv,
    s_back,
    r_back,
):
    n = sz.ctx
    place = where_am_i()
    x, y, k, z = place
    load = pltpu.make_async_copy(watt.at[section], w, w_sem)
    load.start()
    greet(list(pair_peers(x, y, k, z)) + line_peers(n, x, y, k, z))
    group = 2 * x + y
    values = x_ref[...].astype(F32)
    n1_all[group] = (values * row_norm(values) * gain[...]).astype(BF)
    copies = gather_pair(n1_all, place, s_in, r_in)
    load.wait()
    gathered_pair(n1_all, place, copies, r_in)
    rows = 4 * sz.rows
    normed = n1_all[...].reshape(rows, sz.width)
    kv = mm(normed, w[:, sz.qcols : sz.acols]) + bias[:, sz.qcols : sz.acols]
    cos, sin = cosine[...], sine[...]
    key = kv[:, : sz.kcols]
    kv_all[z, :, : sz.kcols] = (key * cos + half_turn(key) * sin).astype(BF)
    kv_all[z, :, sz.kcols :] = kv[:, sz.kcols :].astype(BF)
    kv_copies = []
    for step, device in enumerate(line_peers(n, x, y, k, z)):
        own = kv_all.at[z]
        kv_copies.append(remote(own, own, s_kv.at[step], r_kv.at[step], device))
        kv_copies[-1].start()
    queries = mm(normed, w[:, : sz.qcols]) + bias[:, : sz.qcols]
    for head in range(sz.per_group):
        cols = slice(head * HEAD_WIDTH_SIZE, (head + 1) * HEAD_WIDTH_SIZE)
        query = queries[:, cols]
        q_out[:, cols] = (query * cos + half_turn(query) * sin).astype(BF)
    for step in range(n - 1):
        arrived(kv_all.at[lax.rem(z + n - 1 - step, n)], r_kv.at[step])
    keys = kv_all[:, :, : sz.kcols].reshape(n * rows, sz.kcols)
    vals = kv_all[:, :, sz.kcols :].reshape(n * rows, sz.kcols)
    allowed = kpos[...] <= qpos[...]
    scale = 1.0 / math.sqrt(HEAD_WIDTH_SIZE)
    for head in range(sz.per_group):
        cols = slice(head * HEAD_WIDTH_SIZE, (head + 1) * HEAD_WIDTH_SIZE)
        scores = jnp.where(allowed, mm(q_out[:, cols], keys, NT) * scale, -1e30)
        highest = jnp.max(scores, axis=-1, keepdims=True)
        weights = jnp.exp(scores - highest)
        total = jnp.sum(weights, axis=-1, keepdims=True)
        o_out[:, cols] = mm(weights.astype(BF), vals) / total
        lse_out[head] = jnp.broadcast_to(highest + jnp.log(total), (rows, LANES))
    partial = mm(o_out[...].astype(BF), w[:, sz.acols :], NT)
    parts[...] = partial.astype(BF).reshape(4, sz.rows, sz.width)
    back = scatter_pair(parts, landed, place, s_back, r_back)
    for copy in copies + kv_copies:
        copy.wait_send()
    out = values + parts[group].astype(F32)
    for i in range(3):
        back[i].wait_recv()
        out = out + landed[i].astype(F32)
    h1_out[...] = out
    for copy in back:
        copy.wait_send()


def attend(sz, section, x_own, gain, bias, watt, tables, qpos, kpos):
    n, rows = sz.ctx, 4 * sz.rows
    shapes = (
        jax.ShapeDtypeStruct((sz.rows, sz.width), F32),
        jax.ShapeDtypeStruct((4, sz.rows, sz.width), BF),
        jax.ShapeDtypeStruct((rows, sz.qcols), BF),
        jax.ShapeDtypeStruct((n, rows, 2 * sz.kcols), BF),
        jax.ShapeDtypeStruct((rows, sz.qcols), F32),
        jax.ShapeDtypeStruct((sz.per_group, rows, LANES), F32),
    )
    return pl.pallas_call(
        functools.partial(attend_kernel, sz, section),
        out_shape=shapes,
        in_specs=[vmem()] * 3 + [hbm()] + [vmem()] * 4,
        out_specs=[vmem()] * 6,
        scratch_shapes=[
            pltpu.VMEM((sz.width, sz.atot), BF),
            pltpu.VMEM((4, sz.rows, sz.width), BF),
            pltpu.VMEM((3, sz.rows, sz.width), BF),
            DMA,
            DMA((3,)),
            DMA((3,)),
            DMA((n,)),
            DMA((n,)),
            DMA((3,)),
            DMA((3,)),
        ],
        compiler_params=params(3 + section),
        name="attend_forward",
    )(x_own, gain, bias, watt, *tables, qpos, kpos)


def attend_back_kernel(
    sz,
    section,
    dh1,
    x_ref,
    gain,
    watt,
    cosine,
    sine,
    qpos,
    kpos,
    n1_all,
    q_in,
    kv_all,
    o_in,
    lse_in,
    dx_out,
    dw_out,
    gain_grad,
    bias_grad,
    w,
    dh_all,
    dkv,
    dkv_in,
    da,
    parts,
    landed,
    w_sem,
    s_in,
    r_in,
    s_kv,
    r_kv,
    s_back,
    r_back,
):
    n = sz.ctx
    place = where_am_i()
    x, y, k, z = place
    load = pltpu.make_async_copy(watt.at[section], w, w_sem)
    load.start()
    greet(list(pair_peers(x, y, k, z)) + line_peers(n, x, y, k, z))
    group = 2 * x + y
    rows = 4 * sz.rows
    dh_all[group] = dh1[...].astype(BF)
    copies = gather_pair(dh_all, place, s_in, r_in)
    load.wait()
    gathered_pair(dh_all, place, copies, r_in)
    dh = dh_all[...].reshape(rows, sz.width)
    dout = mm(dh, w[:, sz.acols :]).astype(BF)
    keys = kv_all[:, :, : sz.kcols].reshape(n * rows, sz.kcols)
    vals = kv_all[:, :, sz.kcols :].reshape(n * rows, sz.kcols)
    allowed = kpos[...] <= qpos[...]
    scale = 1.0 / math.sqrt(HEAD_WIDTH_SIZE)
    cos, sin = cosine[...], sine[...]
    dkeys, dvals = None, None
    for head in range(sz.per_group):
        cols = slice(head * HEAD_WIDTH_SIZE, (head + 1) * HEAD_WIDTH_SIZE)
        query, grad = q_in[:, cols], dout[:, cols]
        delta = jnp.sum(grad.astype(F32) * o_in[:, cols], axis=-1, keepdims=True)
        scores = mm(query, keys, NT) * scale
        probs = jnp.where(allowed, jnp.exp(scores - lse_in[head][:, :1]), 0.0)
        dscores = (probs * (mm(grad, vals, NT) - delta)).astype(BF)
        dquery = (mm(dscores, keys) * scale).astype(BF).astype(F32)
        da[:, cols] = (dquery * cos - half_turn(dquery) * sin).astype(BF)
        one_key = mm(dscores, query, TN)
        one_val = mm(probs.astype(BF), grad, TN)
        dkeys = one_key if dkeys is None else dkeys + one_key
        dvals = one_val if dvals is None else dvals + one_val
    dkv[:, :, : sz.kcols] = (dkeys * scale).astype(BF).reshape(n, rows, sz.kcols)
    dkv[:, :, sz.kcols :] = dvals.astype(BF).reshape(n, rows, sz.kcols)
    kv_copies = []
    for step, device in enumerate(line_peers(n, x, y, k, z)):
        kv_copies.append(
            remote(
                dkv.at[lax.rem(z + 1 + step, n)],
                dkv_in.at[step],
                s_kv.at[step],
                r_kv.at[step],
                device,
            )
        )
        kv_copies[-1].start()
    dw_out[:, sz.acols :] = mm(dh, o_in[...].astype(BF), TN).astype(BF)
    total = dkv[z].astype(F32)
    for step in range(n - 1):
        kv_copies[step].wait_recv()
        total = total + dkv_in[step].astype(F32)
    dkey = total[:, : sz.kcols]
    da[:, sz.qcols : sz.qcols + sz.kcols] = (dkey * cos - half_turn(dkey) * sin).astype(BF)
    da[:, sz.qcols + sz.kcols :] = total[:, sz.kcols :].astype(BF)
    parts[...] = mm(da[...], w[:, : sz.acols], NT).astype(BF).reshape(4, sz.rows, sz.width)
    back = scatter_pair(parts, landed, place, s_back, r_back)
    dw_out[:, : sz.acols] = mm(n1_all[...].reshape(rows, sz.width), da[...], TN).astype(BF)
    bias_grad[...] = jnp.sum(da[...].astype(F32), axis=0, keepdims=True)
    for copy in copies + kv_copies:
        copy.wait_send()
    dn1 = parts[group].astype(F32)
    for i in range(3):
        back[i].wait_recv()
        dn1 = dn1 + landed[i].astype(F32)
    values = x_ref[...].astype(F32)
    inverse = row_norm(values)
    weighted = dn1 * gain[...]
    inner = jnp.mean(weighted * values, axis=-1, keepdims=True)
    dx = dh1[...] + inverse * weighted - values * (inverse * inverse * inverse) * inner
    dx_out[...] = dx.astype(BF)
    gain_grad[...] = jnp.sum(dn1 * values * inverse, axis=0, keepdims=True)
    for copy in back:
        copy.wait_send()


def attend_back(sz, section, dh1, x_own, gain, watt, tables, qpos, kpos, kept):
    n, rows = sz.ctx, 4 * sz.rows
    shapes = (
        jax.ShapeDtypeStruct((sz.rows, sz.width), BF),
        jax.ShapeDtypeStruct((sz.width, sz.atot), BF),
        jax.ShapeDtypeStruct((1, sz.width), F32),
        jax.ShapeDtypeStruct((1, sz.acols), F32),
    )
    return pl.pallas_call(
        functools.partial(attend_back_kernel, sz, section),
        out_shape=shapes,
        in_specs=[vmem()] * 3 + [hbm()] + [vmem()] * 9,
        out_specs=[vmem()] * 4,
        scratch_shapes=[
            pltpu.VMEM((sz.width, sz.atot), BF),
            pltpu.VMEM((4, sz.rows, sz.width), BF),
            pltpu.VMEM((n, rows, 2 * sz.kcols), BF),
            pltpu.VMEM((n, rows, 2 * sz.kcols), BF),
            pltpu.VMEM((rows, sz.acols), BF),
            pltpu.VMEM((4, sz.rows, sz.width), BF),
            pltpu.VMEM((3, sz.rows, sz.width), BF),
            DMA,
            DMA((3,)),
            DMA((3,)),
            DMA((n,)),
            DMA((n,)),
            DMA((3,)),
            DMA((3,)),
        ],
        compiler_params=params(5 + section),
        name="attend_backward",
    )(dh1, x_own, gain, watt, *tables, qpos, kpos, *kept)


def tree_peers(n, x, y, k, z):
    return [at(1 - x, y, k, z), at(x, 1 - y, k, z), at(x, y, 1 - k, z)] + line_peers(n, x, y, k, z)


class Gather:
    SEMS = 12

    @staticmethod
    def scratch(n):
        return [DMA((n,))] * 10 + [DMA((4, n))] * 2

    def __init__(self, n, rows, buffer, place, sems):
        self.n, self.half, self.buffer = n, rows // 2, buffer
        self.x, self.y, self.k, self.z = place
        x, y = self.x, self.y
        self.groups = (2 * x + y, 2 * x + 1 - y, 2 * (1 - x) + y, 2 * (1 - x) + 1 - y)
        (
            self.sz,
            self.rz,
            self.sy,
            self.ry,
            self.sx,
            self.rx,
            self.syd,
            self.ryd,
            self.sxd,
            self.rxd,
            self.sc,
            self.rc,
        ) = sems

    def src(self, step):
        return lax.rem(self.z + self.n - step, self.n)

    def line(self, step):
        own = self.buffer.at[self.k, self.groups[0], self.z]
        device = at(self.x, self.y, self.k, lax.rem(self.z + step, self.n))
        return remote(own, own, self.sz.at[step], self.rz.at[step], device)

    def to_y(self, step):
        part = self.buffer.at[self.k, self.groups[0], self.src(step)]
        device = at(self.x, 1 - self.y, self.k, self.z)
        return remote(part, part, self.sy.at[step], self.ry.at[step], device)

    def to_x(self, step):
        part = self.buffer.at[self.k, self.groups[0], self.src(step)]
        device = at(1 - self.x, self.y, self.k, self.z)
        return remote(part, part, self.sx.at[step], self.rx.at[step], device)

    def on_x(self, step):
        part = self.buffer.at[self.k, self.groups[1], self.src(step), pl.ds(0, self.half)]
        device = at(1 - self.x, self.y, self.k, self.z)
        return remote(part, part, self.sxd.at[step], self.rxd.at[step], device)

    def on_y(self, step):
        part = self.buffer.at[self.k, self.groups[2], self.src(step), pl.ds(self.half, self.half)]
        device = at(self.x, 1 - self.y, self.k, self.z)
        return remote(part, part, self.syd.at[step], self.ryd.at[step], device)

    def core(self, which, step):
        part = self.buffer.at[self.k, self.groups[which], self.src(step)]
        device = at(self.x, self.y, 1 - self.k, self.z)
        return remote(part, part, self.sc.at[which, step], self.rc.at[which, step], device)

    def begin(self):
        for step in range(1, self.n):
            self.line(step).start()
        self.spread(0)

    def spread(self, step):
        if step:
            arrived(self.buffer.at[self.k, self.groups[0], self.src(step)], self.rz.at[step])
        self.to_y(step).start()
        self.to_x(step).start()
        self.core(0, step).start()

    def second(self, step):
        arrived(self.buffer.at[self.k, self.groups[1], self.src(step)], self.ry.at[step])
        self.on_x(step).start()
        self.core(1, step).start()
        arrived(self.buffer.at[self.k, self.groups[2], self.src(step)], self.rx.at[step])
        self.on_y(step).start()
        self.core(2, step).start()

    def third(self, step):
        part = self.buffer.at[self.k, self.groups[3], self.src(step)]
        arrived(part.at[pl.ds(0, self.half)], self.rxd.at[step])
        arrived(part.at[pl.ds(self.half, self.half)], self.ryd.at[step])
        self.core(3, step).start()

    def other(self, which):
        for step in range(self.n):
            part = self.buffer.at[1 - self.k, self.groups[which], self.src(step)]
            arrived(part, self.rc.at[which, step])

    def finish(self):
        for step in range(self.n):
            if step:
                self.line(step).wait_send()
            self.to_y(step).wait_send()
            self.to_x(step).wait_send()
            self.on_x(step).wait_send()
            self.on_y(step).wait_send()
            for which in range(4):
                self.core(which, step).wait_send()

    def run(self, column):
        k, groups, steps = self.k, self.groups, range(self.n)
        for step in range(1, self.n):
            self.spread(step)
        column(k, 0)
        for step in steps:
            self.second(step)
        self.other(0)
        column(1 - k, 0)
        column(k, 1)
        column(k, 2)
        for step in steps:
            self.third(step)
        self.other(1)
        column(1 - k, 1)
        self.other(2)
        column(1 - k, 2)
        column(k, 3)
        self.other(3)
        column(1 - k, 3)


class Scatter:
    @staticmethod
    def scratch(n, rows, width):
        return [
            pltpu.VMEM((2, 4, n, rows, width), BF),
            pltpu.VMEM((4, n, rows, width), BF),
            pltpu.VMEM((2, n, rows // 2, width), BF),
            pltpu.VMEM((2, n, rows, width), BF),
            pltpu.VMEM((n, rows, width), BF),
            DMA((4,)),
            DMA((4,)),
            DMA((2, n)),
            DMA((2, n)),
            DMA((2, 2, n)),
            DMA((2, 2, n)),
            DMA((n,)),
            DMA((n,)),
        ]

    def __init__(self, n, rows, place, refs):
        self.n, self.rows, self.half = n, rows, rows // 2
        self.x, self.y, self.k, self.z = place
        x, y = self.x, self.y
        self.groups = (2 * x + y, 2 * x + 1 - y, 2 * (1 - x) + y, 2 * (1 - x) + 1 - y)
        (
            self.parts,
            self.from_core,
            self.from_diag,
            self.from_near,
            self.from_line,
            self.s_core,
            self.r_core,
            self.s_diag,
            self.r_diag,
            self.s_near,
            self.r_near,
            self.s_line,
            self.r_line,
        ) = refs
        self.near = (at(x, 1 - y, self.k, self.z), at(1 - x, y, self.k, self.z))

    def slot(self, step):
        return lax.rem(self.z + step, self.n)

    def order(self):
        return list(range(1, self.n)) + [0]

    def core(self, which):
        return remote(
            self.parts.at[1 - self.k, self.groups[which]],
            self.from_core.at[which],
            self.s_core.at[which],
            self.r_core.at[which],
            at(self.x, self.y, 1 - self.k, self.z),
        )

    def diag(self, direction, step):
        rows = pl.ds(self.half if direction == 0 else 0, self.half)
        return remote(
            self.parts.at[self.k, self.groups[3], self.slot(step), rows],
            self.from_diag.at[direction, step],
            self.s_diag.at[direction, step],
            self.r_diag.at[direction, step],
            self.near[direction],
        )

    def close(self, direction, part, step):
        rows = pl.ds(part * self.half, self.half)
        return remote(
            self.parts.at[self.k, self.groups[1 + direction], self.slot(step), rows],
            self.from_near.at[direction, step, rows],
            self.s_near.at[direction, part, step],
            self.r_near.at[direction, part, step],
            self.near[direction],
        )

    def line(self, step):
        return remote(
            self.parts.at[self.k, self.groups[0], self.slot(step)],
            self.from_line.at[step],
            self.s_line.at[step],
            self.r_line.at[step],
            at(self.x, self.y, self.k, self.slot(step)),
        )

    def add_core(self, which):
        self.core(which).wait_recv()
        group = self.groups[which]
        self.parts[self.k, group] = (
            self.parts[self.k, group].astype(F32) + self.from_core[which].astype(F32)
        ).astype(BF)

    def run(self, fill):
        fill = list(fill) + [lambda: None] * 4
        self.add_core(3)
        for step in self.order():
            self.diag(1, step).start()
            self.diag(0, step).start()
        for direction, part in ((0, 1), (1, 0)):
            self.add_core(1 + direction)
            for step in self.order():
                self.close(direction, part, step).start()
        self.add_core(0)
        fill[0]()
        for step in self.order():
            slot = self.slot(step)
            for direction, part in ((0, 0), (1, 1)):
                came = 1 - direction
                self.diag(came, step).wait_recv()
                rows = pl.ds(part * self.half, self.half)
                group = self.groups[1 + direction]
                self.parts[self.k, group, slot, rows] = (
                    self.parts[self.k, group, slot, rows].astype(F32)
                    + self.from_diag[came, step].astype(F32)
                ).astype(BF)
                self.close(direction, part, step).start()
        fill[1]()
        group = self.groups[0]
        result = None
        for step in self.order():
            slot = self.slot(step)
            for direction in range(2):
                for part in range(2):
                    self.close(direction, part, step).wait_recv()
            total = (
                self.parts[self.k, group, slot].astype(F32)
                + self.from_near[0, step].astype(F32)
                + self.from_near[1, step].astype(F32)
            )
            if step:
                self.parts[self.k, group, slot] = total.astype(BF)
                self.line(step).start()
            else:
                result = total
        fill[2]()
        for step in range(1, self.n):
            self.line(step).wait_recv()
            result = result + self.from_line[step].astype(F32)
        return result

    def finish(self):
        for which in range(4):
            self.core(which).wait_send()
        for step in range(self.n):
            for direction in range(2):
                self.diag(direction, step).wait_send()
                for part in range(2):
                    self.close(direction, part, step).wait_send()
            if step:
                self.line(step).wait_send()


def feed_kernel(sz, section, h1, gain, w_all, act_out, n2_all, gate_out, up_out, hm_out, w, w_sem, *refs):
    n = sz.ctx
    place = where_am_i()
    x, y, k, z = place
    load = pltpu.make_async_copy(w_all.at[section], w, w_sem)
    load.start()
    greet(tree_peers(n, x, y, k, z))
    gather = Gather(n, sz.rows, n2_all, place, refs[:12])
    scatter = Scatter(n, sz.rows, place, refs[12:])
    values = h1[...]
    n2_all[k, gather.groups[0], z] = (values * row_norm(values) * gain[...]).astype(BF)
    gather.begin()
    load.wait()
    rows = n * sz.rows

    def column(core, which):
        group = gather.groups[which]
        normed = n2_all[core, group].reshape(rows, sz.width)
        gate = mm(normed, w[0])
        up = mm(normed, w[1])
        hidden = (gate * jax.nn.sigmoid(gate) * up).astype(BF)
        gate_out[core, group] = gate.astype(BF)
        up_out[core, group] = up.astype(BF)
        hm_out[core, group] = hidden
        scatter.parts[core, group] = (
            mm(hidden, w[2], NT).astype(BF).reshape(n, sz.rows, sz.width)
        )

    def column_and_send(core, which):
        column(core, which)
        if core is not k:
            scatter.core(which).start()

    gather.run(column_and_send)
    result = scatter.run(())
    act_out[...] = (values + result).astype(BF)
    gather.finish()
    scatter.finish()


def feed(sz, section, h1, gain, w_all):
    n = sz.ctx
    kept = jax.ShapeDtypeStruct((2, 4, n * sz.rows, sz.hidden), BF)
    shapes = (
        jax.ShapeDtypeStruct((sz.rows, sz.width), BF),
        jax.ShapeDtypeStruct((2, 4, n, sz.rows, sz.width), BF),
        kept,
        kept,
        kept,
    )
    return pl.pallas_call(
        functools.partial(feed_kernel, sz, section),
        out_shape=shapes,
        in_specs=[vmem()] * 2 + [hbm()],
        out_specs=[vmem()] * 5,
        scratch_shapes=[pltpu.VMEM((3, sz.width, sz.hidden), BF), DMA]
        + Gather.scratch(n)
        + Scatter.scratch(n, sz.rows, sz.width),
        compiler_params=params(7 + section),
        name="feed_forward",
    )(h1, gain, w_all)


def feed_back_kernel(
    sz,
    section,
    dy,
    h1,
    gain,
    w_all,
    n2_all,
    gate_in,
    up_in,
    hm_in,
    dh1_out,
    dw_out,
    gain_grad,
    w,
    dy_all,
    dgate_all,
    dup_all,
    w_sem,
    *refs,
):
    n = sz.ctx
    place = where_am_i()
    x, y, k, z = place
    load = pltpu.make_async_copy(w_all.at[section], w, w_sem)
    load.start()
    greet(tree_peers(n, x, y, k, z))
    gather = Gather(n, sz.rows, dy_all, place, refs[:12])
    scatter = Scatter(n, sz.rows, place, refs[12:])
    dy_all[k, gather.groups[0], z] = dy[...]
    gather.begin()
    load.wait()
    rows = n * sz.rows

    def column(core, which):
        group = gather.groups[which]
        dhidden = mm(dy_all[core, group].reshape(rows, sz.width), w[2])
        gate = gate_in[core, group].astype(F32)
        up = up_in[core, group].astype(F32)
        sigmoid = jax.nn.sigmoid(gate)
        dgate = (dhidden * up * sigmoid * (1.0 + gate * (1.0 - sigmoid))).astype(BF)
        dup = (dhidden * gate * sigmoid).astype(BF)
        dgate_all[core, group] = dgate
        dup_all[core, group] = dup
        partial = mm(dgate, w[0], NT) + mm(dup, w[1], NT)
        scatter.parts[core, group] = partial.astype(BF).reshape(n, sz.rows, sz.width)
        if core is not k:
            scatter.core(which).start()

    gather.run(column)
    total = 8 * rows
    tile = 256 if sz.width % 256 == 0 else 128

    def weight_grad(slot, left, right):
        def work():
            grads = right[...].reshape(total, sz.hidden)

            @pl.loop(0, sz.width // tile)
            def _(step):
                cols = pl.ds(pl.multiple_of(step * tile, tile), tile)
                side = left[:, :, :, :, cols].reshape(total, tile)
                dw_out[slot, cols] = mm(side, grads, TN).astype(BF)

        return work

    dn2 = scatter.run(
        (
            weight_grad(0, n2_all, dgate_all),
            weight_grad(1, n2_all, dup_all),
            weight_grad(2, dy_all, hm_in),
        )
    )
    values = h1[...]
    inverse = row_norm(values)
    weighted = dn2 * gain[...]
    inner = jnp.mean(weighted * values, axis=-1, keepdims=True)
    dh1_out[...] = (
        dy[...].astype(F32) + inverse * weighted - values * (inverse * inverse * inverse) * inner
    )
    gain_grad[...] = jnp.sum(dn2 * values * inverse, axis=0, keepdims=True)
    gather.finish()
    scatter.finish()


def feed_back(sz, section, dy, h1, gain, w_all, kept):
    n = sz.ctx
    shapes = (
        jax.ShapeDtypeStruct((sz.rows, sz.width), F32),
        jax.ShapeDtypeStruct((3, sz.width, sz.hidden), BF),
        jax.ShapeDtypeStruct((1, sz.width), F32),
    )
    inner = pltpu.VMEM((2, 4, n * sz.rows, sz.hidden), BF)
    return pl.pallas_call(
        functools.partial(feed_back_kernel, sz, section),
        out_shape=shapes,
        in_specs=[vmem()] * 3 + [hbm()] + [vmem()] * 4,
        out_specs=[vmem()] * 3,
        scratch_shapes=[
            pltpu.VMEM((3, sz.width, sz.hidden), BF),
            pltpu.VMEM((2, 4, n, sz.rows, sz.width), BF),
            inner,
            inner,
            DMA,
        ]
        + Gather.scratch(n)
        + Scatter.scratch(n, sz.rows, sz.width),
        compiler_params=params(9 + section),
        name="feed_backward",
    )(dy, h1, gain, w_all, *kept)


def local_columns(
    sz,
    tokens,
    positions,
    norm1_gain,
    qkv_bias,
    qkv_weight,
    out_weight,
    norm2_gain,
    gate_up_weight,
    down_weight,
    cotangent,
):
    n, group = sz.ctx, sz.group
    x, y, k, z = where_am_i()
    mine = 2 * x + y
    bias_owned = qkv_bias.shape[1]

    def line(values):
        return jnp.pad(values, ((0, 0), (0, LANES - values.shape[1])))

    small = jnp.concatenate(
        [line(norm1_gain), line(norm2_gain), line(qkv_bias), jnp.zeros((13, LANES), BF)], axis=0
    )
    small_all, tok_own, cot_own, att_all, w_all = spread(
        sz, small, tokens, cotangent, qkv_weight[0], out_weight[0], gate_up_weight[0], down_weight[0]
    )
    per_section = small_all.reshape(2, group, 16, LANES).astype(F32)
    gain1 = per_section[:, :, 0, : sz.owned].reshape(2, 1, sz.width)
    gain2 = per_section[:, :, 1, : sz.owned].reshape(2, 1, sz.width)
    bias = per_section[:, :, 2, :bias_owned].reshape(2, 1, group * bias_owned)
    query_columns = QUERY_HEADS * HEAD_WIDTH_SIZE
    key_columns = KEY_VALUE_HEADS * HEAD_WIDTH_SIZE
    kv = mine // (4 // KEY_VALUE_HEADS)
    starts = (
        (mine * sz.qcols, sz.qcols),
        (query_columns + kv * sz.kcols, sz.kcols),
        (query_columns + key_columns + kv * sz.kcols, sz.kcols),
    )
    own_bias = jnp.concatenate(
        [lax.dynamic_slice_in_dim(bias, start, size, 2) for start, size in starts], axis=2
    )
    ordered = lax.dynamic_index_in_dim(positions, k, 0, keepdims=False)
    ordered = ordered.reshape(4, n, sz.rows).transpose(1, 0, 2)
    own_pos = lax.dynamic_index_in_dim(ordered, z, 0, keepdims=False).reshape(4 * sz.rows)
    kpos = ordered.reshape(1, sz.seq)
    qpos = own_pos[:, None]
    cosine, sine = rope_tables(own_pos, HEAD_WIDTH_SIZE)
    half = HEAD_WIDTH_SIZE // 2
    sign = jnp.where(jnp.arange(HEAD_WIDTH_SIZE) < half, -1.0, 1.0)
    tables = (cosine[:, 0], sine[:, 0] * sign)

    inputs, acts, kept_att, kept_feed, middles = [tok_own], [], [], [], []
    for section in range(2):
        h1, *kept = attend(
            sz, section, inputs[section], gain1[section], own_bias[section], att_all, tables, qpos, kpos
        )
        kept_att.append(kept)
        middles.append(h1)
        act, *kept = feed(sz, section, h1, gain2[section], w_all)
        kept_feed.append(kept)
        acts.append(act)
        inputs.append(act)
    grads, dws, das, smalls = [None, None], [None, None], [None, None], [None, None]
    dy = cot_own
    for section in (1, 0):
        dh1, dws[section], gain2_grad = feed_back(
            sz, section, dy, middles[section], gain2[section], w_all, kept_feed[section]
        )
        dy, das[section], gain1_grad, bias_grad = attend_back(
            sz,
            section,
            dh1,
            inputs[section],
            gain1[section],
            att_all,
            tables,
            qpos,
            kpos,
            kept_att[section],
        )
        grads[section] = dy
        whole_bias = jnp.zeros((1, query_columns + 2 * key_columns), F32)
        offset = 0
        for start, size in starts:
            whole_bias = lax.dynamic_update_slice(
                whole_bias, bias_grad[:, offset : offset + size], (0, start)
            )
            offset += size
        split = query_columns + key_columns
        rows = [gain1_grad, gain2_grad, whole_bias[:, :split], whole_bias[:, split:]]
        rows = [line(row.reshape(group, -1))[:, None] for row in rows]
        smalls[section] = jnp.concatenate(rows + [jnp.zeros((group, 4, LANES), F32)], axis=1)
    small_out = jnp.concatenate(smalls, axis=0)
    w_in, att_in, small_in, act_out, grad_out = collect(sz, dws, das, small_out, acts, grads)
    small_sum = jnp.sum(small_in, axis=0)
    gate_up_grad = jnp.concatenate([w_in[0], w_in[1]], axis=1).astype(F32)[None]
    down_grad = w_in[2].astype(F32)[None]
    att_sum = jnp.sum(att_in.astype(F32).reshape(4, n, sz.owned, sz.atot), axis=1)
    q_grad = att_sum[:, :, : sz.qcols].transpose(1, 0, 2).reshape(sz.owned, query_columns)
    kv_grad = jnp.sum(
        att_sum[:, :, sz.qcols : sz.acols].reshape(
            KEY_VALUE_HEADS, 4 // KEY_VALUE_HEADS, sz.owned, 2, sz.kcols
        ),
        axis=1,
    )
    kv_grad = kv_grad.transpose(1, 2, 0, 3).reshape(sz.owned, 2 * key_columns)
    qkv_grad = jnp.concatenate([q_grad, kv_grad], axis=1)[None]
    out_grad = att_sum[:, :, sz.acols :].transpose(1, 0, 2).reshape(1, sz.owned, query_columns)
    return (
        act_out[None],
        grad_out[None],
        small_sum[0:1, : sz.owned],
        small_sum[2:3, : (query_columns + key_columns) // group],
        small_sum[3:4, : key_columns // group],
        qkv_grad,
        out_grad,
        small_sum[1:2, : sz.owned],
        gate_up_grad,
        down_grad,
    )


def solution(mesh):
    placed = (
        P(None, ("head", "ctx"), None),
        P(),
        P("section", ("head", "ctx")),
        P("section", ("head", "ctx")),
        P("section", ("head", "ctx"), None),
        P("section", ("head", "ctx"), None),
        P("section", ("head", "ctx")),
        P("section", ("head", "ctx"), None),
        P("section", ("head", "ctx"), None),
        P(None, ("head", "ctx"), None),
    )
    returned = (
        P("section", None, ("head", "ctx"), None),
        P("section", None, ("head", "ctx"), None),
        P("section", ("head", "ctx")),
        P("section", ("head", "ctx")),
        P("section", ("head", "ctx")),
        P("section", ("head", "ctx"), None),
        P("section", ("head", "ctx"), None),
        P("section", ("head", "ctx")),
        P("section", ("head", "ctx"), None),
        P("section", ("head", "ctx"), None),
    )

    def program(*arrays):
        sizes = Sizes(mesh, arrays[0], arrays[4], arrays[7], arrays[8])
        body = functools.partial(local_columns, sizes) if sizes.fits() else local
        return jax.shard_map(
            body, mesh=mesh, in_specs=placed, out_specs=returned, check_vma=False
        )(*arrays)

    return program
```

```python
import functools
import math

import jax
import jax.numpy as jnp
from jax import lax
from jax.experimental import pallas as pl
from jax.experimental.pallas import tpu as pltpu
from jax.sharding import PartitionSpec as P

FF = 8960
QUERY_HEADS = 12
KEY_VALUE_HEADS = 2
HEAD_WIDTH_SIZE = 128


EPSILON = 1e-06
THETA = 1000000.0


def from_behind(value, axis, steps):
    count = lax.axis_size(axis)
    first, last = (max(0, -steps), min(count, count - steps))
    return lax.ppermute(value, axis, [(source, source + steps) for source in range(first, last)])


def rope_tables(position_ids, head_width):
    frequencies = THETA ** (-(jnp.arange(head_width // 2).astype(jnp.float32) * 2.0) / head_width)
    angles = position_ids.astype(jnp.float32)[..., None] * frequencies
    angles = jnp.concatenate([angles, angles], axis=-1)
    return (jnp.cos(angles)[..., None, :], jnp.sin(angles)[..., None, :])


def rotate(values, cosine_table, sine_table):
    half_width = values.shape[-1] // 2
    turned = jnp.concatenate([-values[..., half_width:], values[..., :half_width]], axis=-1)
    return values * cosine_table + turned * sine_table


def unrotate(grad_values, cosine_table, sine_table):
    half_width = grad_values.shape[-1] // 2
    scaled = grad_values * sine_table
    return grad_values * cosine_table + jnp.concatenate(
        [scaled[..., half_width:], -scaled[..., :half_width]], axis=-1
    )


def norm_rows(values, gain_row):
    inverse = lax.rsqrt(jnp.mean(values * values, axis=-1, keepdims=True) + EPSILON)
    return (values * inverse * gain_row, inverse)


def norm_back(values, inverse, gain_row, grad_values):
    weighted = grad_values * gain_row
    inner_mean = jnp.mean(weighted * values, axis=-1, keepdims=True)
    input_grad = inverse * weighted - values * inverse**3 * inner_mean
    gain_grad = jnp.sum((grad_values * values * inverse).reshape(-1, values.shape[-1]), axis=0)
    return (input_grad, gain_grad)


def pick(flag, first_tree, second_tree):
    return jax.tree.map(
        lambda left_side, right_side: jnp.where(flag, left_side, right_side),
        first_tree,
        second_tree,
    )


def masked_scores(queries, keys_now, query_pos, key_now):
    score_scale = 1.0 / math.sqrt(queries.shape[-1])
    allowed = (key_now[:, None, :] <= query_pos[:, :, None])[:, :, None, :]
    scores = (
        jnp.einsum("grhd,gkd->grhk", queries, keys_now, preferred_element_type=jnp.float32)
        * score_scale
    )
    return (jnp.where(allowed, scores, -1e30), allowed)


def attend_forward(queries, pair_group, query_pos, key_pos):
    head_width = queries.shape[-1]
    row_shape = queries.shape[:3]
    shard_piece = lax.all_gather(pair_group, "ctx", axis=1, tiled=True)
    running = jnp.full(row_shape, -1e30, jnp.float32)
    keys_now = shard_piece[:, :, 0, :head_width]
    values_now = shard_piece[:, :, 0, head_width:]
    scores, allowed = masked_scores(queries, keys_now, query_pos, key_pos)
    highest = jnp.maximum(running, jnp.max(scores, axis=-1))
    probs_now = jnp.where(allowed, jnp.exp(scores - highest[..., None]), 0.0)
    totals = jnp.sum(probs_now, axis=-1)
    accumulated = jnp.einsum(
        "grhk,gkd->grhd",
        probs_now.astype(jnp.bfloat16),
        values_now,
        preferred_element_type=jnp.float32,
    )
    running, totals, accumulated = (highest, totals, accumulated)
    return (accumulated / totals[..., None], running + jnp.log(totals))


def attend_backward(queries, pair_group, query_pos, key_pos, out_grads, lse_rows, delta_rows):
    head_width = queries.shape[-1]
    score_scale = 1.0 / math.sqrt(head_width)
    shard_piece = lax.all_gather(pair_group, "ctx", axis=1, tiled=True)
    keys_now = shard_piece[:, :, 0, :head_width]
    values_now = shard_piece[:, :, 0, head_width:]
    scores, allowed = masked_scores(queries, keys_now, query_pos, key_pos)
    probs_now = jnp.where(allowed, jnp.exp(scores - lse_rows[..., None]), 0.0)
    prob_grads = jnp.einsum(
        "grhd,gkd->grhk", out_grads, values_now, preferred_element_type=jnp.float32
    )
    score_grads = (probs_now * (prob_grads - delta_rows[..., None])).astype(jnp.bfloat16)
    query_grads = score_scale * jnp.einsum(
        "grhk,gkd->grhd", score_grads, keys_now, preferred_element_type=jnp.float32
    )
    key_part = score_scale * jnp.einsum(
        "grhk,grhd->gkd", score_grads, queries, preferred_element_type=jnp.float32
    )
    value_part = jnp.einsum(
        "grhk,grhd->gkd",
        probs_now.astype(jnp.bfloat16),
        out_grads,
        preferred_element_type=jnp.float32,
    )
    piece_term = jnp.concatenate([key_part, value_part], axis=-1)[:, :, None, :]
    return (query_grads, piece_term)


def layer_forward(inputs, own_pos, query_pos, key_pos, weights, heads_total):
    gain_one, bias_all, w_qkv, w_out, gain_two, w_gate_up, w_down = weights
    batch_length = inputs.shape[0]
    rows_total = inputs.shape[1]
    per_device = QUERY_HEADS // heads_total
    copy_count = heads_total // KEY_VALUE_HEADS
    query_columns = QUERY_HEADS * HEAD_WIDTH_SIZE
    key_columns = KEY_VALUE_HEADS * HEAD_WIDTH_SIZE
    residual = inputs.astype(jnp.float32)
    normed_one, inverse_one = norm_rows(residual, gain_one.astype(jnp.float32))
    normed_low = normed_one.astype(jnp.bfloat16)
    projected_rows = jnp.einsum(
        "grd,dc->grc", normed_low, w_qkv, preferred_element_type=jnp.float32
    ) + bias_all.astype(jnp.float32)
    cosine_table, sine_table = rope_tables(own_pos, HEAD_WIDTH_SIZE)
    queries = rotate(
        projected_rows[..., :query_columns].reshape(
            batch_length, rows_total, QUERY_HEADS, HEAD_WIDTH_SIZE
        ),
        cosine_table,
        sine_table,
    )
    key_row_block = rotate(
        projected_rows[..., query_columns : query_columns + key_columns].reshape(
            batch_length, rows_total, KEY_VALUE_HEADS, HEAD_WIDTH_SIZE
        ),
        cosine_table,
        sine_table,
    )
    value_row_block = projected_rows[..., query_columns + key_columns :].reshape(
        batch_length, rows_total, KEY_VALUE_HEADS, HEAD_WIDTH_SIZE
    )
    pair_rows = jnp.concatenate(
        [
            jnp.repeat(key_row_block, copy_count, axis=2),
            jnp.repeat(value_row_block, copy_count, axis=2),
        ],
        axis=-1,
    ).astype(jnp.bfloat16)
    query_send = queries.astype(jnp.bfloat16).reshape(
        batch_length, rows_total, heads_total, per_device * HEAD_WIDTH_SIZE
    )
    query_group, pair_group = (
        lax.all_to_all(query_send, "head", split_axis=2, concat_axis=1, tiled=True),
        lax.all_to_all(pair_rows, "head", split_axis=2, concat_axis=1, tiled=True),
    )
    group_rows = query_group.shape[1]
    query_group = query_group.reshape(batch_length, group_rows, per_device, HEAD_WIDTH_SIZE)
    attended, lse_rows = attend_forward(query_group, pair_group, query_pos, key_pos)
    out_send = attended.astype(jnp.bfloat16).reshape(
        batch_length, group_rows, 1, per_device * HEAD_WIDTH_SIZE
    )
    out_rows = lax.all_to_all(out_send, "head", split_axis=1, concat_axis=2, tiled=True).reshape(
        batch_length, rows_total, QUERY_HEADS * HEAD_WIDTH_SIZE
    )
    middle = residual + jnp.einsum(
        "grc,dc->grd", out_rows, w_out, preferred_element_type=jnp.float32
    )
    normed_two, inverse_two = norm_rows(middle, gain_two.astype(jnp.float32))
    normed_two_low = normed_two.astype(jnp.bfloat16)
    gate_up = jnp.einsum(
        "grd,dc->grc", normed_two_low, w_gate_up, preferred_element_type=jnp.float32
    )
    hidden_low = (jax.nn.silu(gate_up[..., :FF]) * gate_up[..., FF:]).astype(jnp.bfloat16)
    output = middle + jnp.einsum(
        "grf,df->grd", hidden_low, w_down, preferred_element_type=jnp.float32
    )
    kept_now = (
        residual,
        inverse_one,
        normed_low,
        query_group,
        pair_group,
        attended,
        lse_rows,
        out_rows,
        middle,
        inverse_two,
        normed_two_low,
        gate_up,
        hidden_low,
    )
    return (output, kept_now)


def layer_backward(out_grad, kept_now, own_pos, query_pos, key_pos, weights, heads_total):
    gain_one, bias_all, w_qkv, w_out, gain_two, w_gate_up, w_down = weights
    (
        residual,
        inverse_one,
        normed_low,
        query_group,
        pair_group,
        attended,
        lse_rows,
        out_rows,
        middle,
        inverse_two,
        normed_two_low,
        gate_up,
        hidden_low,
    ) = kept_now
    batch_length = out_grad.shape[0]
    rows_total = out_grad.shape[1]
    per_device = QUERY_HEADS // heads_total
    copy_count = heads_total // KEY_VALUE_HEADS
    branch_low = out_grad.astype(jnp.bfloat16)
    hidden_grad = jnp.einsum("grd,df->grf", branch_low, w_down, preferred_element_type=jnp.float32)
    gate_values = gate_up[..., :FF]
    up_values = gate_up[..., FF:]
    sigmoid_gate = jax.nn.sigmoid(gate_values)
    gate_grad = hidden_grad * up_values * sigmoid_gate * (1.0 + gate_values * (1.0 - sigmoid_gate))
    up_grad = hidden_grad * gate_values * sigmoid_gate
    gate_up_low = jnp.concatenate([gate_grad, up_grad], axis=-1).astype(jnp.bfloat16)
    normed_two_grad = jnp.einsum(
        "grc,dc->grd", gate_up_low, w_gate_up, preferred_element_type=jnp.float32
    )
    middle_part, gain_two_grad = norm_back(
        middle, inverse_two, gain_two.astype(jnp.float32), normed_two_grad
    )
    middle_grad = out_grad + middle_part
    middle_low = middle_grad.astype(jnp.bfloat16)
    out_grad_rows = jnp.einsum(
        "grd,dc->grc", middle_low, w_out, preferred_element_type=jnp.float32
    ).astype(jnp.bfloat16)
    out_grad_rows = out_grad_rows.reshape(
        batch_length, rows_total, heads_total, per_device * HEAD_WIDTH_SIZE
    )
    out_grad_group = lax.all_to_all(out_grad_rows, "head", split_axis=2, concat_axis=1, tiled=True)
    group_rows = out_grad_group.shape[1]
    out_grad_group = out_grad_group.reshape(batch_length, group_rows, per_device, HEAD_WIDTH_SIZE)
    delta_rows = jnp.sum(out_grad_group.astype(jnp.float32) * attended, axis=-1)
    query_grads, key_grads = attend_backward(
        query_group, pair_group, query_pos, key_pos, out_grad_group, lse_rows, delta_rows
    )
    pair_own = lax.psum_scatter(
        key_grads.astype(jnp.bfloat16), "ctx", scatter_dimension=1, tiled=True
    )
    query_send = query_grads.astype(jnp.bfloat16).reshape(
        batch_length, group_rows, 1, per_device * HEAD_WIDTH_SIZE
    )
    query_back, paired_backward = (
        lax.all_to_all(query_send, "head", split_axis=1, concat_axis=2, tiled=True),
        lax.all_to_all(pair_own, "head", split_axis=1, concat_axis=2, tiled=True),
    )
    query_rows = query_back.astype(jnp.float32).reshape(
        batch_length, rows_total, QUERY_HEADS, HEAD_WIDTH_SIZE
    )
    paired_sum = jnp.sum(
        paired_backward.astype(jnp.float32).reshape(
            batch_length, rows_total, KEY_VALUE_HEADS, copy_count, 2 * HEAD_WIDTH_SIZE
        ),
        axis=3,
    )
    cosine_table, sine_table = rope_tables(own_pos, HEAD_WIDTH_SIZE)
    query_pre = unrotate(query_rows, cosine_table, sine_table).reshape(
        batch_length, rows_total, QUERY_HEADS * HEAD_WIDTH_SIZE
    )
    key_pre = unrotate(paired_sum[..., :HEAD_WIDTH_SIZE], cosine_table, sine_table).reshape(
        batch_length, rows_total, KEY_VALUE_HEADS * HEAD_WIDTH_SIZE
    )
    value_before_rotation = paired_sum[..., HEAD_WIDTH_SIZE:].reshape(
        batch_length, rows_total, KEY_VALUE_HEADS * HEAD_WIDTH_SIZE
    )
    projected_low = jnp.concatenate([query_pre, key_pre, value_before_rotation], axis=-1).astype(
        jnp.bfloat16
    )
    bias_grad = jnp.sum(
        projected_low.astype(jnp.float32).reshape(-1, projected_low.shape[-1]), axis=0
    )
    normed_grad = jnp.einsum(
        "grc,dc->grd", projected_low, w_qkv, preferred_element_type=jnp.float32
    )
    input_part, gain_one_grad = norm_back(
        residual, inverse_one, gain_one.astype(jnp.float32), normed_grad
    )
    input_grad = middle_grad + input_part
    pieces = (
        normed_low,
        projected_low,
        middle_low,
        out_rows,
        normed_two_low,
        gate_up_low,
        branch_low,
        hidden_low,
    )
    return (input_grad, pieces, (gain_one_grad, bias_grad, gain_two_grad))


def reduce_block(left_side, columns):
    block_term = jnp.einsum("rd,rc->dc", left_side, columns, preferred_element_type=jnp.float32)
    return lax.psum_scatter(block_term, ("head", "ctx"), scatter_dimension=0, tiled=True)


def local(
    tokens,
    positions,
    norm1_gain,
    qkv_bias,
    qkv_weight,
    out_weight,
    norm2_gain,
    gate_up_weight,
    down_weight,
    cotangent,
):
    heads_total = lax.axis_size("head")
    rank_count = lax.axis_size("ctx")
    batch_count = tokens.shape[0]
    rows_total = tokens.shape[1]
    seq_total = positions.shape[1]
    group_rows = heads_total * rows_total
    section_index = lax.axis_index("section")
    rank_index = lax.axis_index("ctx")
    block_index = lax.axis_index("head") * rank_count + rank_index
    ordered = (
        positions.reshape(batch_count, heads_total, rank_count, rows_total)
        .transpose(0, 2, 1, 3)
        .reshape(batch_count, seq_total)
    )
    group_count = batch_count // batch_count
    tick_count = group_count + 1

    def positions_for(group_index):
        first_row = group_index * batch_count
        own_pos = lax.dynamic_slice(
            positions, (first_row, block_index * rows_total), (batch_count, rows_total)
        )
        query_pos = lax.dynamic_slice_in_dim(ordered, rank_index * group_rows, group_rows, 1)
        return (own_pos, query_pos, ordered)

    shards = (norm1_gain, qkv_bias, qkv_weight, out_weight, norm2_gain, gate_up_weight, down_weight)
    weights = tuple(
        (
            shard_value[0]
            for shard_value in (
                lax.all_gather(shards[0], ("head", "ctx"), axis=1, tiled=True),
                lax.all_gather(shards[1], ("head", "ctx"), axis=1, tiled=True),
                lax.all_gather(shards[2], ("head", "ctx"), axis=1, tiled=True),
                lax.all_gather(shards[3], ("head", "ctx"), axis=1, tiled=True),
                lax.all_gather(shards[4], ("head", "ctx"), axis=1, tiled=True),
                lax.all_gather(shards[5], ("head", "ctx"), axis=1, tiled=True),
                lax.all_gather(shards[6], ("head", "ctx"), axis=1, tiled=True),
            )
        )
    )
    received = jnp.zeros((batch_count, rows_total, tokens.shape[2]), jnp.bfloat16)
    outputs = []
    kept_list = []
    for tick_now in range(tick_count):
        first_row = min(tick_now, group_count - 1) * batch_count
        inputs = jnp.where(section_index == 0, tokens, received)
        own_pos, query_pos, key_pos = positions_for(
            jnp.clip(tick_now - section_index, 0, group_count - 1)
        )
        result, kept_now = layer_forward(inputs, own_pos, query_pos, key_pos, weights, heads_total)
        result_low = result.astype(jnp.bfloat16)
        outputs.append(result_low)
        kept_list.append(kept_now)
        if tick_now + 1 < tick_count:
            received = from_behind(result_low, "section", 1)
    received = jnp.zeros((batch_count, rows_total, tokens.shape[2]), jnp.bfloat16)
    grads_in = []
    piece_list = []
    small_sums = None
    for tick_now in range(tick_count):
        first_row = min(tick_now, group_count - 1) * batch_count
        incoming = jnp.where(section_index == 1, cotangent, received).astype(jnp.float32)
        kept_now = pick(
            section_index == 0,
            kept_list[max(tick_now - 1, 0)],
            kept_list[min(tick_now + 1, tick_count - 1)],
        )
        group_number = tick_now - 1 + section_index
        own_pos, query_pos, key_pos = positions_for(jnp.clip(group_number, 0, group_count - 1))
        input_grad, pieces, smalls = layer_backward(
            incoming, kept_now, own_pos, query_pos, key_pos, weights, heads_total
        )
        valid_flag = jnp.logical_and(group_number >= 0, group_number < group_count)
        smalls = tuple((jnp.where(valid_flag, entry_value, 0.0) for entry_value in smalls))
        if small_sums is None:
            small_sums = smalls
        else:
            small_sums = tuple(
                (left_side + right_side for left_side, right_side in zip(small_sums, smalls))
            )
        grad_low = input_grad.astype(jnp.bfloat16)
        grads_in.append(grad_low)
        piece_list.append(pieces)
        if tick_now + 1 < tick_count:
            received = from_behind(grad_low, "section", -1)
    activations = jnp.where(section_index == 0, outputs[0], outputs[1])[None]
    input_grads = jnp.where(section_index == 0, grads_in[1], grads_in[0])[None]
    chosen = [pick(section_index == 0, piece_list[1], piece_list[0])]
    merged = tuple(
        (
            jnp.concatenate([chosen_set[slot_number] for chosen_set in chosen], axis=0).reshape(
                batch_count * rows_total, -1
            )
            for slot_number in range(8)
        )
    )
    (
        normed_all,
        projected_all,
        middle_all,
        attn_all,
        normed_two_all,
        gate_up_all,
        branch_all,
        hidden_all,
    ) = merged
    pair_list = (
        (normed_all, projected_all),
        (middle_all, attn_all),
        (normed_two_all, gate_up_all),
        (branch_all, hidden_all),
    )
    share_list = []
    for left_side, right_side in pair_list:
        width_total = right_side.shape[1]
        piece_count = width_total // 4480 if width_total % 4480 == 0 else 1
        piece_width = width_total // piece_count
        piece_shares = []
        for piece_number in range(piece_count):
            columns = right_side[:, piece_number * piece_width : (piece_number + 1) * piece_width]
            piece_shares.append(reduce_block(left_side, columns))
        share_list.append(jnp.concatenate(piece_shares, axis=1)[None])
    qkv_weight_grad, out_weight_grad, gate_up_grad, down_grad = share_list
    split_width = (QUERY_HEADS + KEY_VALUE_HEADS) * HEAD_WIDTH_SIZE
    bias_sum = small_sums[1]
    gain_one_share, query_key_share, value_share, gain_two_share = (
        lax.psum_scatter(small_sums[0][None], ("head", "ctx"), scatter_dimension=1, tiled=True),
        lax.psum_scatter(
            bias_sum[None, :split_width], ("head", "ctx"), scatter_dimension=1, tiled=True
        ),
        lax.psum_scatter(
            bias_sum[None, split_width:], ("head", "ctx"), scatter_dimension=1, tiled=True
        ),
        lax.psum_scatter(small_sums[2][None], ("head", "ctx"), scatter_dimension=1, tiled=True),
    )
    return (
        activations,
        input_grads,
        gain_one_share,
        query_key_share,
        value_share,
        qkv_weight_grad,
        out_weight_grad,
        gain_two_share,
        gate_up_grad,
        down_grad,
    )


MESH_ID = pl.DeviceIdType.MESH
BF = jnp.bfloat16
F32 = jnp.float32
LANES = 128
HB = 128
VMEM_LIMIT = 60 * 1024 * 1024
DMA = pltpu.SemaphoreType.DMA
NT = (((1,), (1,)), ((), ()))
TN = (((0,), (0,)), ((), ()))
NN = (((1,), (0,)), ((), ()))


def mm(left_side, right_side, form=NN):
    return lax.dot_general(left_side, right_side, form, preferred_element_type=F32)


def where_am_i():
    head = lax.axis_index("head")
    return (lax.axis_index("section"), head // 2, lax.rem(head, 2), lax.axis_index("ctx"))


def at(x, y, k, z):
    return (x, y * 2 + k, z)


def remote(source, target, send_sem, recv_sem, device):
    return pltpu.make_async_remote_copy(
        src_ref=source,
        dst_ref=target,
        send_sem=send_sem,
        recv_sem=recv_sem,
        device_id=device,
        device_id_type=MESH_ID,
    )


def arrived(ref, sem):
    pltpu.make_async_copy(ref, ref, sem).wait()


def greet(devices):
    barrier = pltpu.get_barrier_semaphore()
    for device in devices:
        pl.semaphore_signal(barrier, inc=1, device_id=device, device_id_type=MESH_ID)
    pl.semaphore_wait(barrier, len(devices))


def greet_all(index, total, device_of):
    barrier = pltpu.get_barrier_semaphore()

    @pl.loop(1, total)
    def _(step):
        device = device_of(lax.rem(index + step, total))
        pl.semaphore_signal(barrier, inc=1, device_id=device, device_id_type=MESH_ID)

    pl.semaphore_wait(barrier, total - 1)


def params(collective_id):
    return pltpu.CompilerParams(
        collective_id=collective_id, has_side_effects=True, vmem_limit_bytes=VMEM_LIMIT
    )


def vmem():
    return pl.BlockSpec(memory_space=pltpu.VMEM)


def hbm():
    return pl.BlockSpec(memory_space=pl.ANY)


def row_norm(values):
    return lax.rsqrt(jnp.mean(values * values, axis=-1, keepdims=True) + EPSILON)


class Sizes:
    def __init__(self, mesh, tokens, qkv_weight, gate_up, down):
        self.ctx = mesh.shape["ctx"]
        self.group = 4 * self.ctx
        self.total = 2 * self.group
        self.batches, self.seq, self.width = tokens.shape
        self.rows = self.seq // self.group
        self.ff = down.shape[2]
        self.owned = self.width // self.group
        self.blocks = self.ff // HB
        self.most = -(-self.blocks // self.total)
        self.least = self.blocks // self.total
        self.extra = self.blocks % self.total
        self.hidden = self.most * HB
        self.per_group = QUERY_HEADS // 4
        self.qcols = self.per_group * HEAD_WIDTH_SIZE
        self.kcols = HEAD_WIDTH_SIZE
        self.acols = self.qcols + 2 * self.kcols
        self.atot = self.acols + self.qcols

    def fits(self):
        gathered = self.batches * self.seq * self.width * 2
        return (
            self.batches == 2
            and gathered * 3 < VMEM_LIMIT // 2
            and self.ff % HB == 0
            and self.least >= 1
            and self.owned % 16 == 0
            and self.rows % 32 == 0
        )


def flat_place(index, group, ctx):
    inside = lax.rem(index, group)
    return (index // group, inside // ctx, lax.rem(inside, ctx))


def first_column(sz, owner):
    return pl.multiple_of((owner * sz.least + jnp.minimum(owner, sz.extra)) * HB, HB)


def plane_blocks(sz, plane):
    start = plane * sz.group * sz.least + min(plane * sz.group, sz.extra)
    stop = (plane + 1) * sz.group * sz.least + min((plane + 1) * sz.group, sz.extra)
    return (start, stop - start)


def half_turn(values):
    return pltpu.roll(values, HEAD_WIDTH_SIZE // 2, 1)


def pair_peers(x, y, k, z):
    return (at(1 - x, y, k, z), at(x, 1 - y, k, z), at(1 - x, 1 - y, k, z))


def pair_groups(x, y):
    return (2 * (1 - x) + y, 2 * x + 1 - y, 2 * (1 - x) + 1 - y)


def line_peers(n, x, y, k, z):
    return [at(x, y, k, lax.rem(z + step, n)) for step in range(1, n)]


def tree_peers(n, x, y, k, z):
    return [at(1 - x, y, k, z), at(x, 1 - y, k, z), at(x, y, 1 - k, z)] + line_peers(n, x, y, k, z)


def meet(sz, place, near, across, jobs):
    x, y, k, z = place
    n = sz.ctx
    inside = (y * 2 + k) * n + z
    reach = max([job.reach for job in jobs], default=0)
    if reach == 2:
        greet_all(x * sz.group + inside, sz.total, lambda index: flat_place(index, sz.group, n))
    elif reach == 1:
        barrier = pltpu.get_barrier_semaphore()
        for device in across:
            pl.semaphore_signal(barrier, inc=1, device_id=device, device_id_type=MESH_ID)

        @pl.loop(1, sz.group)
        def _(step):
            device = flat_place(x * sz.group + lax.rem(inside + step, sz.group), sz.group, n)
            pl.semaphore_signal(barrier, inc=1, device_id=device, device_id_type=MESH_ID)

        pl.semaphore_wait(barrier, sz.group - 1 + len(across))
    else:
        greet(near)


def run_call(body, ins, outs, scratch, jobs, collective_id, name):
    fg_in, fg_out, fg_scratch = len(ins), len(outs), len(scratch)
    ins, outs, scratch = list(ins), list(outs), list(scratch)
    for job in jobs:
        ins += [(array, hbm() if spec is None else spec) for array, spec in job.ins]
        outs += [(shape, hbm()) for shape in job.outs]
        scratch += job.scratch

    def kernel(*refs):
        given, made, own = (
            refs[: len(ins)],
            refs[len(ins) : len(ins) + len(outs)],
            refs[len(ins) + len(outs) :],
        )
        a, b, c = fg_in, fg_out, fg_scratch
        for job in jobs:
            job.bind(
                given[a : a + len(job.ins)],
                made[b : b + len(job.outs)],
                own[c : c + len(job.scratch)],
            )
            a, b, c = a + len(job.ins), b + len(job.outs), c + len(job.scratch)
        body(given[:fg_in], made[:fg_out], own[:fg_scratch], jobs)

    results = pl.pallas_call(
        kernel,
        out_shape=tuple(shape for shape, _ in outs),
        in_specs=[spec for _, spec in ins],
        out_specs=tuple(spec for _, spec in outs),
        scratch_shapes=scratch,
        compiler_params=params(collective_id),
        name=name,
    )(*[array for array, _ in ins])
    at_out, extra = fg_out, []
    for job in jobs:
        extra.append(results[at_out : at_out + len(job.outs)])
        at_out += len(job.outs)
    return (results[:fg_out], extra)


def plane_order(n, place, index):
    x, y, k, z = place
    head = y * 2 + k
    far = 4 * (n - 1)
    if isinstance(index, int) and index == 4 * n - 1:
        return head * n + z
    rest = index - far
    head_to = lax.rem(head + jnp.where(index < far, index // (n - 1), rest + 1), 4)
    ctx_to = lax.rem(z + jnp.where(index < far, 1 + lax.rem(index, n - 1), 0), n)
    return head_to * n + ctx_to


def span_of(count, low, high):
    return (int(count * low), int(count * high))


class Columns:
    reach = 1

    def __init__(self, sz, section, part, gate_up, down, staged):
        self.sz, self.section, self.part = sz, section, part
        self.ins = [(down if part == 2 else gate_up, None), (staged, None)]
        self.outs = [jax.ShapeDtypeStruct((sz.width, sz.hidden), BF)]
        self.scratch = [DMA((2,)), DMA((2,))]

    def bind(self, ins, outs, scratch):
        self.source, self.staged = ins
        self.target = outs[0]
        self.send, self.recv = scratch

    def begin(self, place, low=0.0, high=1.0):
        sz = self.sz
        n = sz.ctx
        x, y, k, z = place
        inside = (y * 2 + k) * n + z
        me = x * sz.group + inside
        first, stop = span_of(sz.group, low, high)
        rows = pl.ds(pl.multiple_of(inside * sz.owned, 16), sz.owned)
        wide = sz.least * HB
        base = sz.ff if self.part == 1 else 0

        def pair(owner, offset, width, own):
            target = self.target.at[rows, pl.ds(offset, width)]
            if own:
                first = pl.multiple_of(base + first_column(sz, owner) + offset, HB)
                return (self.source.at[:, pl.ds(first, width)], target)
            first = first_column(sz, owner) - first_column(sz, x * sz.group) + offset
            first = pl.multiple_of(first, HB)
            return (self.staged.at[self.part, :, pl.ds(first, width)], target)

        for own in (True, False):

            @pl.when((x == self.section) == own)
            def _():
                @pl.loop(first, min(stop, sz.group - 1))
                def _(step):
                    owner = x * sz.group + plane_order(n, place, step)
                    device = flat_place(owner, sz.group, n)
                    source, target = pair(owner, 0, wide, own)
                    remote(source, target, self.send.at[0], self.recv.at[0], device).start()
                    if sz.extra:

                        @pl.when(owner < sz.extra)
                        def _():
                            source, target = pair(owner, wide, HB, own)
                            remote(source, target, self.send.at[1], self.recv.at[1], device).start()

                if stop < sz.group:
                    return
                source, target = pair(me, 0, wide, own)
                pltpu.make_async_copy(source, target, self.send.at[0]).start()
                if sz.extra:

                    @pl.when(me < sz.extra)
                    def _():
                        source, target = pair(me, wide, HB, own)
                        pltpu.make_async_copy(source, target, self.send.at[1]).start()

    def middle(self, place):
        pass

    def finish(self, place):
        sz = self.sz
        x, y, k, z = place
        me = x * sz.group + (y * 2 + k) * sz.ctx + z
        wide = sz.least * HB
        arrived(self.target.at[pl.ds(0, sz.width - sz.owned), pl.ds(0, wide)], self.recv.at[0])
        arrived(self.target.at[:, pl.ds(0, wide)], self.send.at[0])
        for plane in range(2):
            count = min(max(sz.extra - plane * sz.group, 0), sz.group)
            if count:

                @pl.when(x == plane)
                def _():
                    arrived(self.target.at[pl.ds(0, count * sz.owned), pl.ds(0, HB)], self.send.at[1])

                    @pl.when(me < sz.extra)
                    def _():
                        arrived(
                            self.target.at[pl.ds(0, sz.width - sz.owned), pl.ds(0, HB)],
                            self.recv.at[1],
                        )


def head_columns(sz, g, qkv, out_w):
    kv = g // (4 // KEY_VALUE_HEADS)
    q0 = pl.multiple_of(g * sz.qcols, HB)
    k0 = pl.multiple_of(QUERY_HEADS * HEAD_WIDTH_SIZE + kv * sz.kcols, HB)
    v0 = pl.multiple_of((QUERY_HEADS + KEY_VALUE_HEADS) * HEAD_WIDTH_SIZE + kv * sz.kcols, HB)
    return (
        (qkv.at[:, pl.ds(q0, sz.qcols)], pl.ds(0, sz.qcols)),
        (qkv.at[:, pl.ds(k0, sz.kcols)], pl.ds(sz.qcols, sz.kcols)),
        (qkv.at[:, pl.ds(v0, sz.kcols)], pl.ds(sz.qcols + sz.kcols, sz.kcols)),
        (out_w.at[:, pl.ds(q0, sz.qcols)], pl.ds(sz.acols, sz.qcols)),
    )


class Heads:
    reach = 1

    def __init__(self, sz, section, qkv, out_w, staged):
        self.sz, self.section = sz, section
        self.ins = [(qkv, None), (out_w, None), (staged, None)]
        self.outs = [jax.ShapeDtypeStruct((sz.width, sz.atot), BF)]
        self.scratch = [DMA, DMA, DMA((2,)), DMA((2,))]

    def bind(self, ins, outs, scratch):
        self.qkv, self.out_w, self.staged = ins
        self.target = outs[0]
        self.send, self.recv, self.s_core, self.r_core = scratch

    def begin(self, place, low=0.0, high=1.0):
        sz = self.sz
        n = sz.ctx
        x, y, k, z = place
        rows = pl.ds(pl.multiple_of(((y * 2 + k) * n + z) * sz.owned, 16), sz.owned)
        mine = y * n + z

        def pairs(y_to, own):
            if own:
                return [
                    (source, self.target.at[rows, cols])
                    for source, cols in head_columns(sz, 2 * x + y_to, self.qkv, self.out_w)
                ]
            return [(self.staged.at[y_to], self.target.at[rows])]

        for own in (True, False):

            @pl.when((x == self.section) == own)
            def _():
                @pl.loop(1, 2 * n)
                def _(step):
                    index = lax.rem(mine + step, 2 * n)
                    for source, target in pairs(index // n, own):
                        remote(
                            source, target, self.send, self.recv, at(x, index // n, k, lax.rem(index, n))
                        ).start()

                for source, target in pairs(y, own):
                    pltpu.make_async_copy(source, target, self.send).start()

    def span(self, part, k):
        stretch = self.sz.width // 4
        return self.target.at[pl.ds(pl.multiple_of((part * 2 + k) * stretch, 16), stretch)]

    def middle(self, place):
        sz = self.sz
        x, y, k, z = place
        half = sz.width // 2
        arrived(self.target.at[pl.ds(0, half - sz.owned)], self.recv)
        arrived(self.target.at[pl.ds(0, half)], self.send)
        for part in range(2):
            span = self.span(part, k)
            remote(span, span, self.s_core.at[part], self.r_core.at[part], at(x, y, 1 - k, z)).start()

    def finish(self, place):
        x, y, k, z = place
        for part in range(2):
            span = self.span(part, 1 - k)
            arrived(span, self.r_core.at[part])
            arrived(span, self.s_core.at[part])


class Returned:
    reach = 2

    def __init__(self, sz, section, parts, grads):
        self.sz, self.section, self.parts = sz, section, parts
        self.ins = [(grads, None)]
        self.outs = [jax.ShapeDtypeStruct((sz.owned, sz.ff), BF) for _ in parts]
        self.scratch = [DMA((2, len(parts))), DMA((2, len(parts)))]

    def bind(self, ins, outs, scratch):
        self.source, self.targets = ins[0], outs
        self.send, self.recv = scratch

    def begin(self, place, low=0.0, high=1.0):
        sz = self.sz
        n = sz.ctx
        x, y, k, z = place
        inside = (y * 2 + k) * n + z
        me = x * sz.group + inside
        first, stop = span_of(sz.group, low, high)
        wide = sz.least * HB
        cols = pl.ds(first_column(sz, me), wide)
        more = pl.ds(pl.multiple_of(first_column(sz, me) + wide, HB), HB)

        def moves(device, slot):
            rows = pl.ds(pl.multiple_of(device * sz.owned, 16), sz.owned)
            source = self.source.at[self.parts[slot], rows]
            base = (source.at[:, pl.ds(0, wide)], self.targets[slot].at[:, cols])
            last = (source.at[:, pl.ds(wide, HB)], self.targets[slot].at[:, more])
            return (base, last)

        def go(device, local):
            for slot in range(len(self.parts)):
                base, last = moves(device, slot)

                def start(pair, kind):
                    if local:
                        pltpu.make_async_copy(*pair, self.send.at[kind, slot]).start()
                    else:
                        remote(
                            *pair,
                            self.send.at[kind, slot],
                            self.recv.at[kind, slot],
                            (self.section, device // n, lax.rem(device, n)),
                        ).start()

                start(base, 0)
                if sz.extra:

                    @pl.when(me < sz.extra)
                    def _():
                        start(last, 1)

        @pl.loop(first, min(stop, sz.group - 1))
        def _(step):
            go(plane_order(n, place, step), False)

        if stop < sz.group:
            return
        for own in (True, False):

            @pl.when((x == self.section) == own)
            def _():
                go(inside, own)

    def middle(self, place):
        pass

    def finish(self, place):
        sz = self.sz
        x, y, k, z = place
        me = x * sz.group + (y * 2 + k) * sz.ctx + z
        wide = sz.least * HB
        for slot, target in enumerate(self.targets):
            arrived(target.at[:, pl.ds(0, sz.group * wide)], self.send.at[0, slot])
            if sz.extra:

                @pl.when(me < sz.extra)
                def _():
                    arrived(target.at[:, pl.ds(0, sz.group * HB)], self.send.at[1, slot])

            @pl.when(x == self.section)
            def _():
                arrived(target.at[:, pl.ds(0, (sz.total - 1) * wide)], self.recv.at[0, slot])
                if sz.extra:

                    @pl.when(me >= sz.extra)
                    def _():
                        arrived(target.at[:, pl.ds(0, sz.extra * HB)], self.recv.at[1, slot])

                    if sz.extra > 1:

                        @pl.when(me < sz.extra)
                        def _():
                            arrived(target.at[:, pl.ds(0, (sz.extra - 1) * HB)], self.recv.at[1, slot])


class ReturnedHeads:
    reach = 2

    def __init__(self, sz, section, grads):
        self.sz, self.section = sz, section
        stretch = sz.width // 4
        self.ins = [(grads, vmem())]
        self.outs = [jax.ShapeDtypeStruct((sz.group, sz.owned, sz.atot), BF)]
        self.scratch = [
            pltpu.VMEM((2, stretch, sz.atot), BF),
            pltpu.VMEM((2, stretch, sz.atot), BF),
            DMA((2,)),
            DMA((2,)),
            DMA,
            DMA,
        ]

    def bind(self, ins, outs, scratch):
        self.source, self.target = ins[0], outs[0]
        self.got, self.summed, self.s_core, self.r_core, self.send, self.recv = scratch

    def rows(self, part, k):
        stretch = self.sz.width // 4
        return pl.ds(pl.multiple_of((part * 2 + k) * stretch, 16), stretch)

    def core(self, place, part):
        x, y, k, z = place
        return remote(
            self.source.at[self.rows(part, 1 - k)],
            self.got.at[part],
            self.s_core.at[part],
            self.r_core.at[part],
            at(x, y, 1 - k, z),
        )

    def begin(self, place, low=0.0, high=1.0):
        for part in range(2):
            self.core(place, part).start()

    def middle(self, place):
        sz = self.sz
        n = sz.ctx
        x, y, k, z = place
        for part in range(2):
            self.core(place, part).wait_recv()
            total = self.source[self.rows(part, k)].astype(F32) + self.got[part].astype(F32)
            self.summed[part] = total.astype(BF)
        slot = (2 * x + y) * n + z
        mine = y * n + z

        def pair(index):
            rows = pl.ds(pl.multiple_of(lax.rem(index, n) * sz.owned, 16), sz.owned)
            return (self.summed.at[index // n, rows], self.target.at[slot])

        def go(index):
            device = at(self.section, index // n, k, lax.rem(index, n))
            remote(*pair(index), self.send, self.recv, device).start()

        @pl.loop(1, 2 * n)
        def _(step):
            go(lax.rem(mine + step, 2 * n))

        @pl.when(x == self.section)
        def _():
            pltpu.make_async_copy(*pair(mine), self.send).start()

        @pl.when(x != self.section)
        def _():
            go(mine)

    def finish(self, place):
        sz = self.sz
        x, y, k, z = place
        for part in range(2):
            self.core(place, part).wait_send()
        arrived(self.target.at[pl.ds(0, 2 * sz.ctx)], self.send)

        @pl.when(x == self.section)
        def _():
            arrived(self.target.at[pl.ds(0, sz.group - 1)], self.recv)


def begin(jobs, place, low=0.0, high=1.0):
    for job in jobs:
        job.begin(place, low, high)


def middle(jobs, place):
    for job in jobs:
        job.middle(place)


def finish(jobs, place):
    for job in jobs:
        job.finish(place)


class Gather:
    SEMS = 12

    @staticmethod
    def scratch(n):
        return [DMA((n,))] * 10 + [DMA((4, n))] * 2

    def __init__(self, n, rows, buffer, place, sems):
        self.n, self.half, self.buffer = n, rows // 2, buffer
        self.x, self.y, self.k, self.z = place
        x, y = self.x, self.y
        self.groups = (2 * x + y, 2 * x + 1 - y, 2 * (1 - x) + y, 2 * (1 - x) + 1 - y)
        (
            self.sz,
            self.rz,
            self.sy,
            self.ry,
            self.sx,
            self.rx,
            self.syd,
            self.ryd,
            self.sxd,
            self.rxd,
            self.sc,
            self.rc,
        ) = sems

    def src(self, step):
        return lax.rem(self.z + self.n - step, self.n)

    def line(self, step):
        own = self.buffer.at[self.k, self.groups[0], self.z]
        device = at(self.x, self.y, self.k, lax.rem(self.z + step, self.n))
        return remote(own, own, self.sz.at[step], self.rz.at[step], device)

    def to_y(self, step):
        part = self.buffer.at[self.k, self.groups[0], self.src(step)]
        device = at(self.x, 1 - self.y, self.k, self.z)
        return remote(part, part, self.sy.at[step], self.ry.at[step], device)

    def to_x(self, step):
        part = self.buffer.at[self.k, self.groups[0], self.src(step)]
        device = at(1 - self.x, self.y, self.k, self.z)
        return remote(part, part, self.sx.at[step], self.rx.at[step], device)

    def on_x(self, step):
        part = self.buffer.at[self.k, self.groups[1], self.src(step), pl.ds(0, self.half)]
        device = at(1 - self.x, self.y, self.k, self.z)
        return remote(part, part, self.sxd.at[step], self.rxd.at[step], device)

    def on_y(self, step):
        part = self.buffer.at[self.k, self.groups[2], self.src(step), pl.ds(self.half, self.half)]
        device = at(self.x, 1 - self.y, self.k, self.z)
        return remote(part, part, self.syd.at[step], self.ryd.at[step], device)

    def core(self, which, step):
        part = self.buffer.at[self.k, self.groups[which], self.src(step)]
        device = at(self.x, self.y, 1 - self.k, self.z)
        return remote(part, part, self.sc.at[which, step], self.rc.at[which, step], device)

    def begin(self):
        for step in range(1, self.n):
            self.line(step).start()
        self.spread(0)

    def spread(self, step):
        if step:
            arrived(self.buffer.at[self.k, self.groups[0], self.src(step)], self.rz.at[step])
        self.to_y(step).start()
        self.to_x(step).start()
        self.core(0, step).start()

    def second(self, step):
        arrived(self.buffer.at[self.k, self.groups[1], self.src(step)], self.ry.at[step])
        self.on_x(step).start()
        self.core(1, step).start()
        arrived(self.buffer.at[self.k, self.groups[2], self.src(step)], self.rx.at[step])
        self.on_y(step).start()
        self.core(2, step).start()

    def third(self, step):
        part = self.buffer.at[self.k, self.groups[3], self.src(step)]
        arrived(part.at[pl.ds(0, self.half)], self.rxd.at[step])
        arrived(part.at[pl.ds(self.half, self.half)], self.ryd.at[step])
        self.core(3, step).start()

    def other(self, which):
        for step in range(self.n):
            part = self.buffer.at[1 - self.k, self.groups[which], self.src(step)]
            arrived(part, self.rc.at[which, step])

    def finish(self):
        for step in range(self.n):
            if step:
                self.line(step).wait_send()
            self.to_y(step).wait_send()
            self.to_x(step).wait_send()
            self.on_x(step).wait_send()
            self.on_y(step).wait_send()
            for which in range(4):
                self.core(which, step).wait_send()

    def run(self, column, nearly):
        k, steps = self.k, range(self.n)
        for step in range(1, self.n):
            self.spread(step)
        column(k, 0)
        for step in steps:
            self.second(step)
        self.other(0)
        column(1 - k, 0)
        column(k, 1)
        column(k, 2)
        for step in steps:
            self.third(step)
        self.other(1)
        column(1 - k, 1)
        self.other(2)
        column(1 - k, 2)
        nearly()
        column(k, 3)
        self.other(3)
        column(1 - k, 3)


class Scatter:
    @staticmethod
    def scratch(n, rows, width):
        return [
            pltpu.VMEM((2, 4, n, rows, width), BF),
            pltpu.VMEM((4, n, rows, width), BF),
            pltpu.VMEM((2, n, rows // 2, width), BF),
            pltpu.VMEM((2, n, rows, width), BF),
            pltpu.VMEM((n, rows, width), BF),
            DMA((4,)),
            DMA((4,)),
            DMA((2, n)),
            DMA((2, n)),
            DMA((2, 2, n)),
            DMA((2, 2, n)),
            DMA((n,)),
            DMA((n,)),
        ]

    def __init__(self, n, rows, place, refs):
        self.n, self.rows, self.half = n, rows, rows // 2
        self.x, self.y, self.k, self.z = place
        x, y = self.x, self.y
        self.groups = (2 * x + y, 2 * x + 1 - y, 2 * (1 - x) + y, 2 * (1 - x) + 1 - y)
        (
            self.parts,
            self.from_core,
            self.from_diag,
            self.from_near,
            self.from_line,
            self.s_core,
            self.r_core,
            self.s_diag,
            self.r_diag,
            self.s_near,
            self.r_near,
            self.s_line,
            self.r_line,
        ) = refs
        self.near = (at(x, 1 - y, self.k, self.z), at(1 - x, y, self.k, self.z))

    def slot(self, step):
        return lax.rem(self.z + step, self.n)

    def order(self):
        return list(range(1, self.n)) + [0]

    def core(self, which):
        return remote(
            self.parts.at[1 - self.k, self.groups[which]],
            self.from_core.at[which],
            self.s_core.at[which],
            self.r_core.at[which],
            at(self.x, self.y, 1 - self.k, self.z),
        )

    def diag(self, direction, step):
        rows = pl.ds(self.half if direction == 0 else 0, self.half)
        return remote(
            self.parts.at[self.k, self.groups[3], self.slot(step), rows],
            self.from_diag.at[direction, step],
            self.s_diag.at[direction, step],
            self.r_diag.at[direction, step],
            self.near[direction],
        )

    def close(self, direction, part, step):
        rows = pl.ds(part * self.half, self.half)
        return remote(
            self.parts.at[self.k, self.groups[1 + direction], self.slot(step), rows],
            self.from_near.at[direction, step, rows],
            self.s_near.at[direction, part, step],
            self.r_near.at[direction, part, step],
            self.near[direction],
        )

    def line(self, step):
        return remote(
            self.parts.at[self.k, self.groups[0], self.slot(step)],
            self.from_line.at[step],
            self.s_line.at[step],
            self.r_line.at[step],
            at(self.x, self.y, self.k, self.slot(step)),
        )

    def add_core(self, which):
        self.core(which).wait_recv()
        group = self.groups[which]
        self.parts[self.k, group] = (
            self.parts[self.k, group].astype(F32) + self.from_core[which].astype(F32)
        ).astype(BF)

    def early(self):
        for direction, part in ((0, 1), (1, 0)):
            self.add_core(1 + direction)
            for step in self.order():
                self.close(direction, part, step).start()

    def run(self, fill):
        fill = list(fill) + [lambda: None] * 3
        self.add_core(3)
        for step in self.order():
            self.diag(1, step).start()
            self.diag(0, step).start()
        self.add_core(0)
        fill[0]()
        for step in self.order():
            slot = self.slot(step)
            for direction, part in ((0, 0), (1, 1)):
                came = 1 - direction
                self.diag(came, step).wait_recv()
                rows = pl.ds(part * self.half, self.half)
                group = self.groups[1 + direction]
                self.parts[self.k, group, slot, rows] = (
                    self.parts[self.k, group, slot, rows].astype(F32)
                    + self.from_diag[came, step].astype(F32)
                ).astype(BF)
                self.close(direction, part, step).start()
        fill[1]()
        group = self.groups[0]
        result = None
        for step in self.order():
            slot = self.slot(step)
            for direction in range(2):
                for part in range(2):
                    self.close(direction, part, step).wait_recv()
            total = (
                self.parts[self.k, group, slot].astype(F32)
                + self.from_near[0, step].astype(F32)
                + self.from_near[1, step].astype(F32)
            )
            if step:
                self.parts[self.k, group, slot] = total.astype(BF)
                self.line(step).start()
            else:
                result = total
        fill[2]()
        for step in range(1, self.n):
            self.line(step).wait_recv()
            result = result + self.from_line[step].astype(F32)
        return result

    def finish(self):
        for which in range(4):
            self.core(which).wait_send()
        for step in range(self.n):
            for direction in range(2):
                self.diag(direction, step).wait_send()
                for part in range(2):
                    self.close(direction, part, step).wait_send()
            if step:
                self.line(step).wait_send()


def spread(sz, small, tokens, cotangent, qkv, out_w, gate_up, down):
    n = sz.ctx
    counts = [plane_blocks(sz, plane) for plane in range(2)]
    staged_cols = max(count for _, count in counts) * HB

    def body(ins, outs, scratch, jobs):
        small, tokens, cotangent, qkv, out_w, gate_up, down = ins
        small_all, tok_own, cot_own, heads_x, cols_x = outs
        s_small, r_small, s_own, r_own, s_hx, r_hx, s_cx, r_cx = scratch
        place = where_am_i()
        x, y, k, z = place
        me = x * sz.group + (y * 2 + k) * n + z
        everyone = lambda index: flat_place(index, sz.group, n)
        greet_all(me, sz.total, everyone)
        across = at(1 - x, y, k, z)

        def heads_over():
            return [
                remote(source, heads_x.at[y_to, :, cols], s_hx, r_hx, across)
                for y_to in range(2)
                for source, cols in head_columns(sz, 2 * (1 - x) + y_to, qkv, out_w)
            ]

        for copy in heads_over():
            copy.start()

        def owns(starting):
            @pl.when(x == y)
            def _():
                for batch in range(2):
                    pairs = ((tokens, tok_own, 0), (cotangent, cot_own, 1))
                    for source, target, slot in pairs:
                        own = jnp.logical_and(k == y, k == batch)

                        @pl.when(jnp.logical_not(own))
                        def _():
                            copy = remote(
                                source.at[batch],
                                target,
                                s_own.at[batch, slot],
                                r_own.at[slot],
                                at(x, k, batch, z),
                            )
                            copy.start() if starting else copy.wait_send()

                        if starting:

                            @pl.when(own)
                            def _():
                                pltpu.make_async_copy(
                                    source.at[batch], target, r_own.at[slot]
                                ).start()

        owns(True)

        @pl.loop(1, sz.total)
        def _(step):
            device = everyone(lax.rem(me + step, sz.total))
            remote(small, small_all.at[me], s_small, r_small, device).start()

        pltpu.make_async_copy(small, small_all.at[me], s_small).start()

        def columns_over(plane, part):
            start, count = counts[1 - plane]
            base = (sz.ff if part == 1 else 0) + start * HB
            source = (down if part == 2 else gate_up).at[:, pl.ds(base, count * HB)]
            target = cols_x.at[part, :, pl.ds(0, count * HB)]
            return remote(source, target, s_cx.at[part], r_cx.at[part], across)

        def for_plane(act):
            for plane in range(2):

                @pl.when(x == plane)
                def _():
                    for part in range(3):
                        act(plane, part)

        heads, first = jobs
        heads.use(ins, outs)
        first.use(ins, outs)

        @pl.when(x == heads.section)
        def _():
            heads.begin(place)

        for_plane(lambda plane, part: columns_over(plane, part).start())
        arrived(heads_x, r_hx)

        @pl.when(x != heads.section)
        def _():
            heads.begin(place)

        def came(plane, part):
            width = counts[plane][1] * HB
            arrived(cols_x.at[part, :, pl.ds(0, width)], r_cx.at[part])

        for plane in range(2):

            @pl.when(x == plane)
            def _():
                came(plane, 0)

        first.begin(place)
        heads.middle(place)
        arrived(small_all.at[pl.ds(0, sz.total - 1)], r_small)
        arrived(small_all, s_small)
        arrived(tok_own, r_own.at[0])
        arrived(cot_own, r_own.at[1])
        owns(False)
        heads.finish(place)

        def rest(plane, part):
            if part:
                came(plane, part)
            columns_over(plane, part).wait_send()

        for_plane(rest)
        arrived(heads_x, s_hx)
        first.finish(place)

    shape = jax.ShapeDtypeStruct
    outs = [
        (shape((sz.total, 16, LANES), BF), hbm()),
        (shape((sz.rows, sz.width), BF), hbm()),
        (shape((sz.rows, sz.width), BF), hbm()),
        (shape((2, sz.owned, sz.atot), BF), hbm()),
        (shape((3, sz.owned, staged_cols), BF), hbm()),
    ]
    arrays = (small, tokens, cotangent, qkv, out_w, gate_up, down)
    scratch = [DMA, DMA, DMA((2, 2)), DMA((2,)), DMA, DMA, DMA((3,)), DMA((3,))]
    jobs = [OwnHeads(sz, 0, 3, 4, 3), OwnColumns(sz, 0, 0, 5, 4)]
    return run_call(body, [(a, hbm()) for a in arrays], outs, scratch, jobs, 1, "spread_weights")


class OwnHeads(Heads):
    def __init__(self, sz, section, qkv, out_w, staged):
        super().__init__(sz, section, None, None, None)
        self.ins = []
        self.named = (qkv, out_w, staged)

    def bind(self, ins, outs, scratch):
        self.target = outs[0]
        self.send, self.recv, self.s_core, self.r_core = scratch

    def use(self, ins, outs):
        qkv, out_w, staged = self.named
        self.qkv, self.out_w, self.staged = ins[qkv], ins[out_w], outs[staged]


class OwnColumns(Columns):
    def __init__(self, sz, section, part, source, staged):
        super().__init__(sz, section, part, None, None, None)
        self.ins = []
        self.named = (source, staged)

    def bind(self, ins, outs, scratch):
        self.target = outs[0]
        self.send, self.recv = scratch

    def use(self, ins, outs):
        source, staged = self.named
        self.source, self.staged = ins[source], outs[staged]


def gather_pair(buffer, place, send, recv):
    x, y, k, z = place
    own = buffer.at[2 * x + y]
    copies = [
        remote(own, own, send.at[i], recv.at[i], device)
        for i, device in enumerate(pair_peers(x, y, k, z))
    ]
    for copy in copies:
        copy.start()
    return copies


def gathered_pair(buffer, place, copies, recv):
    x, y, k, z = place
    for i, group in enumerate(pair_groups(x, y)):
        arrived(buffer.at[group], recv.at[i])


def scatter_pair(parts, landed, place, send, recv):
    x, y, k, z = place
    groups = pair_groups(x, y)
    copies = [
        remote(parts.at[groups[i]], landed.at[i], send.at[i], recv.at[i], device)
        for i, device in enumerate(pair_peers(x, y, k, z))
    ]
    for copy in copies:
        copy.start()
    return copies


def meet_pair(sz, place, jobs):
    x, y, k, z = place
    peers = pair_peers(x, y, k, z)
    meet(sz, place, list(peers) + line_peers(sz.ctx, x, y, k, z), [peers[0], peers[2]], jobs)


def attend(sz, section, x_own, gain, bias, watt, tables, qpos, kpos, jobs):
    n, rows = sz.ctx, 4 * sz.rows

    def body(ins, outs, scratch, jobs):
        x_ref, gain, bias, watt, cosine, sine, qpos, kpos = ins
        h1_out, n1_all, q_out, kv_all, o_out, lse_out = outs
        w, parts, landed, w_sem, s_in, r_in, s_kv, r_kv, s_back, r_back = scratch
        place = where_am_i()
        x, y, k, z = place
        load = pltpu.make_async_copy(watt, w, w_sem)
        load.start()
        meet_pair(sz, place, jobs)
        group = 2 * x + y
        values = x_ref[...].astype(F32)
        n1_all[group] = (values * row_norm(values) * gain[...]).astype(BF)
        copies = gather_pair(n1_all, place, s_in, r_in)
        begin(jobs, place, 0.0, 0.3)
        load.wait()
        gathered_pair(n1_all, place, copies, r_in)
        normed = n1_all[...].reshape(rows, sz.width)
        kv = mm(normed, w[:, sz.qcols : sz.acols]) + bias[:, sz.qcols : sz.acols]
        cos, sin = cosine[...], sine[...]
        key = kv[:, : sz.kcols]
        kv_all[z, :, : sz.kcols] = (key * cos + half_turn(key) * sin).astype(BF)
        kv_all[z, :, sz.kcols :] = kv[:, sz.kcols :].astype(BF)
        kv_copies = []
        for step, device in enumerate(line_peers(n, x, y, k, z)):
            own = kv_all.at[z]
            kv_copies.append(remote(own, own, s_kv.at[step], r_kv.at[step], device))
            kv_copies[-1].start()
        begin(jobs, place, 0.3, 1.0)
        queries = mm(normed, w[:, : sz.qcols]) + bias[:, : sz.qcols]
        for head in range(sz.per_group):
            cols = slice(head * HEAD_WIDTH_SIZE, (head + 1) * HEAD_WIDTH_SIZE)
            query = queries[:, cols]
            q_out[:, cols] = (query * cos + half_turn(query) * sin).astype(BF)
        for step in range(n - 1):
            arrived(kv_all.at[lax.rem(z + n - 1 - step, n)], r_kv.at[step])
        keys = kv_all[:, :, : sz.kcols].reshape(n * rows, sz.kcols)
        vals = kv_all[:, :, sz.kcols :].reshape(n * rows, sz.kcols)
        allowed = kpos[...] <= qpos[...]
        scale = 1.0 / math.sqrt(HEAD_WIDTH_SIZE)
        for head in range(sz.per_group):
            cols = slice(head * HEAD_WIDTH_SIZE, (head + 1) * HEAD_WIDTH_SIZE)
            scores = jnp.where(allowed, mm(q_out[:, cols], keys, NT) * scale, -1e30)
            highest = jnp.max(scores, axis=-1, keepdims=True)
            weights = jnp.exp(scores - highest)
            total = jnp.sum(weights, axis=-1, keepdims=True)
            o_out[:, cols] = mm(weights.astype(BF), vals) / total
            lse_out[head] = jnp.broadcast_to(highest + jnp.log(total), (rows, LANES))
        partial = mm(o_out[...].astype(BF), w[:, sz.acols :], NT)
        parts[...] = partial.astype(BF).reshape(4, sz.rows, sz.width)
        back = scatter_pair(parts, landed, place, s_back, r_back)
        middle(jobs, place)
        for copy in copies + kv_copies:
            copy.wait_send()
        out = values + parts[group].astype(F32)
        for i in range(3):
            back[i].wait_recv()
            out = out + landed[i].astype(F32)
        h1_out[...] = out
        for copy in back:
            copy.wait_send()
        finish(jobs, place)

    shapes = (
        jax.ShapeDtypeStruct((sz.rows, sz.width), F32),
        jax.ShapeDtypeStruct((4, sz.rows, sz.width), BF),
        jax.ShapeDtypeStruct((rows, sz.qcols), BF),
        jax.ShapeDtypeStruct((n, rows, 2 * sz.kcols), BF),
        jax.ShapeDtypeStruct((rows, sz.qcols), F32),
        jax.ShapeDtypeStruct((sz.per_group, rows, LANES), F32),
    )
    arrays = (x_own, gain, bias, watt, *tables, qpos, kpos)
    specs = [vmem()] * 3 + [hbm()] + [vmem()] * 4
    scratch = [
        pltpu.VMEM((sz.width, sz.atot), BF),
        pltpu.VMEM((4, sz.rows, sz.width), BF),
        pltpu.VMEM((3, sz.rows, sz.width), BF),
        DMA,
        DMA((3,)),
        DMA((3,)),
        DMA((n,)),
        DMA((n,)),
        DMA((3,)),
        DMA((3,)),
    ]
    return run_call(
        body,
        list(zip(arrays, specs)),
        [(shape, vmem()) for shape in shapes],
        scratch,
        jobs,
        3 + section,
        "attend_forward",
    )


def attend_back(sz, section, dh1, x_own, gain, watt, tables, qpos, kpos, kept, jobs):
    n, rows = sz.ctx, 4 * sz.rows

    def body(ins, outs, scratch, jobs):
        dh1, x_ref, gain, watt, cosine, sine, qpos, kpos, n1_all, q_in, kv_all, o_in, lse_in = ins
        dx_out, dw_out, gain_grad, bias_grad = outs
        w, dh_all, dkv, dkv_in, da, parts, landed, w_sem, s_in, r_in, s_kv, r_kv, s_back, r_back = scratch
        place = where_am_i()
        x, y, k, z = place
        load = pltpu.make_async_copy(watt, w, w_sem)
        load.start()
        meet_pair(sz, place, jobs)
        group = 2 * x + y
        dh_all[group] = dh1[...].astype(BF)
        copies = gather_pair(dh_all, place, s_in, r_in)
        begin(jobs, place, 0.0, 0.4)
        load.wait()
        gathered_pair(dh_all, place, copies, r_in)
        dh = dh_all[...].reshape(rows, sz.width)
        dout = mm(dh, w[:, sz.acols :]).astype(BF)
        keys = kv_all[:, :, : sz.kcols].reshape(n * rows, sz.kcols)
        vals = kv_all[:, :, sz.kcols :].reshape(n * rows, sz.kcols)
        allowed = kpos[...] <= qpos[...]
        scale = 1.0 / math.sqrt(HEAD_WIDTH_SIZE)
        cos, sin = cosine[...], sine[...]
        dkeys, dvals = None, None
        for head in range(sz.per_group):
            cols = slice(head * HEAD_WIDTH_SIZE, (head + 1) * HEAD_WIDTH_SIZE)
            query, grad = q_in[:, cols], dout[:, cols]
            delta = jnp.sum(grad.astype(F32) * o_in[:, cols], axis=-1, keepdims=True)
            scores = mm(query, keys, NT) * scale
            probs = jnp.where(allowed, jnp.exp(scores - lse_in[head][:, :1]), 0.0)
            dscores = (probs * (mm(grad, vals, NT) - delta)).astype(BF)
            dquery = (mm(dscores, keys) * scale).astype(BF).astype(F32)
            da[:, cols] = (dquery * cos - half_turn(dquery) * sin).astype(BF)
            one_key = mm(dscores, query, TN)
            one_val = mm(probs.astype(BF), grad, TN)
            dkeys = one_key if dkeys is None else dkeys + one_key
            dvals = one_val if dvals is None else dvals + one_val
        dkv[:, :, : sz.kcols] = (dkeys * scale).astype(BF).reshape(n, rows, sz.kcols)
        dkv[:, :, sz.kcols :] = dvals.astype(BF).reshape(n, rows, sz.kcols)
        kv_copies = []
        for step, device in enumerate(line_peers(n, x, y, k, z)):
            kv_copies.append(
                remote(
                    dkv.at[lax.rem(z + 1 + step, n)],
                    dkv_in.at[step],
                    s_kv.at[step],
                    r_kv.at[step],
                    device,
                )
            )
            kv_copies[-1].start()
        begin(jobs, place, 0.4, 1.0)
        dw_out[:, sz.acols :] = mm(dh, o_in[...].astype(BF), TN).astype(BF)
        total = dkv[z].astype(F32)
        for step in range(n - 1):
            kv_copies[step].wait_recv()
            total = total + dkv_in[step].astype(F32)
        dkey = total[:, : sz.kcols]
        da[:, sz.qcols : sz.qcols + sz.kcols] = (dkey * cos - half_turn(dkey) * sin).astype(BF)
        da[:, sz.qcols + sz.kcols :] = total[:, sz.kcols :].astype(BF)
        parts[...] = mm(da[...], w[:, : sz.acols], NT).astype(BF).reshape(4, sz.rows, sz.width)
        back = scatter_pair(parts, landed, place, s_back, r_back)
        dw_out[:, : sz.acols] = mm(n1_all[...].reshape(rows, sz.width), da[...], TN).astype(BF)
        bias_grad[...] = jnp.sum(da[...].astype(F32), axis=0, keepdims=True)
        middle(jobs, place)
        for copy in copies + kv_copies:
            copy.wait_send()
        dn1 = parts[group].astype(F32)
        for i in range(3):
            back[i].wait_recv()
            dn1 = dn1 + landed[i].astype(F32)
        values = x_ref[...].astype(F32)
        inverse = row_norm(values)
        weighted = dn1 * gain[...]
        inner = jnp.mean(weighted * values, axis=-1, keepdims=True)
        dx = dh1[...] + inverse * weighted - values * (inverse * inverse * inverse) * inner
        dx_out[...] = dx.astype(BF)
        gain_grad[...] = jnp.sum(dn1 * values * inverse, axis=0, keepdims=True)
        for copy in back:
            copy.wait_send()
        finish(jobs, place)

    shapes = (
        jax.ShapeDtypeStruct((sz.rows, sz.width), BF),
        jax.ShapeDtypeStruct((sz.width, sz.atot), BF),
        jax.ShapeDtypeStruct((1, sz.width), F32),
        jax.ShapeDtypeStruct((1, sz.acols), F32),
    )
    arrays = (dh1, x_own, gain, watt, *tables, qpos, kpos, *kept)
    specs = [vmem()] * 3 + [hbm()] + [vmem()] * 9
    scratch = [
        pltpu.VMEM((sz.width, sz.atot), BF),
        pltpu.VMEM((4, sz.rows, sz.width), BF),
        pltpu.VMEM((n, rows, 2 * sz.kcols), BF),
        pltpu.VMEM((n, rows, 2 * sz.kcols), BF),
        pltpu.VMEM((rows, sz.acols), BF),
        pltpu.VMEM((4, sz.rows, sz.width), BF),
        pltpu.VMEM((3, sz.rows, sz.width), BF),
        DMA,
        DMA((3,)),
        DMA((3,)),
        DMA((n,)),
        DMA((n,)),
        DMA((3,)),
        DMA((3,)),
    ]
    return run_call(
        body,
        list(zip(arrays, specs)),
        [(shape, vmem()) for shape in shapes],
        scratch,
        jobs,
        5 + section,
        "attend_backward",
    )


class HiddenWeights:
    def __init__(self, sz, place, sources, w, sems):
        x, y, k, z = place
        self.sz, self.sources, self.w, self.sems = sz, sources, w, sems
        self.more = x * sz.group + (y * 2 + k) * sz.ctx + z < sz.extra
        self.wide = sz.least * HB

    def copies(self, offset, width, kind):
        cols = pl.ds(offset, width)
        return [
            pltpu.make_async_copy(
                self.sources[part].at[:, cols], self.w.at[part, :, cols], self.sems.at[kind, part]
            )
            for part in range(3)
        ]

    def start(self):
        for copy in self.copies(0, self.wide, 0):
            copy.start()
        if self.sz.extra:

            @pl.when(self.more)
            def _():
                for copy in self.copies(self.wide, HB, 1):
                    copy.start()

            @pl.when(jnp.logical_not(self.more))
            def _():
                self.w[:, :, self.wide :] = jnp.zeros((3, self.sz.width, HB), BF)

    def wait(self):
        for copy in self.copies(0, self.wide, 0):
            copy.wait()
        if self.sz.extra:

            @pl.when(self.more)
            def _():
                for copy in self.copies(self.wide, HB, 1):
                    copy.wait()


def meet_tree(sz, place, jobs):
    x, y, k, z = place
    peers = tree_peers(sz.ctx, x, y, k, z)
    meet(sz, place, peers, peers[:1], jobs)


def feed(sz, section, h1, gain, weights, jobs):
    n = sz.ctx

    def body(ins, outs, scratch, jobs):
        h1, gain, *sources = ins
        act_out, n2_all, gate_out, up_out, hm_out = outs
        w, w_sems, *refs = scratch
        place = where_am_i()
        x, y, k, z = place
        hidden_weights = HiddenWeights(sz, place, sources, w, w_sems)
        hidden_weights.start()
        meet_tree(sz, place, jobs)
        gather = Gather(n, sz.rows, n2_all, place, refs[:12])
        scatter = Scatter(n, sz.rows, place, refs[12:])
        values = h1[...]
        n2_all[k, gather.groups[0], z] = (values * row_norm(values) * gain[...]).astype(BF)
        gather.begin()
        begin(jobs[:1], place)
        begin(jobs[1:], place, 0.0, 0.75)
        hidden_weights.wait()
        rows = n * sz.rows

        def column(core, which):
            group = gather.groups[which]
            normed = n2_all[core, group].reshape(rows, sz.width)
            gate = mm(normed, w[0])
            up = mm(normed, w[1])
            hidden = (gate * jax.nn.sigmoid(gate) * up).astype(BF)
            gate_out[core, group] = gate.astype(BF)
            up_out[core, group] = up.astype(BF)
            hm_out[core, group] = hidden
            scatter.parts[core, group] = (
                mm(hidden, w[2], NT).astype(BF).reshape(n, sz.rows, sz.width)
            )
            if core is not k:
                scatter.core(which).start()

        gather.run(column, scatter.early)

        def later():
            begin(jobs[1:], place, 0.75, 1.0)
            middle(jobs, place)

        result = scatter.run((later,))
        act_out[...] = (values + result).astype(BF)
        gather.finish()
        scatter.finish()
        finish(jobs, place)

    kept = jax.ShapeDtypeStruct((2, 4, n * sz.rows, sz.hidden), BF)
    shapes = (
        jax.ShapeDtypeStruct((sz.rows, sz.width), BF),
        jax.ShapeDtypeStruct((2, 4, n, sz.rows, sz.width), BF),
        kept,
        kept,
        kept,
    )
    scratch = (
        [pltpu.VMEM((3, sz.width, sz.hidden), BF), DMA((2, 3))]
        + Gather.scratch(n)
        + Scatter.scratch(n, sz.rows, sz.width)
    )
    return run_call(
        body,
        [(h1, vmem()), (gain, vmem())] + [(w, hbm()) for w in weights],
        [(shape, vmem()) for shape in shapes],
        scratch,
        jobs,
        7 + section,
        "feed_forward",
    )


def feed_back(sz, section, dy, h1, gain, weights, kept, jobs):
    n = sz.ctx

    def body(ins, outs, scratch, jobs):
        dy, h1, gain, *sources = ins[:6]
        n2_all, gate_in, up_in, hm_in = ins[6:]
        dh1_out, dw_out, gain_grad = outs
        w, dy_all, dgate_all, dup_all, w_sems, *refs = scratch
        place = where_am_i()
        x, y, k, z = place
        hidden_weights = HiddenWeights(sz, place, sources, w, w_sems)
        hidden_weights.start()
        meet_tree(sz, place, jobs)
        gather = Gather(n, sz.rows, dy_all, place, refs[:12])
        scatter = Scatter(n, sz.rows, place, refs[12:])
        dy_all[k, gather.groups[0], z] = dy[...]
        gather.begin()
        begin(jobs[:1], place)
        hidden_weights.wait()
        middle(jobs, place)
        begin(jobs[1:], place)
        rows = n * sz.rows

        def column(core, which):
            group = gather.groups[which]
            dhidden = mm(dy_all[core, group].reshape(rows, sz.width), w[2])
            gate = gate_in[core, group].astype(F32)
            up = up_in[core, group].astype(F32)
            sigmoid = jax.nn.sigmoid(gate)
            dgate = (dhidden * up * sigmoid * (1.0 + gate * (1.0 - sigmoid))).astype(BF)
            dup = (dhidden * gate * sigmoid).astype(BF)
            dgate_all[core, group] = dgate
            dup_all[core, group] = dup
            partial = mm(dgate, w[0], NT) + mm(dup, w[1], NT)
            scatter.parts[core, group] = partial.astype(BF).reshape(n, sz.rows, sz.width)
            if core is not k:
                scatter.core(which).start()

        gather.run(column, scatter.early)
        total = 8 * rows
        tile = 256 if sz.width % 256 == 0 else 128

        def weight_grad(slot, left, right):
            grads = right[...].reshape(total, sz.hidden)

            @pl.loop(0, sz.width // tile)
            def _(step):
                cols = pl.ds(pl.multiple_of(step * tile, tile), tile)
                side = left[:, :, :, :, cols].reshape(total, tile)
                dw_out[slot, cols] = mm(side, grads, TN).astype(BF)

        dn2 = scatter.run(
            (
                lambda: weight_grad(0, n2_all, dgate_all),
                lambda: weight_grad(1, n2_all, dup_all),
                lambda: weight_grad(2, dy_all, hm_in),
            )
        )
        values = h1[...]
        inverse = row_norm(values)
        weighted = dn2 * gain[...]
        inner = jnp.mean(weighted * values, axis=-1, keepdims=True)
        dh1_out[...] = (
            dy[...].astype(F32) + inverse * weighted - values * (inverse * inverse * inverse) * inner
        )
        gain_grad[...] = jnp.sum(dn2 * values * inverse, axis=0, keepdims=True)
        gather.finish()
        scatter.finish()
        finish(jobs, place)

    shapes = (
        jax.ShapeDtypeStruct((sz.rows, sz.width), F32),
        jax.ShapeDtypeStruct((3, sz.width, sz.hidden), BF),
        jax.ShapeDtypeStruct((1, sz.width), F32),
    )
    inner = pltpu.VMEM((2, 4, n * sz.rows, sz.hidden), BF)
    scratch = (
        [
            pltpu.VMEM((3, sz.width, sz.hidden), BF),
            pltpu.VMEM((2, 4, n, sz.rows, sz.width), BF),
            inner,
            inner,
            DMA((2, 3)),
        ]
        + Gather.scratch(n)
        + Scatter.scratch(n, sz.rows, sz.width)
    )
    arrays = (dy, h1, gain, *weights, *kept)
    specs = [vmem()] * 3 + [hbm()] * 3 + [vmem()] * 4
    return run_call(
        body,
        list(zip(arrays, specs)),
        [(shape, vmem()) for shape in shapes],
        scratch,
        jobs,
        9 + section,
        "feed_backward",
    )


def collect(sz, small, acts, grads, jobs):
    n = sz.ctx

    def body(ins, outs, scratch, jobs):
        small, act0, act1, grad0, grad1 = ins
        small_in, act_out, grad_out = outs
        s_small, r_small, s_out, r_out = scratch
        place = where_am_i()
        x, y, k, z = place
        me = x * sz.group + (y * 2 + k) * n + z
        meet(sz, place, [], [], jobs)
        begin(jobs, place)

        @pl.loop(1, sz.total)
        def _(step):
            device = lax.rem(me + step, sz.total)
            remote(
                small.at[device], small_in.at[me], s_small, r_small, flat_place(device, sz.group, n)
            ).start()

        pltpu.make_async_copy(small.at[me], small_in.at[me], s_small).start()

        def results(starting):
            for section in range(2):
                for slot, (source, target) in enumerate(
                    (((act0, act1)[section], act_out), ((grad0, grad1)[section], grad_out))
                ):
                    own = jnp.logical_and(x == section, jnp.logical_and(x == y, y == k))

                    @pl.when(jnp.logical_not(own))
                    def _():
                        copy = remote(
                            source,
                            target.at[k],
                            s_out.at[section, slot],
                            r_out.at[slot, k],
                            at(section, x, y, z),
                        )
                        copy.start() if starting else copy.wait_send()

                    if starting:

                        @pl.when(own)
                        def _():
                            pltpu.make_async_copy(source, target.at[k], r_out.at[slot, k]).start()

        middle(jobs, place)
        results(True)
        results(False)
        for slot, target in enumerate((act_out, grad_out)):
            for batch in range(2):
                arrived(target.at[batch], r_out.at[slot, batch])
        arrived(small_in.at[pl.ds(0, sz.total - 1)], r_small)
        arrived(small_in, s_small)
        finish(jobs, place)

    shapes = (
        jax.ShapeDtypeStruct((sz.total, 8, LANES), F32),
        jax.ShapeDtypeStruct((2, sz.rows, sz.width), BF),
        jax.ShapeDtypeStruct((2, sz.rows, sz.width), BF),
    )
    return run_call(
        body,
        [(array, hbm()) for array in (small, *acts, *grads)],
        [(shape, hbm()) for shape in shapes],
        [DMA, DMA, DMA((2, 2)), DMA((2, 2))],
        jobs,
        2,
        "collect_gradients",
    )


def local_columns(
    sz,
    tokens,
    positions,
    norm1_gain,
    qkv_bias,
    qkv_weight,
    out_weight,
    norm2_gain,
    gate_up_weight,
    down_weight,
    cotangent,
):
    n, group = sz.ctx, sz.group
    x, y, k, z = where_am_i()
    mine = 2 * x + y
    bias_owned = qkv_bias.shape[1]
    qkv_weight, out_weight = (qkv_weight[0], out_weight[0])
    gate_up_weight, down_weight = (gate_up_weight[0], down_weight[0])

    def line(values):
        return jnp.pad(values, ((0, 0), (0, LANES - values.shape[1])))

    small = jnp.concatenate(
        [line(norm1_gain), line(norm2_gain), line(qkv_bias), jnp.zeros((13, LANES), BF)], axis=0
    )
    (small_all, tok_own, cot_own, heads_x, cols_x), ((att0,), (gate0,)) = spread(
        sz, small, tokens, cotangent, qkv_weight, out_weight, gate_up_weight, down_weight
    )
    per_section = small_all.reshape(2, group, 16, LANES).astype(F32)
    gain1 = per_section[:, :, 0, : sz.owned].reshape(2, 1, sz.width)
    gain2 = per_section[:, :, 1, : sz.owned].reshape(2, 1, sz.width)
    bias = per_section[:, :, 2, :bias_owned].reshape(2, 1, group * bias_owned)
    query_columns = QUERY_HEADS * HEAD_WIDTH_SIZE
    key_columns = KEY_VALUE_HEADS * HEAD_WIDTH_SIZE
    kv = mine // (4 // KEY_VALUE_HEADS)
    starts = (
        (mine * sz.qcols, sz.qcols),
        (query_columns + kv * sz.kcols, sz.kcols),
        (query_columns + key_columns + kv * sz.kcols, sz.kcols),
    )
    own_bias = jnp.concatenate(
        [lax.dynamic_slice_in_dim(bias, start, size, 2) for start, size in starts], axis=2
    )
    ordered = lax.dynamic_index_in_dim(positions, k, 0, keepdims=False)
    ordered = ordered.reshape(4, n, sz.rows).transpose(1, 0, 2)
    own_pos = lax.dynamic_index_in_dim(ordered, z, 0, keepdims=False).reshape(4 * sz.rows)
    kpos = ordered.reshape(1, sz.seq)
    qpos = own_pos[:, None]
    cosine, sine = rope_tables(own_pos, HEAD_WIDTH_SIZE)
    half = HEAD_WIDTH_SIZE // 2
    sign = jnp.where(jnp.arange(HEAD_WIDTH_SIZE) < half, -1.0, 1.0)
    tables = (cosine[:, 0], sine[:, 0] * sign)

    def columns(section, part):
        return Columns(sz, section, part, gate_up_weight, down_weight, cols_x)

    att, gates, weights = [att0, None], [gate0, None], []
    inputs, acts, kept_att, kept_feed, middles = [tok_own], [], [], [], []
    for section in range(2):
        (h1, *kept), ((up,), (down,)) = attend(
            sz,
            section,
            inputs[section],
            gain1[section],
            own_bias[section],
            att[section],
            tables,
            qpos,
            kpos,
            [columns(section, 1), columns(section, 2)],
        )
        kept_att.append(kept)
        middles.append(h1)
        weights.append((gates[section], up, down))
        jobs = []
        if section == 0:
            jobs = [Heads(sz, 1, qkv_weight, out_weight, heads_x), columns(1, 0)]
        (act, *kept), more = feed(sz, section, h1, gain2[section], weights[section], jobs)
        if section == 0:
            (att[1],), (gates[1],) = more
        kept_feed.append(kept)
        acts.append(act)
        inputs.append(act)
    grads, das, smalls = [None, None], [None, None], [None, None]
    came = [[None] * 3, [None] * 3]
    came_heads = [None, None]
    dy = cot_own
    for section in (1, 0):
        jobs = []
        if section == 0:
            jobs = [ReturnedHeads(sz, 1, das[1]), Returned(sz, 1, (2,), dw)]
        (dh1, dw, gain2_grad), more = feed_back(
            sz, section, dy, middles[section], gain2[section], weights[section], kept_feed[section], jobs
        )
        if section == 0:
            (came_heads[1],), (came[1][2],) = more
        (dy, das[section], gain1_grad, bias_grad), (returned,) = attend_back(
            sz,
            section,
            dh1,
            inputs[section],
            gain1[section],
            att[section],
            tables,
            qpos,
            kpos,
            kept_att[section],
            [Returned(sz, section, (0, 1) if section else (0, 1, 2), dw)],
        )
        for part, grad in enumerate(returned):
            came[section][part] = grad
        grads[section] = dy
        whole_bias = jnp.zeros((1, query_columns + 2 * key_columns), F32)
        offset = 0
        for start, size in starts:
            whole_bias = lax.dynamic_update_slice(
                whole_bias, bias_grad[:, offset : offset + size], (0, start)
            )
            offset += size
        split = query_columns + key_columns
        rows = [gain1_grad, gain2_grad, whole_bias[:, :split], whole_bias[:, split:]]
        rows = [line(row.reshape(group, -1))[:, None] for row in rows]
        smalls[section] = jnp.concatenate(rows + [jnp.zeros((group, 4, LANES), F32)], axis=1)
    small_out = jnp.concatenate(smalls, axis=0)
    (small_in, act_out, grad_out), ((came_heads[0],),) = collect(
        sz, small_out, acts, grads, [ReturnedHeads(sz, 0, das[0])]
    )

    def own(parts):
        return jnp.where(x == 0, parts[0], parts[1])

    small_sum = jnp.sum(small_in, axis=0)
    gate_up_grad = jnp.concatenate(
        [own((came[0][part], came[1][part])).astype(F32) for part in range(2)], axis=1
    )[None]
    down_grad = own((came[0][2], came[1][2])).astype(F32)[None]
    att_in = own(came_heads)
    att_sum = jnp.sum(att_in.astype(F32).reshape(4, n, sz.owned, sz.atot), axis=1)
    q_grad = att_sum[:, :, : sz.qcols].transpose(1, 0, 2).reshape(sz.owned, query_columns)
    kv_grad = jnp.sum(
        att_sum[:, :, sz.qcols : sz.acols].reshape(
            KEY_VALUE_HEADS, 4 // KEY_VALUE_HEADS, sz.owned, 2, sz.kcols
        ),
        axis=1,
    )
    kv_grad = kv_grad.transpose(1, 2, 0, 3).reshape(sz.owned, 2 * key_columns)
    qkv_grad = jnp.concatenate([q_grad, kv_grad], axis=1)[None]
    out_grad = att_sum[:, :, sz.acols :].transpose(1, 0, 2).reshape(1, sz.owned, query_columns)
    return (
        act_out[None],
        grad_out[None],
        small_sum[0:1, : sz.owned],
        small_sum[2:3, : (query_columns + key_columns) // group],
        small_sum[3:4, : key_columns // group],
        qkv_grad,
        out_grad,
        small_sum[1:2, : sz.owned],
        gate_up_grad,
        down_grad,
    )


def solution(mesh):
    placed = (
        P(None, ("head", "ctx"), None),
        P(),
        P("section", ("head", "ctx")),
        P("section", ("head", "ctx")),
        P("section", ("head", "ctx"), None),
        P("section", ("head", "ctx"), None),
        P("section", ("head", "ctx")),
        P("section", ("head", "ctx"), None),
        P("section", ("head", "ctx"), None),
        P(None, ("head", "ctx"), None),
    )
    returned = (
        P("section", None, ("head", "ctx"), None),
        P("section", None, ("head", "ctx"), None),
        P("section", ("head", "ctx")),
        P("section", ("head", "ctx")),
        P("section", ("head", "ctx")),
        P("section", ("head", "ctx"), None),
        P("section", ("head", "ctx"), None),
        P("section", ("head", "ctx")),
        P("section", ("head", "ctx"), None),
        P("section", ("head", "ctx"), None),
    )

    def program(*arrays):
        sizes = Sizes(mesh, arrays[0], arrays[4], arrays[7], arrays[8])
        body = functools.partial(local_columns, sizes) if sizes.fits() else local
        return jax.shard_map(
            body, mesh=mesh, in_specs=placed, out_specs=returned, check_vma=False
        )(*arrays)

    return program
```

```python
import functools
import math

import jax
import jax.numpy as jnp
from jax import lax
from jax.experimental import pallas as pl
from jax.experimental.pallas import tpu as pltpu
from jax.sharding import PartitionSpec as P

FF = 8960
QUERY_HEADS = 12
KEY_VALUE_HEADS = 2
HEAD_WIDTH_SIZE = 128


EPSILON = 1e-06
THETA = 1000000.0


def from_behind(value, axis, steps):
    count = lax.axis_size(axis)
    first, last = (max(0, -steps), min(count, count - steps))
    return lax.ppermute(value, axis, [(source, source + steps) for source in range(first, last)])


def rope_tables(position_ids, head_width):
    frequencies = THETA ** (-(jnp.arange(head_width // 2).astype(jnp.float32) * 2.0) / head_width)
    angles = position_ids.astype(jnp.float32)[..., None] * frequencies
    angles = jnp.concatenate([angles, angles], axis=-1)
    return (jnp.cos(angles)[..., None, :], jnp.sin(angles)[..., None, :])


def rotate(values, cosine_table, sine_table):
    half_width = values.shape[-1] // 2
    turned = jnp.concatenate([-values[..., half_width:], values[..., :half_width]], axis=-1)
    return values * cosine_table + turned * sine_table


def unrotate(grad_values, cosine_table, sine_table):
    half_width = grad_values.shape[-1] // 2
    scaled = grad_values * sine_table
    return grad_values * cosine_table + jnp.concatenate(
        [scaled[..., half_width:], -scaled[..., :half_width]], axis=-1
    )


def norm_rows(values, gain_row):
    inverse = lax.rsqrt(jnp.mean(values * values, axis=-1, keepdims=True) + EPSILON)
    return (values * inverse * gain_row, inverse)


def norm_back(values, inverse, gain_row, grad_values):
    weighted = grad_values * gain_row
    inner_mean = jnp.mean(weighted * values, axis=-1, keepdims=True)
    input_grad = inverse * weighted - values * inverse**3 * inner_mean
    gain_grad = jnp.sum((grad_values * values * inverse).reshape(-1, values.shape[-1]), axis=0)
    return (input_grad, gain_grad)


def pick(flag, first_tree, second_tree):
    return jax.tree.map(
        lambda left_side, right_side: jnp.where(flag, left_side, right_side),
        first_tree,
        second_tree,
    )


def masked_scores(queries, keys_now, query_pos, key_now):
    score_scale = 1.0 / math.sqrt(queries.shape[-1])
    allowed = (key_now[:, None, :] <= query_pos[:, :, None])[:, :, None, :]
    scores = (
        jnp.einsum("grhd,gkd->grhk", queries, keys_now, preferred_element_type=jnp.float32)
        * score_scale
    )
    return (jnp.where(allowed, scores, -1e30), allowed)


def attend_forward(queries, pair_group, query_pos, key_pos):
    head_width = queries.shape[-1]
    row_shape = queries.shape[:3]
    shard_piece = lax.all_gather(pair_group, "ctx", axis=1, tiled=True)
    running = jnp.full(row_shape, -1e30, jnp.float32)
    keys_now = shard_piece[:, :, 0, :head_width]
    values_now = shard_piece[:, :, 0, head_width:]
    scores, allowed = masked_scores(queries, keys_now, query_pos, key_pos)
    highest = jnp.maximum(running, jnp.max(scores, axis=-1))
    probs_now = jnp.where(allowed, jnp.exp(scores - highest[..., None]), 0.0)
    totals = jnp.sum(probs_now, axis=-1)
    accumulated = jnp.einsum(
        "grhk,gkd->grhd",
        probs_now.astype(jnp.bfloat16),
        values_now,
        preferred_element_type=jnp.float32,
    )
    running, totals, accumulated = (highest, totals, accumulated)
    return (accumulated / totals[..., None], running + jnp.log(totals))


def attend_backward(queries, pair_group, query_pos, key_pos, out_grads, lse_rows, delta_rows):
    head_width = queries.shape[-1]
    score_scale = 1.0 / math.sqrt(head_width)
    shard_piece = lax.all_gather(pair_group, "ctx", axis=1, tiled=True)
    keys_now = shard_piece[:, :, 0, :head_width]
    values_now = shard_piece[:, :, 0, head_width:]
    scores, allowed = masked_scores(queries, keys_now, query_pos, key_pos)
    probs_now = jnp.where(allowed, jnp.exp(scores - lse_rows[..., None]), 0.0)
    prob_grads = jnp.einsum(
        "grhd,gkd->grhk", out_grads, values_now, preferred_element_type=jnp.float32
    )
    score_grads = (probs_now * (prob_grads - delta_rows[..., None])).astype(jnp.bfloat16)
    query_grads = score_scale * jnp.einsum(
        "grhk,gkd->grhd", score_grads, keys_now, preferred_element_type=jnp.float32
    )
    key_part = score_scale * jnp.einsum(
        "grhk,grhd->gkd", score_grads, queries, preferred_element_type=jnp.float32
    )
    value_part = jnp.einsum(
        "grhk,grhd->gkd",
        probs_now.astype(jnp.bfloat16),
        out_grads,
        preferred_element_type=jnp.float32,
    )
    piece_term = jnp.concatenate([key_part, value_part], axis=-1)[:, :, None, :]
    return (query_grads, piece_term)


def layer_forward(inputs, own_pos, query_pos, key_pos, weights, heads_total):
    gain_one, bias_all, w_qkv, w_out, gain_two, w_gate_up, w_down = weights
    batch_length = inputs.shape[0]
    rows_total = inputs.shape[1]
    per_device = QUERY_HEADS // heads_total
    copy_count = heads_total // KEY_VALUE_HEADS
    query_columns = QUERY_HEADS * HEAD_WIDTH_SIZE
    key_columns = KEY_VALUE_HEADS * HEAD_WIDTH_SIZE
    residual = inputs.astype(jnp.float32)
    normed_one, inverse_one = norm_rows(residual, gain_one.astype(jnp.float32))
    normed_low = normed_one.astype(jnp.bfloat16)
    projected_rows = jnp.einsum(
        "grd,dc->grc", normed_low, w_qkv, preferred_element_type=jnp.float32
    ) + bias_all.astype(jnp.float32)
    cosine_table, sine_table = rope_tables(own_pos, HEAD_WIDTH_SIZE)
    queries = rotate(
        projected_rows[..., :query_columns].reshape(
            batch_length, rows_total, QUERY_HEADS, HEAD_WIDTH_SIZE
        ),
        cosine_table,
        sine_table,
    )
    key_row_block = rotate(
        projected_rows[..., query_columns : query_columns + key_columns].reshape(
            batch_length, rows_total, KEY_VALUE_HEADS, HEAD_WIDTH_SIZE
        ),
        cosine_table,
        sine_table,
    )
    value_row_block = projected_rows[..., query_columns + key_columns :].reshape(
        batch_length, rows_total, KEY_VALUE_HEADS, HEAD_WIDTH_SIZE
    )
    pair_rows = jnp.concatenate(
        [
            jnp.repeat(key_row_block, copy_count, axis=2),
            jnp.repeat(value_row_block, copy_count, axis=2),
        ],
        axis=-1,
    ).astype(jnp.bfloat16)
    query_send = queries.astype(jnp.bfloat16).reshape(
        batch_length, rows_total, heads_total, per_device * HEAD_WIDTH_SIZE
    )
    query_group, pair_group = (
        lax.all_to_all(query_send, "head", split_axis=2, concat_axis=1, tiled=True),
        lax.all_to_all(pair_rows, "head", split_axis=2, concat_axis=1, tiled=True),
    )
    group_rows = query_group.shape[1]
    query_group = query_group.reshape(batch_length, group_rows, per_device, HEAD_WIDTH_SIZE)
    attended, lse_rows = attend_forward(query_group, pair_group, query_pos, key_pos)
    out_send = attended.astype(jnp.bfloat16).reshape(
        batch_length, group_rows, 1, per_device * HEAD_WIDTH_SIZE
    )
    out_rows = lax.all_to_all(out_send, "head", split_axis=1, concat_axis=2, tiled=True).reshape(
        batch_length, rows_total, QUERY_HEADS * HEAD_WIDTH_SIZE
    )
    middle = residual + jnp.einsum(
        "grc,dc->grd", out_rows, w_out, preferred_element_type=jnp.float32
    )
    normed_two, inverse_two = norm_rows(middle, gain_two.astype(jnp.float32))
    normed_two_low = normed_two.astype(jnp.bfloat16)
    gate_up = jnp.einsum(
        "grd,dc->grc", normed_two_low, w_gate_up, preferred_element_type=jnp.float32
    )
    hidden_low = (jax.nn.silu(gate_up[..., :FF]) * gate_up[..., FF:]).astype(jnp.bfloat16)
    output = middle + jnp.einsum(
        "grf,df->grd", hidden_low, w_down, preferred_element_type=jnp.float32
    )
    kept_now = (
        residual,
        inverse_one,
        normed_low,
        query_group,
        pair_group,
        attended,
        lse_rows,
        out_rows,
        middle,
        inverse_two,
        normed_two_low,
        gate_up,
        hidden_low,
    )
    return (output, kept_now)


def layer_backward(out_grad, kept_now, own_pos, query_pos, key_pos, weights, heads_total):
    gain_one, bias_all, w_qkv, w_out, gain_two, w_gate_up, w_down = weights
    (
        residual,
        inverse_one,
        normed_low,
        query_group,
        pair_group,
        attended,
        lse_rows,
        out_rows,
        middle,
        inverse_two,
        normed_two_low,
        gate_up,
        hidden_low,
    ) = kept_now
    batch_length = out_grad.shape[0]
    rows_total = out_grad.shape[1]
    per_device = QUERY_HEADS // heads_total
    copy_count = heads_total // KEY_VALUE_HEADS
    branch_low = out_grad.astype(jnp.bfloat16)
    hidden_grad = jnp.einsum("grd,df->grf", branch_low, w_down, preferred_element_type=jnp.float32)
    gate_values = gate_up[..., :FF]
    up_values = gate_up[..., FF:]
    sigmoid_gate = jax.nn.sigmoid(gate_values)
    gate_grad = hidden_grad * up_values * sigmoid_gate * (1.0 + gate_values * (1.0 - sigmoid_gate))
    up_grad = hidden_grad * gate_values * sigmoid_gate
    gate_up_low = jnp.concatenate([gate_grad, up_grad], axis=-1).astype(jnp.bfloat16)
    normed_two_grad = jnp.einsum(
        "grc,dc->grd", gate_up_low, w_gate_up, preferred_element_type=jnp.float32
    )
    middle_part, gain_two_grad = norm_back(
        middle, inverse_two, gain_two.astype(jnp.float32), normed_two_grad
    )
    middle_grad = out_grad + middle_part
    middle_low = middle_grad.astype(jnp.bfloat16)
    out_grad_rows = jnp.einsum(
        "grd,dc->grc", middle_low, w_out, preferred_element_type=jnp.float32
    ).astype(jnp.bfloat16)
    out_grad_rows = out_grad_rows.reshape(
        batch_length, rows_total, heads_total, per_device * HEAD_WIDTH_SIZE
    )
    out_grad_group = lax.all_to_all(out_grad_rows, "head", split_axis=2, concat_axis=1, tiled=True)
    group_rows = out_grad_group.shape[1]
    out_grad_group = out_grad_group.reshape(batch_length, group_rows, per_device, HEAD_WIDTH_SIZE)
    delta_rows = jnp.sum(out_grad_group.astype(jnp.float32) * attended, axis=-1)
    query_grads, key_grads = attend_backward(
        query_group, pair_group, query_pos, key_pos, out_grad_group, lse_rows, delta_rows
    )
    pair_own = lax.psum_scatter(
        key_grads.astype(jnp.bfloat16), "ctx", scatter_dimension=1, tiled=True
    )
    query_send = query_grads.astype(jnp.bfloat16).reshape(
        batch_length, group_rows, 1, per_device * HEAD_WIDTH_SIZE
    )
    query_back, paired_backward = (
        lax.all_to_all(query_send, "head", split_axis=1, concat_axis=2, tiled=True),
        lax.all_to_all(pair_own, "head", split_axis=1, concat_axis=2, tiled=True),
    )
    query_rows = query_back.astype(jnp.float32).reshape(
        batch_length, rows_total, QUERY_HEADS, HEAD_WIDTH_SIZE
    )
    paired_sum = jnp.sum(
        paired_backward.astype(jnp.float32).reshape(
            batch_length, rows_total, KEY_VALUE_HEADS, copy_count, 2 * HEAD_WIDTH_SIZE
        ),
        axis=3,
    )
    cosine_table, sine_table = rope_tables(own_pos, HEAD_WIDTH_SIZE)
    query_pre = unrotate(query_rows, cosine_table, sine_table).reshape(
        batch_length, rows_total, QUERY_HEADS * HEAD_WIDTH_SIZE
    )
    key_pre = unrotate(paired_sum[..., :HEAD_WIDTH_SIZE], cosine_table, sine_table).reshape(
        batch_length, rows_total, KEY_VALUE_HEADS * HEAD_WIDTH_SIZE
    )
    value_before_rotation = paired_sum[..., HEAD_WIDTH_SIZE:].reshape(
        batch_length, rows_total, KEY_VALUE_HEADS * HEAD_WIDTH_SIZE
    )
    projected_low = jnp.concatenate([query_pre, key_pre, value_before_rotation], axis=-1).astype(
        jnp.bfloat16
    )
    bias_grad = jnp.sum(
        projected_low.astype(jnp.float32).reshape(-1, projected_low.shape[-1]), axis=0
    )
    normed_grad = jnp.einsum(
        "grc,dc->grd", projected_low, w_qkv, preferred_element_type=jnp.float32
    )
    input_part, gain_one_grad = norm_back(
        residual, inverse_one, gain_one.astype(jnp.float32), normed_grad
    )
    input_grad = middle_grad + input_part
    pieces = (
        normed_low,
        projected_low,
        middle_low,
        out_rows,
        normed_two_low,
        gate_up_low,
        branch_low,
        hidden_low,
    )
    return (input_grad, pieces, (gain_one_grad, bias_grad, gain_two_grad))


def reduce_block(left_side, columns):
    block_term = jnp.einsum("rd,rc->dc", left_side, columns, preferred_element_type=jnp.float32)
    return lax.psum_scatter(block_term, ("head", "ctx"), scatter_dimension=0, tiled=True)


def local(
    tokens,
    positions,
    norm1_gain,
    qkv_bias,
    qkv_weight,
    out_weight,
    norm2_gain,
    gate_up_weight,
    down_weight,
    cotangent,
):
    heads_total = lax.axis_size("head")
    rank_count = lax.axis_size("ctx")
    batch_count = tokens.shape[0]
    rows_total = tokens.shape[1]
    seq_total = positions.shape[1]
    group_rows = heads_total * rows_total
    section_index = lax.axis_index("section")
    rank_index = lax.axis_index("ctx")
    block_index = lax.axis_index("head") * rank_count + rank_index
    ordered = (
        positions.reshape(batch_count, heads_total, rank_count, rows_total)
        .transpose(0, 2, 1, 3)
        .reshape(batch_count, seq_total)
    )
    group_count = batch_count // batch_count
    tick_count = group_count + 1

    def positions_for(group_index):
        first_row = group_index * batch_count
        own_pos = lax.dynamic_slice(
            positions, (first_row, block_index * rows_total), (batch_count, rows_total)
        )
        query_pos = lax.dynamic_slice_in_dim(ordered, rank_index * group_rows, group_rows, 1)
        return (own_pos, query_pos, ordered)

    shards = (norm1_gain, qkv_bias, qkv_weight, out_weight, norm2_gain, gate_up_weight, down_weight)
    weights = tuple(
        (
            shard_value[0]
            for shard_value in (
                lax.all_gather(shards[0], ("head", "ctx"), axis=1, tiled=True),
                lax.all_gather(shards[1], ("head", "ctx"), axis=1, tiled=True),
                lax.all_gather(shards[2], ("head", "ctx"), axis=1, tiled=True),
                lax.all_gather(shards[3], ("head", "ctx"), axis=1, tiled=True),
                lax.all_gather(shards[4], ("head", "ctx"), axis=1, tiled=True),
                lax.all_gather(shards[5], ("head", "ctx"), axis=1, tiled=True),
                lax.all_gather(shards[6], ("head", "ctx"), axis=1, tiled=True),
            )
        )
    )
    received = jnp.zeros((batch_count, rows_total, tokens.shape[2]), jnp.bfloat16)
    outputs = []
    kept_list = []
    for tick_now in range(tick_count):
        first_row = min(tick_now, group_count - 1) * batch_count
        inputs = jnp.where(section_index == 0, tokens, received)
        own_pos, query_pos, key_pos = positions_for(
            jnp.clip(tick_now - section_index, 0, group_count - 1)
        )
        result, kept_now = layer_forward(inputs, own_pos, query_pos, key_pos, weights, heads_total)
        result_low = result.astype(jnp.bfloat16)
        outputs.append(result_low)
        kept_list.append(kept_now)
        if tick_now + 1 < tick_count:
            received = from_behind(result_low, "section", 1)
    received = jnp.zeros((batch_count, rows_total, tokens.shape[2]), jnp.bfloat16)
    grads_in = []
    piece_list = []
    small_sums = None
    for tick_now in range(tick_count):
        first_row = min(tick_now, group_count - 1) * batch_count
        incoming = jnp.where(section_index == 1, cotangent, received).astype(jnp.float32)
        kept_now = pick(
            section_index == 0,
            kept_list[max(tick_now - 1, 0)],
            kept_list[min(tick_now + 1, tick_count - 1)],
        )
        group_number = tick_now - 1 + section_index
        own_pos, query_pos, key_pos = positions_for(jnp.clip(group_number, 0, group_count - 1))
        input_grad, pieces, smalls = layer_backward(
            incoming, kept_now, own_pos, query_pos, key_pos, weights, heads_total
        )
        valid_flag = jnp.logical_and(group_number >= 0, group_number < group_count)
        smalls = tuple((jnp.where(valid_flag, entry_value, 0.0) for entry_value in smalls))
        if small_sums is None:
            small_sums = smalls
        else:
            small_sums = tuple(
                (left_side + right_side for left_side, right_side in zip(small_sums, smalls))
            )
        grad_low = input_grad.astype(jnp.bfloat16)
        grads_in.append(grad_low)
        piece_list.append(pieces)
        if tick_now + 1 < tick_count:
            received = from_behind(grad_low, "section", -1)
    activations = jnp.where(section_index == 0, outputs[0], outputs[1])[None]
    input_grads = jnp.where(section_index == 0, grads_in[1], grads_in[0])[None]
    chosen = [pick(section_index == 0, piece_list[1], piece_list[0])]
    merged = tuple(
        (
            jnp.concatenate([chosen_set[slot_number] for chosen_set in chosen], axis=0).reshape(
                batch_count * rows_total, -1
            )
            for slot_number in range(8)
        )
    )
    (
        normed_all,
        projected_all,
        middle_all,
        attn_all,
        normed_two_all,
        gate_up_all,
        branch_all,
        hidden_all,
    ) = merged
    pair_list = (
        (normed_all, projected_all),
        (middle_all, attn_all),
        (normed_two_all, gate_up_all),
        (branch_all, hidden_all),
    )
    share_list = []
    for left_side, right_side in pair_list:
        width_total = right_side.shape[1]
        piece_count = width_total // 4480 if width_total % 4480 == 0 else 1
        piece_width = width_total // piece_count
        piece_shares = []
        for piece_number in range(piece_count):
            columns = right_side[:, piece_number * piece_width : (piece_number + 1) * piece_width]
            piece_shares.append(reduce_block(left_side, columns))
        share_list.append(jnp.concatenate(piece_shares, axis=1)[None])
    qkv_weight_grad, out_weight_grad, gate_up_grad, down_grad = share_list
    split_width = (QUERY_HEADS + KEY_VALUE_HEADS) * HEAD_WIDTH_SIZE
    bias_sum = small_sums[1]
    gain_one_share, query_key_share, value_share, gain_two_share = (
        lax.psum_scatter(small_sums[0][None], ("head", "ctx"), scatter_dimension=1, tiled=True),
        lax.psum_scatter(
            bias_sum[None, :split_width], ("head", "ctx"), scatter_dimension=1, tiled=True
        ),
        lax.psum_scatter(
            bias_sum[None, split_width:], ("head", "ctx"), scatter_dimension=1, tiled=True
        ),
        lax.psum_scatter(small_sums[2][None], ("head", "ctx"), scatter_dimension=1, tiled=True),
    )
    return (
        activations,
        input_grads,
        gain_one_share,
        query_key_share,
        value_share,
        qkv_weight_grad,
        out_weight_grad,
        gain_two_share,
        gate_up_grad,
        down_grad,
    )


MESH_ID = pl.DeviceIdType.MESH
BF = jnp.bfloat16
F32 = jnp.float32
LANES = 128
HB = 128
VMEM_LIMIT = 60 * 1024 * 1024
DMA = pltpu.SemaphoreType.DMA
NT = (((1,), (1,)), ((), ()))
TN = (((0,), (0,)), ((), ()))
NN = (((1,), (0,)), ((), ()))


def mm(left_side, right_side, form=NN):
    return lax.dot_general(left_side, right_side, form, preferred_element_type=F32)


def where_am_i():
    head = lax.axis_index("head")
    return (lax.axis_index("section"), head // 2, lax.rem(head, 2), lax.axis_index("ctx"))


def at(x, y, k, z):
    return (x, y * 2 + k, z)


def remote(source, target, send_sem, recv_sem, device):
    return pltpu.make_async_remote_copy(
        src_ref=source,
        dst_ref=target,
        send_sem=send_sem,
        recv_sem=recv_sem,
        device_id=device,
        device_id_type=MESH_ID,
    )


def arrived(ref, sem):
    pltpu.make_async_copy(ref, ref, sem).wait()


def greet(devices):
    barrier = pltpu.get_barrier_semaphore()
    for device in devices:
        pl.semaphore_signal(barrier, inc=1, device_id=device, device_id_type=MESH_ID)
    pl.semaphore_wait(barrier, len(devices))


def greet_all(index, total, device_of):
    barrier = pltpu.get_barrier_semaphore()

    @pl.loop(1, total)
    def _(step):
        device = device_of(lax.rem(index + step, total))
        pl.semaphore_signal(barrier, inc=1, device_id=device, device_id_type=MESH_ID)

    pl.semaphore_wait(barrier, total - 1)


def params(collective_id):
    return pltpu.CompilerParams(
        collective_id=collective_id, has_side_effects=True, vmem_limit_bytes=VMEM_LIMIT
    )


def vmem():
    return pl.BlockSpec(memory_space=pltpu.VMEM)


def hbm():
    return pl.BlockSpec(memory_space=pl.ANY)


def row_norm(values):
    return lax.rsqrt(jnp.mean(values * values, axis=-1, keepdims=True) + EPSILON)


class Sizes:
    def __init__(self, mesh, tokens, qkv_weight, gate_up, down):
        self.ctx = mesh.shape["ctx"]
        self.group = 4 * self.ctx
        self.total = 2 * self.group
        self.batches, self.seq, self.width = tokens.shape
        self.rows = self.seq // self.group
        self.ff = down.shape[2]
        self.owned = self.width // self.group
        self.blocks = self.ff // HB
        self.plane = self.blocks // 2
        self.most = -(-self.plane // self.group)
        self.least = self.plane // self.group
        self.extra = self.plane % self.group
        self.hidden = self.most * HB
        self.per_group = QUERY_HEADS // 4
        self.qcols = self.per_group * HEAD_WIDTH_SIZE
        self.kcols = HEAD_WIDTH_SIZE
        self.acols = self.qcols + 2 * self.kcols
        self.atot = self.acols + self.qcols

    def fits(self):
        gathered = self.batches * self.seq * self.width * 2
        return (
            self.batches == 2
            and gathered * 3 < VMEM_LIMIT // 2
            and self.ff % (2 * HB) == 0
            and self.ctx % 2 == 0
            and self.least >= 1
            and self.owned % 16 == 0
            and self.rows % 32 == 0
        )


def flat_place(index, group, ctx):
    inside = lax.rem(index, group)
    return (index // group, inside // ctx, lax.rem(inside, ctx))


def block_rank(sz, inside):
    head, z = (inside // sz.ctx, lax.rem(inside, sz.ctx))
    y, k = (head // 2, lax.rem(head, 2))
    turn = jnp.where(z < sz.ctx // 2, 2 * z, 2 * (sz.ctx - 1 - z) + 1)
    return turn + sz.ctx * (2 * k + lax.rem(y + z, 2))


def first_column(sz, owner):
    rank = block_rank(sz, lax.rem(owner, sz.group))
    plane = owner // sz.group * sz.plane
    return pl.multiple_of((plane + rank * sz.least + jnp.minimum(rank, sz.extra)) * HB, HB)


def has_more(sz, owner):
    return block_rank(sz, lax.rem(owner, sz.group)) < sz.extra


def extras_of_head(sz, head):
    count = 0
    for z in range(sz.ctx):
        turn = 2 * z if z < sz.ctx // 2 else 2 * (sz.ctx - 1 - z) + 1
        count += turn + sz.ctx * (2 * (head % 2) + (head // 2 + z) % 2) < sz.extra
    return count


def half_turn(values):
    return pltpu.roll(values, HEAD_WIDTH_SIZE // 2, 1)


def pair_peers(x, y, k, z):
    return (at(1 - x, y, k, z), at(x, 1 - y, k, z), at(1 - x, 1 - y, k, z))


def pair_groups(x, y):
    return (2 * (1 - x) + y, 2 * x + 1 - y, 2 * (1 - x) + 1 - y)


def line_peers(n, x, y, k, z):
    return [at(x, y, k, lax.rem(z + step, n)) for step in range(1, n)]


def tree_peers(n, x, y, k, z):
    return [at(1 - x, y, k, z), at(x, 1 - y, k, z), at(x, y, 1 - k, z)] + line_peers(n, x, y, k, z)


def meet(sz, place, near, across, jobs):
    x, y, k, z = place
    n = sz.ctx
    inside = (y * 2 + k) * n + z
    reach = max([job.reach for job in jobs], default=0)
    if reach == 2:
        greet_all(x * sz.group + inside, sz.total, lambda index: flat_place(index, sz.group, n))
    elif reach == 1:
        barrier = pltpu.get_barrier_semaphore()
        for device in across:
            pl.semaphore_signal(barrier, inc=1, device_id=device, device_id_type=MESH_ID)

        @pl.loop(1, sz.group)
        def _(step):
            device = flat_place(x * sz.group + lax.rem(inside + step, sz.group), sz.group, n)
            pl.semaphore_signal(barrier, inc=1, device_id=device, device_id_type=MESH_ID)

        pl.semaphore_wait(barrier, sz.group - 1 + len(across))
    else:
        greet(near)


def run_call(body, ins, outs, scratch, jobs, collective_id, name):
    fg_in, fg_out, fg_scratch = len(ins), len(outs), len(scratch)
    ins, outs, scratch = list(ins), list(outs), list(scratch)
    for job in jobs:
        ins += [(array, hbm() if spec is None else spec) for array, spec in job.ins]
        outs += [(shape, hbm()) for shape in job.outs]
        scratch += job.scratch

    def kernel(*refs):
        given, made, own = (
            refs[: len(ins)],
            refs[len(ins) : len(ins) + len(outs)],
            refs[len(ins) + len(outs) :],
        )
        a, b, c = fg_in, fg_out, fg_scratch
        for job in jobs:
            job.bind(
                given[a : a + len(job.ins)],
                made[b : b + len(job.outs)],
                own[c : c + len(job.scratch)],
            )
            a, b, c = a + len(job.ins), b + len(job.outs), c + len(job.scratch)
        body(given[:fg_in], made[:fg_out], own[:fg_scratch], jobs)

    results = pl.pallas_call(
        kernel,
        out_shape=tuple(shape for shape, _ in outs),
        in_specs=[spec for _, spec in ins],
        out_specs=tuple(spec for _, spec in outs),
        scratch_shapes=scratch,
        compiler_params=params(collective_id),
        name=name,
    )(*[array for array, _ in ins])
    at_out, extra = fg_out, []
    for job in jobs:
        extra.append(results[at_out : at_out + len(job.outs)])
        at_out += len(job.outs)
    return (results[:fg_out], extra)


def plane_order(n, place, index):
    x, y, k, z = place
    head = y * 2 + k
    far = 4 * (n - 1)
    if isinstance(index, int) and index == 4 * n - 1:
        return head * n + z
    rest = index - far
    head_to = lax.rem(head + jnp.where(index < far, index // (n - 1), rest + 1), 4)
    ctx_to = lax.rem(z + jnp.where(index < far, 1 + lax.rem(index, n - 1), 0), n)
    return head_to * n + ctx_to


def span_of(count, low, high):
    return (int(count * low), int(count * high))


class Columns:
    reach = 1

    def __init__(self, sz, section, part, gate_up, down, staged):
        self.sz, self.section, self.part = sz, section, part
        self.ins = [(down if part == 2 else gate_up, None), (staged, None)]
        self.outs = [jax.ShapeDtypeStruct((sz.width, sz.hidden), BF)]
        self.scratch = [DMA((2,)), DMA((2,))]

    def bind(self, ins, outs, scratch):
        self.source, self.staged = ins
        self.target = outs[0]
        self.send, self.recv = scratch

    def begin(self, place, low=0.0, high=1.0):
        sz = self.sz
        n = sz.ctx
        x, y, k, z = place
        inside = (y * 2 + k) * n + z
        me = x * sz.group + inside
        first, stop = span_of(sz.group, low, high)
        rows = pl.ds(pl.multiple_of(inside * sz.owned, 16), sz.owned)
        wide = sz.least * HB
        base = sz.ff if self.part == 1 else 0

        def pair(owner, offset, width, own):
            target = self.target.at[rows, pl.ds(offset, width)]
            if own:
                first = pl.multiple_of(base + first_column(sz, owner) + offset, HB)
                return (self.source.at[:, pl.ds(first, width)], target)
            first = first_column(sz, owner) - x * sz.plane * HB + offset
            first = pl.multiple_of(first, HB)
            return (self.staged.at[self.part, :, pl.ds(first, width)], target)

        for own in (True, False):

            @pl.when((x == self.section) == own)
            def _():
                @pl.loop(first, min(stop, sz.group - 1))
                def _(step):
                    owner = x * sz.group + plane_order(n, place, step)
                    device = flat_place(owner, sz.group, n)
                    source, target = pair(owner, 0, wide, own)
                    remote(source, target, self.send.at[0], self.recv.at[0], device).start()
                    if sz.extra:

                        @pl.when(has_more(sz, owner))
                        def _():
                            source, target = pair(owner, wide, HB, own)
                            remote(source, target, self.send.at[1], self.recv.at[1], device).start()

                if stop < sz.group:
                    return
                source, target = pair(me, 0, wide, own)
                pltpu.make_async_copy(source, target, self.send.at[0]).start()
                if sz.extra:

                    @pl.when(has_more(sz, me))
                    def _():
                        source, target = pair(me, wide, HB, own)
                        pltpu.make_async_copy(source, target, self.send.at[1]).start()

    def middle(self, place):
        pass

    def finish(self, place):
        sz = self.sz
        x, y, k, z = place
        me = x * sz.group + (y * 2 + k) * sz.ctx + z
        wide = sz.least * HB
        arrived(self.target.at[pl.ds(0, sz.width - sz.owned), pl.ds(0, wide)], self.recv.at[0])
        arrived(self.target.at[:, pl.ds(0, wide)], self.send.at[0])
        if sz.extra:
            arrived(self.target.at[pl.ds(0, sz.extra * sz.owned), pl.ds(0, HB)], self.send.at[1])

            @pl.when(has_more(sz, me))
            def _():
                arrived(
                    self.target.at[pl.ds(0, sz.width - sz.owned), pl.ds(0, HB)], self.recv.at[1]
                )


def head_columns(sz, g, qkv, out_w):
    kv = g // (4 // KEY_VALUE_HEADS)
    q0 = pl.multiple_of(g * sz.qcols, HB)
    k0 = pl.multiple_of(QUERY_HEADS * HEAD_WIDTH_SIZE + kv * sz.kcols, HB)
    v0 = pl.multiple_of((QUERY_HEADS + KEY_VALUE_HEADS) * HEAD_WIDTH_SIZE + kv * sz.kcols, HB)
    return (
        (qkv.at[:, pl.ds(q0, sz.qcols)], pl.ds(0, sz.qcols)),
        (qkv.at[:, pl.ds(k0, sz.kcols)], pl.ds(sz.qcols, sz.kcols)),
        (qkv.at[:, pl.ds(v0, sz.kcols)], pl.ds(sz.qcols + sz.kcols, sz.kcols)),
        (out_w.at[:, pl.ds(q0, sz.qcols)], pl.ds(sz.acols, sz.qcols)),
    )


class Heads:
    reach = 1

    def __init__(self, sz, section, qkv, out_w, staged):
        self.sz, self.section = sz, section
        self.ins = [(qkv, None), (out_w, None), (staged, None)]
        self.outs = [jax.ShapeDtypeStruct((sz.width, sz.atot), BF)]
        self.scratch = [DMA, DMA, DMA((2,)), DMA((2,))]

    def bind(self, ins, outs, scratch):
        self.qkv, self.out_w, self.staged = ins
        self.target = outs[0]
        self.send, self.recv, self.s_core, self.r_core = scratch

    def begin(self, place, low=0.0, high=1.0):
        sz = self.sz
        n = sz.ctx
        x, y, k, z = place
        rows = pl.ds(pl.multiple_of(((y * 2 + k) * n + z) * sz.owned, 16), sz.owned)
        mine = y * n + z

        def pairs(y_to, own):
            if own:
                return [
                    (source, self.target.at[rows, cols])
                    for source, cols in head_columns(sz, 2 * x + y_to, self.qkv, self.out_w)
                ]
            return [(self.staged.at[y_to], self.target.at[rows])]

        for own in (True, False):

            @pl.when((x == self.section) == own)
            def _():
                @pl.loop(1, 2 * n)
                def _(step):
                    index = lax.rem(mine + step, 2 * n)
                    for source, target in pairs(index // n, own):
                        remote(
                            source, target, self.send, self.recv, at(x, index // n, k, lax.rem(index, n))
                        ).start()

                for source, target in pairs(y, own):
                    pltpu.make_async_copy(source, target, self.send).start()

    def span(self, part, k):
        stretch = self.sz.width // 4
        return self.target.at[pl.ds(pl.multiple_of((part * 2 + k) * stretch, 16), stretch)]

    def middle(self, place):
        sz = self.sz
        x, y, k, z = place
        half = sz.width // 2
        arrived(self.target.at[pl.ds(0, half - sz.owned)], self.recv)
        arrived(self.target.at[pl.ds(0, half)], self.send)
        for part in range(2):
            span = self.span(part, k)
            remote(span, span, self.s_core.at[part], self.r_core.at[part], at(x, y, 1 - k, z)).start()

    def finish(self, place):
        x, y, k, z = place
        for part in range(2):
            span = self.span(part, 1 - k)
            arrived(span, self.r_core.at[part])
            arrived(span, self.s_core.at[part])


class LineShares:
    reach = 0

    def __init__(self, sz, part, grads=None):
        self.sz, self.part = sz, part
        self.ins = [] if grads is None else [(grads, None)]
        self.outs = [jax.ShapeDtypeStruct((sz.ctx, 4, sz.owned, sz.hidden), BF)]
        self.scratch = [DMA((2, sz.ctx)), DMA((2, sz.ctx))]

    def bind(self, ins, outs, scratch):
        if ins:
            self.source = ins[0]
        self.target = outs[0]
        self.send, self.recv = scratch

    def moves(self, place, step, offset, width):
        sz = self.sz
        x, y, k, z = place
        ctx = lax.rem(z + step, sz.ctx)
        for head in range(4):
            rows = pl.ds(pl.multiple_of((head * sz.ctx + ctx) * sz.owned, 16), sz.owned)
            cols = pl.ds(offset, width)
            yield (self.source.at[self.part, rows, cols], self.target.at[z, head, :, cols])

    def begin(self, place):
        sz = self.sz
        n = sz.ctx
        x, y, k, z = place
        me = x * sz.group + (y * 2 + k) * n + z
        wide = sz.least * HB

        def go(kind, offset, width):
            for step in list(range(1, n)) + [0]:
                for source, target in self.moves(place, step, offset, width):
                    if step:
                        remote(
                            source,
                            target,
                            self.send.at[kind, step],
                            self.recv.at[kind, step],
                            at(x, y, k, lax.rem(z + step, n)),
                        ).start()
                    else:
                        pltpu.make_async_copy(source, target, self.send.at[kind, 0]).start()

        go(0, 0, wide)
        if sz.extra:

            @pl.when(has_more(sz, me))
            def _():
                go(1, wide, HB)

    def finish(self, place):
        sz = self.sz
        n = sz.ctx
        x, y, k, z = place
        first = x * sz.group + (y * 2 + k) * n
        wide = sz.least * HB
        for step in range(n):
            ctx = lax.rem(z + n - step, n)
            arrived(self.target.at[ctx, :, :, pl.ds(0, wide)], self.send.at[0, step])
            if step:
                arrived(self.target.at[ctx, :, :, pl.ds(0, wide)], self.recv.at[0, step])
            if sz.extra:

                @pl.when(has_more(sz, first + z))
                def _():
                    arrived(self.target.at[ctx, :, :, pl.ds(wide, HB)], self.send.at[1, step])

                if step:

                    @pl.when(has_more(sz, first + ctx))
                    def _():
                        arrived(self.target.at[ctx, :, :, pl.ds(wide, HB)], self.recv.at[1, step])


class PlaneShares:
    def __init__(self, sz, section, part, source, target, sems):
        self.sz, self.section, self.part = sz, section, part
        self.source, self.target = source, target
        self.send, self.recv, self.local, self.s_over, self.r_over = sems

    def begin(self, place):
        sz = self.sz
        n = sz.ctx
        x, y, k, z = place
        head = y * 2 + k
        wide = sz.least * HB
        slot = jnp.where(x == self.section, 0, 1)

        def go(to, device, local):
            for ctx in range(n):
                owner = x * sz.group + head * n + ctx
                first = first_column(sz, owner)

                def one(kind, offset, width):
                    source = self.source.at[ctx, to, :, pl.ds(offset, width)]
                    cols = pl.ds(pl.multiple_of(first + offset, HB), width)
                    target = self.target.at[slot, self.part, :, cols]
                    if local:
                        pltpu.make_async_copy(source, target, self.local.at[kind]).start()
                    else:
                        recv = self.recv.at[0] if kind == 0 else self.recv.at[1 + head]
                        remote(source, target, self.send.at[kind], recv, device).start()

                one(0, 0, wide)
                if sz.extra:

                    @pl.when(has_more(sz, owner))
                    def _():
                        one(1, wide, HB)

        for step in range(1, 4):
            to = lax.rem(head + step, 4)
            go(to, (x, to, z), False)
        go(head, None, True)

    def cross(self, place):
        sz = self.sz
        n = sz.ctx
        x, y, k, z = place
        head = y * 2 + k
        wide = sz.least * HB
        row = self.target.at[0, self.part]
        arrived(row.at[:, pl.ds(0, 3 * n * wide)], self.recv.at[0])
        arrived(row.at[:, pl.ds(0, 3 * n * wide)], self.send.at[0])
        arrived(row.at[:, pl.ds(0, n * wide)], self.local.at[0])
        for other in range(4):
            count = extras_of_head(sz, other)
            if count:

                @pl.when(head != other)
                def _():
                    arrived(row.at[:, pl.ds(0, count * HB)], self.recv.at[1 + other])

                @pl.when(head == other)
                def _():
                    arrived(row.at[:, pl.ds(0, 3 * count * HB)], self.send.at[1])
                    arrived(row.at[:, pl.ds(0, count * HB)], self.local.at[1])

        @pl.when(x != self.section)
        def _():
            self.over(place).start()

    def over(self, place):
        x, y, k, z = place
        plane = 1 - self.section
        cols = pl.ds(plane * self.sz.plane * HB, self.sz.plane * HB)
        return remote(
            self.target.at[1, self.part, :, cols],
            self.target.at[0, self.part, :, cols],
            self.s_over,
            self.r_over,
            at(1 - x, y, k, z),
        )

    def finish(self, place):
        x = place[0]

        @pl.when(x != self.section)
        def _():
            self.over(place).wait_send()

        @pl.when(x == self.section)
        def _():
            self.over(place).wait_recv()


class ReturnedHeads:
    reach = 0

    def __init__(self, sz, section, grads):
        self.sz, self.section = sz, section
        stretch = sz.width // 4
        self.ins = [(grads, vmem())]
        self.outs = [jax.ShapeDtypeStruct((4, sz.owned, sz.atot), BF)]
        self.scratch = [
            pltpu.VMEM((2, stretch, sz.atot), BF),
            pltpu.VMEM((2, stretch, sz.atot), BF),
            pltpu.VMEM((sz.ctx, 2, sz.owned, sz.atot), BF),
            DMA((2,)),
            DMA((2,)),
            DMA((sz.ctx,)),
            DMA((sz.ctx,)),
            DMA((2,)),
            DMA((4,)),
        ]

    def bind(self, ins, outs, scratch):
        self.source, self.target = ins[0], outs[0]
        (
            self.got,
            self.summed,
            self.lined,
            self.s_core,
            self.r_core,
            self.s_line,
            self.r_line,
            self.send,
            self.recv,
        ) = scratch

    def rows(self, part, k):
        stretch = self.sz.width // 4
        return pl.ds(pl.multiple_of((part * 2 + k) * stretch, 16), stretch)

    def core(self, place, part):
        x, y, k, z = place
        return remote(
            self.source.at[self.rows(part, 1 - k)],
            self.got.at[part],
            self.s_core.at[part],
            self.r_core.at[part],
            at(x, y, 1 - k, z),
        )

    def own(self, ctx):
        return pl.ds(pl.multiple_of(ctx * self.sz.owned, 16), self.sz.owned)

    def line(self, place, step):
        x, y, k, z = place
        ctx = lax.rem(z + step, self.sz.ctx)
        return remote(
            self.summed.at[:, self.own(ctx)],
            self.lined.at[step],
            self.s_line.at[step],
            self.r_line.at[step],
            at(x, y, k, ctx),
        )

    def begin(self, place):
        for part in range(2):
            self.core(place, part).start()

    def middle(self, place):
        k = place[2]
        for part in range(2):
            self.core(place, part).wait_recv()
            total = self.source[self.rows(part, k)].astype(F32) + self.got[part].astype(F32)
            self.summed[part] = total.astype(BF)
        for step in range(1, self.sz.ctx):
            self.line(place, step).start()

    def home(self, place, part):
        x, y, k, z = place
        group = 2 * x + y
        device = at(self.section, part, k, z)
        return (self.lined.at[0, part], self.target.at[group], self.send.at[part], self.recv.at[group], device)

    def homes(self, place, starting):
        x, y, k, z = place
        for part in range(2):
            own = jnp.logical_and(x == self.section, y == part)

            @pl.when(jnp.logical_not(own))
            def _():
                copy = remote(*self.home(place, part))
                copy.start() if starting else copy.wait_send()

            @pl.when(own)
            def _():
                source, target, send, _, _ = self.home(place, part)
                copy = pltpu.make_async_copy(source, target, send)
                copy.start() if starting else copy.wait()

    def late(self, place):
        x, y, k, z = place
        total = self.summed[:, self.own(z)].astype(F32)
        for step in range(1, self.sz.ctx):
            self.line(place, step).wait_recv()
            total = total + self.lined[step].astype(F32)
        self.lined[0] = total.astype(BF)
        self.homes(place, True)

    def finish(self, place):
        x, y, k, z = place
        for part in range(2):
            self.core(place, part).wait_send()
        for step in range(1, self.sz.ctx):
            self.line(place, step).wait_send()
        self.homes(place, False)

        @pl.when(x == self.section)
        def _():
            for group in range(4):

                @pl.when(group != 2 * x + y)
                def _():
                    arrived(self.target.at[group], self.recv.at[group])


def begin(jobs, place, low=0.0, high=1.0):
    for job in jobs:
        job.begin(place, low, high)


def middle(jobs, place):
    for job in jobs:
        job.middle(place)


def finish(jobs, place):
    for job in jobs:
        job.finish(place)


class Gather:
    SEMS = 12

    @staticmethod
    def scratch(n):
        return [DMA((n,))] * 10 + [DMA((4, n))] * 2

    def __init__(self, n, rows, buffer, place, sems):
        self.n, self.half, self.buffer = n, rows // 2, buffer
        self.x, self.y, self.k, self.z = place
        x, y = self.x, self.y
        self.groups = (2 * x + y, 2 * x + 1 - y, 2 * (1 - x) + y, 2 * (1 - x) + 1 - y)
        (
            self.sz,
            self.rz,
            self.sy,
            self.ry,
            self.sx,
            self.rx,
            self.syd,
            self.ryd,
            self.sxd,
            self.rxd,
            self.sc,
            self.rc,
        ) = sems

    def src(self, step):
        return lax.rem(self.z + self.n - step, self.n)

    def line(self, step):
        own = self.buffer.at[self.k, self.groups[0], self.z]
        device = at(self.x, self.y, self.k, lax.rem(self.z + step, self.n))
        return remote(own, own, self.sz.at[step], self.rz.at[step], device)

    def to_y(self, step):
        part = self.buffer.at[self.k, self.groups[0], self.src(step)]
        device = at(self.x, 1 - self.y, self.k, self.z)
        return remote(part, part, self.sy.at[step], self.ry.at[step], device)

    def to_x(self, step):
        part = self.buffer.at[self.k, self.groups[0], self.src(step)]
        device = at(1 - self.x, self.y, self.k, self.z)
        return remote(part, part, self.sx.at[step], self.rx.at[step], device)

    def on_x(self, step):
        part = self.buffer.at[self.k, self.groups[1], self.src(step), pl.ds(0, self.half)]
        device = at(1 - self.x, self.y, self.k, self.z)
        return remote(part, part, self.sxd.at[step], self.rxd.at[step], device)

    def on_y(self, step):
        part = self.buffer.at[self.k, self.groups[2], self.src(step), pl.ds(self.half, self.half)]
        device = at(self.x, 1 - self.y, self.k, self.z)
        return remote(part, part, self.syd.at[step], self.ryd.at[step], device)

    def core(self, which, step):
        part = self.buffer.at[self.k, self.groups[which], self.src(step)]
        device = at(self.x, self.y, 1 - self.k, self.z)
        return remote(part, part, self.sc.at[which, step], self.rc.at[which, step], device)

    def begin(self):
        for step in range(1, self.n):
            self.line(step).start()
        self.spread(0)

    def spread(self, step):
        if step:
            arrived(self.buffer.at[self.k, self.groups[0], self.src(step)], self.rz.at[step])
        self.to_y(step).start()
        self.to_x(step).start()
        self.core(0, step).start()

    def second(self, step):
        arrived(self.buffer.at[self.k, self.groups[1], self.src(step)], self.ry.at[step])
        self.on_x(step).start()
        self.core(1, step).start()
        arrived(self.buffer.at[self.k, self.groups[2], self.src(step)], self.rx.at[step])
        self.on_y(step).start()
        self.core(2, step).start()

    def third(self, step):
        part = self.buffer.at[self.k, self.groups[3], self.src(step)]
        arrived(part.at[pl.ds(0, self.half)], self.rxd.at[step])
        arrived(part.at[pl.ds(self.half, self.half)], self.ryd.at[step])
        self.core(3, step).start()

    def other(self, which):
        for step in range(self.n):
            part = self.buffer.at[1 - self.k, self.groups[which], self.src(step)]
            arrived(part, self.rc.at[which, step])

    def finish(self):
        for step in range(self.n):
            if step:
                self.line(step).wait_send()
            self.to_y(step).wait_send()
            self.to_x(step).wait_send()
            self.on_x(step).wait_send()
            self.on_y(step).wait_send()
            for which in range(4):
                self.core(which, step).wait_send()

    def run(self, column, nearly):
        k, steps = self.k, range(self.n)
        for step in range(1, self.n):
            self.spread(step)
        column(k, 0)
        for step in steps:
            self.second(step)
        self.other(0)
        column(1 - k, 0)
        column(k, 1)
        column(k, 2)
        for step in steps:
            self.third(step)
        self.other(1)
        column(1 - k, 1)
        self.other(2)
        column(1 - k, 2)
        nearly()
        column(k, 3)
        self.other(3)
        column(1 - k, 3)


class Scatter:
    @staticmethod
    def scratch(n, rows, width):
        return [
            pltpu.VMEM((2, 4, n, rows, width), BF),
            pltpu.VMEM((4, n, rows, width), BF),
            pltpu.VMEM((2, n, rows // 2, width), BF),
            pltpu.VMEM((2, n, rows, width), BF),
            pltpu.VMEM((n, rows, width), BF),
            DMA((4,)),
            DMA((4,)),
            DMA((2, n)),
            DMA((2, n)),
            DMA((2, 2, n)),
            DMA((2, 2, n)),
            DMA((n,)),
            DMA((n,)),
        ]

    def __init__(self, n, rows, place, refs):
        self.n, self.rows, self.half = n, rows, rows // 2
        self.x, self.y, self.k, self.z = place
        x, y = self.x, self.y
        self.groups = (2 * x + y, 2 * x + 1 - y, 2 * (1 - x) + y, 2 * (1 - x) + 1 - y)
        (
            self.parts,
            self.from_core,
            self.from_diag,
            self.from_near,
            self.from_line,
            self.s_core,
            self.r_core,
            self.s_diag,
            self.r_diag,
            self.s_near,
            self.r_near,
            self.s_line,
            self.r_line,
        ) = refs
        self.near = (at(x, 1 - y, self.k, self.z), at(1 - x, y, self.k, self.z))

    def slot(self, step):
        return lax.rem(self.z + step, self.n)

    def order(self):
        return list(range(1, self.n)) + [0]

    def core(self, which):
        return remote(
            self.parts.at[1 - self.k, self.groups[which]],
            self.from_core.at[which],
            self.s_core.at[which],
            self.r_core.at[which],
            at(self.x, self.y, 1 - self.k, self.z),
        )

    def diag(self, direction, step):
        rows = pl.ds(self.half if direction == 0 else 0, self.half)
        return remote(
            self.parts.at[self.k, self.groups[3], self.slot(step), rows],
            self.from_diag.at[direction, step],
            self.s_diag.at[direction, step],
            self.r_diag.at[direction, step],
            self.near[direction],
        )

    def close(self, direction, part, step):
        rows = pl.ds(part * self.half, self.half)
        return remote(
            self.parts.at[self.k, self.groups[1 + direction], self.slot(step), rows],
            self.from_near.at[direction, step, rows],
            self.s_near.at[direction, part, step],
            self.r_near.at[direction, part, step],
            self.near[direction],
        )

    def line(self, step):
        return remote(
            self.parts.at[self.k, self.groups[0], self.slot(step)],
            self.from_line.at[step],
            self.s_line.at[step],
            self.r_line.at[step],
            at(self.x, self.y, self.k, self.slot(step)),
        )

    def add_core(self, which):
        self.core(which).wait_recv()
        group = self.groups[which]
        self.parts[self.k, group] = (
            self.parts[self.k, group].astype(F32) + self.from_core[which].astype(F32)
        ).astype(BF)

    def early(self):
        for direction, part in ((0, 1), (1, 0)):
            self.add_core(1 + direction)
            for step in self.order():
                self.close(direction, part, step).start()

    def run(self, fill):
        fill = list(fill) + [lambda: None] * 3
        self.add_core(3)
        for step in self.order():
            self.diag(1, step).start()
            self.diag(0, step).start()
        self.add_core(0)
        fill[0]()
        for step in self.order():
            slot = self.slot(step)
            for direction, part in ((0, 0), (1, 1)):
                came = 1 - direction
                self.diag(came, step).wait_recv()
                rows = pl.ds(part * self.half, self.half)
                group = self.groups[1 + direction]
                self.parts[self.k, group, slot, rows] = (
                    self.parts[self.k, group, slot, rows].astype(F32)
                    + self.from_diag[came, step].astype(F32)
                ).astype(BF)
                self.close(direction, part, step).start()
        fill[1]()
        group = self.groups[0]
        result = None
        for step in self.order():
            slot = self.slot(step)
            for direction in range(2):
                for part in range(2):
                    self.close(direction, part, step).wait_recv()
            total = (
                self.parts[self.k, group, slot].astype(F32)
                + self.from_near[0, step].astype(F32)
                + self.from_near[1, step].astype(F32)
            )
            if step:
                self.parts[self.k, group, slot] = total.astype(BF)
                self.line(step).start()
            else:
                result = total
        fill[2]()
        for step in range(1, self.n):
            self.line(step).wait_recv()
            result = result + self.from_line[step].astype(F32)
        return result

    def finish(self):
        for which in range(4):
            self.core(which).wait_send()
        for step in range(self.n):
            for direction in range(2):
                self.diag(direction, step).wait_send()
                for part in range(2):
                    self.close(direction, part, step).wait_send()
            if step:
                self.line(step).wait_send()


def spread(sz, small, tokens, cotangent, qkv, out_w, gate_up, down):
    n = sz.ctx
    half = sz.plane * HB

    def body(ins, outs, scratch, jobs):
        small, tokens, cotangent, qkv, out_w, gate_up, down = ins
        small_all, tok_own, cot_own, heads_x, cols_x = outs
        s_small, r_small, s_own, r_own, s_hx, r_hx, s_cx, r_cx = scratch
        place = where_am_i()
        x, y, k, z = place
        me = x * sz.group + (y * 2 + k) * n + z
        everyone = lambda index: flat_place(index, sz.group, n)
        greet_all(me, sz.total, everyone)
        across = at(1 - x, y, k, z)

        def heads_over():
            return [
                remote(source, heads_x.at[y_to, :, cols], s_hx, r_hx, across)
                for y_to in range(2)
                for source, cols in head_columns(sz, 2 * (1 - x) + y_to, qkv, out_w)
            ]

        for copy in heads_over():
            copy.start()

        def owns(starting):
            @pl.when(x == y)
            def _():
                for batch in range(2):
                    pairs = ((tokens, tok_own, 0), (cotangent, cot_own, 1))
                    for source, target, slot in pairs:
                        own = jnp.logical_and(k == y, k == batch)

                        @pl.when(jnp.logical_not(own))
                        def _():
                            copy = remote(
                                source.at[batch],
                                target,
                                s_own.at[batch, slot],
                                r_own.at[slot],
                                at(x, k, batch, z),
                            )
                            copy.start() if starting else copy.wait_send()

                        if starting:

                            @pl.when(own)
                            def _():
                                pltpu.make_async_copy(
                                    source.at[batch], target, r_own.at[slot]
                                ).start()

        owns(True)

        @pl.loop(1, sz.total)
        def _(step):
            device = everyone(lax.rem(me + step, sz.total))
            remote(small, small_all.at[me], s_small, r_small, device).start()

        pltpu.make_async_copy(small, small_all.at[me], s_small).start()

        def columns_over(part):
            base = (sz.ff if part == 1 else 0) + (1 - x) * half
            source = (down if part == 2 else gate_up).at[:, pl.ds(pl.multiple_of(base, HB), half)]
            return remote(source, cols_x.at[part], s_cx.at[part], r_cx.at[part], across)

        heads, first = jobs
        heads.use(ins, outs)
        first.use(ins, outs)

        @pl.when(x == heads.section)
        def _():
            heads.begin(place)

        for part in range(3):
            columns_over(part).start()
        arrived(heads_x, r_hx)

        @pl.when(x != heads.section)
        def _():
            heads.begin(place)

        columns_over(0).wait_recv()
        first.begin(place)
        heads.middle(place)
        arrived(small_all.at[pl.ds(0, sz.total - 1)], r_small)
        arrived(small_all, s_small)
        arrived(tok_own, r_own.at[0])
        arrived(cot_own, r_own.at[1])
        owns(False)
        heads.finish(place)

        for part in range(3):
            if part:
                columns_over(part).wait_recv()
            columns_over(part).wait_send()
        arrived(heads_x, s_hx)
        first.finish(place)

    shape = jax.ShapeDtypeStruct
    outs = [
        (shape((sz.total, 16, LANES), BF), hbm()),
        (shape((sz.rows, sz.width), BF), hbm()),
        (shape((sz.rows, sz.width), BF), hbm()),
        (shape((2, sz.owned, sz.atot), BF), hbm()),
        (shape((3, sz.owned, half), BF), hbm()),
    ]
    arrays = (small, tokens, cotangent, qkv, out_w, gate_up, down)
    scratch = [DMA, DMA, DMA((2, 2)), DMA((2,)), DMA, DMA, DMA((3,)), DMA((3,))]
    jobs = [OwnHeads(sz, 0, 3, 4, 3), OwnColumns(sz, 0, 0, 5, 4)]
    return run_call(body, [(a, hbm()) for a in arrays], outs, scratch, jobs, 1, "spread_weights")


class OwnHeads(Heads):
    def __init__(self, sz, section, qkv, out_w, staged):
        super().__init__(sz, section, None, None, None)
        self.ins = []
        self.named = (qkv, out_w, staged)

    def bind(self, ins, outs, scratch):
        self.target = outs[0]
        self.send, self.recv, self.s_core, self.r_core = scratch

    def use(self, ins, outs):
        qkv, out_w, staged = self.named
        self.qkv, self.out_w, self.staged = ins[qkv], ins[out_w], outs[staged]


class OwnColumns(Columns):
    def __init__(self, sz, section, part, source, staged):
        super().__init__(sz, section, part, None, None, None)
        self.ins = []
        self.named = (source, staged)

    def bind(self, ins, outs, scratch):
        self.target = outs[0]
        self.send, self.recv = scratch

    def use(self, ins, outs):
        source, staged = self.named
        self.source, self.staged = ins[source], outs[staged]


def gather_pair(buffer, place, send, recv):
    x, y, k, z = place
    own = buffer.at[2 * x + y]
    copies = [
        remote(own, own, send.at[i], recv.at[i], device)
        for i, device in enumerate(pair_peers(x, y, k, z))
    ]
    for copy in copies:
        copy.start()
    return copies


def gathered_pair(buffer, place, copies, recv):
    x, y, k, z = place
    for i, group in enumerate(pair_groups(x, y)):
        arrived(buffer.at[group], recv.at[i])


def scatter_pair(parts, landed, place, send, recv):
    x, y, k, z = place
    groups = pair_groups(x, y)
    copies = [
        remote(parts.at[groups[i]], landed.at[i], send.at[i], recv.at[i], device)
        for i, device in enumerate(pair_peers(x, y, k, z))
    ]
    for copy in copies:
        copy.start()
    return copies


def meet_pair(sz, place, jobs):
    x, y, k, z = place
    peers = pair_peers(x, y, k, z)
    meet(sz, place, list(peers) + line_peers(sz.ctx, x, y, k, z), [peers[0], peers[2]], jobs)


def attend(sz, section, x_own, gain, bias, watt, tables, qpos, kpos, jobs):
    n, rows = sz.ctx, 4 * sz.rows

    def body(ins, outs, scratch, jobs):
        x_ref, gain, bias, watt, cosine, sine, qpos, kpos = ins
        h1_out, n1_all, q_out, kv_all, o_out, lse_out = outs
        w, parts, landed, w_sem, s_in, r_in, s_kv, r_kv, s_back, r_back = scratch
        place = where_am_i()
        x, y, k, z = place
        load = pltpu.make_async_copy(watt, w, w_sem)
        load.start()
        meet_pair(sz, place, jobs)
        group = 2 * x + y
        values = x_ref[...].astype(F32)
        n1_all[group] = (values * row_norm(values) * gain[...]).astype(BF)
        copies = gather_pair(n1_all, place, s_in, r_in)
        begin(jobs, place, 0.0, 0.3)
        load.wait()
        gathered_pair(n1_all, place, copies, r_in)
        normed = n1_all[...].reshape(rows, sz.width)
        kv = mm(normed, w[:, sz.qcols : sz.acols]) + bias[:, sz.qcols : sz.acols]
        cos, sin = cosine[...], sine[...]
        key = kv[:, : sz.kcols]
        kv_all[z, :, : sz.kcols] = (key * cos + half_turn(key) * sin).astype(BF)
        kv_all[z, :, sz.kcols :] = kv[:, sz.kcols :].astype(BF)
        kv_copies = []
        for step, device in enumerate(line_peers(n, x, y, k, z)):
            own = kv_all.at[z]
            kv_copies.append(remote(own, own, s_kv.at[step], r_kv.at[step], device))
            kv_copies[-1].start()
        begin(jobs, place, 0.3, 1.0)
        queries = mm(normed, w[:, : sz.qcols]) + bias[:, : sz.qcols]
        for head in range(sz.per_group):
            cols = slice(head * HEAD_WIDTH_SIZE, (head + 1) * HEAD_WIDTH_SIZE)
            query = queries[:, cols]
            q_out[:, cols] = (query * cos + half_turn(query) * sin).astype(BF)
        for step in range(n - 1):
            arrived(kv_all.at[lax.rem(z + n - 1 - step, n)], r_kv.at[step])
        keys = kv_all[:, :, : sz.kcols].reshape(n * rows, sz.kcols)
        vals = kv_all[:, :, sz.kcols :].reshape(n * rows, sz.kcols)
        allowed = kpos[...] <= qpos[...]
        scale = 1.0 / math.sqrt(HEAD_WIDTH_SIZE)
        for head in range(sz.per_group):
            cols = slice(head * HEAD_WIDTH_SIZE, (head + 1) * HEAD_WIDTH_SIZE)
            scores = jnp.where(allowed, mm(q_out[:, cols], keys, NT) * scale, -1e30)
            highest = jnp.max(scores, axis=-1, keepdims=True)
            weights = jnp.exp(scores - highest)
            total = jnp.sum(weights, axis=-1, keepdims=True)
            o_out[:, cols] = mm(weights.astype(BF), vals) / total
            lse_out[head] = jnp.broadcast_to(highest + jnp.log(total), (rows, LANES))
        partial = mm(o_out[...].astype(BF), w[:, sz.acols :], NT)
        parts[...] = partial.astype(BF).reshape(4, sz.rows, sz.width)
        back = scatter_pair(parts, landed, place, s_back, r_back)
        middle(jobs, place)
        for copy in copies + kv_copies:
            copy.wait_send()
        out = values + parts[group].astype(F32)
        for i in range(3):
            back[i].wait_recv()
            out = out + landed[i].astype(F32)
        h1_out[...] = out
        for copy in back:
            copy.wait_send()
        finish(jobs, place)

    shapes = (
        jax.ShapeDtypeStruct((sz.rows, sz.width), F32),
        jax.ShapeDtypeStruct((4, sz.rows, sz.width), BF),
        jax.ShapeDtypeStruct((rows, sz.qcols), BF),
        jax.ShapeDtypeStruct((n, rows, 2 * sz.kcols), BF),
        jax.ShapeDtypeStruct((rows, sz.qcols), F32),
        jax.ShapeDtypeStruct((sz.per_group, rows, LANES), F32),
    )
    arrays = (x_own, gain, bias, watt, *tables, qpos, kpos)
    specs = [vmem()] * 3 + [hbm()] + [vmem()] * 4
    scratch = [
        pltpu.VMEM((sz.width, sz.atot), BF),
        pltpu.VMEM((4, sz.rows, sz.width), BF),
        pltpu.VMEM((3, sz.rows, sz.width), BF),
        DMA,
        DMA((3,)),
        DMA((3,)),
        DMA((n,)),
        DMA((n,)),
        DMA((3,)),
        DMA((3,)),
    ]
    return run_call(
        body,
        list(zip(arrays, specs)),
        [(shape, vmem()) for shape in shapes],
        scratch,
        jobs,
        3 + section,
        "attend_forward",
    )


def attend_back(sz, section, dh1, x_own, gain, watt, tables, qpos, kpos, kept, jobs):
    n, rows = sz.ctx, 4 * sz.rows

    def body(ins, outs, scratch, jobs):
        dh1, x_ref, gain, watt, cosine, sine, qpos, kpos, n1_all, q_in, kv_all, o_in, lse_in = ins
        dx_out, dw_out, gain_grad, bias_grad = outs
        w, dh_all, dkv, dkv_in, da, parts, landed, w_sem, s_in, r_in, s_kv, r_kv, s_back, r_back = scratch
        place = where_am_i()
        x, y, k, z = place
        load = pltpu.make_async_copy(watt, w, w_sem)
        load.start()
        meet_pair(sz, place, jobs)
        group = 2 * x + y
        dh_all[group] = dh1[...].astype(BF)
        copies = gather_pair(dh_all, place, s_in, r_in)
        jobs[0].begin(place)
        load.wait()
        gathered_pair(dh_all, place, copies, r_in)
        dh = dh_all[...].reshape(rows, sz.width)
        dout = mm(dh, w[:, sz.acols :]).astype(BF)
        keys = kv_all[:, :, : sz.kcols].reshape(n * rows, sz.kcols)
        vals = kv_all[:, :, sz.kcols :].reshape(n * rows, sz.kcols)
        allowed = kpos[...] <= qpos[...]
        scale = 1.0 / math.sqrt(HEAD_WIDTH_SIZE)
        cos, sin = cosine[...], sine[...]
        dkeys, dvals = None, None
        for head in range(sz.per_group):
            cols = slice(head * HEAD_WIDTH_SIZE, (head + 1) * HEAD_WIDTH_SIZE)
            query, grad = q_in[:, cols], dout[:, cols]
            delta = jnp.sum(grad.astype(F32) * o_in[:, cols], axis=-1, keepdims=True)
            scores = mm(query, keys, NT) * scale
            probs = jnp.where(allowed, jnp.exp(scores - lse_in[head][:, :1]), 0.0)
            dscores = (probs * (mm(grad, vals, NT) - delta)).astype(BF)
            dquery = (mm(dscores, keys) * scale).astype(BF).astype(F32)
            da[:, cols] = (dquery * cos - half_turn(dquery) * sin).astype(BF)
            one_key = mm(dscores, query, TN)
            one_val = mm(probs.astype(BF), grad, TN)
            dkeys = one_key if dkeys is None else dkeys + one_key
            dvals = one_val if dvals is None else dvals + one_val
        dkv[:, :, : sz.kcols] = (dkeys * scale).astype(BF).reshape(n, rows, sz.kcols)
        dkv[:, :, sz.kcols :] = dvals.astype(BF).reshape(n, rows, sz.kcols)
        kv_copies = []
        for step, device in enumerate(line_peers(n, x, y, k, z)):
            kv_copies.append(
                remote(
                    dkv.at[lax.rem(z + 1 + step, n)],
                    dkv_in.at[step],
                    s_kv.at[step],
                    r_kv.at[step],
                    device,
                )
            )
            kv_copies[-1].start()
        jobs[1].begin(place)
        dw_out[:, sz.acols :] = mm(dh, o_in[...].astype(BF), TN).astype(BF)
        total = dkv[z].astype(F32)
        for step in range(n - 1):
            kv_copies[step].wait_recv()
            total = total + dkv_in[step].astype(F32)
        dkey = total[:, : sz.kcols]
        da[:, sz.qcols : sz.qcols + sz.kcols] = (dkey * cos - half_turn(dkey) * sin).astype(BF)
        da[:, sz.qcols + sz.kcols :] = total[:, sz.kcols :].astype(BF)
        parts[...] = mm(da[...], w[:, : sz.acols], NT).astype(BF).reshape(4, sz.rows, sz.width)
        back = scatter_pair(parts, landed, place, s_back, r_back)
        dw_out[:, : sz.acols] = mm(n1_all[...].reshape(rows, sz.width), da[...], TN).astype(BF)
        bias_grad[...] = jnp.sum(da[...].astype(F32), axis=0, keepdims=True)
        for copy in copies + kv_copies:
            copy.wait_send()
        dn1 = parts[group].astype(F32)
        for i in range(3):
            back[i].wait_recv()
            dn1 = dn1 + landed[i].astype(F32)
        values = x_ref[...].astype(F32)
        inverse = row_norm(values)
        weighted = dn1 * gain[...]
        inner = jnp.mean(weighted * values, axis=-1, keepdims=True)
        dx = dh1[...] + inverse * weighted - values * (inverse * inverse * inverse) * inner
        dx_out[...] = dx.astype(BF)
        gain_grad[...] = jnp.sum(dn1 * values * inverse, axis=0, keepdims=True)
        for copy in back:
            copy.wait_send()
        finish(jobs, place)

    shapes = (
        jax.ShapeDtypeStruct((sz.rows, sz.width), BF),
        jax.ShapeDtypeStruct((sz.width, sz.atot), BF),
        jax.ShapeDtypeStruct((1, sz.width), F32),
        jax.ShapeDtypeStruct((1, sz.acols), F32),
    )
    arrays = (dh1, x_own, gain, watt, *tables, qpos, kpos, *kept)
    specs = [vmem()] * 3 + [hbm()] + [vmem()] * 9
    scratch = [
        pltpu.VMEM((sz.width, sz.atot), BF),
        pltpu.VMEM((4, sz.rows, sz.width), BF),
        pltpu.VMEM((n, rows, 2 * sz.kcols), BF),
        pltpu.VMEM((n, rows, 2 * sz.kcols), BF),
        pltpu.VMEM((rows, sz.acols), BF),
        pltpu.VMEM((4, sz.rows, sz.width), BF),
        pltpu.VMEM((3, sz.rows, sz.width), BF),
        DMA,
        DMA((3,)),
        DMA((3,)),
        DMA((n,)),
        DMA((n,)),
        DMA((3,)),
        DMA((3,)),
    ]
    return run_call(
        body,
        list(zip(arrays, specs)),
        [(shape, vmem()) for shape in shapes],
        scratch,
        jobs,
        5 + section,
        "attend_backward",
    )


class HiddenWeights:
    def __init__(self, sz, place, sources, w, sems):
        x, y, k, z = place
        self.sz, self.sources, self.w, self.sems = sz, sources, w, sems
        self.more = has_more(sz, x * sz.group + (y * 2 + k) * sz.ctx + z)
        self.wide = sz.least * HB

    def copies(self, offset, width, kind):
        cols = pl.ds(offset, width)
        return [
            pltpu.make_async_copy(
                self.sources[part].at[:, cols], self.w.at[part, :, cols], self.sems.at[kind, part]
            )
            for part in range(3)
        ]

    def start(self):
        for copy in self.copies(0, self.wide, 0):
            copy.start()
        if self.sz.extra:

            @pl.when(self.more)
            def _():
                for copy in self.copies(self.wide, HB, 1):
                    copy.start()

            @pl.when(jnp.logical_not(self.more))
            def _():
                self.w[:, :, self.wide :] = jnp.zeros((3, self.sz.width, HB), BF)

    def wait(self):
        for copy in self.copies(0, self.wide, 0):
            copy.wait()
        if self.sz.extra:

            @pl.when(self.more)
            def _():
                for copy in self.copies(self.wide, HB, 1):
                    copy.wait()


def meet_tree(sz, place, jobs, diagonal=False):
    x, y, k, z = place
    peers = tree_peers(sz.ctx, x, y, k, z)
    if diagonal:
        peers.append(at(1 - x, 1 - y, k, z))
    meet(sz, place, peers, peers[:1], jobs)


def feed(sz, section, h1, gain, weights, jobs):
    n = sz.ctx

    def body(ins, outs, scratch, jobs):
        h1, gain, *sources = ins
        act_out, n2_all, gate_out, up_out, hm_out = outs
        w, w_sems, *refs = scratch
        place = where_am_i()
        x, y, k, z = place
        hidden_weights = HiddenWeights(sz, place, sources, w, w_sems)
        hidden_weights.start()
        meet_tree(sz, place, jobs)
        gather = Gather(n, sz.rows, n2_all, place, refs[:12])
        scatter = Scatter(n, sz.rows, place, refs[12:])
        values = h1[...]
        n2_all[k, gather.groups[0], z] = (values * row_norm(values) * gain[...]).astype(BF)
        gather.begin()
        begin(jobs[:1], place)
        begin(jobs[1:], place, 0.0, 0.75)
        hidden_weights.wait()
        rows = n * sz.rows

        def column(core, which):
            group = gather.groups[which]
            normed = n2_all[core, group].reshape(rows, sz.width)
            gate = mm(normed, w[0])
            up = mm(normed, w[1])
            hidden = (gate * jax.nn.sigmoid(gate) * up).astype(BF)
            gate_out[core, group] = gate.astype(BF)
            up_out[core, group] = up.astype(BF)
            hm_out[core, group] = hidden
            scatter.parts[core, group] = (
                mm(hidden, w[2], NT).astype(BF).reshape(n, sz.rows, sz.width)
            )
            if core is not k:
                scatter.core(which).start()

        gather.run(column, scatter.early)

        def later():
            begin(jobs[1:], place, 0.75, 1.0)
            middle(jobs, place)

        result = scatter.run((later,))
        act_out[...] = (values + result).astype(BF)
        gather.finish()
        scatter.finish()
        finish(jobs, place)

    kept = jax.ShapeDtypeStruct((2, 4, n * sz.rows, sz.hidden), BF)
    shapes = (
        jax.ShapeDtypeStruct((sz.rows, sz.width), BF),
        jax.ShapeDtypeStruct((2, 4, n, sz.rows, sz.width), BF),
        kept,
        kept,
        kept,
    )
    scratch = (
        [pltpu.VMEM((3, sz.width, sz.hidden), BF), DMA((2, 3))]
        + Gather.scratch(n)
        + Scatter.scratch(n, sz.rows, sz.width)
    )
    return run_call(
        body,
        [(h1, vmem()), (gain, vmem())] + [(w, hbm()) for w in weights],
        [(shape, vmem()) for shape in shapes],
        scratch,
        jobs,
        7 + section,
        "feed_forward",
    )


def feed_back(sz, section, dy, h1, gain, weights, kept, jobs):
    n = sz.ctx

    def body(ins, outs, scratch, jobs):
        dy, h1, gain, *sources = ins[:6]
        n2_all, gate_in, up_in, hm_in = ins[6:]
        dh1_out, dw_out, gain_grad = outs
        w, dy_all, dgate_all, dup_all, w_sems, *refs = scratch
        place = where_am_i()
        x, y, k, z = place
        hidden_weights = HiddenWeights(sz, place, sources, w, w_sems)
        hidden_weights.start()
        meet_tree(sz, place, jobs, len(jobs) > 1)
        gather = Gather(n, sz.rows, dy_all, place, refs[:12])
        scatter = Scatter(n, sz.rows, place, refs[12:])
        dy_all[k, gather.groups[0], z] = dy[...]
        gather.begin()
        down_share, *heads = jobs
        down_share.source = dw_out
        for job in heads:
            job.begin(place)
        hidden_weights.wait()
        for job in heads:
            job.middle(place)
        rows = n * sz.rows

        def column(core, which):
            group = gather.groups[which]
            dhidden = mm(dy_all[core, group].reshape(rows, sz.width), w[2])
            gate = gate_in[core, group].astype(F32)
            up = up_in[core, group].astype(F32)
            sigmoid = jax.nn.sigmoid(gate)
            dgate = (dhidden * up * sigmoid * (1.0 + gate * (1.0 - sigmoid))).astype(BF)
            dup = (dhidden * gate * sigmoid).astype(BF)
            dgate_all[core, group] = dgate
            dup_all[core, group] = dup
            partial = mm(dgate, w[0], NT) + mm(dup, w[1], NT)
            scatter.parts[core, group] = partial.astype(BF).reshape(n, sz.rows, sz.width)
            if core is not k:
                scatter.core(which).start()

        gather.run(column, scatter.early)
        total = 8 * rows
        tile = 256 if sz.width % 256 == 0 else 128

        def weight_grad(slot, left, right):
            grads = right[...].reshape(total, sz.hidden)

            @pl.loop(0, sz.width // tile)
            def _(step):
                cols = pl.ds(pl.multiple_of(step * tile, tile), tile)
                side = left[:, :, :, :, cols].reshape(total, tile)
                dw_out[slot, cols] = mm(side, grads, TN).astype(BF)

        def down_first():
            weight_grad(2, dy_all, hm_in)
            down_share.begin(place)

        def last():
            weight_grad(1, n2_all, dup_all)
            for job in heads:
                job.late(place)

        dn2 = scatter.run((down_first, lambda: weight_grad(0, n2_all, dgate_all), last))
        values = h1[...]
        inverse = row_norm(values)
        weighted = dn2 * gain[...]
        inner = jnp.mean(weighted * values, axis=-1, keepdims=True)
        dh1_out[...] = (
            dy[...].astype(F32) + inverse * weighted - values * (inverse * inverse * inverse) * inner
        )
        gain_grad[...] = jnp.sum(dn2 * values * inverse, axis=0, keepdims=True)
        gather.finish()
        scatter.finish()
        finish(jobs, place)

    shapes = (
        jax.ShapeDtypeStruct((sz.rows, sz.width), F32),
        jax.ShapeDtypeStruct((3, sz.width, sz.hidden), BF),
        jax.ShapeDtypeStruct((1, sz.width), F32),
    )
    inner = pltpu.VMEM((2, 4, n * sz.rows, sz.hidden), BF)
    scratch = (
        [
            pltpu.VMEM((3, sz.width, sz.hidden), BF),
            pltpu.VMEM((2, 4, n, sz.rows, sz.width), BF),
            inner,
            inner,
            DMA((2, 3)),
        ]
        + Gather.scratch(n)
        + Scatter.scratch(n, sz.rows, sz.width)
    )
    arrays = (dy, h1, gain, *weights, *kept)
    specs = [vmem()] * 3 + [hbm()] * 3 + [vmem()] * 4
    return run_call(
        body,
        list(zip(arrays, specs)),
        [(shape, vmem()) for shape in shapes],
        scratch,
        jobs,
        9 + section,
        "feed_backward",
    )


def collect(sz, small, acts, grads, shares, heads):
    n = sz.ctx
    order = [(section, part) for part in (2, 0, 1) for section in (1, 0)]

    def body(ins, outs, scratch, jobs):
        small, act0, act1, grad0, grad1, *shares = ins
        small_in, act_out, grad_out, w_out = outs
        s_small, r_small, s_out, r_out, send, recv, local, s_over, r_over = scratch
        (heads,) = jobs
        place = where_am_i()
        x, y, k, z = place
        me = x * sz.group + (y * 2 + k) * n + z
        greet_all(me, sz.total, lambda index: flat_place(index, sz.group, n))
        heads.begin(place)
        moves = []
        for number, (section, part) in enumerate(order):
            sems = (
                send.at[number],
                recv.at[number],
                local.at[number],
                s_over.at[number],
                r_over.at[number],
            )
            moves.append(PlaneShares(sz, section, part, shares[number], w_out, sems))
            moves[-1].begin(place)

        @pl.loop(1, sz.total)
        def _(step):
            device = lax.rem(me + step, sz.total)
            remote(
                small.at[device], small_in.at[me], s_small, r_small, flat_place(device, sz.group, n)
            ).start()

        pltpu.make_async_copy(small.at[me], small_in.at[me], s_small).start()

        def results(starting):
            for section in range(2):
                for slot, (source, target) in enumerate(
                    (((act0, act1)[section], act_out), ((grad0, grad1)[section], grad_out))
                ):
                    own = jnp.logical_and(x == section, jnp.logical_and(x == y, y == k))

                    @pl.when(jnp.logical_not(own))
                    def _():
                        copy = remote(
                            source,
                            target.at[k],
                            s_out.at[section, slot],
                            r_out.at[slot, k],
                            at(section, x, y, z),
                        )
                        copy.start() if starting else copy.wait_send()

                    if starting:

                        @pl.when(own)
                        def _():
                            pltpu.make_async_copy(source, target.at[k], r_out.at[slot, k]).start()

        heads.middle(place)
        for move in moves[:4]:
            move.cross(place)
        heads.late(place)
        for move in moves[4:]:
            move.cross(place)
        results(True)
        results(False)
        for slot, target in enumerate((act_out, grad_out)):
            for batch in range(2):
                arrived(target.at[batch], r_out.at[slot, batch])
        arrived(small_in.at[pl.ds(0, sz.total - 1)], r_small)
        arrived(small_in, s_small)
        heads.finish(place)
        for move in moves:
            move.finish(place)

    shapes = (
        jax.ShapeDtypeStruct((sz.total, 8, LANES), F32),
        jax.ShapeDtypeStruct((2, sz.rows, sz.width), BF),
        jax.ShapeDtypeStruct((2, sz.rows, sz.width), BF),
        jax.ShapeDtypeStruct((2, 3, sz.owned, sz.ff), BF),
    )
    arrays = (small, *acts, *grads, *[shares[section][part] for section, part in order])
    many = len(order)
    return run_call(
        body,
        [(array, hbm()) for array in arrays],
        [(shape, hbm()) for shape in shapes],
        [
            DMA,
            DMA,
            DMA((2, 2)),
            DMA((2, 2)),
            DMA((many, 2)),
            DMA((many, 5)),
            DMA((many, 2)),
            DMA((many,)),
            DMA((many,)),
        ],
        [heads],
        2,
        "collect_gradients",
    )


def local_columns(
    sz,
    tokens,
    positions,
    norm1_gain,
    qkv_bias,
    qkv_weight,
    out_weight,
    norm2_gain,
    gate_up_weight,
    down_weight,
    cotangent,
):
    n, group = sz.ctx, sz.group
    x, y, k, z = where_am_i()
    mine = 2 * x + y
    bias_owned = qkv_bias.shape[1]
    qkv_weight, out_weight = (qkv_weight[0], out_weight[0])
    gate_up_weight, down_weight = (gate_up_weight[0], down_weight[0])

    def line(values):
        return jnp.pad(values, ((0, 0), (0, LANES - values.shape[1])))

    small = jnp.concatenate(
        [line(norm1_gain), line(norm2_gain), line(qkv_bias), jnp.zeros((13, LANES), BF)], axis=0
    )
    (small_all, tok_own, cot_own, heads_x, cols_x), ((att0,), (gate0,)) = spread(
        sz, small, tokens, cotangent, qkv_weight, out_weight, gate_up_weight, down_weight
    )
    per_section = small_all.reshape(2, group, 16, LANES).astype(F32)
    gain1 = per_section[:, :, 0, : sz.owned].reshape(2, 1, sz.width)
    gain2 = per_section[:, :, 1, : sz.owned].reshape(2, 1, sz.width)
    bias = per_section[:, :, 2, :bias_owned].reshape(2, 1, group * bias_owned)
    query_columns = QUERY_HEADS * HEAD_WIDTH_SIZE
    key_columns = KEY_VALUE_HEADS * HEAD_WIDTH_SIZE
    kv = mine // (4 // KEY_VALUE_HEADS)
    starts = (
        (mine * sz.qcols, sz.qcols),
        (query_columns + kv * sz.kcols, sz.kcols),
        (query_columns + key_columns + kv * sz.kcols, sz.kcols),
    )
    own_bias = jnp.concatenate(
        [lax.dynamic_slice_in_dim(bias, start, size, 2) for start, size in starts], axis=2
    )
    ordered = lax.dynamic_index_in_dim(positions, k, 0, keepdims=False)
    ordered = ordered.reshape(4, n, sz.rows).transpose(1, 0, 2)
    own_pos = lax.dynamic_index_in_dim(ordered, z, 0, keepdims=False).reshape(4 * sz.rows)
    kpos = ordered.reshape(1, sz.seq)
    qpos = own_pos[:, None]
    cosine, sine = rope_tables(own_pos, HEAD_WIDTH_SIZE)
    half = HEAD_WIDTH_SIZE // 2
    sign = jnp.where(jnp.arange(HEAD_WIDTH_SIZE) < half, -1.0, 1.0)
    tables = (cosine[:, 0], sine[:, 0] * sign)

    def columns(section, part):
        return Columns(sz, section, part, gate_up_weight, down_weight, cols_x)

    att, gates, weights = [att0, None], [gate0, None], []
    inputs, acts, kept_att, kept_feed, middles = [tok_own], [], [], [], []
    for section in range(2):
        (h1, *kept), ((up,), (down,)) = attend(
            sz,
            section,
            inputs[section],
            gain1[section],
            own_bias[section],
            att[section],
            tables,
            qpos,
            kpos,
            [columns(section, 1), columns(section, 2)],
        )
        kept_att.append(kept)
        middles.append(h1)
        weights.append((gates[section], up, down))
        jobs = []
        if section == 0:
            jobs = [Heads(sz, 1, qkv_weight, out_weight, heads_x), columns(1, 0)]
        (act, *kept), more = feed(sz, section, h1, gain2[section], weights[section], jobs)
        if section == 0:
            (att[1],), (gates[1],) = more
        kept_feed.append(kept)
        acts.append(act)
        inputs.append(act)
    grads, das, smalls = [None, None], [None, None], [None, None]
    shares = [[None] * 3, [None] * 3]
    came_heads = [None, None]
    dy = cot_own
    for section in (1, 0):
        jobs = [LineShares(sz, 2)]
        if section == 0:
            jobs.append(ReturnedHeads(sz, 1, das[1]))
        (dh1, dw, gain2_grad), ((shares[section][2],), *more) = feed_back(
            sz, section, dy, middles[section], gain2[section], weights[section], kept_feed[section], jobs
        )
        if section == 0:
            ((came_heads[1],),) = more
        (dy, das[section], gain1_grad, bias_grad), ((shares[section][0],), (shares[section][1],)) = attend_back(
            sz,
            section,
            dh1,
            inputs[section],
            gain1[section],
            att[section],
            tables,
            qpos,
            kpos,
            kept_att[section],
            [LineShares(sz, 0, dw), LineShares(sz, 1, dw)],
        )
        grads[section] = dy
        whole_bias = jnp.zeros((1, query_columns + 2 * key_columns), F32)
        offset = 0
        for start, size in starts:
            whole_bias = lax.dynamic_update_slice(
                whole_bias, bias_grad[:, offset : offset + size], (0, start)
            )
            offset += size
        split = query_columns + key_columns
        rows = [gain1_grad, gain2_grad, whole_bias[:, :split], whole_bias[:, split:]]
        rows = [line(row.reshape(group, -1))[:, None] for row in rows]
        smalls[section] = jnp.concatenate(rows + [jnp.zeros((group, 4, LANES), F32)], axis=1)
    small_out = jnp.concatenate(smalls, axis=0)
    (small_in, act_out, grad_out, w_out), ((came_heads[0],),) = collect(
        sz, small_out, acts, grads, shares, ReturnedHeads(sz, 0, das[0])
    )
    small_sum = jnp.sum(small_in, axis=0)
    gate_up_grad = jnp.concatenate([w_out[0, 0], w_out[0, 1]], axis=1).astype(F32)[None]
    down_grad = w_out[0, 2].astype(F32)[None]
    att_sum = jnp.where(x == 0, came_heads[0], came_heads[1]).astype(F32)
    q_grad = att_sum[:, :, : sz.qcols].transpose(1, 0, 2).reshape(sz.owned, query_columns)
    kv_grad = jnp.sum(
        att_sum[:, :, sz.qcols : sz.acols].reshape(
            KEY_VALUE_HEADS, 4 // KEY_VALUE_HEADS, sz.owned, 2, sz.kcols
        ),
        axis=1,
    )
    kv_grad = kv_grad.transpose(1, 2, 0, 3).reshape(sz.owned, 2 * key_columns)
    qkv_grad = jnp.concatenate([q_grad, kv_grad], axis=1)[None]
    out_grad = att_sum[:, :, sz.acols :].transpose(1, 0, 2).reshape(1, sz.owned, query_columns)
    return (
        act_out[None],
        grad_out[None],
        small_sum[0:1, : sz.owned],
        small_sum[2:3, : (query_columns + key_columns) // group],
        small_sum[3:4, : key_columns // group],
        qkv_grad,
        out_grad,
        small_sum[1:2, : sz.owned],
        gate_up_grad,
        down_grad,
    )


def solution(mesh):
    placed = (
        P(None, ("head", "ctx"), None),
        P(),
        P("section", ("head", "ctx")),
        P("section", ("head", "ctx")),
        P("section", ("head", "ctx"), None),
        P("section", ("head", "ctx"), None),
        P("section", ("head", "ctx")),
        P("section", ("head", "ctx"), None),
        P("section", ("head", "ctx"), None),
        P(None, ("head", "ctx"), None),
    )
    returned = (
        P("section", None, ("head", "ctx"), None),
        P("section", None, ("head", "ctx"), None),
        P("section", ("head", "ctx")),
        P("section", ("head", "ctx")),
        P("section", ("head", "ctx")),
        P("section", ("head", "ctx"), None),
        P("section", ("head", "ctx"), None),
        P("section", ("head", "ctx")),
        P("section", ("head", "ctx"), None),
        P("section", ("head", "ctx"), None),
    )

    def program(*arrays):
        sizes = Sizes(mesh, arrays[0], arrays[4], arrays[7], arrays[8])
        body = functools.partial(local_columns, sizes) if sizes.fits() else local
        return jax.shard_map(
            body, mesh=mesh, in_specs=placed, out_specs=returned, check_vma=False
        )(*arrays)

    return program
```

```python
import functools
import math

import jax
import jax.numpy as jnp
from jax import lax
from jax.experimental import pallas as pl
from jax.experimental.pallas import tpu as pltpu
from jax.sharding import PartitionSpec as P

FF = 8960
QUERY_HEADS = 12
KEY_VALUE_HEADS = 2
HEAD_WIDTH_SIZE = 128


EPSILON = 1e-06
THETA = 1000000.0


def from_behind(value, axis, steps):
    count = lax.axis_size(axis)
    first, last = (max(0, -steps), min(count, count - steps))
    return lax.ppermute(value, axis, [(source, source + steps) for source in range(first, last)])


def rope_tables(position_ids, head_width):
    frequencies = THETA ** (-(jnp.arange(head_width // 2).astype(jnp.float32) * 2.0) / head_width)
    angles = position_ids.astype(jnp.float32)[..., None] * frequencies
    angles = jnp.concatenate([angles, angles], axis=-1)
    return (jnp.cos(angles)[..., None, :], jnp.sin(angles)[..., None, :])


def rotate(values, cosine_table, sine_table):
    half_width = values.shape[-1] // 2
    turned = jnp.concatenate([-values[..., half_width:], values[..., :half_width]], axis=-1)
    return values * cosine_table + turned * sine_table


def unrotate(grad_values, cosine_table, sine_table):
    half_width = grad_values.shape[-1] // 2
    scaled = grad_values * sine_table
    return grad_values * cosine_table + jnp.concatenate(
        [scaled[..., half_width:], -scaled[..., :half_width]], axis=-1
    )


def norm_rows(values, gain_row):
    inverse = lax.rsqrt(jnp.mean(values * values, axis=-1, keepdims=True) + EPSILON)
    return (values * inverse * gain_row, inverse)


def norm_back(values, inverse, gain_row, grad_values):
    weighted = grad_values * gain_row
    inner_mean = jnp.mean(weighted * values, axis=-1, keepdims=True)
    input_grad = inverse * weighted - values * inverse**3 * inner_mean
    gain_grad = jnp.sum((grad_values * values * inverse).reshape(-1, values.shape[-1]), axis=0)
    return (input_grad, gain_grad)


def pick(flag, first_tree, second_tree):
    return jax.tree.map(
        lambda left_side, right_side: jnp.where(flag, left_side, right_side),
        first_tree,
        second_tree,
    )


def masked_scores(queries, keys_now, query_pos, key_now):
    score_scale = 1.0 / math.sqrt(queries.shape[-1])
    allowed = (key_now[:, None, :] <= query_pos[:, :, None])[:, :, None, :]
    scores = (
        jnp.einsum("grhd,gkd->grhk", queries, keys_now, preferred_element_type=jnp.float32)
        * score_scale
    )
    return (jnp.where(allowed, scores, -1e30), allowed)


def attend_forward(queries, pair_group, query_pos, key_pos):
    head_width = queries.shape[-1]
    row_shape = queries.shape[:3]
    shard_piece = lax.all_gather(pair_group, "ctx", axis=1, tiled=True)
    running = jnp.full(row_shape, -1e30, jnp.float32)
    keys_now = shard_piece[:, :, 0, :head_width]
    values_now = shard_piece[:, :, 0, head_width:]
    scores, allowed = masked_scores(queries, keys_now, query_pos, key_pos)
    highest = jnp.maximum(running, jnp.max(scores, axis=-1))
    probs_now = jnp.where(allowed, jnp.exp(scores - highest[..., None]), 0.0)
    totals = jnp.sum(probs_now, axis=-1)
    accumulated = jnp.einsum(
        "grhk,gkd->grhd",
        probs_now.astype(jnp.bfloat16),
        values_now,
        preferred_element_type=jnp.float32,
    )
    running, totals, accumulated = (highest, totals, accumulated)
    return (accumulated / totals[..., None], running + jnp.log(totals))


def attend_backward(queries, pair_group, query_pos, key_pos, out_grads, lse_rows, delta_rows):
    head_width = queries.shape[-1]
    score_scale = 1.0 / math.sqrt(head_width)
    shard_piece = lax.all_gather(pair_group, "ctx", axis=1, tiled=True)
    keys_now = shard_piece[:, :, 0, :head_width]
    values_now = shard_piece[:, :, 0, head_width:]
    scores, allowed = masked_scores(queries, keys_now, query_pos, key_pos)
    probs_now = jnp.where(allowed, jnp.exp(scores - lse_rows[..., None]), 0.0)
    prob_grads = jnp.einsum(
        "grhd,gkd->grhk", out_grads, values_now, preferred_element_type=jnp.float32
    )
    score_grads = (probs_now * (prob_grads - delta_rows[..., None])).astype(jnp.bfloat16)
    query_grads = score_scale * jnp.einsum(
        "grhk,gkd->grhd", score_grads, keys_now, preferred_element_type=jnp.float32
    )
    key_part = score_scale * jnp.einsum(
        "grhk,grhd->gkd", score_grads, queries, preferred_element_type=jnp.float32
    )
    value_part = jnp.einsum(
        "grhk,grhd->gkd",
        probs_now.astype(jnp.bfloat16),
        out_grads,
        preferred_element_type=jnp.float32,
    )
    piece_term = jnp.concatenate([key_part, value_part], axis=-1)[:, :, None, :]
    return (query_grads, piece_term)


def layer_forward(inputs, own_pos, query_pos, key_pos, weights, heads_total):
    gain_one, bias_all, w_qkv, w_out, gain_two, w_gate_up, w_down = weights
    batch_length = inputs.shape[0]
    rows_total = inputs.shape[1]
    per_device = QUERY_HEADS // heads_total
    copy_count = heads_total // KEY_VALUE_HEADS
    query_columns = QUERY_HEADS * HEAD_WIDTH_SIZE
    key_columns = KEY_VALUE_HEADS * HEAD_WIDTH_SIZE
    residual = inputs.astype(jnp.float32)
    normed_one, inverse_one = norm_rows(residual, gain_one.astype(jnp.float32))
    normed_low = normed_one.astype(jnp.bfloat16)
    projected_rows = jnp.einsum(
        "grd,dc->grc", normed_low, w_qkv, preferred_element_type=jnp.float32
    ) + bias_all.astype(jnp.float32)
    cosine_table, sine_table = rope_tables(own_pos, HEAD_WIDTH_SIZE)
    queries = rotate(
        projected_rows[..., :query_columns].reshape(
            batch_length, rows_total, QUERY_HEADS, HEAD_WIDTH_SIZE
        ),
        cosine_table,
        sine_table,
    )
    key_row_block = rotate(
        projected_rows[..., query_columns : query_columns + key_columns].reshape(
            batch_length, rows_total, KEY_VALUE_HEADS, HEAD_WIDTH_SIZE
        ),
        cosine_table,
        sine_table,
    )
    value_row_block = projected_rows[..., query_columns + key_columns :].reshape(
        batch_length, rows_total, KEY_VALUE_HEADS, HEAD_WIDTH_SIZE
    )
    pair_rows = jnp.concatenate(
        [
            jnp.repeat(key_row_block, copy_count, axis=2),
            jnp.repeat(value_row_block, copy_count, axis=2),
        ],
        axis=-1,
    ).astype(jnp.bfloat16)
    query_send = queries.astype(jnp.bfloat16).reshape(
        batch_length, rows_total, heads_total, per_device * HEAD_WIDTH_SIZE
    )
    query_group, pair_group = (
        lax.all_to_all(query_send, "head", split_axis=2, concat_axis=1, tiled=True),
        lax.all_to_all(pair_rows, "head", split_axis=2, concat_axis=1, tiled=True),
    )
    group_rows = query_group.shape[1]
    query_group = query_group.reshape(batch_length, group_rows, per_device, HEAD_WIDTH_SIZE)
    attended, lse_rows = attend_forward(query_group, pair_group, query_pos, key_pos)
    out_send = attended.astype(jnp.bfloat16).reshape(
        batch_length, group_rows, 1, per_device * HEAD_WIDTH_SIZE
    )
    out_rows = lax.all_to_all(out_send, "head", split_axis=1, concat_axis=2, tiled=True).reshape(
        batch_length, rows_total, QUERY_HEADS * HEAD_WIDTH_SIZE
    )
    middle = residual + jnp.einsum(
        "grc,dc->grd", out_rows, w_out, preferred_element_type=jnp.float32
    )
    normed_two, inverse_two = norm_rows(middle, gain_two.astype(jnp.float32))
    normed_two_low = normed_two.astype(jnp.bfloat16)
    gate_up = jnp.einsum(
        "grd,dc->grc", normed_two_low, w_gate_up, preferred_element_type=jnp.float32
    )
    hidden_low = (jax.nn.silu(gate_up[..., :FF]) * gate_up[..., FF:]).astype(jnp.bfloat16)
    output = middle + jnp.einsum(
        "grf,df->grd", hidden_low, w_down, preferred_element_type=jnp.float32
    )
    kept_now = (
        residual,
        inverse_one,
        normed_low,
        query_group,
        pair_group,
        attended,
        lse_rows,
        out_rows,
        middle,
        inverse_two,
        normed_two_low,
        gate_up,
        hidden_low,
    )
    return (output, kept_now)


def layer_backward(out_grad, kept_now, own_pos, query_pos, key_pos, weights, heads_total):
    gain_one, bias_all, w_qkv, w_out, gain_two, w_gate_up, w_down = weights
    (
        residual,
        inverse_one,
        normed_low,
        query_group,
        pair_group,
        attended,
        lse_rows,
        out_rows,
        middle,
        inverse_two,
        normed_two_low,
        gate_up,
        hidden_low,
    ) = kept_now
    batch_length = out_grad.shape[0]
    rows_total = out_grad.shape[1]
    per_device = QUERY_HEADS // heads_total
    copy_count = heads_total // KEY_VALUE_HEADS
    branch_low = out_grad.astype(jnp.bfloat16)
    hidden_grad = jnp.einsum("grd,df->grf", branch_low, w_down, preferred_element_type=jnp.float32)
    gate_values = gate_up[..., :FF]
    up_values = gate_up[..., FF:]
    sigmoid_gate = jax.nn.sigmoid(gate_values)
    gate_grad = hidden_grad * up_values * sigmoid_gate * (1.0 + gate_values * (1.0 - sigmoid_gate))
    up_grad = hidden_grad * gate_values * sigmoid_gate
    gate_up_low = jnp.concatenate([gate_grad, up_grad], axis=-1).astype(jnp.bfloat16)
    normed_two_grad = jnp.einsum(
        "grc,dc->grd", gate_up_low, w_gate_up, preferred_element_type=jnp.float32
    )
    middle_part, gain_two_grad = norm_back(
        middle, inverse_two, gain_two.astype(jnp.float32), normed_two_grad
    )
    middle_grad = out_grad + middle_part
    middle_low = middle_grad.astype(jnp.bfloat16)
    out_grad_rows = jnp.einsum(
        "grd,dc->grc", middle_low, w_out, preferred_element_type=jnp.float32
    ).astype(jnp.bfloat16)
    out_grad_rows = out_grad_rows.reshape(
        batch_length, rows_total, heads_total, per_device * HEAD_WIDTH_SIZE
    )
    out_grad_group = lax.all_to_all(out_grad_rows, "head", split_axis=2, concat_axis=1, tiled=True)
    group_rows = out_grad_group.shape[1]
    out_grad_group = out_grad_group.reshape(batch_length, group_rows, per_device, HEAD_WIDTH_SIZE)
    delta_rows = jnp.sum(out_grad_group.astype(jnp.float32) * attended, axis=-1)
    query_grads, key_grads = attend_backward(
        query_group, pair_group, query_pos, key_pos, out_grad_group, lse_rows, delta_rows
    )
    pair_own = lax.psum_scatter(
        key_grads.astype(jnp.bfloat16), "ctx", scatter_dimension=1, tiled=True
    )
    query_send = query_grads.astype(jnp.bfloat16).reshape(
        batch_length, group_rows, 1, per_device * HEAD_WIDTH_SIZE
    )
    query_back, paired_backward = (
        lax.all_to_all(query_send, "head", split_axis=1, concat_axis=2, tiled=True),
        lax.all_to_all(pair_own, "head", split_axis=1, concat_axis=2, tiled=True),
    )
    query_rows = query_back.astype(jnp.float32).reshape(
        batch_length, rows_total, QUERY_HEADS, HEAD_WIDTH_SIZE
    )
    paired_sum = jnp.sum(
        paired_backward.astype(jnp.float32).reshape(
            batch_length, rows_total, KEY_VALUE_HEADS, copy_count, 2 * HEAD_WIDTH_SIZE
        ),
        axis=3,
    )
    cosine_table, sine_table = rope_tables(own_pos, HEAD_WIDTH_SIZE)
    query_pre = unrotate(query_rows, cosine_table, sine_table).reshape(
        batch_length, rows_total, QUERY_HEADS * HEAD_WIDTH_SIZE
    )
    key_pre = unrotate(paired_sum[..., :HEAD_WIDTH_SIZE], cosine_table, sine_table).reshape(
        batch_length, rows_total, KEY_VALUE_HEADS * HEAD_WIDTH_SIZE
    )
    value_before_rotation = paired_sum[..., HEAD_WIDTH_SIZE:].reshape(
        batch_length, rows_total, KEY_VALUE_HEADS * HEAD_WIDTH_SIZE
    )
    projected_low = jnp.concatenate([query_pre, key_pre, value_before_rotation], axis=-1).astype(
        jnp.bfloat16
    )
    bias_grad = jnp.sum(
        projected_low.astype(jnp.float32).reshape(-1, projected_low.shape[-1]), axis=0
    )
    normed_grad = jnp.einsum(
        "grc,dc->grd", projected_low, w_qkv, preferred_element_type=jnp.float32
    )
    input_part, gain_one_grad = norm_back(
        residual, inverse_one, gain_one.astype(jnp.float32), normed_grad
    )
    input_grad = middle_grad + input_part
    pieces = (
        normed_low,
        projected_low,
        middle_low,
        out_rows,
        normed_two_low,
        gate_up_low,
        branch_low,
        hidden_low,
    )
    return (input_grad, pieces, (gain_one_grad, bias_grad, gain_two_grad))


def reduce_block(left_side, columns):
    block_term = jnp.einsum("rd,rc->dc", left_side, columns, preferred_element_type=jnp.float32)
    return lax.psum_scatter(block_term, ("head", "ctx"), scatter_dimension=0, tiled=True)


def local(
    tokens,
    positions,
    norm1_gain,
    qkv_bias,
    qkv_weight,
    out_weight,
    norm2_gain,
    gate_up_weight,
    down_weight,
    cotangent,
):
    heads_total = lax.axis_size("head")
    rank_count = lax.axis_size("ctx")
    batch_count = tokens.shape[0]
    rows_total = tokens.shape[1]
    seq_total = positions.shape[1]
    group_rows = heads_total * rows_total
    section_index = lax.axis_index("section")
    rank_index = lax.axis_index("ctx")
    block_index = lax.axis_index("head") * rank_count + rank_index
    ordered = (
        positions.reshape(batch_count, heads_total, rank_count, rows_total)
        .transpose(0, 2, 1, 3)
        .reshape(batch_count, seq_total)
    )
    group_count = batch_count // batch_count
    tick_count = group_count + 1

    def positions_for(group_index):
        first_row = group_index * batch_count
        own_pos = lax.dynamic_slice(
            positions, (first_row, block_index * rows_total), (batch_count, rows_total)
        )
        query_pos = lax.dynamic_slice_in_dim(ordered, rank_index * group_rows, group_rows, 1)
        return (own_pos, query_pos, ordered)

    shards = (norm1_gain, qkv_bias, qkv_weight, out_weight, norm2_gain, gate_up_weight, down_weight)
    weights = tuple(
        (
            shard_value[0]
            for shard_value in (
                lax.all_gather(shards[0], ("head", "ctx"), axis=1, tiled=True),
                lax.all_gather(shards[1], ("head", "ctx"), axis=1, tiled=True),
                lax.all_gather(shards[2], ("head", "ctx"), axis=1, tiled=True),
                lax.all_gather(shards[3], ("head", "ctx"), axis=1, tiled=True),
                lax.all_gather(shards[4], ("head", "ctx"), axis=1, tiled=True),
                lax.all_gather(shards[5], ("head", "ctx"), axis=1, tiled=True),
                lax.all_gather(shards[6], ("head", "ctx"), axis=1, tiled=True),
            )
        )
    )
    received = jnp.zeros((batch_count, rows_total, tokens.shape[2]), jnp.bfloat16)
    outputs = []
    kept_list = []
    for tick_now in range(tick_count):
        first_row = min(tick_now, group_count - 1) * batch_count
        inputs = jnp.where(section_index == 0, tokens, received)
        own_pos, query_pos, key_pos = positions_for(
            jnp.clip(tick_now - section_index, 0, group_count - 1)
        )
        result, kept_now = layer_forward(inputs, own_pos, query_pos, key_pos, weights, heads_total)
        result_low = result.astype(jnp.bfloat16)
        outputs.append(result_low)
        kept_list.append(kept_now)
        if tick_now + 1 < tick_count:
            received = from_behind(result_low, "section", 1)
    received = jnp.zeros((batch_count, rows_total, tokens.shape[2]), jnp.bfloat16)
    grads_in = []
    piece_list = []
    small_sums = None
    for tick_now in range(tick_count):
        first_row = min(tick_now, group_count - 1) * batch_count
        incoming = jnp.where(section_index == 1, cotangent, received).astype(jnp.float32)
        kept_now = pick(
            section_index == 0,
            kept_list[max(tick_now - 1, 0)],
            kept_list[min(tick_now + 1, tick_count - 1)],
        )
        group_number = tick_now - 1 + section_index
        own_pos, query_pos, key_pos = positions_for(jnp.clip(group_number, 0, group_count - 1))
        input_grad, pieces, smalls = layer_backward(
            incoming, kept_now, own_pos, query_pos, key_pos, weights, heads_total
        )
        valid_flag = jnp.logical_and(group_number >= 0, group_number < group_count)
        smalls = tuple((jnp.where(valid_flag, entry_value, 0.0) for entry_value in smalls))
        if small_sums is None:
            small_sums = smalls
        else:
            small_sums = tuple(
                (left_side + right_side for left_side, right_side in zip(small_sums, smalls))
            )
        grad_low = input_grad.astype(jnp.bfloat16)
        grads_in.append(grad_low)
        piece_list.append(pieces)
        if tick_now + 1 < tick_count:
            received = from_behind(grad_low, "section", -1)
    activations = jnp.where(section_index == 0, outputs[0], outputs[1])[None]
    input_grads = jnp.where(section_index == 0, grads_in[1], grads_in[0])[None]
    chosen = [pick(section_index == 0, piece_list[1], piece_list[0])]
    merged = tuple(
        (
            jnp.concatenate([chosen_set[slot_number] for chosen_set in chosen], axis=0).reshape(
                batch_count * rows_total, -1
            )
            for slot_number in range(8)
        )
    )
    (
        normed_all,
        projected_all,
        middle_all,
        attn_all,
        normed_two_all,
        gate_up_all,
        branch_all,
        hidden_all,
    ) = merged
    pair_list = (
        (normed_all, projected_all),
        (middle_all, attn_all),
        (normed_two_all, gate_up_all),
        (branch_all, hidden_all),
    )
    share_list = []
    for left_side, right_side in pair_list:
        width_total = right_side.shape[1]
        piece_count = width_total // 4480 if width_total % 4480 == 0 else 1
        piece_width = width_total // piece_count
        piece_shares = []
        for piece_number in range(piece_count):
            columns = right_side[:, piece_number * piece_width : (piece_number + 1) * piece_width]
            piece_shares.append(reduce_block(left_side, columns))
        share_list.append(jnp.concatenate(piece_shares, axis=1)[None])
    qkv_weight_grad, out_weight_grad, gate_up_grad, down_grad = share_list
    split_width = (QUERY_HEADS + KEY_VALUE_HEADS) * HEAD_WIDTH_SIZE
    bias_sum = small_sums[1]
    gain_one_share, query_key_share, value_share, gain_two_share = (
        lax.psum_scatter(small_sums[0][None], ("head", "ctx"), scatter_dimension=1, tiled=True),
        lax.psum_scatter(
            bias_sum[None, :split_width], ("head", "ctx"), scatter_dimension=1, tiled=True
        ),
        lax.psum_scatter(
            bias_sum[None, split_width:], ("head", "ctx"), scatter_dimension=1, tiled=True
        ),
        lax.psum_scatter(small_sums[2][None], ("head", "ctx"), scatter_dimension=1, tiled=True),
    )
    return (
        activations,
        input_grads,
        gain_one_share,
        query_key_share,
        value_share,
        qkv_weight_grad,
        out_weight_grad,
        gain_two_share,
        gate_up_grad,
        down_grad,
    )


MESH_ID = pl.DeviceIdType.MESH
BF = jnp.bfloat16
F32 = jnp.float32
LANES = 128
HB = 128
VMEM_LIMIT = 60 * 1024 * 1024
DMA = pltpu.SemaphoreType.DMA
NT = (((1,), (1,)), ((), ()))
TN = (((0,), (0,)), ((), ()))
NN = (((1,), (0,)), ((), ()))


def mm(left_side, right_side, form=NN):
    return lax.dot_general(left_side, right_side, form, preferred_element_type=F32)


def where_am_i():
    head = lax.axis_index("head")
    return (lax.axis_index("section"), head // 2, lax.rem(head, 2), lax.axis_index("ctx"))


def at(x, y, k, z):
    return (x, y * 2 + k, z)


def remote(source, target, send_sem, recv_sem, device):
    return pltpu.make_async_remote_copy(
        src_ref=source,
        dst_ref=target,
        send_sem=send_sem,
        recv_sem=recv_sem,
        device_id=device,
        device_id_type=MESH_ID,
    )


def arrived(ref, sem):
    pltpu.make_async_copy(ref, ref, sem).wait()


def greet(devices):
    barrier = pltpu.get_barrier_semaphore()
    for device in devices:
        pl.semaphore_signal(barrier, inc=1, device_id=device, device_id_type=MESH_ID)
    pl.semaphore_wait(barrier, len(devices))


def greet_all(index, total, device_of):
    barrier = pltpu.get_barrier_semaphore()

    @pl.loop(1, total)
    def _(step):
        device = device_of(lax.rem(index + step, total))
        pl.semaphore_signal(barrier, inc=1, device_id=device, device_id_type=MESH_ID)

    pl.semaphore_wait(barrier, total - 1)


def params(collective_id):
    return pltpu.CompilerParams(
        collective_id=collective_id, has_side_effects=True, vmem_limit_bytes=VMEM_LIMIT
    )


def vmem():
    return pl.BlockSpec(memory_space=pltpu.VMEM)


def hbm():
    return pl.BlockSpec(memory_space=pl.ANY)


def row_norm(values):
    return lax.rsqrt(jnp.mean(values * values, axis=-1, keepdims=True) + EPSILON)


class Sizes:
    def __init__(self, mesh, tokens, qkv_weight, gate_up, down):
        self.ctx = mesh.shape["ctx"]
        self.group = 4 * self.ctx
        self.total = 2 * self.group
        self.batches, self.seq, self.width = tokens.shape
        self.rows = self.seq // self.group
        self.ff = down.shape[2]
        self.owned = self.width // self.group
        self.blocks = self.ff // HB
        self.plane = self.blocks // 2
        self.most = -(-self.plane // self.group)
        self.least = self.plane // self.group
        self.extra = self.plane % self.group
        self.hidden = self.most * HB
        self.per_group = QUERY_HEADS // 4
        self.qcols = self.per_group * HEAD_WIDTH_SIZE
        self.kcols = HEAD_WIDTH_SIZE
        self.acols = self.qcols + 2 * self.kcols
        self.atot = self.acols + self.qcols

    def fits(self):
        gathered = self.batches * self.seq * self.width * 2
        return (
            self.batches == 2
            and gathered * 3 < VMEM_LIMIT // 2
            and self.ff % (2 * HB) == 0
            and self.ctx % 2 == 0
            and self.least >= 1
            and self.owned % 16 == 0
            and self.rows % 32 == 0
        )


def flat_place(index, group, ctx):
    inside = lax.rem(index, group)
    return (index // group, inside // ctx, lax.rem(inside, ctx))


def block_rank(sz, inside):
    head, z = (inside // sz.ctx, lax.rem(inside, sz.ctx))
    y, k = (head // 2, lax.rem(head, 2))
    turn = jnp.where(z < sz.ctx // 2, 2 * z, 2 * (sz.ctx - 1 - z) + 1)
    return turn + sz.ctx * (2 * k + lax.rem(y + z, 2))


def first_column(sz, owner):
    rank = block_rank(sz, lax.rem(owner, sz.group))
    plane = owner // sz.group * sz.plane
    return pl.multiple_of((plane + rank * sz.least + jnp.minimum(rank, sz.extra)) * HB, HB)


def has_more(sz, owner):
    return block_rank(sz, lax.rem(owner, sz.group)) < sz.extra


def extras_of_head(sz, head):
    count = 0
    for z in range(sz.ctx):
        turn = 2 * z if z < sz.ctx // 2 else 2 * (sz.ctx - 1 - z) + 1
        count += turn + sz.ctx * (2 * (head % 2) + (head // 2 + z) % 2) < sz.extra
    return count


def half_turn(values):
    return pltpu.roll(values, HEAD_WIDTH_SIZE // 2, 1)


def pair_peers(x, y, k, z):
    return (at(1 - x, y, k, z), at(x, 1 - y, k, z), at(1 - x, 1 - y, k, z))


def pair_groups(x, y):
    return (2 * (1 - x) + y, 2 * x + 1 - y, 2 * (1 - x) + 1 - y)


def line_peers(n, x, y, k, z):
    return [at(x, y, k, lax.rem(z + step, n)) for step in range(1, n)]


def tree_peers(n, x, y, k, z):
    return [at(1 - x, y, k, z), at(x, 1 - y, k, z), at(x, y, 1 - k, z)] + line_peers(n, x, y, k, z)


def meet(sz, place, near, across, jobs):
    x, y, k, z = place
    n = sz.ctx
    inside = (y * 2 + k) * n + z
    reach = max([job.reach for job in jobs], default=0)
    if reach == 2:
        greet_all(x * sz.group + inside, sz.total, lambda index: flat_place(index, sz.group, n))
    elif reach == 1:
        barrier = pltpu.get_barrier_semaphore()
        for device in across:
            pl.semaphore_signal(barrier, inc=1, device_id=device, device_id_type=MESH_ID)

        @pl.loop(1, sz.group)
        def _(step):
            device = flat_place(x * sz.group + lax.rem(inside + step, sz.group), sz.group, n)
            pl.semaphore_signal(barrier, inc=1, device_id=device, device_id_type=MESH_ID)

        pl.semaphore_wait(barrier, sz.group - 1 + len(across))
    else:
        greet(near)


def run_call(body, ins, outs, scratch, jobs, collective_id, name):
    fg_in, fg_out, fg_scratch = len(ins), len(outs), len(scratch)
    ins, outs, scratch = list(ins), list(outs), list(scratch)
    for job in jobs:
        ins += [(array, hbm() if spec is None else spec) for array, spec in job.ins]
        outs += [(shape, hbm()) for shape in job.outs]
        scratch += job.scratch

    def kernel(*refs):
        given, made, own = (
            refs[: len(ins)],
            refs[len(ins) : len(ins) + len(outs)],
            refs[len(ins) + len(outs) :],
        )
        a, b, c = fg_in, fg_out, fg_scratch
        for job in jobs:
            job.bind(
                given[a : a + len(job.ins)],
                made[b : b + len(job.outs)],
                own[c : c + len(job.scratch)],
            )
            a, b, c = a + len(job.ins), b + len(job.outs), c + len(job.scratch)
        body(given[:fg_in], made[:fg_out], own[:fg_scratch], jobs)

    results = pl.pallas_call(
        kernel,
        out_shape=tuple(shape for shape, _ in outs),
        in_specs=[spec for _, spec in ins],
        out_specs=tuple(spec for _, spec in outs),
        scratch_shapes=scratch,
        compiler_params=params(collective_id),
        name=name,
    )(*[array for array, _ in ins])
    at_out, extra = fg_out, []
    for job in jobs:
        extra.append(results[at_out : at_out + len(job.outs)])
        at_out += len(job.outs)
    return (results[:fg_out], extra)


def plane_order(n, place, index):
    x, y, k, z = place
    head = y * 2 + k
    far = 4 * (n - 1)
    if isinstance(index, int) and index == 4 * n - 1:
        return head * n + z
    rest = index - far
    head_to = lax.rem(head + jnp.where(index < far, index // (n - 1), rest + 1), 4)
    ctx_to = lax.rem(z + jnp.where(index < far, 1 + lax.rem(index, n - 1), 0), n)
    return head_to * n + ctx_to


def span_of(count, low, high):
    return (int(count * low), int(count * high))


class Columns:
    reach = 1

    def __init__(self, sz, section, part, gate_up, down, staged):
        self.sz, self.section, self.part = sz, section, part
        self.ins = [(down if part == 2 else gate_up, None), (staged, None)]
        self.outs = [jax.ShapeDtypeStruct((sz.width, sz.hidden), BF)]
        self.scratch = [DMA((2,)), DMA((2,))]

    def bind(self, ins, outs, scratch):
        self.source, self.staged = ins
        self.target = outs[0]
        self.send, self.recv = scratch

    def begin(self, place, low=0.0, high=1.0):
        sz = self.sz
        n = sz.ctx
        x, y, k, z = place
        inside = (y * 2 + k) * n + z
        me = x * sz.group + inside
        first, stop = span_of(sz.group, low, high)
        rows = pl.ds(pl.multiple_of(inside * sz.owned, 16), sz.owned)
        wide = sz.least * HB
        base = sz.ff if self.part == 1 else 0

        def pair(owner, offset, width, own):
            target = self.target.at[rows, pl.ds(offset, width)]
            if own:
                first = pl.multiple_of(base + first_column(sz, owner) + offset, HB)
                return (self.source.at[:, pl.ds(first, width)], target)
            first = first_column(sz, owner) - x * sz.plane * HB + offset
            first = pl.multiple_of(first, HB)
            return (self.staged.at[self.part, :, pl.ds(first, width)], target)

        for own in (True, False):

            @pl.when((x == self.section) == own)
            def _():
                @pl.loop(first, min(stop, sz.group - 1))
                def _(step):
                    owner = x * sz.group + plane_order(n, place, step)
                    device = flat_place(owner, sz.group, n)
                    source, target = pair(owner, 0, wide, own)
                    remote(source, target, self.send.at[0], self.recv.at[0], device).start()
                    if sz.extra:

                        @pl.when(has_more(sz, owner))
                        def _():
                            source, target = pair(owner, wide, HB, own)
                            remote(source, target, self.send.at[1], self.recv.at[1], device).start()

                if stop < sz.group:
                    return
                source, target = pair(me, 0, wide, own)
                pltpu.make_async_copy(source, target, self.send.at[0]).start()
                if sz.extra:

                    @pl.when(has_more(sz, me))
                    def _():
                        source, target = pair(me, wide, HB, own)
                        pltpu.make_async_copy(source, target, self.send.at[1]).start()

    def middle(self, place):
        pass

    def finish(self, place):
        sz = self.sz
        x, y, k, z = place
        me = x * sz.group + (y * 2 + k) * sz.ctx + z
        wide = sz.least * HB
        arrived(self.target.at[pl.ds(0, sz.width - sz.owned), pl.ds(0, wide)], self.recv.at[0])
        arrived(self.target.at[:, pl.ds(0, wide)], self.send.at[0])
        if sz.extra:
            arrived(self.target.at[pl.ds(0, sz.extra * sz.owned), pl.ds(0, HB)], self.send.at[1])

            @pl.when(has_more(sz, me))
            def _():
                arrived(
                    self.target.at[pl.ds(0, sz.width - sz.owned), pl.ds(0, HB)], self.recv.at[1]
                )


def head_columns(sz, g, qkv, out_w):
    kv = g // (4 // KEY_VALUE_HEADS)
    q0 = pl.multiple_of(g * sz.qcols, HB)
    k0 = pl.multiple_of(QUERY_HEADS * HEAD_WIDTH_SIZE + kv * sz.kcols, HB)
    v0 = pl.multiple_of((QUERY_HEADS + KEY_VALUE_HEADS) * HEAD_WIDTH_SIZE + kv * sz.kcols, HB)
    return (
        (qkv.at[:, pl.ds(q0, sz.qcols)], pl.ds(0, sz.qcols)),
        (qkv.at[:, pl.ds(k0, sz.kcols)], pl.ds(sz.qcols, sz.kcols)),
        (qkv.at[:, pl.ds(v0, sz.kcols)], pl.ds(sz.qcols + sz.kcols, sz.kcols)),
        (out_w.at[:, pl.ds(q0, sz.qcols)], pl.ds(sz.acols, sz.qcols)),
    )


class Heads:
    reach = 1

    def __init__(self, sz, section, qkv, out_w, staged):
        self.sz, self.section = sz, section
        self.ins = [(qkv, None), (out_w, None), (staged, None)]
        self.outs = [jax.ShapeDtypeStruct((sz.width, sz.atot), BF)]
        self.scratch = [DMA, DMA, DMA((2,)), DMA((2,))]

    def bind(self, ins, outs, scratch):
        self.qkv, self.out_w, self.staged = ins
        self.target = outs[0]
        self.send, self.recv, self.s_core, self.r_core = scratch

    def begin(self, place, low=0.0, high=1.0):
        sz = self.sz
        n = sz.ctx
        x, y, k, z = place
        rows = pl.ds(pl.multiple_of(((y * 2 + k) * n + z) * sz.owned, 16), sz.owned)
        mine = y * n + z

        def pairs(y_to, own):
            if own:
                return [
                    (source, self.target.at[rows, cols])
                    for source, cols in head_columns(sz, 2 * x + y_to, self.qkv, self.out_w)
                ]
            return [(self.staged.at[y_to], self.target.at[rows])]

        for own in (True, False):

            @pl.when((x == self.section) == own)
            def _():
                @pl.loop(1, 2 * n)
                def _(step):
                    index = lax.rem(mine + step, 2 * n)
                    for source, target in pairs(index // n, own):
                        remote(
                            source, target, self.send, self.recv, at(x, index // n, k, lax.rem(index, n))
                        ).start()

                for source, target in pairs(y, own):
                    pltpu.make_async_copy(source, target, self.send).start()

    def span(self, part, k):
        stretch = self.sz.width // 4
        return self.target.at[pl.ds(pl.multiple_of((part * 2 + k) * stretch, 16), stretch)]

    def middle(self, place):
        sz = self.sz
        x, y, k, z = place
        half = sz.width // 2
        arrived(self.target.at[pl.ds(0, half - sz.owned)], self.recv)
        arrived(self.target.at[pl.ds(0, half)], self.send)
        for part in range(2):
            span = self.span(part, k)
            remote(span, span, self.s_core.at[part], self.r_core.at[part], at(x, y, 1 - k, z)).start()

    def finish(self, place):
        x, y, k, z = place
        for part in range(2):
            span = self.span(part, 1 - k)
            arrived(span, self.r_core.at[part])
            arrived(span, self.s_core.at[part])


class LineShares:
    reach = 0

    def __init__(self, sz, part, grads=None):
        self.sz, self.part = sz, part
        self.ins = [] if grads is None else [(grads, None)]
        self.outs = [jax.ShapeDtypeStruct((sz.ctx, 4, sz.owned, sz.hidden), BF)]
        self.scratch = [DMA((2, sz.ctx)), DMA((2, sz.ctx))]

    def bind(self, ins, outs, scratch):
        if ins:
            self.source = ins[0]
        self.target = outs[0]
        self.send, self.recv = scratch

    def moves(self, place, step, offset, width):
        sz = self.sz
        x, y, k, z = place
        ctx = lax.rem(z + step, sz.ctx)
        for head in range(4):
            rows = pl.ds(pl.multiple_of((head * sz.ctx + ctx) * sz.owned, 16), sz.owned)
            cols = pl.ds(offset, width)
            yield (self.source.at[self.part, rows, cols], self.target.at[z, head, :, cols])

    def begin(self, place, steps=None):
        sz = self.sz
        n = sz.ctx
        x, y, k, z = place
        me = x * sz.group + (y * 2 + k) * n + z
        wide = sz.least * HB

        def go(kind, offset, width):
            for step in list(range(1, n)) + [0] if steps is None else steps:
                for source, target in self.moves(place, step, offset, width):
                    if step:
                        remote(
                            source,
                            target,
                            self.send.at[kind, step],
                            self.recv.at[kind, step],
                            at(x, y, k, lax.rem(z + step, n)),
                        ).start()
                    else:
                        pltpu.make_async_copy(source, target, self.send.at[kind, 0]).start()

        go(0, 0, wide)
        if sz.extra:

            @pl.when(has_more(sz, me))
            def _():
                go(1, wide, HB)

    def finish(self, place):
        sz = self.sz
        n = sz.ctx
        x, y, k, z = place
        first = x * sz.group + (y * 2 + k) * n
        wide = sz.least * HB
        for step in range(n):
            ctx = lax.rem(z + n - step, n)
            arrived(self.target.at[ctx, :, :, pl.ds(0, wide)], self.send.at[0, step])
            if step:
                arrived(self.target.at[ctx, :, :, pl.ds(0, wide)], self.recv.at[0, step])
            if sz.extra:

                @pl.when(has_more(sz, first + z))
                def _():
                    arrived(self.target.at[ctx, :, :, pl.ds(wide, HB)], self.send.at[1, step])

                if step:

                    @pl.when(has_more(sz, first + ctx))
                    def _():
                        arrived(self.target.at[ctx, :, :, pl.ds(wide, HB)], self.recv.at[1, step])


class PlaneShares:
    def __init__(self, sz, section, part, source, target, sems):
        self.sz, self.section, self.part = sz, section, part
        self.source, self.target = source, target
        self.send, self.recv, self.local, self.s_over, self.r_over = sems
        self.row = target.at[0, part]

    def place_in(self, slot):
        return self.target.at[slot, self.part]

    def begin(self, place):
        sz = self.sz
        n = sz.ctx
        x, y, k, z = place
        head = y * 2 + k
        wide = sz.least * HB
        slot = jnp.where(x == self.section, 0, 1)

        def go(to, device, local):
            for ctx in range(n):
                owner = x * sz.group + head * n + ctx
                first = first_column(sz, owner)

                def one(kind, offset, width):
                    source = self.source.at[ctx, to, :, pl.ds(offset, width)]
                    cols = pl.ds(pl.multiple_of(first + offset, HB), width)
                    target = self.place_in(slot).at[:, cols]
                    if local:
                        pltpu.make_async_copy(source, target, self.local.at[kind]).start()
                    else:
                        recv = self.recv.at[0] if kind == 0 else self.recv.at[1 + head]
                        remote(source, target, self.send.at[kind], recv, device).start()

                one(0, 0, wide)
                if sz.extra:

                    @pl.when(has_more(sz, owner))
                    def _():
                        one(1, wide, HB)

        for step in range(1, 4):
            to = lax.rem(head + step, 4)
            go(to, (x, to, z), False)
        go(head, None, True)

    def settled(self, place):
        sz = self.sz
        n = sz.ctx
        x, y, k, z = place
        head = y * 2 + k
        wide = sz.least * HB
        row = self.row
        arrived(row.at[:, pl.ds(0, 3 * n * wide)], self.recv.at[0])
        arrived(row.at[:, pl.ds(0, 3 * n * wide)], self.send.at[0])
        arrived(row.at[:, pl.ds(0, n * wide)], self.local.at[0])
        for other in range(4):
            count = extras_of_head(sz, other)
            if count:

                @pl.when(head != other)
                def _():
                    arrived(row.at[:, pl.ds(0, count * HB)], self.recv.at[1 + other])

                @pl.when(head == other)
                def _():
                    arrived(row.at[:, pl.ds(0, 3 * count * HB)], self.send.at[1])
                    arrived(row.at[:, pl.ds(0, count * HB)], self.local.at[1])

    def cross(self, place):
        self.settled(place)

        @pl.when(place[0] != self.section)
        def _():
            self.over(place).start()

    def over(self, place):
        x, y, k, z = place
        plane = 1 - self.section
        cols = pl.ds(plane * self.sz.plane * HB, self.sz.plane * HB)
        return remote(
            self.target.at[1, self.part, :, cols],
            self.target.at[0, self.part, :, cols],
            self.s_over,
            self.r_over,
            at(1 - x, y, k, z),
        )

    def finish(self, place):
        x = place[0]

        @pl.when(x != self.section)
        def _():
            self.over(place).wait_send()

        @pl.when(x == self.section)
        def _():
            self.over(place).wait_recv()


class ReadyShares(PlaneShares):
    reach = 0

    def __init__(self, sz, section, part, source):
        self.sz, self.section, self.part = sz, section, part
        self.ins = [(source, None)]
        self.outs = [jax.ShapeDtypeStruct((sz.owned, sz.ff), BF)]
        self.scratch = [DMA((2,)), DMA((5,)), DMA((2,))]

    def bind(self, ins, outs, scratch):
        self.source, self.row = ins[0], outs[0]
        self.send, self.recv, self.local = scratch

    def place_in(self, slot):
        return self.row

    def finish(self, place):
        self.settled(place)


class ReturnedHeads:
    reach = 0

    def __init__(self, sz, section, part, grads):
        self.sz, self.section, self.part = sz, section, part
        stretch = sz.width // 4
        self.ins = [] if grads is None else [(grads, None)]
        self.outs = [jax.ShapeDtypeStruct((4, sz.owned, sz.atot), BF)]
        self.scratch = [
            pltpu.VMEM((stretch, sz.atot), BF),
            pltpu.VMEM((stretch, sz.atot), BF),
            pltpu.VMEM((sz.ctx, sz.owned, sz.atot), BF),
            DMA,
            DMA,
            DMA,
            DMA((sz.ctx,)),
            DMA((sz.ctx,)),
            DMA,
            DMA((4,)),
        ]

    def bind(self, ins, outs, scratch):
        if ins:
            self.source = ins[0]
        self.target = outs[0]
        (
            self.got,
            self.summed,
            self.lined,
            self.load,
            self.s_core,
            self.r_core,
            self.s_line,
            self.r_line,
            self.send,
            self.recv,
        ) = scratch

    def rows(self, k):
        stretch = self.sz.width // 4
        return pl.ds(pl.multiple_of((self.part * 2 + k) * stretch, 16), stretch)

    def own_rows(self, place):
        return pltpu.make_async_copy(self.source.at[self.rows(place[2])], self.summed, self.load)

    def core(self, place):
        x, y, k, z = place
        return remote(
            self.source.at[self.rows(1 - k)], self.got, self.s_core, self.r_core, at(x, y, 1 - k, z)
        )

    def own(self, ctx):
        return pl.ds(pl.multiple_of(ctx * self.sz.owned, 16), self.sz.owned)

    def line(self, place, step):
        x, y, k, z = place
        ctx = lax.rem(z + step, self.sz.ctx)
        return remote(
            self.summed.at[self.own(ctx)],
            self.lined.at[step],
            self.s_line.at[step],
            self.r_line.at[step],
            at(x, y, k, ctx),
        )

    def begin(self, place):
        self.own_rows(place).start()
        self.core(place).start()

    def middle(self, place):
        self.own_rows(place).wait()
        self.core(place).wait_recv()
        self.summed[...] = (self.summed[...].astype(F32) + self.got[...].astype(F32)).astype(BF)
        for step in range(1, self.sz.ctx):
            self.line(place, step).start()

    def homes(self, place, starting):
        x, y, k, z = place
        own = jnp.logical_and(x == self.section, y == self.part)
        target = self.target.at[2 * x + y]

        @pl.when(jnp.logical_not(own))
        def _():
            device = at(self.section, self.part, k, z)
            copy = remote(self.lined.at[0], target, self.send, self.recv.at[2 * x + y], device)
            copy.start() if starting else copy.wait_send()

        @pl.when(own)
        def _():
            copy = pltpu.make_async_copy(self.lined.at[0], target, self.send)
            copy.start() if starting else copy.wait()

    def late(self, place):
        x, y, k, z = place
        total = self.summed[self.own(z)].astype(F32)
        for step in range(1, self.sz.ctx):
            self.line(place, step).wait_recv()
            total = total + self.lined[step].astype(F32)
        self.lined[0] = total.astype(BF)
        self.homes(place, True)

    def finish(self, place):
        x, y, k, z = place
        self.core(place).wait_send()
        for step in range(1, self.sz.ctx):
            self.line(place, step).wait_send()
        self.homes(place, False)

        @pl.when(jnp.logical_and(x == self.section, y == self.part))
        def _():
            for group in range(4):

                @pl.when(group != 2 * x + y)
                def _():
                    arrived(self.target.at[group], self.recv.at[group])


def begin(jobs, place, low=0.0, high=1.0):
    for job in jobs:
        job.begin(place, low, high)


def middle(jobs, place):
    for job in jobs:
        job.middle(place)


def finish(jobs, place):
    for job in jobs:
        job.finish(place)


class Gather:
    SEMS = 12

    @staticmethod
    def scratch(n):
        return [DMA((n,))] * 10 + [DMA((4, n))] * 2

    def __init__(self, n, rows, buffer, place, sems):
        self.n, self.half, self.buffer = n, rows // 2, buffer
        self.x, self.y, self.k, self.z = place
        x, y = self.x, self.y
        self.groups = (2 * x + y, 2 * x + 1 - y, 2 * (1 - x) + y, 2 * (1 - x) + 1 - y)
        (
            self.sz,
            self.rz,
            self.sy,
            self.ry,
            self.sx,
            self.rx,
            self.syd,
            self.ryd,
            self.sxd,
            self.rxd,
            self.sc,
            self.rc,
        ) = sems

    def src(self, step):
        return lax.rem(self.z + self.n - step, self.n)

    def line(self, step):
        own = self.buffer.at[self.k, self.groups[0], self.z]
        device = at(self.x, self.y, self.k, lax.rem(self.z + step, self.n))
        return remote(own, own, self.sz.at[step], self.rz.at[step], device)

    def to_y(self, step):
        part = self.buffer.at[self.k, self.groups[0], self.src(step)]
        device = at(self.x, 1 - self.y, self.k, self.z)
        return remote(part, part, self.sy.at[step], self.ry.at[step], device)

    def to_x(self, step):
        part = self.buffer.at[self.k, self.groups[0], self.src(step)]
        device = at(1 - self.x, self.y, self.k, self.z)
        return remote(part, part, self.sx.at[step], self.rx.at[step], device)

    def on_x(self, step):
        part = self.buffer.at[self.k, self.groups[1], self.src(step), pl.ds(0, self.half)]
        device = at(1 - self.x, self.y, self.k, self.z)
        return remote(part, part, self.sxd.at[step], self.rxd.at[step], device)

    def on_y(self, step):
        part = self.buffer.at[self.k, self.groups[2], self.src(step), pl.ds(self.half, self.half)]
        device = at(self.x, 1 - self.y, self.k, self.z)
        return remote(part, part, self.syd.at[step], self.ryd.at[step], device)

    def core(self, which, step):
        part = self.buffer.at[self.k, self.groups[which], self.src(step)]
        device = at(self.x, self.y, 1 - self.k, self.z)
        return remote(part, part, self.sc.at[which, step], self.rc.at[which, step], device)

    def begin(self):
        for step in range(1, self.n):
            self.line(step).start()
        self.spread(0)

    def spread(self, step):
        if step:
            arrived(self.buffer.at[self.k, self.groups[0], self.src(step)], self.rz.at[step])
        self.to_y(step).start()
        self.to_x(step).start()
        self.core(0, step).start()

    def second(self, step):
        arrived(self.buffer.at[self.k, self.groups[1], self.src(step)], self.ry.at[step])
        self.on_x(step).start()
        self.core(1, step).start()
        arrived(self.buffer.at[self.k, self.groups[2], self.src(step)], self.rx.at[step])
        self.on_y(step).start()
        self.core(2, step).start()

    def third(self, step):
        part = self.buffer.at[self.k, self.groups[3], self.src(step)]
        arrived(part.at[pl.ds(0, self.half)], self.rxd.at[step])
        arrived(part.at[pl.ds(self.half, self.half)], self.ryd.at[step])
        self.core(3, step).start()

    def other(self, which):
        for step in range(self.n):
            part = self.buffer.at[1 - self.k, self.groups[which], self.src(step)]
            arrived(part, self.rc.at[which, step])

    def finish(self):
        for step in range(self.n):
            if step:
                self.line(step).wait_send()
            self.to_y(step).wait_send()
            self.to_x(step).wait_send()
            self.on_x(step).wait_send()
            self.on_y(step).wait_send()
            for which in range(4):
                self.core(which, step).wait_send()

    def stages(self, column, nearly):
        k, steps = self.k, range(self.n)

        def spread():
            for step in range(1, self.n):
                self.spread(step)

        def second():
            for step in steps:
                self.second(step)

        def near():
            self.other(0)
            column(1 - k, 0)
            column(k, 1)
            column(k, 2)

        def third():
            for step in steps:
                self.third(step)

        def far():
            self.other(1)
            column(1 - k, 1)
            self.other(2)
            column(1 - k, 2)
            nearly()

        def last():
            column(k, 3)
            self.other(3)
            column(1 - k, 3)

        return [self.begin, spread, lambda: column(k, 0), second, near, third, far, last]


class Scatter:
    @staticmethod
    def scratch(n, rows, width):
        return [
            pltpu.VMEM((2, 4, n, rows, width), BF),
            pltpu.VMEM((4, n, rows, width), BF),
            pltpu.VMEM((2, n, rows // 2, width), BF),
            pltpu.VMEM((2, n, rows, width), BF),
            pltpu.VMEM((n, rows, width), BF),
            DMA((4,)),
            DMA((4,)),
            DMA((2, n)),
            DMA((2, n)),
            DMA((2, 2, n)),
            DMA((2, 2, n)),
            DMA((n,)),
            DMA((n,)),
        ]

    def __init__(self, n, rows, place, refs):
        self.n, self.rows, self.half = n, rows, rows // 2
        self.x, self.y, self.k, self.z = place
        x, y = self.x, self.y
        self.groups = (2 * x + y, 2 * x + 1 - y, 2 * (1 - x) + y, 2 * (1 - x) + 1 - y)
        (
            self.parts,
            self.from_core,
            self.from_diag,
            self.from_near,
            self.from_line,
            self.s_core,
            self.r_core,
            self.s_diag,
            self.r_diag,
            self.s_near,
            self.r_near,
            self.s_line,
            self.r_line,
        ) = refs
        self.near = (at(x, 1 - y, self.k, self.z), at(1 - x, y, self.k, self.z))

    def slot(self, step):
        return lax.rem(self.z + step, self.n)

    def order(self):
        return list(range(1, self.n)) + [0]

    def core(self, which):
        return remote(
            self.parts.at[1 - self.k, self.groups[which]],
            self.from_core.at[which],
            self.s_core.at[which],
            self.r_core.at[which],
            at(self.x, self.y, 1 - self.k, self.z),
        )

    def diag(self, direction, step):
        rows = pl.ds(self.half if direction == 0 else 0, self.half)
        return remote(
            self.parts.at[self.k, self.groups[3], self.slot(step), rows],
            self.from_diag.at[direction, step],
            self.s_diag.at[direction, step],
            self.r_diag.at[direction, step],
            self.near[direction],
        )

    def close(self, direction, part, step):
        rows = pl.ds(part * self.half, self.half)
        return remote(
            self.parts.at[self.k, self.groups[1 + direction], self.slot(step), rows],
            self.from_near.at[direction, step, rows],
            self.s_near.at[direction, part, step],
            self.r_near.at[direction, part, step],
            self.near[direction],
        )

    def line(self, step):
        return remote(
            self.parts.at[self.k, self.groups[0], self.slot(step)],
            self.from_line.at[step],
            self.s_line.at[step],
            self.r_line.at[step],
            at(self.x, self.y, self.k, self.slot(step)),
        )

    def add_core(self, which):
        self.core(which).wait_recv()
        group = self.groups[which]
        self.parts[self.k, group] = (
            self.parts[self.k, group].astype(F32) + self.from_core[which].astype(F32)
        ).astype(BF)

    def early(self):
        for direction, part in ((0, 1), (1, 0)):
            self.add_core(1 + direction)
            for step in self.order():
                self.close(direction, part, step).start()

    def open(self):
        self.add_core(3)
        for step in self.order():
            self.diag(1, step).start()
            self.diag(0, step).start()
        self.add_core(0)

    def late(self):
        for step in self.order():
            slot = self.slot(step)
            for direction, part in ((0, 0), (1, 1)):
                came = 1 - direction
                self.diag(came, step).wait_recv()
                rows = pl.ds(part * self.half, self.half)
                group = self.groups[1 + direction]
                self.parts[self.k, group, slot, rows] = (
                    self.parts[self.k, group, slot, rows].astype(F32)
                    + self.from_diag[came, step].astype(F32)
                ).astype(BF)
                self.close(direction, part, step).start()

    def along(self):
        group = self.groups[0]
        for step in self.order():
            slot = self.slot(step)
            for direction in range(2):
                for part in range(2):
                    self.close(direction, part, step).wait_recv()
            total = (
                self.parts[self.k, group, slot].astype(F32)
                + self.from_near[0, step].astype(F32)
                + self.from_near[1, step].astype(F32)
            )
            if step:
                self.parts[self.k, group, slot] = total.astype(BF)
                self.line(step).start()
            else:
                self.own = total

    def result(self):
        result = self.own
        for step in range(1, self.n):
            self.line(step).wait_recv()
            result = result + self.from_line[step].astype(F32)
        return result

    def stages(self):
        return [self.open, self.late, self.along]

    def finish(self):
        for which in range(4):
            self.core(which).wait_send()
        for step in range(self.n):
            for direction in range(2):
                self.diag(direction, step).wait_send()
                for part in range(2):
                    self.close(direction, part, step).wait_send()
            if step:
                self.line(step).wait_send()


CHUNKS = 2
A, B = 0, 1
TOGETHER = (
    (A, 0), (B, 0), (A, 1), (A, 2), (A, 3), (A, 4), (B, 1), (A, 5), (B, 2), (A, 6), (B, 3), (A, 7),
    (A, 8), (B, 4), (B, 5), (A, 9), (B, 6), (B, 7), (B, 8), (A, 10), (B, 9), (B, 10),
)


def run_together(first, second, after):
    for stream, number in TOGETHER:
        (first, second)[stream][number]()
        if (stream, number) in after:
            after[stream, number]()


def spread(sz, small, tokens, cotangent, qkv, out_w, gate_up, down):
    n = sz.ctx
    half = sz.plane * HB

    def body(ins, outs, scratch, jobs):
        small, tokens, cotangent, qkv, out_w, gate_up, down = ins
        small_all, tok_own, cot_own, heads_x, cols_x = outs
        s_small, r_small, s_own, r_own, s_hx, r_hx, s_cx, r_cx = scratch
        place = where_am_i()
        x, y, k, z = place
        me = x * sz.group + (y * 2 + k) * n + z
        everyone = lambda index: flat_place(index, sz.group, n)
        greet_all(me, sz.total, everyone)
        across = at(1 - x, y, k, z)

        def heads_over():
            return [
                remote(source, heads_x.at[y_to, :, cols], s_hx, r_hx, across)
                for y_to in range(2)
                for source, cols in head_columns(sz, 2 * (1 - x) + y_to, qkv, out_w)
            ]

        for copy in heads_over():
            copy.start()

        def owns(starting):
            @pl.when(x == y)
            def _():
                for batch in range(2):
                    pairs = ((tokens, tok_own, 0), (cotangent, cot_own, 1))
                    for source, target, slot in pairs:
                        own = jnp.logical_and(k == y, k == batch)

                        @pl.when(jnp.logical_not(own))
                        def _():
                            copy = remote(
                                source.at[batch],
                                target,
                                s_own.at[batch, slot],
                                r_own.at[slot],
                                at(x, k, batch, z),
                            )
                            copy.start() if starting else copy.wait_send()

                        if starting:

                            @pl.when(own)
                            def _():
                                pltpu.make_async_copy(
                                    source.at[batch], target, r_own.at[slot]
                                ).start()

        owns(True)

        @pl.loop(1, sz.total)
        def _(step):
            device = everyone(lax.rem(me + step, sz.total))
            remote(small, small_all.at[me], s_small, r_small, device).start()

        pltpu.make_async_copy(small, small_all.at[me], s_small).start()

        def columns_over(part):
            base = (sz.ff if part == 1 else 0) + (1 - x) * half
            source = (down if part == 2 else gate_up).at[:, pl.ds(pl.multiple_of(base, HB), half)]
            return remote(source, cols_x.at[part], s_cx.at[part], r_cx.at[part], across)

        heads, first = jobs
        heads.use(ins, outs)
        first.use(ins, outs)

        @pl.when(x == heads.section)
        def _():
            heads.begin(place)

        for part in range(3):
            columns_over(part).start()
        arrived(heads_x, r_hx)

        @pl.when(x != heads.section)
        def _():
            heads.begin(place)

        columns_over(0).wait_recv()
        first.begin(place)
        heads.middle(place)
        arrived(small_all.at[pl.ds(0, sz.total - 1)], r_small)
        arrived(small_all, s_small)
        arrived(tok_own, r_own.at[0])
        arrived(cot_own, r_own.at[1])
        owns(False)
        heads.finish(place)

        for part in range(3):
            if part:
                columns_over(part).wait_recv()
            columns_over(part).wait_send()
        arrived(heads_x, s_hx)
        first.finish(place)

    shape = jax.ShapeDtypeStruct
    outs = [
        (shape((sz.total, 16, LANES), BF), hbm()),
        (shape((sz.rows, sz.width), BF), hbm()),
        (shape((sz.rows, sz.width), BF), hbm()),
        (shape((2, sz.owned, sz.atot), BF), hbm()),
        (shape((3, sz.owned, half), BF), hbm()),
    ]
    arrays = (small, tokens, cotangent, qkv, out_w, gate_up, down)
    scratch = [DMA, DMA, DMA((2, 2)), DMA((2,)), DMA, DMA, DMA((3,)), DMA((3,))]
    jobs = [OwnHeads(sz, 0, 3, 4, 3), OwnColumns(sz, 0, 0, 5, 4)]
    return run_call(body, [(a, hbm()) for a in arrays], outs, scratch, jobs, 1, "spread_weights")


class OwnHeads(Heads):
    def __init__(self, sz, section, qkv, out_w, staged):
        super().__init__(sz, section, None, None, None)
        self.ins = []
        self.named = (qkv, out_w, staged)

    def bind(self, ins, outs, scratch):
        self.target = outs[0]
        self.send, self.recv, self.s_core, self.r_core = scratch

    def use(self, ins, outs):
        qkv, out_w, staged = self.named
        self.qkv, self.out_w, self.staged = ins[qkv], ins[out_w], outs[staged]


class OwnColumns(Columns):
    def __init__(self, sz, section, part, source, staged):
        super().__init__(sz, section, part, None, None, None)
        self.ins = []
        self.named = (source, staged)

    def bind(self, ins, outs, scratch):
        self.target = outs[0]
        self.send, self.recv = scratch

    def use(self, ins, outs):
        source, staged = self.named
        self.source, self.staged = ins[source], outs[staged]


class Part:
    def __init__(self, body, ins, outs, scratch):
        self.body, self.ins, self.outs, self.scratch = body, ins, outs, scratch


def joined(sz, first, first_jobs, second, second_jobs, link, cores, collective_id, name):
    a, b, c = len(first.ins), len(first.outs), len(first.scratch)
    count = len(first_jobs)

    def body(ins, outs, scratch, jobs):
        place = where_am_i()
        x, y, k, z = place
        peers = pair_peers(x, y, k, z)
        near = list(peers) + line_peers(sz.ctx, x, y, k, z) + [at(x, y, 1 - k, z)]
        if cores:
            near.append(at(x, 1 - y, 1 - k, z))
        meet(sz, place, near, [peers[0], peers[2]], jobs)
        own, later = (jobs[:count], jobs[count:])
        first.body(ins[:a], outs[:b], scratch[:c], own, place)
        second.body(link(outs[:b], ins[a:], own, later), outs[b:], scratch[c:], later, place, own)

    results, extra = run_call(
        body,
        first.ins + second.ins,
        first.outs + second.outs,
        first.scratch + second.scratch,
        list(first_jobs) + list(second_jobs),
        collective_id,
        name,
    )
    return (results[:b], results[b:], extra[:count], extra[count:])


def alone(sz, part, jobs, meeting, collective_id, name):
    def body(ins, outs, scratch, jobs):
        place = where_am_i()
        meeting(place, jobs)
        part.body(ins, outs, scratch, jobs, place)
        finish(jobs, place)

    return run_call(body, part.ins, part.outs, part.scratch, jobs, collective_id, name)


def gather_pair(buffer, place, send, recv):
    x, y, k, z = place
    own = buffer.at[2 * x + y]
    copies = [
        remote(own, own, send.at[i], recv.at[i], device)
        for i, device in enumerate(pair_peers(x, y, k, z))
    ]
    for copy in copies:
        copy.start()
    return copies


def gathered_pair(buffer, place, copies, recv):
    x, y, k, z = place
    for i, group in enumerate(pair_groups(x, y)):
        arrived(buffer.at[group], recv.at[i])


def scatter_pair(parts, landed, place, send, recv):
    x, y, k, z = place
    groups = pair_groups(x, y)
    copies = [
        remote(parts.at[groups[i]], landed.at[i], send.at[i], recv.at[i], device)
        for i, device in enumerate(pair_peers(x, y, k, z))
    ]
    for copy in copies:
        copy.start()
    return copies


def meet_pair(sz, place, jobs, cores=False):
    x, y, k, z = place
    peers = pair_peers(x, y, k, z)
    near = list(peers) + line_peers(sz.ctx, x, y, k, z)
    if cores:
        near += [at(x, y, 1 - k, z), at(x, 1 - y, 1 - k, z)]
    meet(sz, place, near, [peers[0], peers[2]], jobs)


def attend(sz, x_own, gain, bias, watt, tables, qpos, kpos):
    n, rows = sz.ctx, 4 * sz.rows

    def body(ins, outs, scratch, jobs, place):
        x_ref, gain, bias, watt, cosine, sine, qpos, kpos = ins
        h1_out, n1_all, q_out, kv_all, o_out, lse_out = outs
        w, parts, landed, w_sem, s_in, r_in, s_kv, r_kv, s_back, r_back = scratch
        x, y, k, z = place
        load = pltpu.make_async_copy(watt, w, w_sem)
        load.start()
        group = 2 * x + y
        values = x_ref[...].astype(F32)
        n1_all[group] = (values * row_norm(values) * gain[...]).astype(BF)
        copies = gather_pair(n1_all, place, s_in, r_in)
        begin(jobs, place, 0.0, 0.3)
        load.wait()
        gathered_pair(n1_all, place, copies, r_in)
        normed = n1_all[...].reshape(rows, sz.width)
        kv = mm(normed, w[:, sz.qcols : sz.acols]) + bias[:, sz.qcols : sz.acols]
        cos, sin = cosine[...], sine[...]
        key = kv[:, : sz.kcols]
        kv_all[z, :, : sz.kcols] = (key * cos + half_turn(key) * sin).astype(BF)
        kv_all[z, :, sz.kcols :] = kv[:, sz.kcols :].astype(BF)
        kv_copies = []
        for step, device in enumerate(line_peers(n, x, y, k, z)):
            own = kv_all.at[z]
            kv_copies.append(remote(own, own, s_kv.at[step], r_kv.at[step], device))
            kv_copies[-1].start()
        begin(jobs, place, 0.3, 1.0)
        queries = mm(normed, w[:, : sz.qcols]) + bias[:, : sz.qcols]
        for head in range(sz.per_group):
            cols = slice(head * HEAD_WIDTH_SIZE, (head + 1) * HEAD_WIDTH_SIZE)
            query = queries[:, cols]
            q_out[:, cols] = (query * cos + half_turn(query) * sin).astype(BF)
        for step in range(n - 1):
            arrived(kv_all.at[lax.rem(z + n - 1 - step, n)], r_kv.at[step])
        keys = kv_all[:, :, : sz.kcols].reshape(n * rows, sz.kcols)
        vals = kv_all[:, :, sz.kcols :].reshape(n * rows, sz.kcols)
        allowed = kpos[...] <= qpos[...]
        scale = 1.0 / math.sqrt(HEAD_WIDTH_SIZE)
        for head in range(sz.per_group):
            cols = slice(head * HEAD_WIDTH_SIZE, (head + 1) * HEAD_WIDTH_SIZE)
            scores = jnp.where(allowed, mm(q_out[:, cols], keys, NT) * scale, -1e30)
            highest = jnp.max(scores, axis=-1, keepdims=True)
            weights = jnp.exp(scores - highest)
            total = jnp.sum(weights, axis=-1, keepdims=True)
            o_out[:, cols] = mm(weights.astype(BF), vals) / total
            lse_out[head] = jnp.broadcast_to(highest + jnp.log(total), (rows, LANES))
        partial = mm(o_out[...].astype(BF), w[:, sz.acols :], NT)
        parts[...] = partial.astype(BF).reshape(4, sz.rows, sz.width)
        back = scatter_pair(parts, landed, place, s_back, r_back)
        middle(jobs, place)
        for copy in copies + kv_copies:
            copy.wait_send()
        out = values + parts[group].astype(F32)
        for i in range(3):
            back[i].wait_recv()
            out = out + landed[i].astype(F32)
        h1_out[...] = out
        for copy in back:
            copy.wait_send()

    shapes = (
        jax.ShapeDtypeStruct((sz.rows, sz.width), F32),
        jax.ShapeDtypeStruct((4, sz.rows, sz.width), BF),
        jax.ShapeDtypeStruct((rows, sz.qcols), BF),
        jax.ShapeDtypeStruct((n, rows, 2 * sz.kcols), BF),
        jax.ShapeDtypeStruct((rows, sz.qcols), F32),
        jax.ShapeDtypeStruct((sz.per_group, rows, LANES), F32),
    )
    arrays = (x_own, gain, bias, watt, *tables, qpos, kpos)
    specs = [vmem()] * 3 + [hbm()] + [vmem()] * 4
    scratch = [
        pltpu.VMEM((sz.width, sz.atot), BF),
        pltpu.VMEM((4, sz.rows, sz.width), BF),
        pltpu.VMEM((3, sz.rows, sz.width), BF),
        DMA,
        DMA((3,)),
        DMA((3,)),
        DMA((n,)),
        DMA((n,)),
        DMA((3,)),
        DMA((3,)),
    ]
    return Part(body, list(zip(arrays, specs)), [(shape, vmem()) for shape in shapes], scratch)


def attend_back(sz, dh1, x_own, gain, watt, tables, qpos, kpos, kept, part_later=False):
    n, rows = sz.ctx, 4 * sz.rows

    def body(ins, outs, scratch, jobs, place):
        dh1, x_ref, gain, watt, cosine, sine, qpos, kpos, n1_all, q_in, kv_all, o_in, lse_in = ins
        dx_out, dw_out, gain_grad, bias_grad = outs
        w, dh_all, dkv, dkv_in, da, parts, landed, w_sem, s_in, r_in, s_kv, r_kv, s_back, r_back = scratch
        x, y, k, z = place
        load = pltpu.make_async_copy(watt, w, w_sem)
        load.start()
        group = 2 * x + y
        dh_all[group] = dh1[...].astype(BF)
        copies = gather_pair(dh_all, place, s_in, r_in)
        jobs[0].begin(place)
        load.wait()
        gathered_pair(dh_all, place, copies, r_in)
        for job in jobs[2:]:
            job.begin(place)
        dh = dh_all[...].reshape(rows, sz.width)
        dout = mm(dh, w[:, sz.acols :]).astype(BF)
        keys = kv_all[:, :, : sz.kcols].reshape(n * rows, sz.kcols)
        vals = kv_all[:, :, sz.kcols :].reshape(n * rows, sz.kcols)
        allowed = kpos[...] <= qpos[...]
        scale = 1.0 / math.sqrt(HEAD_WIDTH_SIZE)
        cos, sin = cosine[...], sine[...]
        dkeys, dvals = None, None
        for head in range(sz.per_group):
            cols = slice(head * HEAD_WIDTH_SIZE, (head + 1) * HEAD_WIDTH_SIZE)
            query, grad = q_in[:, cols], dout[:, cols]
            delta = jnp.sum(grad.astype(F32) * o_in[:, cols], axis=-1, keepdims=True)
            scores = mm(query, keys, NT) * scale
            probs = jnp.where(allowed, jnp.exp(scores - lse_in[head][:, :1]), 0.0)
            dscores = (probs * (mm(grad, vals, NT) - delta)).astype(BF)
            dquery = (mm(dscores, keys) * scale).astype(BF).astype(F32)
            da[:, cols] = (dquery * cos - half_turn(dquery) * sin).astype(BF)
            one_key = mm(dscores, query, TN)
            one_val = mm(probs.astype(BF), grad, TN)
            dkeys = one_key if dkeys is None else dkeys + one_key
            dvals = one_val if dvals is None else dvals + one_val
        dkv[:, :, : sz.kcols] = (dkeys * scale).astype(BF).reshape(n, rows, sz.kcols)
        dkv[:, :, sz.kcols :] = dvals.astype(BF).reshape(n, rows, sz.kcols)
        kv_copies = []
        for step, device in enumerate(line_peers(n, x, y, k, z)):
            kv_copies.append(
                remote(
                    dkv.at[lax.rem(z + 1 + step, n)],
                    dkv_in.at[step],
                    s_kv.at[step],
                    r_kv.at[step],
                    device,
                )
            )
            kv_copies[-1].start()
        jobs[1].begin(place, (1,) if part_later else None)
        dw_out[:, sz.acols :] = mm(dh, o_in[...].astype(BF), TN).astype(BF)
        total = dkv[z].astype(F32)
        for step in range(n - 1):
            kv_copies[step].wait_recv()
            total = total + dkv_in[step].astype(F32)
        dkey = total[:, : sz.kcols]
        da[:, sz.qcols : sz.qcols + sz.kcols] = (dkey * cos - half_turn(dkey) * sin).astype(BF)
        da[:, sz.qcols + sz.kcols :] = total[:, sz.kcols :].astype(BF)
        parts[...] = mm(da[...], w[:, : sz.acols], NT).astype(BF).reshape(4, sz.rows, sz.width)
        back = scatter_pair(parts, landed, place, s_back, r_back)
        dw_out[:, : sz.acols] = mm(n1_all[...].reshape(rows, sz.width), da[...], TN).astype(BF)
        bias_grad[...] = jnp.sum(da[...].astype(F32), axis=0, keepdims=True)
        for copy in copies + kv_copies:
            copy.wait_send()
        dn1 = parts[group].astype(F32)
        for i in range(3):
            back[i].wait_recv()
            dn1 = dn1 + landed[i].astype(F32)
        values = x_ref[...].astype(F32)
        inverse = row_norm(values)
        weighted = dn1 * gain[...]
        inner = jnp.mean(weighted * values, axis=-1, keepdims=True)
        dx = dh1[...] + inverse * weighted - values * (inverse * inverse * inverse) * inner
        dx_out[...] = dx.astype(BF)
        gain_grad[...] = jnp.sum(dn1 * values * inverse, axis=0, keepdims=True)
        for copy in back:
            copy.wait_send()

    shapes = (
        jax.ShapeDtypeStruct((sz.rows, sz.width), BF),
        jax.ShapeDtypeStruct((sz.width, sz.atot), BF),
        jax.ShapeDtypeStruct((1, sz.width), F32),
        jax.ShapeDtypeStruct((1, sz.acols), F32),
    )
    arrays = (dh1, x_own, gain, watt, *tables, qpos, kpos, *kept)
    specs = [vmem()] * 3 + [hbm()] + [vmem()] * 9
    scratch = [
        pltpu.VMEM((sz.width, sz.atot), BF),
        pltpu.VMEM((4, sz.rows, sz.width), BF),
        pltpu.VMEM((n, rows, 2 * sz.kcols), BF),
        pltpu.VMEM((n, rows, 2 * sz.kcols), BF),
        pltpu.VMEM((rows, sz.acols), BF),
        pltpu.VMEM((4, sz.rows, sz.width), BF),
        pltpu.VMEM((3, sz.rows, sz.width), BF),
        DMA,
        DMA((3,)),
        DMA((3,)),
        DMA((n,)),
        DMA((n,)),
        DMA((3,)),
        DMA((3,)),
    ]
    return Part(body, list(zip(arrays, specs)), [(shape, vmem()) for shape in shapes], scratch)


class HiddenWeights:
    def __init__(self, sz, place, sources, w, sems):
        x, y, k, z = place
        self.sz, self.sources, self.w, self.sems = sz, sources, w, sems
        self.more = has_more(sz, x * sz.group + (y * 2 + k) * sz.ctx + z)
        self.wide = sz.least * HB

    def copies(self, offset, width, kind, parts):
        cols = pl.ds(offset, width)
        return [
            pltpu.make_async_copy(
                self.sources[part].at[:, cols], self.w.at[part, :, cols], self.sems.at[kind, part]
            )
            for part in parts
        ]

    def start(self, parts=(0, 1, 2)):
        for copy in self.copies(0, self.wide, 0, parts):
            copy.start()
        if self.sz.extra:

            @pl.when(self.more)
            def _():
                for copy in self.copies(self.wide, HB, 1, parts):
                    copy.start()

            @pl.when(jnp.logical_not(self.more))
            def _():
                for part in parts:
                    self.w[part, :, self.wide :] = jnp.zeros((self.sz.width, HB), BF)

    def wait(self, parts=(0, 1, 2)):
        for copy in self.copies(0, self.wide, 0, parts):
            copy.wait()
        if self.sz.extra:

            @pl.when(self.more)
            def _():
                for copy in self.copies(self.wide, HB, 1, parts):
                    copy.wait()


def halves(n, rows, gathered, place, refs):
    count = len(Gather.scratch(n)) + len(Scatter.scratch(n, rows, 0))
    made = []
    for chunk in range(CHUNKS):
        own = refs[chunk * count : (chunk + 1) * count]
        made.append(
            (Gather(n, rows, gathered.at[chunk], place, own[:12]), Scatter(n, rows, place, own[12:]))
        )
    return made


def halves_scratch(n, rows, width):
    return (Gather.scratch(n) + Scatter.scratch(n, rows, width)) * CHUNKS


def feed(sz, gain, gate):
    n = sz.ctx
    rows = sz.rows // CHUNKS

    def body(ins, outs, scratch, jobs, place, pending):
        h1, gain, *sources = ins
        act_out, *kept_out = outs
        w, n2_all, gate_out, up_out, hm_out, w_sems, kept_sems, *refs = scratch
        x, y, k, z = place
        hidden_weights = HiddenWeights(sz, place, sources, w, w_sems)
        pairs = halves(n, rows, n2_all, place, refs)
        values = h1[...]
        normed = (values * row_norm(values) * gain[...]).astype(BF)
        for chunk in range(CHUNKS):
            n2_all[chunk, k, 2 * x + y, z] = normed[chunk * rows : (chunk + 1) * rows]

        def columns(chunk):
            gather, scatter = pairs[chunk]

            def column(core, which):
                group = gather.groups[which]
                normed = n2_all[chunk, core, group].reshape(n * rows, sz.width)
                gate = mm(normed, w[0])
                up = mm(normed, w[1])
                hidden = (gate * jax.nn.sigmoid(gate) * up).astype(BF)
                gate_out[chunk, core, group] = gate.astype(BF)
                up_out[chunk, core, group] = up.astype(BF)
                hm_out[chunk, core, group] = hidden
                scatter.parts[core, group] = (
                    mm(hidden, w[2], NT).astype(BF).reshape(n, rows, sz.width)
                )
                if core is not k:
                    scatter.core(which).start()

            return gather.stages(column, scatter.early) + scatter.stages()

        def started():
            for job in jobs[:1]:
                job.begin(place)
            begin(jobs[1:], place, 0.0, 0.75)
            finish(pending, place)
            hidden_weights.start()
            hidden_weights.wait()

        keep = [
            pltpu.make_async_copy(source, target, kept_sems.at[i])
            for i, (source, target) in enumerate(zip((n2_all, gate_out, up_out, hm_out), kept_out))
        ]

        def later():
            for copy in keep:
                copy.start()
            begin(jobs[1:], place, 0.75, 1.0)
            middle(jobs, place)

        run_together(columns(0), columns(1), {(B, 0): started, (B, 8): later})
        for chunk, (gather, scatter) in enumerate(pairs):
            span = slice(chunk * rows, (chunk + 1) * rows)
            act_out[span] = (values[span] + scatter.result()).astype(BF)
        for gather, scatter in pairs:
            gather.finish()
            scatter.finish()
        for copy in keep:
            copy.wait()
        finish(jobs, place)

    kept = jax.ShapeDtypeStruct((CHUNKS, 2, 4, n * rows, sz.hidden), BF)
    shapes = (
        jax.ShapeDtypeStruct((sz.rows, sz.width), BF),
        jax.ShapeDtypeStruct((CHUNKS, 2, 4, n, rows, sz.width), BF),
        kept,
        kept,
        kept,
    )
    scratch = [pltpu.VMEM((3, sz.width, sz.hidden), BF)]
    scratch += [pltpu.VMEM(shape.shape, BF) for shape in shapes[1:]]
    scratch += [DMA((2, 3)), DMA((4,))] + halves_scratch(n, rows, sz.width)
    outs = [(shape, hbm() if i else vmem()) for i, shape in enumerate(shapes)]
    return Part(body, [(gain, vmem()), (gate, hbm())], outs, scratch)


def both(sz, dy, gain, gate):
    n, rows = sz.ctx, sz.rows

    def body(ins, outs, scratch, jobs, place, pending):
        dy, h1, gain, *sources = ins
        act_out, dh1_out, dw_out, gain_grad = outs
        w, n2_all, dy_all, gate_all, up_all, hm_all, w_sems, *refs = scratch
        x, y, k, z = place
        hidden_weights = HiddenWeights(sz, place, sources, w, w_sems)
        count = len(refs) // 2
        (gather_f, scatter_f), (gather_b, scatter_b) = [
            (Gather(n, rows, buffer, place, own[:12]), Scatter(n, rows, place, own[12:]))
            for buffer, own in ((n2_all, refs[:count]), (dy_all, refs[count:]))
        ]
        values = h1[...]
        inverse = row_norm(values)
        n2_all[k, 2 * x + y, z] = (values * inverse * gain[...]).astype(BF)
        dy_all[k, 2 * x + y, z] = dy[...]

        waiting = []

        def down_product(core, which):
            group = gather_f.groups[which]
            partial = mm(hm_all[core, group], w[2], NT)
            scatter_f.parts[core, group] = partial.astype(BF).reshape(n, rows, sz.width)
            if core is not k:
                scatter_f.core(which).start()

        def down_here():
            nonlocal waiting
            finish(jobs, place)
            hidden_weights.start((2,))
            hidden_weights.wait((2,))
            for core, which in waiting:
                down_product(core, which)
            waiting = None

        def forward(core, which):
            group = gather_f.groups[which]
            normed = n2_all[core, group].reshape(n * rows, sz.width)
            gate = mm(normed, w[0])
            up = mm(normed, w[1])
            hidden = (gate * jax.nn.sigmoid(gate) * up).astype(BF)
            gate_all[core, group] = gate.astype(BF)
            up_all[core, group] = up.astype(BF)
            hm_all[core, group] = hidden
            if waiting is None:
                down_product(core, which)
            else:
                waiting.append((core, which))

        def backward(core, which):
            group = gather_b.groups[which]
            dhidden = mm(dy_all[core, group].reshape(n * rows, sz.width), w[2])
            gate = gate_all[core, group].astype(F32)
            up = up_all[core, group].astype(F32)
            sigmoid = jax.nn.sigmoid(gate)
            dgate = (dhidden * up * sigmoid * (1.0 + gate * (1.0 - sigmoid))).astype(BF)
            dup = (dhidden * gate * sigmoid).astype(BF)
            gate_all[core, group] = dgate
            up_all[core, group] = dup
            partial = mm(dgate, w[0], NT) + mm(dup, w[1], NT)
            scatter_b.parts[core, group] = partial.astype(BF).reshape(n, rows, sz.width)
            if core is not k:
                scatter_b.core(which).start()

        def weight_grad(slot, left, right):
            total = 8 * n * rows
            tile = 256 if sz.width % 256 == 0 else 128
            grads = right[...].reshape(total, sz.hidden)

            @pl.loop(0, sz.width // tile)
            def _(step):
                cols = pl.ds(pl.multiple_of(step * tile, tile), tile)
                side = left[:, :, :, :, cols].reshape(total, tile)
                dw_out[slot, cols] = mm(side, grads, TN).astype(BF)

        def result():
            act_out[...] = (h1[...] + scatter_f.result()).astype(BF)

        def started():
            finish(pending, place)
            hidden_weights.start((0, 1))
            hidden_weights.wait((0, 1))

        run_together(
            gather_f.stages(forward, scatter_f.early) + scatter_f.stages(),
            gather_b.stages(backward, scatter_b.early) + scatter_b.stages(),
            {
                (A, 0): lambda: begin(jobs, place),
                (B, 0): started,
                (A, 5): down_here,
                (B, 8): lambda: weight_grad(2, dy_all, hm_all),
                (B, 9): lambda: weight_grad(0, n2_all, gate_all),
                (B, 10): lambda: weight_grad(1, n2_all, up_all),
            },
        )
        result()
        dn2 = scatter_b.result()
        values = h1[...]
        inverse = row_norm(values)
        weighted = dn2 * gain[...]
        inner = jnp.mean(weighted * values, axis=-1, keepdims=True)
        dh1_out[...] = (
            dy[...].astype(F32) + inverse * weighted - values * (inverse * inverse * inverse) * inner
        )
        gain_grad[...] = jnp.sum(dn2 * values * inverse, axis=0, keepdims=True)
        for job in (gather_f, scatter_f, gather_b, scatter_b):
            job.finish()

    shapes = (
        jax.ShapeDtypeStruct((sz.rows, sz.width), BF),
        jax.ShapeDtypeStruct((sz.rows, sz.width), F32),
        jax.ShapeDtypeStruct((3, sz.width, sz.hidden), BF),
        jax.ShapeDtypeStruct((1, sz.width), F32),
    )
    gathered = pltpu.VMEM((2, 4, n, rows, sz.width), BF)
    inner = pltpu.VMEM((2, 4, n * rows, sz.hidden), BF)
    scratch = [
        pltpu.VMEM((3, sz.width, sz.hidden), BF),
        gathered,
        gathered,
        inner,
        inner,
        inner,
        DMA((2, 3)),
    ] + (Gather.scratch(n) + Scatter.scratch(n, rows, sz.width)) * 2
    ins = [(dy, vmem()), (gain, vmem()), (gate, hbm())]
    return Part(body, ins, [(shape, vmem()) for shape in shapes], scratch)


def feed_back(sz, h1, gain, weights, kept):
    n = sz.ctx
    rows = sz.rows // CHUNKS

    def body(ins, outs, scratch, jobs, place, pending):
        dy, h1, gain, *sources = ins[:6]
        dh1_out, dw_out, gain_grad = outs
        w, dy_all, dgate_all, dup_all, *scratch = scratch
        n2_all, gate_in, up_in, hm_in, w_sems, kept_sems, *refs = scratch
        kept = [
            pltpu.make_async_copy(source, target, kept_sems.at[i])
            for i, (source, target) in enumerate(zip(ins[6:], (n2_all, gate_in, up_in, hm_in)))
        ]
        x, y, k, z = place
        hidden_weights = HiddenWeights(sz, place, sources, w, w_sems)
        hidden_weights.start()
        for copy in kept[1:] + kept[:1]:
            copy.start()
        pairs = halves(n, rows, dy_all, place, refs)
        for chunk in range(CHUNKS):
            dy_all[chunk, k, 2 * x + y, z] = dy[chunk * rows : (chunk + 1) * rows]
        line_jobs = [job for job in jobs if isinstance(job, LineShares)]
        heads = [job for job in jobs if isinstance(job, ReturnedHeads)]

        def columns(chunk):
            gather, scatter = pairs[chunk]

            def column(core, which):
                group = gather.groups[which]
                dhidden = mm(dy_all[chunk, core, group].reshape(n * rows, sz.width), w[2])
                gate = gate_in[chunk, core, group].astype(F32)
                up = up_in[chunk, core, group].astype(F32)
                sigmoid = jax.nn.sigmoid(gate)
                dgate = (dhidden * up * sigmoid * (1.0 + gate * (1.0 - sigmoid))).astype(BF)
                dup = (dhidden * gate * sigmoid).astype(BF)
                dgate_all[chunk, core, group] = dgate
                dup_all[chunk, core, group] = dup
                partial = mm(dgate, w[0], NT) + mm(dup, w[1], NT)
                scatter.parts[core, group] = partial.astype(BF).reshape(n, rows, sz.width)
                if core is not k:
                    scatter.core(which).start()

            return gather.stages(column, scatter.early) + scatter.stages()

        total = 8 * n * sz.rows
        tile = 256 if sz.width % 256 == 0 else 128

        def weight_grad(slot, left, right):
            grads = right[...].reshape(total, sz.hidden)

            @pl.loop(0, sz.width // tile)
            def _(step):
                cols = pl.ds(pl.multiple_of(step * tile, tile), tile)
                side = left[:, :, :, :, :, cols].reshape(total, tile)
                dw_out[slot, cols] = mm(side, grads, TN).astype(BF)

        def started():
            for job in heads:
                job.begin(place)
            pending[1].begin(place, range(2, n))
            pending[1].begin(place, (0,))
            for job in line_jobs:
                job.begin(place)
            hidden_weights.wait()
            kept[1].wait()
            kept[2].wait()
            for job in heads:
                job.middle(place)

        def down_grad():
            kept[3].wait()
            kept[0].wait()
            weight_grad(2, dy_all, hm_in)

        def last():
            weight_grad(1, n2_all, dup_all)
            for job in heads:
                job.late(place)

        run_together(
            columns(0),
            columns(1),
            {
                (B, 0): started,
                (B, 8): down_grad,
                (B, 9): lambda: weight_grad(0, n2_all, dgate_all),
                (B, 10): last,
            },
        )
        dn2 = jnp.concatenate([scatter.result() for _, scatter in pairs], axis=0)
        values = h1[...]
        inverse = row_norm(values)
        weighted = dn2 * gain[...]
        inner = jnp.mean(weighted * values, axis=-1, keepdims=True)
        dh1_out[...] = (
            dy[...].astype(F32) + inverse * weighted - values * (inverse * inverse * inverse) * inner
        )
        gain_grad[...] = jnp.sum(dn2 * values * inverse, axis=0, keepdims=True)
        for gather, scatter in pairs:
            gather.finish()
            scatter.finish()
        finish(pending, place)
        finish(jobs, place)

    shapes = (
        jax.ShapeDtypeStruct((sz.rows, sz.width), F32),
        jax.ShapeDtypeStruct((3, sz.width, sz.hidden), BF),
        jax.ShapeDtypeStruct((1, sz.width), F32),
    )
    inner = pltpu.VMEM((CHUNKS, 2, 4, n * rows, sz.hidden), BF)
    scratch = [
        pltpu.VMEM((3, sz.width, sz.hidden), BF),
        pltpu.VMEM((CHUNKS, 2, 4, n, rows, sz.width), BF),
        inner,
        inner,
        pltpu.VMEM((CHUNKS, 2, 4, n, rows, sz.width), BF),
        inner,
        inner,
        inner,
        DMA((2, 3)),
        DMA((4,)),
    ] + halves_scratch(n, rows, sz.width)
    arrays = (h1, gain, *weights, *kept)
    specs = [vmem()] * 2 + [hbm()] * 7
    return Part(body, list(zip(arrays, specs)), [(shape, vmem()) for shape in shapes], scratch)


def collect(sz, small, acts, grads, shares, ready, jobs):
    n = sz.ctx
    order = [(0, 2), (1, 1), (0, 0)]
    last = (0, 1)
    early = [2, 0]

    def body(ins, outs, scratch, jobs):
        small, act0, act1, grad0, grad1, *shares = ins
        shares, ready = (shares[: len(order)], shares[len(order) :])
        small_in, act_out, grad_out, w_out = outs
        s_small, r_small, s_out, r_out, send, recv, local, s_over, r_over, s_ready, r_ready = scratch
        line_job, *heads = jobs
        place = where_am_i()
        x, y, k, z = place
        me = x * sz.group + (y * 2 + k) * n + z
        greet_all(me, sz.total, lambda index: flat_place(index, sz.group, n))
        line_job.begin(place)
        for job in heads:
            job.begin(place)
        moves = []
        for number, (section, part) in enumerate(order + [last]):
            sems = (
                send.at[number],
                recv.at[number],
                local.at[number],
                s_over.at[number],
                r_over.at[number],
            )
            source = shares[number] if number < len(order) else line_job.target
            moves.append(PlaneShares(sz, section, part, source, w_out, sems))
        def over(number):
            part = early[number]
            cols = pl.ds(0, sz.plane * HB)
            return remote(
                ready[number].at[:, cols],
                w_out.at[0, part, :, cols],
                s_ready.at[number],
                r_ready.at[number],
                at(1 - x, y, k, z),
            )

        @pl.when(x == 0)
        def _():
            for number in range(len(early)):
                over(number).start()

        for move in moves[:-1]:
            move.begin(place)

        @pl.loop(1, sz.total)
        def _(step):
            device = lax.rem(me + step, sz.total)
            remote(
                small.at[device], small_in.at[me], s_small, r_small, flat_place(device, sz.group, n)
            ).start()

        pltpu.make_async_copy(small.at[me], small_in.at[me], s_small).start()

        def results(starting):
            for section in range(2):
                for slot, (source, target) in enumerate(
                    (((act0, act1)[section], act_out), ((grad0, grad1)[section], grad_out))
                ):
                    own = jnp.logical_and(x == section, jnp.logical_and(x == y, y == k))

                    @pl.when(jnp.logical_not(own))
                    def _():
                        copy = remote(
                            source,
                            target.at[k],
                            s_out.at[section, slot],
                            r_out.at[slot, k],
                            at(section, x, y, z),
                        )
                        copy.start() if starting else copy.wait_send()

                    if starting:

                        @pl.when(own)
                        def _():
                            pltpu.make_async_copy(source, target.at[k], r_out.at[slot, k]).start()

        for job in heads:
            job.middle(place)
        moves[0].cross(place)
        line_job.finish(place)
        moves[-1].begin(place)
        results(True)
        moves[1].cross(place)
        moves[2].cross(place)
        heads[0].late(place)
        moves[3].cross(place)
        for job in heads[1:]:
            job.late(place)
        results(False)

        @pl.when(x == 0)
        def _():
            for number in range(len(early)):
                over(number).wait_send()

        @pl.when(x == 1)
        def _():
            for number in range(len(early)):
                over(number).wait_recv()

        for slot, target in enumerate((act_out, grad_out)):
            for batch in range(2):
                arrived(target.at[batch], r_out.at[slot, batch])
        arrived(small_in.at[pl.ds(0, sz.total - 1)], r_small)
        arrived(small_in, s_small)
        for move in moves:
            move.finish(place)
        for job in heads:
            job.finish(place)

    shapes = (
        jax.ShapeDtypeStruct((sz.total, 8, LANES), F32),
        jax.ShapeDtypeStruct((2, sz.rows, sz.width), BF),
        jax.ShapeDtypeStruct((2, sz.rows, sz.width), BF),
        jax.ShapeDtypeStruct((2, 3, sz.owned, sz.ff), BF),
    )
    arrays = (small, *acts, *grads, *[shares[section][part] for section, part in order], *ready)
    many = len(order) + 1
    return run_call(
        body,
        [(array, hbm()) for array in arrays],
        [(shape, hbm()) for shape in shapes],
        [
            DMA,
            DMA,
            DMA((2, 2)),
            DMA((2, 2)),
            DMA((many, 2)),
            DMA((many, 5)),
            DMA((many, 2)),
            DMA((many,)),
            DMA((many,)),
            DMA((len(early),)),
            DMA((len(early),)),
        ],
        jobs,
        2,
        "collect_gradients",
    )


def local_columns(
    sz,
    tokens,
    positions,
    norm1_gain,
    qkv_bias,
    qkv_weight,
    out_weight,
    norm2_gain,
    gate_up_weight,
    down_weight,
    cotangent,
):
    n, group = sz.ctx, sz.group
    x, y, k, z = where_am_i()
    mine = 2 * x + y
    bias_owned = qkv_bias.shape[1]
    qkv_weight, out_weight = (qkv_weight[0], out_weight[0])
    gate_up_weight, down_weight = (gate_up_weight[0], down_weight[0])

    def line(values):
        return jnp.pad(values, ((0, 0), (0, LANES - values.shape[1])))

    small = jnp.concatenate(
        [line(norm1_gain), line(norm2_gain), line(qkv_bias), jnp.zeros((13, LANES), BF)], axis=0
    )
    (small_all, tok_own, cot_own, heads_x, cols_x), ((att0,), (gate0,)) = spread(
        sz, small, tokens, cotangent, qkv_weight, out_weight, gate_up_weight, down_weight
    )
    per_section = small_all.reshape(2, group, 16, LANES).astype(F32)
    gain1 = per_section[:, :, 0, : sz.owned].reshape(2, 1, sz.width)
    gain2 = per_section[:, :, 1, : sz.owned].reshape(2, 1, sz.width)
    bias = per_section[:, :, 2, :bias_owned].reshape(2, 1, group * bias_owned)
    query_columns = QUERY_HEADS * HEAD_WIDTH_SIZE
    key_columns = KEY_VALUE_HEADS * HEAD_WIDTH_SIZE
    kv = mine // (4 // KEY_VALUE_HEADS)
    starts = (
        (mine * sz.qcols, sz.qcols),
        (query_columns + kv * sz.kcols, sz.kcols),
        (query_columns + key_columns + kv * sz.kcols, sz.kcols),
    )
    own_bias = jnp.concatenate(
        [lax.dynamic_slice_in_dim(bias, start, size, 2) for start, size in starts], axis=2
    )
    ordered = lax.dynamic_index_in_dim(positions, k, 0, keepdims=False)
    ordered = ordered.reshape(4, n, sz.rows).transpose(1, 0, 2)
    own_pos = lax.dynamic_index_in_dim(ordered, z, 0, keepdims=False).reshape(4 * sz.rows)
    kpos = ordered.reshape(1, sz.seq)
    qpos = own_pos[:, None]
    cosine, sine = rope_tables(own_pos, HEAD_WIDTH_SIZE)
    half = HEAD_WIDTH_SIZE // 2
    sign = jnp.where(jnp.arange(HEAD_WIDTH_SIZE) < half, -1.0, 1.0)
    tables = (cosine[:, 0], sine[:, 0] * sign)

    def columns(section, part):
        return Columns(sz, section, part, gate_up_weight, down_weight, cols_x)

    def attention(section, x_own, watt):
        return attend(sz, x_own, gain1[section], own_bias[section], watt, tables, qpos, kpos)

    (mid0, *kept_att0), (act0, *kept_feed), ((up0,), (down0,)), ((att1,), (gate1,)) = joined(
        sz,
        attention(0, tok_own, att0),
        [columns(0, 1), columns(0, 2)],
        feed(sz, gain2[0], gate0),
        [Heads(sz, 1, qkv_weight, out_weight, heads_x), columns(1, 0)],
        lambda made, given, own, later: (made[0], *given, own[0].target, own[1].target),
        False,
        3,
        "layer_forward",
    )
    (_, *kept_att1), (act1, dh1, dw1, gain2_grad1), _, _ = joined(
        sz,
        attention(1, act0, att1),
        [columns(1, 1)],
        both(sz, cot_own, gain2[1], gate1),
        [columns(1, 2)],
        lambda made, given, own, later: (given[0], made[0], *given[1:], own[0].target, later[0].target),
        False,
        4,
        "layer_turn",
    )
    acts = [act0, act1]

    def attention_back(section, dh1, x_own, watt, kept):
        return attend_back(
            sz, dh1, x_own, gain1[section], watt, tables, qpos, kpos, kept, part_later=section == 1
        )

    def heads_linked(made, given, own, later):
        later[1].source = made[1]
        return (made[0], *given)

    (
        (grad1, da1, gain1_grad1, bias_grad1),
        (dh1, dw0, gain2_grad0),
        ((down_share1,), (gate_share1,)),
        ((up_share1,), (heads10,)),
    ) = joined(
        sz,
        attention_back(1, dh1, act0, att1, kept_att1),
        [LineShares(sz, 2, dw1), LineShares(sz, 0, dw1)],
        feed_back(sz, mid0, gain2[0], (gate0, up0, down0), kept_feed),
        [LineShares(sz, 1, dw1), ReturnedHeads(sz, 1, 0, None)],
        heads_linked,
        False,
        5,
        "layer_backward",
    )
    (grad0, da0, gain1_grad0, bias_grad0), ((down_share0,), (gate_share0,), *ready) = alone(
        sz,
        attention_back(0, dh1, tok_own, att0, kept_att0),
        [LineShares(sz, 2, dw0), LineShares(sz, 0, dw0)]
        + [ReadyShares(sz, 1, part, share) for part, share in ((2, down_share1), (0, gate_share1))],
        lambda place, jobs: meet_pair(sz, place, jobs, True),
        6,
        "attend_backward",
    )
    grads = [grad0, grad1]
    shares = [[gate_share0, None, down_share0], [gate_share1, up_share1, down_share1]]
    came_heads = [[None, None], [heads10, None]]
    smalls = []
    for gain1_grad, gain2_grad, bias_grad in (
        (gain1_grad0, gain2_grad0, bias_grad0),
        (gain1_grad1, gain2_grad1, bias_grad1),
    ):
        whole_bias = jnp.zeros((1, query_columns + 2 * key_columns), F32)
        offset = 0
        for start, size in starts:
            whole_bias = lax.dynamic_update_slice(
                whole_bias, bias_grad[:, offset : offset + size], (0, start)
            )
            offset += size
        split = query_columns + key_columns
        rows = [gain1_grad, gain2_grad, whole_bias[:, :split], whole_bias[:, split:]]
        rows = [line(row.reshape(group, -1))[:, None] for row in rows]
        smalls.append(jnp.concatenate(rows + [jnp.zeros((group, 4, LANES), F32)], axis=1))
    small_out = jnp.concatenate(smalls, axis=0)
    jobs = [LineShares(sz, 1, dw0)]
    jobs += [
        ReturnedHeads(sz, section, part, da) for section, part, da in ((1, 1, da1), (0, 0, da0), (0, 1, da0))
    ]
    (small_in, act_out, grad_out, w_out), more = collect(
        sz, small_out, acts, grads, shares, [array for (array,) in ready], jobs
    )
    (came_heads[1][1],), (came_heads[0][0],), (came_heads[0][1],) = more[1:]
    small_sum = jnp.sum(small_in, axis=0)
    here = jnp.logical_and(x == 1, jnp.arange(sz.ff) >= sz.plane * HB)
    (down_ready,), (gate_ready,) = ready
    gate = jnp.where(here, gate_ready, w_out[0, 0])
    gate_up_grad = jnp.concatenate([gate, w_out[0, 1]], axis=1).astype(F32)[None]
    down_grad = jnp.where(here, down_ready, w_out[0, 2]).astype(F32)[None]
    by_y = [jnp.where(y == 0, parts[0], parts[1]) for parts in came_heads]
    att_sum = jnp.where(x == 0, by_y[0], by_y[1]).astype(F32)
    q_grad = att_sum[:, :, : sz.qcols].transpose(1, 0, 2).reshape(sz.owned, query_columns)
    kv_grad = jnp.sum(
        att_sum[:, :, sz.qcols : sz.acols].reshape(
            KEY_VALUE_HEADS, 4 // KEY_VALUE_HEADS, sz.owned, 2, sz.kcols
        ),
        axis=1,
    )
    kv_grad = kv_grad.transpose(1, 2, 0, 3).reshape(sz.owned, 2 * key_columns)
    qkv_grad = jnp.concatenate([q_grad, kv_grad], axis=1)[None]
    out_grad = att_sum[:, :, sz.acols :].transpose(1, 0, 2).reshape(1, sz.owned, query_columns)
    return (
        act_out[None],
        grad_out[None],
        small_sum[0:1, : sz.owned],
        small_sum[2:3, : (query_columns + key_columns) // group],
        small_sum[3:4, : key_columns // group],
        qkv_grad,
        out_grad,
        small_sum[1:2, : sz.owned],
        gate_up_grad,
        down_grad,
    )


def solution(mesh):
    placed = (
        P(None, ("head", "ctx"), None),
        P(),
        P("section", ("head", "ctx")),
        P("section", ("head", "ctx")),
        P("section", ("head", "ctx"), None),
        P("section", ("head", "ctx"), None),
        P("section", ("head", "ctx")),
        P("section", ("head", "ctx"), None),
        P("section", ("head", "ctx"), None),
        P(None, ("head", "ctx"), None),
    )
    returned = (
        P("section", None, ("head", "ctx"), None),
        P("section", None, ("head", "ctx"), None),
        P("section", ("head", "ctx")),
        P("section", ("head", "ctx")),
        P("section", ("head", "ctx")),
        P("section", ("head", "ctx"), None),
        P("section", ("head", "ctx"), None),
        P("section", ("head", "ctx")),
        P("section", ("head", "ctx"), None),
        P("section", ("head", "ctx"), None),
    )

    def program(*arrays):
        sizes = Sizes(mesh, arrays[0], arrays[4], arrays[7], arrays[8])
        body = functools.partial(local_columns, sizes) if sizes.fits() else local
        return jax.shard_map(
            body, mesh=mesh, in_specs=placed, out_specs=returned, check_vma=False
        )(*arrays)

    return program
```

```python
import functools
import math

import jax
import jax.numpy as jnp
from jax import lax
from jax.experimental import pallas as pl
from jax.experimental.pallas import tpu as pltpu
from jax.sharding import PartitionSpec as P

FF = 8960
QUERY_HEADS = 12
KEY_VALUE_HEADS = 2
HEAD_WIDTH_SIZE = 128


EPSILON = 1e-06
THETA = 1000000.0


def from_behind(value, axis, steps):
    count = lax.axis_size(axis)
    first, last = (max(0, -steps), min(count, count - steps))
    return lax.ppermute(value, axis, [(source, source + steps) for source in range(first, last)])


def rope_tables(position_ids, head_width):
    frequencies = THETA ** (-(jnp.arange(head_width // 2).astype(jnp.float32) * 2.0) / head_width)
    angles = position_ids.astype(jnp.float32)[..., None] * frequencies
    angles = jnp.concatenate([angles, angles], axis=-1)
    return (jnp.cos(angles)[..., None, :], jnp.sin(angles)[..., None, :])


def rotate(values, cosine_table, sine_table):
    half_width = values.shape[-1] // 2
    turned = jnp.concatenate([-values[..., half_width:], values[..., :half_width]], axis=-1)
    return values * cosine_table + turned * sine_table


def unrotate(grad_values, cosine_table, sine_table):
    half_width = grad_values.shape[-1] // 2
    scaled = grad_values * sine_table
    return grad_values * cosine_table + jnp.concatenate(
        [scaled[..., half_width:], -scaled[..., :half_width]], axis=-1
    )


def norm_rows(values, gain_row):
    inverse = lax.rsqrt(jnp.mean(values * values, axis=-1, keepdims=True) + EPSILON)
    return (values * inverse * gain_row, inverse)


def norm_back(values, inverse, gain_row, grad_values):
    weighted = grad_values * gain_row
    inner_mean = jnp.mean(weighted * values, axis=-1, keepdims=True)
    input_grad = inverse * weighted - values * inverse**3 * inner_mean
    gain_grad = jnp.sum((grad_values * values * inverse).reshape(-1, values.shape[-1]), axis=0)
    return (input_grad, gain_grad)


def pick(flag, first_tree, second_tree):
    return jax.tree.map(
        lambda left_side, right_side: jnp.where(flag, left_side, right_side),
        first_tree,
        second_tree,
    )


def masked_scores(queries, keys_now, query_pos, key_now):
    score_scale = 1.0 / math.sqrt(queries.shape[-1])
    allowed = (key_now[:, None, :] <= query_pos[:, :, None])[:, :, None, :]
    scores = (
        jnp.einsum("grhd,gkd->grhk", queries, keys_now, preferred_element_type=jnp.float32)
        * score_scale
    )
    return (jnp.where(allowed, scores, -1e30), allowed)


def attend_forward(queries, pair_group, query_pos, key_pos):
    head_width = queries.shape[-1]
    row_shape = queries.shape[:3]
    shard_piece = lax.all_gather(pair_group, "ctx", axis=1, tiled=True)
    running = jnp.full(row_shape, -1e30, jnp.float32)
    keys_now = shard_piece[:, :, 0, :head_width]
    values_now = shard_piece[:, :, 0, head_width:]
    scores, allowed = masked_scores(queries, keys_now, query_pos, key_pos)
    highest = jnp.maximum(running, jnp.max(scores, axis=-1))
    probs_now = jnp.where(allowed, jnp.exp(scores - highest[..., None]), 0.0)
    totals = jnp.sum(probs_now, axis=-1)
    accumulated = jnp.einsum(
        "grhk,gkd->grhd",
        probs_now.astype(jnp.bfloat16),
        values_now,
        preferred_element_type=jnp.float32,
    )
    running, totals, accumulated = (highest, totals, accumulated)
    return (accumulated / totals[..., None], running + jnp.log(totals))


def attend_backward(queries, pair_group, query_pos, key_pos, out_grads, lse_rows, delta_rows):
    head_width = queries.shape[-1]
    score_scale = 1.0 / math.sqrt(head_width)
    shard_piece = lax.all_gather(pair_group, "ctx", axis=1, tiled=True)
    keys_now = shard_piece[:, :, 0, :head_width]
    values_now = shard_piece[:, :, 0, head_width:]
    scores, allowed = masked_scores(queries, keys_now, query_pos, key_pos)
    probs_now = jnp.where(allowed, jnp.exp(scores - lse_rows[..., None]), 0.0)
    prob_grads = jnp.einsum(
        "grhd,gkd->grhk", out_grads, values_now, preferred_element_type=jnp.float32
    )
    score_grads = (probs_now * (prob_grads - delta_rows[..., None])).astype(jnp.bfloat16)
    query_grads = score_scale * jnp.einsum(
        "grhk,gkd->grhd", score_grads, keys_now, preferred_element_type=jnp.float32
    )
    key_part = score_scale * jnp.einsum(
        "grhk,grhd->gkd", score_grads, queries, preferred_element_type=jnp.float32
    )
    value_part = jnp.einsum(
        "grhk,grhd->gkd",
        probs_now.astype(jnp.bfloat16),
        out_grads,
        preferred_element_type=jnp.float32,
    )
    piece_term = jnp.concatenate([key_part, value_part], axis=-1)[:, :, None, :]
    return (query_grads, piece_term)


def layer_forward(inputs, own_pos, query_pos, key_pos, weights, heads_total):
    gain_one, bias_all, w_qkv, w_out, gain_two, w_gate_up, w_down = weights
    batch_length = inputs.shape[0]
    rows_total = inputs.shape[1]
    per_device = QUERY_HEADS // heads_total
    copy_count = heads_total // KEY_VALUE_HEADS
    query_columns = QUERY_HEADS * HEAD_WIDTH_SIZE
    key_columns = KEY_VALUE_HEADS * HEAD_WIDTH_SIZE
    residual = inputs.astype(jnp.float32)
    normed_one, inverse_one = norm_rows(residual, gain_one.astype(jnp.float32))
    normed_low = normed_one.astype(jnp.bfloat16)
    projected_rows = jnp.einsum(
        "grd,dc->grc", normed_low, w_qkv, preferred_element_type=jnp.float32
    ) + bias_all.astype(jnp.float32)
    cosine_table, sine_table = rope_tables(own_pos, HEAD_WIDTH_SIZE)
    queries = rotate(
        projected_rows[..., :query_columns].reshape(
            batch_length, rows_total, QUERY_HEADS, HEAD_WIDTH_SIZE
        ),
        cosine_table,
        sine_table,
    )
    key_row_block = rotate(
        projected_rows[..., query_columns : query_columns + key_columns].reshape(
            batch_length, rows_total, KEY_VALUE_HEADS, HEAD_WIDTH_SIZE
        ),
        cosine_table,
        sine_table,
    )
    value_row_block = projected_rows[..., query_columns + key_columns :].reshape(
        batch_length, rows_total, KEY_VALUE_HEADS, HEAD_WIDTH_SIZE
    )
    pair_rows = jnp.concatenate(
        [
            jnp.repeat(key_row_block, copy_count, axis=2),
            jnp.repeat(value_row_block, copy_count, axis=2),
        ],
        axis=-1,
    ).astype(jnp.bfloat16)
    query_send = queries.astype(jnp.bfloat16).reshape(
        batch_length, rows_total, heads_total, per_device * HEAD_WIDTH_SIZE
    )
    query_group, pair_group = (
        lax.all_to_all(query_send, "head", split_axis=2, concat_axis=1, tiled=True),
        lax.all_to_all(pair_rows, "head", split_axis=2, concat_axis=1, tiled=True),
    )
    group_rows = query_group.shape[1]
    query_group = query_group.reshape(batch_length, group_rows, per_device, HEAD_WIDTH_SIZE)
    attended, lse_rows = attend_forward(query_group, pair_group, query_pos, key_pos)
    out_send = attended.astype(jnp.bfloat16).reshape(
        batch_length, group_rows, 1, per_device * HEAD_WIDTH_SIZE
    )
    out_rows = lax.all_to_all(out_send, "head", split_axis=1, concat_axis=2, tiled=True).reshape(
        batch_length, rows_total, QUERY_HEADS * HEAD_WIDTH_SIZE
    )
    middle = residual + jnp.einsum(
        "grc,dc->grd", out_rows, w_out, preferred_element_type=jnp.float32
    )
    normed_two, inverse_two = norm_rows(middle, gain_two.astype(jnp.float32))
    normed_two_low = normed_two.astype(jnp.bfloat16)
    gate_up = jnp.einsum(
        "grd,dc->grc", normed_two_low, w_gate_up, preferred_element_type=jnp.float32
    )
    hidden_low = (jax.nn.silu(gate_up[..., :FF]) * gate_up[..., FF:]).astype(jnp.bfloat16)
    output = middle + jnp.einsum(
        "grf,df->grd", hidden_low, w_down, preferred_element_type=jnp.float32
    )
    kept_now = (
        residual,
        inverse_one,
        normed_low,
        query_group,
        pair_group,
        attended,
        lse_rows,
        out_rows,
        middle,
        inverse_two,
        normed_two_low,
        gate_up,
        hidden_low,
    )
    return (output, kept_now)


def layer_backward(out_grad, kept_now, own_pos, query_pos, key_pos, weights, heads_total):
    gain_one, bias_all, w_qkv, w_out, gain_two, w_gate_up, w_down = weights
    (
        residual,
        inverse_one,
        normed_low,
        query_group,
        pair_group,
        attended,
        lse_rows,
        out_rows,
        middle,
        inverse_two,
        normed_two_low,
        gate_up,
        hidden_low,
    ) = kept_now
    batch_length = out_grad.shape[0]
    rows_total = out_grad.shape[1]
    per_device = QUERY_HEADS // heads_total
    copy_count = heads_total // KEY_VALUE_HEADS
    branch_low = out_grad.astype(jnp.bfloat16)
    hidden_grad = jnp.einsum("grd,df->grf", branch_low, w_down, preferred_element_type=jnp.float32)
    gate_values = gate_up[..., :FF]
    up_values = gate_up[..., FF:]
    sigmoid_gate = jax.nn.sigmoid(gate_values)
    gate_grad = hidden_grad * up_values * sigmoid_gate * (1.0 + gate_values * (1.0 - sigmoid_gate))
    up_grad = hidden_grad * gate_values * sigmoid_gate
    gate_up_low = jnp.concatenate([gate_grad, up_grad], axis=-1).astype(jnp.bfloat16)
    normed_two_grad = jnp.einsum(
        "grc,dc->grd", gate_up_low, w_gate_up, preferred_element_type=jnp.float32
    )
    middle_part, gain_two_grad = norm_back(
        middle, inverse_two, gain_two.astype(jnp.float32), normed_two_grad
    )
    middle_grad = out_grad + middle_part
    middle_low = middle_grad.astype(jnp.bfloat16)
    out_grad_rows = jnp.einsum(
        "grd,dc->grc", middle_low, w_out, preferred_element_type=jnp.float32
    ).astype(jnp.bfloat16)
    out_grad_rows = out_grad_rows.reshape(
        batch_length, rows_total, heads_total, per_device * HEAD_WIDTH_SIZE
    )
    out_grad_group = lax.all_to_all(out_grad_rows, "head", split_axis=2, concat_axis=1, tiled=True)
    group_rows = out_grad_group.shape[1]
    out_grad_group = out_grad_group.reshape(batch_length, group_rows, per_device, HEAD_WIDTH_SIZE)
    delta_rows = jnp.sum(out_grad_group.astype(jnp.float32) * attended, axis=-1)
    query_grads, key_grads = attend_backward(
        query_group, pair_group, query_pos, key_pos, out_grad_group, lse_rows, delta_rows
    )
    pair_own = lax.psum_scatter(
        key_grads.astype(jnp.bfloat16), "ctx", scatter_dimension=1, tiled=True
    )
    query_send = query_grads.astype(jnp.bfloat16).reshape(
        batch_length, group_rows, 1, per_device * HEAD_WIDTH_SIZE
    )
    query_back, paired_backward = (
        lax.all_to_all(query_send, "head", split_axis=1, concat_axis=2, tiled=True),
        lax.all_to_all(pair_own, "head", split_axis=1, concat_axis=2, tiled=True),
    )
    query_rows = query_back.astype(jnp.float32).reshape(
        batch_length, rows_total, QUERY_HEADS, HEAD_WIDTH_SIZE
    )
    paired_sum = jnp.sum(
        paired_backward.astype(jnp.float32).reshape(
            batch_length, rows_total, KEY_VALUE_HEADS, copy_count, 2 * HEAD_WIDTH_SIZE
        ),
        axis=3,
    )
    cosine_table, sine_table = rope_tables(own_pos, HEAD_WIDTH_SIZE)
    query_pre = unrotate(query_rows, cosine_table, sine_table).reshape(
        batch_length, rows_total, QUERY_HEADS * HEAD_WIDTH_SIZE
    )
    key_pre = unrotate(paired_sum[..., :HEAD_WIDTH_SIZE], cosine_table, sine_table).reshape(
        batch_length, rows_total, KEY_VALUE_HEADS * HEAD_WIDTH_SIZE
    )
    value_before_rotation = paired_sum[..., HEAD_WIDTH_SIZE:].reshape(
        batch_length, rows_total, KEY_VALUE_HEADS * HEAD_WIDTH_SIZE
    )
    projected_low = jnp.concatenate([query_pre, key_pre, value_before_rotation], axis=-1).astype(
        jnp.bfloat16
    )
    bias_grad = jnp.sum(
        projected_low.astype(jnp.float32).reshape(-1, projected_low.shape[-1]), axis=0
    )
    normed_grad = jnp.einsum(
        "grc,dc->grd", projected_low, w_qkv, preferred_element_type=jnp.float32
    )
    input_part, gain_one_grad = norm_back(
        residual, inverse_one, gain_one.astype(jnp.float32), normed_grad
    )
    input_grad = middle_grad + input_part
    pieces = (
        normed_low,
        projected_low,
        middle_low,
        out_rows,
        normed_two_low,
        gate_up_low,
        branch_low,
        hidden_low,
    )
    return (input_grad, pieces, (gain_one_grad, bias_grad, gain_two_grad))


def reduce_block(left_side, columns):
    block_term = jnp.einsum("rd,rc->dc", left_side, columns, preferred_element_type=jnp.float32)
    return lax.psum_scatter(block_term, ("head", "ctx"), scatter_dimension=0, tiled=True)


def local(
    tokens,
    positions,
    norm1_gain,
    qkv_bias,
    qkv_weight,
    out_weight,
    norm2_gain,
    gate_up_weight,
    down_weight,
    cotangent,
):
    heads_total = lax.axis_size("head")
    rank_count = lax.axis_size("ctx")
    batch_count = tokens.shape[0]
    rows_total = tokens.shape[1]
    seq_total = positions.shape[1]
    group_rows = heads_total * rows_total
    section_index = lax.axis_index("section")
    rank_index = lax.axis_index("ctx")
    block_index = lax.axis_index("head") * rank_count + rank_index
    ordered = (
        positions.reshape(batch_count, heads_total, rank_count, rows_total)
        .transpose(0, 2, 1, 3)
        .reshape(batch_count, seq_total)
    )
    group_count = batch_count // batch_count
    tick_count = group_count + 1

    def positions_for(group_index):
        first_row = group_index * batch_count
        own_pos = lax.dynamic_slice(
            positions, (first_row, block_index * rows_total), (batch_count, rows_total)
        )
        query_pos = lax.dynamic_slice_in_dim(ordered, rank_index * group_rows, group_rows, 1)
        return (own_pos, query_pos, ordered)

    shards = (norm1_gain, qkv_bias, qkv_weight, out_weight, norm2_gain, gate_up_weight, down_weight)
    weights = tuple(
        (
            shard_value[0]
            for shard_value in (
                lax.all_gather(shards[0], ("head", "ctx"), axis=1, tiled=True),
                lax.all_gather(shards[1], ("head", "ctx"), axis=1, tiled=True),
                lax.all_gather(shards[2], ("head", "ctx"), axis=1, tiled=True),
                lax.all_gather(shards[3], ("head", "ctx"), axis=1, tiled=True),
                lax.all_gather(shards[4], ("head", "ctx"), axis=1, tiled=True),
                lax.all_gather(shards[5], ("head", "ctx"), axis=1, tiled=True),
                lax.all_gather(shards[6], ("head", "ctx"), axis=1, tiled=True),
            )
        )
    )
    received = jnp.zeros((batch_count, rows_total, tokens.shape[2]), jnp.bfloat16)
    outputs = []
    kept_list = []
    for tick_now in range(tick_count):
        first_row = min(tick_now, group_count - 1) * batch_count
        inputs = jnp.where(section_index == 0, tokens, received)
        own_pos, query_pos, key_pos = positions_for(
            jnp.clip(tick_now - section_index, 0, group_count - 1)
        )
        result, kept_now = layer_forward(inputs, own_pos, query_pos, key_pos, weights, heads_total)
        result_low = result.astype(jnp.bfloat16)
        outputs.append(result_low)
        kept_list.append(kept_now)
        if tick_now + 1 < tick_count:
            received = from_behind(result_low, "section", 1)
    received = jnp.zeros((batch_count, rows_total, tokens.shape[2]), jnp.bfloat16)
    grads_in = []
    piece_list = []
    small_sums = None
    for tick_now in range(tick_count):
        first_row = min(tick_now, group_count - 1) * batch_count
        incoming = jnp.where(section_index == 1, cotangent, received).astype(jnp.float32)
        kept_now = pick(
            section_index == 0,
            kept_list[max(tick_now - 1, 0)],
            kept_list[min(tick_now + 1, tick_count - 1)],
        )
        group_number = tick_now - 1 + section_index
        own_pos, query_pos, key_pos = positions_for(jnp.clip(group_number, 0, group_count - 1))
        input_grad, pieces, smalls = layer_backward(
            incoming, kept_now, own_pos, query_pos, key_pos, weights, heads_total
        )
        valid_flag = jnp.logical_and(group_number >= 0, group_number < group_count)
        smalls = tuple((jnp.where(valid_flag, entry_value, 0.0) for entry_value in smalls))
        if small_sums is None:
            small_sums = smalls
        else:
            small_sums = tuple(
                (left_side + right_side for left_side, right_side in zip(small_sums, smalls))
            )
        grad_low = input_grad.astype(jnp.bfloat16)
        grads_in.append(grad_low)
        piece_list.append(pieces)
        if tick_now + 1 < tick_count:
            received = from_behind(grad_low, "section", -1)
    activations = jnp.where(section_index == 0, outputs[0], outputs[1])[None]
    input_grads = jnp.where(section_index == 0, grads_in[1], grads_in[0])[None]
    chosen = [pick(section_index == 0, piece_list[1], piece_list[0])]
    merged = tuple(
        (
            jnp.concatenate([chosen_set[slot_number] for chosen_set in chosen], axis=0).reshape(
                batch_count * rows_total, -1
            )
            for slot_number in range(8)
        )
    )
    (
        normed_all,
        projected_all,
        middle_all,
        attn_all,
        normed_two_all,
        gate_up_all,
        branch_all,
        hidden_all,
    ) = merged
    pair_list = (
        (normed_all, projected_all),
        (middle_all, attn_all),
        (normed_two_all, gate_up_all),
        (branch_all, hidden_all),
    )
    share_list = []
    for left_side, right_side in pair_list:
        width_total = right_side.shape[1]
        piece_count = width_total // 4480 if width_total % 4480 == 0 else 1
        piece_width = width_total // piece_count
        piece_shares = []
        for piece_number in range(piece_count):
            columns = right_side[:, piece_number * piece_width : (piece_number + 1) * piece_width]
            piece_shares.append(reduce_block(left_side, columns))
        share_list.append(jnp.concatenate(piece_shares, axis=1)[None])
    qkv_weight_grad, out_weight_grad, gate_up_grad, down_grad = share_list
    split_width = (QUERY_HEADS + KEY_VALUE_HEADS) * HEAD_WIDTH_SIZE
    bias_sum = small_sums[1]
    gain_one_share, query_key_share, value_share, gain_two_share = (
        lax.psum_scatter(small_sums[0][None], ("head", "ctx"), scatter_dimension=1, tiled=True),
        lax.psum_scatter(
            bias_sum[None, :split_width], ("head", "ctx"), scatter_dimension=1, tiled=True
        ),
        lax.psum_scatter(
            bias_sum[None, split_width:], ("head", "ctx"), scatter_dimension=1, tiled=True
        ),
        lax.psum_scatter(small_sums[2][None], ("head", "ctx"), scatter_dimension=1, tiled=True),
    )
    return (
        activations,
        input_grads,
        gain_one_share,
        query_key_share,
        value_share,
        qkv_weight_grad,
        out_weight_grad,
        gain_two_share,
        gate_up_grad,
        down_grad,
    )


MESH_ID = pl.DeviceIdType.MESH
BF = jnp.bfloat16
F32 = jnp.float32
LANES = 128
HB = 128
VMEM_LIMIT = 60 * 1024 * 1024
DMA = pltpu.SemaphoreType.DMA
NT = (((1,), (1,)), ((), ()))
TN = (((0,), (0,)), ((), ()))
NN = (((1,), (0,)), ((), ()))


def mm(left_side, right_side, form=NN):
    return lax.dot_general(left_side, right_side, form, preferred_element_type=F32)


def where_am_i():
    head = lax.axis_index("head")
    return (lax.axis_index("section"), head // 2, lax.rem(head, 2), lax.axis_index("ctx"))


def at(x, y, k, z):
    return (x, y * 2 + k, z)


def remote(source, target, send_sem, recv_sem, device):
    return pltpu.make_async_remote_copy(
        src_ref=source,
        dst_ref=target,
        send_sem=send_sem,
        recv_sem=recv_sem,
        device_id=device,
        device_id_type=MESH_ID,
    )


def arrived(ref, sem):
    pltpu.make_async_copy(ref, ref, sem).wait()


def greet(devices):
    barrier = pltpu.get_barrier_semaphore()
    for device in devices:
        pl.semaphore_signal(barrier, inc=1, device_id=device, device_id_type=MESH_ID)
    pl.semaphore_wait(barrier, len(devices))


def greet_all(index, total, device_of):
    barrier = pltpu.get_barrier_semaphore()

    @pl.loop(1, total)
    def _(step):
        device = device_of(lax.rem(index + step, total))
        pl.semaphore_signal(barrier, inc=1, device_id=device, device_id_type=MESH_ID)

    pl.semaphore_wait(barrier, total - 1)


def params(collective_id):
    return pltpu.CompilerParams(
        collective_id=collective_id, has_side_effects=True, vmem_limit_bytes=VMEM_LIMIT
    )


def vmem():
    return pl.BlockSpec(memory_space=pltpu.VMEM)


def hbm():
    return pl.BlockSpec(memory_space=pl.ANY)


def row_norm(values):
    return lax.rsqrt(jnp.mean(values * values, axis=-1, keepdims=True) + EPSILON)


class Sizes:
    def __init__(self, mesh, tokens, qkv_weight, gate_up, down):
        self.ctx = mesh.shape["ctx"]
        self.group = 4 * self.ctx
        self.total = 2 * self.group
        self.batches, self.seq, self.width = tokens.shape
        self.rows = self.seq // self.group
        self.ff = down.shape[2]
        self.owned = self.width // self.group
        self.blocks = self.ff // HB
        self.plane = self.blocks // 2
        self.most = -(-self.plane // self.group)
        self.least = self.plane // self.group
        self.extra = self.plane % self.group
        self.hidden = self.most * HB
        self.per_group = QUERY_HEADS // 4
        self.qcols = self.per_group * HEAD_WIDTH_SIZE
        self.kcols = HEAD_WIDTH_SIZE
        self.acols = self.qcols + 2 * self.kcols
        self.atot = self.acols + self.qcols

    def fits(self):
        gathered = self.batches * self.seq * self.width * 2
        return (
            self.batches == 2
            and gathered * 3 < VMEM_LIMIT // 2
            and self.ff % (2 * HB) == 0
            and self.ctx % 2 == 0
            and self.least >= 1
            and self.owned % 16 == 0
            and self.rows % 32 == 0
        )


def flat_place(index, group, ctx):
    inside = lax.rem(index, group)
    return (index // group, inside // ctx, lax.rem(inside, ctx))


def block_rank(sz, inside):
    head, z = (inside // sz.ctx, lax.rem(inside, sz.ctx))
    y, k = (head // 2, lax.rem(head, 2))
    turn = jnp.where(z < sz.ctx // 2, 2 * z, 2 * (sz.ctx - 1 - z) + 1)
    return turn + sz.ctx * (2 * k + lax.rem(y + z, 2))


def first_column(sz, owner):
    rank = block_rank(sz, lax.rem(owner, sz.group))
    plane = owner // sz.group * sz.plane
    return pl.multiple_of((plane + rank * sz.least + jnp.minimum(rank, sz.extra)) * HB, HB)


def has_more(sz, owner):
    return block_rank(sz, lax.rem(owner, sz.group)) < sz.extra


def extras_of_head(sz, head):
    count = 0
    for z in range(sz.ctx):
        turn = 2 * z if z < sz.ctx // 2 else 2 * (sz.ctx - 1 - z) + 1
        count += turn + sz.ctx * (2 * (head % 2) + (head // 2 + z) % 2) < sz.extra
    return count


def half_turn(values):
    return pltpu.roll(values, HEAD_WIDTH_SIZE // 2, 1)


def pair_peers(x, y, k, z):
    return (at(1 - x, y, k, z), at(x, 1 - y, k, z), at(1 - x, 1 - y, k, z))


def pair_groups(x, y):
    return (2 * (1 - x) + y, 2 * x + 1 - y, 2 * (1 - x) + 1 - y)


def line_peers(n, x, y, k, z):
    return [at(x, y, k, lax.rem(z + step, n)) for step in range(1, n)]


def tree_peers(n, x, y, k, z):
    return [at(1 - x, y, k, z), at(x, 1 - y, k, z), at(x, y, 1 - k, z)] + line_peers(n, x, y, k, z)


def meet(sz, place, near, across, jobs):
    x, y, k, z = place
    n = sz.ctx
    inside = (y * 2 + k) * n + z
    reach = max([job.reach for job in jobs], default=0)
    if reach == 2:
        greet_all(x * sz.group + inside, sz.total, lambda index: flat_place(index, sz.group, n))
    elif reach == 1:
        barrier = pltpu.get_barrier_semaphore()
        for device in across:
            pl.semaphore_signal(barrier, inc=1, device_id=device, device_id_type=MESH_ID)

        @pl.loop(1, sz.group)
        def _(step):
            device = flat_place(x * sz.group + lax.rem(inside + step, sz.group), sz.group, n)
            pl.semaphore_signal(barrier, inc=1, device_id=device, device_id_type=MESH_ID)

        pl.semaphore_wait(barrier, sz.group - 1 + len(across))
    else:
        greet(near)


def run_call(body, ins, outs, scratch, jobs, collective_id, name):
    fg_in, fg_out, fg_scratch = len(ins), len(outs), len(scratch)
    ins, outs, scratch = list(ins), list(outs), list(scratch)
    for job in jobs:
        ins += [(array, hbm() if spec is None else spec) for array, spec in job.ins]
        outs += [(shape, hbm()) for shape in job.outs]
        scratch += job.scratch

    def kernel(*refs):
        given, made, own = (
            refs[: len(ins)],
            refs[len(ins) : len(ins) + len(outs)],
            refs[len(ins) + len(outs) :],
        )
        a, b, c = fg_in, fg_out, fg_scratch
        for job in jobs:
            job.bind(
                given[a : a + len(job.ins)],
                made[b : b + len(job.outs)],
                own[c : c + len(job.scratch)],
            )
            a, b, c = a + len(job.ins), b + len(job.outs), c + len(job.scratch)
        body(given[:fg_in], made[:fg_out], own[:fg_scratch], jobs)

    results = pl.pallas_call(
        kernel,
        out_shape=tuple(shape for shape, _ in outs),
        in_specs=[spec for _, spec in ins],
        out_specs=tuple(spec for _, spec in outs),
        scratch_shapes=scratch,
        compiler_params=params(collective_id),
        name=name,
    )(*[array for array, _ in ins])
    at_out, extra = fg_out, []
    for job in jobs:
        extra.append(results[at_out : at_out + len(job.outs)])
        at_out += len(job.outs)
    return (results[:fg_out], extra)


def plane_order(n, place, index):
    x, y, k, z = place
    head = y * 2 + k
    far = 4 * (n - 1)
    if isinstance(index, int) and index == 4 * n - 1:
        return head * n + z
    rest = index - far
    head_to = lax.rem(head + jnp.where(index < far, index // (n - 1), rest + 1), 4)
    ctx_to = lax.rem(z + jnp.where(index < far, 1 + lax.rem(index, n - 1), 0), n)
    return head_to * n + ctx_to


def span_of(count, low, high):
    return (int(count * low), int(count * high))


class Columns:
    reach = 1

    def __init__(self, sz, section, part, gate_up, down, staged):
        self.sz, self.section, self.part = sz, section, part
        self.ins = [(down if part == 2 else gate_up, None), (staged, None)]
        self.outs = [jax.ShapeDtypeStruct((sz.width, sz.hidden), BF)]
        self.scratch = [DMA((2,)), DMA((2,))]

    def bind(self, ins, outs, scratch):
        self.source, self.staged = ins
        self.target = outs[0]
        self.send, self.recv = scratch

    def begin(self, place, low=0.0, high=1.0):
        sz = self.sz
        n = sz.ctx
        x, y, k, z = place
        inside = (y * 2 + k) * n + z
        me = x * sz.group + inside
        first, stop = span_of(sz.group, low, high)
        rows = pl.ds(pl.multiple_of(inside * sz.owned, 16), sz.owned)
        wide = sz.least * HB
        base = sz.ff if self.part == 1 else 0

        def pair(owner, offset, width, own):
            target = self.target.at[rows, pl.ds(offset, width)]
            if own:
                first = pl.multiple_of(base + first_column(sz, owner) + offset, HB)
                return (self.source.at[:, pl.ds(first, width)], target)
            first = first_column(sz, owner) - x * sz.plane * HB + offset
            first = pl.multiple_of(first, HB)
            return (self.staged.at[self.part, :, pl.ds(first, width)], target)

        for own in (True, False):

            @pl.when((x == self.section) == own)
            def _():
                @pl.loop(first, min(stop, sz.group - 1))
                def _(step):
                    owner = x * sz.group + plane_order(n, place, step)
                    device = flat_place(owner, sz.group, n)
                    source, target = pair(owner, 0, wide, own)
                    remote(source, target, self.send.at[0], self.recv.at[0], device).start()
                    if sz.extra:

                        @pl.when(has_more(sz, owner))
                        def _():
                            source, target = pair(owner, wide, HB, own)
                            remote(source, target, self.send.at[1], self.recv.at[1], device).start()

                if stop < sz.group:
                    return
                source, target = pair(me, 0, wide, own)
                pltpu.make_async_copy(source, target, self.send.at[0]).start()
                if sz.extra:

                    @pl.when(has_more(sz, me))
                    def _():
                        source, target = pair(me, wide, HB, own)
                        pltpu.make_async_copy(source, target, self.send.at[1]).start()

    def middle(self, place):
        pass

    def finish(self, place):
        sz = self.sz
        x, y, k, z = place
        me = x * sz.group + (y * 2 + k) * sz.ctx + z
        wide = sz.least * HB
        arrived(self.target.at[pl.ds(0, sz.width - sz.owned), pl.ds(0, wide)], self.recv.at[0])
        arrived(self.target.at[:, pl.ds(0, wide)], self.send.at[0])
        if sz.extra:
            arrived(self.target.at[pl.ds(0, sz.extra * sz.owned), pl.ds(0, HB)], self.send.at[1])

            @pl.when(has_more(sz, me))
            def _():
                arrived(
                    self.target.at[pl.ds(0, sz.width - sz.owned), pl.ds(0, HB)], self.recv.at[1]
                )


def head_columns(sz, g, qkv, out_w):
    kv = g // (4 // KEY_VALUE_HEADS)
    q0 = pl.multiple_of(g * sz.qcols, HB)
    k0 = pl.multiple_of(QUERY_HEADS * HEAD_WIDTH_SIZE + kv * sz.kcols, HB)
    v0 = pl.multiple_of((QUERY_HEADS + KEY_VALUE_HEADS) * HEAD_WIDTH_SIZE + kv * sz.kcols, HB)
    return (
        (qkv.at[:, pl.ds(q0, sz.qcols)], pl.ds(0, sz.qcols)),
        (qkv.at[:, pl.ds(k0, sz.kcols)], pl.ds(sz.qcols, sz.kcols)),
        (qkv.at[:, pl.ds(v0, sz.kcols)], pl.ds(sz.qcols + sz.kcols, sz.kcols)),
        (out_w.at[:, pl.ds(q0, sz.qcols)], pl.ds(sz.acols, sz.qcols)),
    )


RELAYED = 4


def ends(n, z, ctx):
    if n != RELAYED:
        return z < 0
    return jnp.abs(z - ctx) == n - 1


def relay_of(n, z, ctx):
    if n != RELAYED:
        return z < 0
    return jnp.logical_or(
        jnp.logical_and(z == 0, ctx == n - 2), jnp.logical_and(z == n - 1, ctx == 1)
    )


def inner(n, z):
    return jnp.logical_and(z > 0, z < n - 1)


class Heads:
    reach = 1

    def __init__(self, sz, section, qkv, out_w, staged):
        self.sz, self.section = sz, section
        self.ins = [(qkv, None), (out_w, None), (staged, None)]
        self.outs = [jax.ShapeDtypeStruct((sz.width, sz.atot), BF)]
        self.scratch = [DMA, DMA((2,)), DMA((2,)), DMA((2,)), DMA]

    def bind(self, ins, outs, scratch):
        self.qkv, self.out_w, self.staged = ins
        self.target = outs[0]
        self.send, self.recv, self.s_core, self.r_core, self.s_relay = scratch

    def begin(self, place, low=0.0, high=1.0):
        sz = self.sz
        n = sz.ctx
        x, y, k, z = place
        rows = pl.ds(pl.multiple_of(((y * 2 + k) * n + z) * sz.owned, 16), sz.owned)
        mine = y * n + z

        def pairs(y_to, own):
            if own:
                return [
                    (source, self.target.at[rows, cols])
                    for source, cols in head_columns(sz, 2 * x + y_to, self.qkv, self.out_w)
                ]
            return [(self.staged.at[y_to], self.target.at[rows])]

        for own in (True, False):

            @pl.when((x == self.section) == own)
            def _():
                @pl.loop(1, 2 * n)
                def _(step):
                    index = lax.rem(mine + step, 2 * n)
                    ctx = lax.rem(index, n)

                    @pl.when(jnp.logical_not(ends(n, z, ctx)))
                    def _():
                        recv = self.recv.at[jnp.where(relay_of(n, z, ctx), 1, 0)]
                        for source, target in pairs(index // n, own):
                            device = at(x, index // n, k, ctx)
                            remote(source, target, self.send, recv, device).start()

                for source, target in pairs(y, own):
                    pltpu.make_async_copy(source, target, self.send).start()

    def span(self, part, k):
        stretch = self.sz.width // 4
        return self.target.at[pl.ds(pl.multiple_of((part * 2 + k) * stretch, 16), stretch)]

    def relay(self, place):
        sz = self.sz
        n = sz.ctx
        x, y, k, z = place
        if n != RELAYED:
            return

        @pl.when(inner(n, z))
        def _():
            arrived(self.target.at[pl.ds(0, 2 * sz.owned)], self.recv.at[1])
            source = jnp.where(z == 1, n - 1, 0)
            for head in range(2):
                rows = ((head * 2 + k) * n + source) * sz.owned
                span = self.target.at[pl.ds(pl.multiple_of(rows, 16), sz.owned)]
                device = at(x, y, k, n - 1 - source)
                remote(span, span, self.s_relay, self.recv.at[0], device).start()

    def middle(self, place):
        sz = self.sz
        x, y, k, z = place
        half = sz.width // 2
        two = 2 * sz.owned if sz.ctx == RELAYED else 0

        @pl.when(inner(sz.ctx, z))
        def _():
            arrived(self.target.at[pl.ds(0, half - sz.owned - two)], self.recv.at[0])
            arrived(self.target.at[pl.ds(0, half)], self.send)
            if two:
                arrived(self.target.at[pl.ds(0, two)], self.s_relay)

        @pl.when(jnp.logical_not(inner(sz.ctx, z)))
        def _():
            arrived(self.target.at[pl.ds(0, half - sz.owned)], self.recv.at[0])
            arrived(self.target.at[pl.ds(0, half - two)], self.send)

        for part in range(2):
            span = self.span(part, k)
            remote(span, span, self.s_core.at[part], self.r_core.at[part], at(x, y, 1 - k, z)).start()

    def finish(self, place):
        x, y, k, z = place
        for part in range(2):
            span = self.span(part, 1 - k)
            arrived(span, self.r_core.at[part])
            arrived(span, self.s_core.at[part])


class LineShares:
    reach = 0

    def __init__(self, sz, part, grads=None):
        self.sz, self.part = sz, part
        self.ins = [] if grads is None else [(grads, None)]
        self.outs = [jax.ShapeDtypeStruct((sz.ctx, 4, sz.owned, sz.hidden), BF)]
        self.scratch = [DMA((2, sz.ctx)), DMA((2, sz.ctx))]

    def bind(self, ins, outs, scratch):
        if ins:
            self.source = ins[0]
        self.target = outs[0]
        self.send, self.recv = scratch

    def moves(self, place, step, offset, width):
        sz = self.sz
        x, y, k, z = place
        ctx = lax.rem(z + step, sz.ctx)
        for head in range(4):
            rows = pl.ds(pl.multiple_of((head * sz.ctx + ctx) * sz.owned, 16), sz.owned)
            cols = pl.ds(offset, width)
            yield (self.source.at[self.part, rows, cols], self.target.at[z, head, :, cols])

    def begin(self, place, steps=None):
        sz = self.sz
        n = sz.ctx
        x, y, k, z = place
        me = x * sz.group + (y * 2 + k) * n + z
        wide = sz.least * HB

        def go(kind, offset, width):
            for step in list(range(1, n)) + [0] if steps is None else steps:
                for source, target in self.moves(place, step, offset, width):
                    if step:
                        remote(
                            source,
                            target,
                            self.send.at[kind, step],
                            self.recv.at[kind, step],
                            at(x, y, k, lax.rem(z + step, n)),
                        ).start()
                    else:
                        pltpu.make_async_copy(source, target, self.send.at[kind, 0]).start()

        go(0, 0, wide)
        if sz.extra:

            @pl.when(has_more(sz, me))
            def _():
                go(1, wide, HB)

    def finish(self, place):
        sz = self.sz
        n = sz.ctx
        x, y, k, z = place
        first = x * sz.group + (y * 2 + k) * n
        wide = sz.least * HB
        for step in range(n):
            ctx = lax.rem(z + n - step, n)
            arrived(self.target.at[ctx, :, :, pl.ds(0, wide)], self.send.at[0, step])
            if step:
                arrived(self.target.at[ctx, :, :, pl.ds(0, wide)], self.recv.at[0, step])
            if sz.extra:

                @pl.when(has_more(sz, first + z))
                def _():
                    arrived(self.target.at[ctx, :, :, pl.ds(wide, HB)], self.send.at[1, step])

                if step:

                    @pl.when(has_more(sz, first + ctx))
                    def _():
                        arrived(self.target.at[ctx, :, :, pl.ds(wide, HB)], self.recv.at[1, step])


class PlaneShares:
    def __init__(self, sz, section, part, source, target, sems):
        self.sz, self.section, self.part = sz, section, part
        self.source, self.target = source, target
        self.send, self.recv, self.local, self.s_over, self.r_over = sems
        self.row = target.at[0, part]

    def place_in(self, slot):
        return self.target.at[slot, self.part]

    def begin(self, place):
        sz = self.sz
        n = sz.ctx
        x, y, k, z = place
        head = y * 2 + k
        wide = sz.least * HB
        slot = jnp.where(x == self.section, 0, 1)

        def go(to, device, local):
            for ctx in range(n):
                owner = x * sz.group + head * n + ctx
                first = first_column(sz, owner)

                def one(kind, offset, width):
                    source = self.source.at[ctx, to, :, pl.ds(offset, width)]
                    cols = pl.ds(pl.multiple_of(first + offset, HB), width)
                    target = self.place_in(slot).at[:, cols]
                    if local:
                        pltpu.make_async_copy(source, target, self.local.at[kind]).start()
                    else:
                        recv = self.recv.at[0] if kind == 0 else self.recv.at[1 + head]
                        remote(source, target, self.send.at[kind], recv, device).start()

                one(0, 0, wide)
                if sz.extra:

                    @pl.when(has_more(sz, owner))
                    def _():
                        one(1, wide, HB)

        for step in range(1, 4):
            to = lax.rem(head + step, 4)
            go(to, (x, to, z), False)
        go(head, None, True)

    def settled(self, place):
        sz = self.sz
        n = sz.ctx
        x, y, k, z = place
        head = y * 2 + k
        wide = sz.least * HB
        row = self.row
        arrived(row.at[:, pl.ds(0, 3 * n * wide)], self.recv.at[0])
        arrived(row.at[:, pl.ds(0, 3 * n * wide)], self.send.at[0])
        arrived(row.at[:, pl.ds(0, n * wide)], self.local.at[0])
        for other in range(4):
            count = extras_of_head(sz, other)
            if count:

                @pl.when(head != other)
                def _():
                    arrived(row.at[:, pl.ds(0, count * HB)], self.recv.at[1 + other])

                @pl.when(head == other)
                def _():
                    arrived(row.at[:, pl.ds(0, 3 * count * HB)], self.send.at[1])
                    arrived(row.at[:, pl.ds(0, count * HB)], self.local.at[1])

    def cross(self, place):
        self.settled(place)

        @pl.when(place[0] != self.section)
        def _():
            self.over(place).start()

    def over(self, place):
        x, y, k, z = place
        plane = 1 - self.section
        cols = pl.ds(plane * self.sz.plane * HB, self.sz.plane * HB)
        return remote(
            self.target.at[1, self.part, :, cols],
            self.target.at[0, self.part, :, cols],
            self.s_over,
            self.r_over,
            at(1 - x, y, k, z),
        )

    def finish(self, place):
        x = place[0]

        @pl.when(x != self.section)
        def _():
            self.over(place).wait_send()

        @pl.when(x == self.section)
        def _():
            self.over(place).wait_recv()


class ReturnedHeads:
    reach = 0

    def __init__(self, sz, section, part, grads):
        self.sz, self.section, self.part = sz, section, part
        stretch = sz.width // 4
        self.ins = [] if grads is None else [(grads, None)]
        self.outs = [jax.ShapeDtypeStruct((4, sz.owned, sz.atot), BF)]
        self.scratch = [
            pltpu.VMEM((stretch, sz.atot), BF),
            pltpu.VMEM((stretch, sz.atot), BF),
            pltpu.VMEM((sz.ctx, sz.owned, sz.atot), BF),
            pltpu.VMEM((sz.owned, sz.atot), BF),
            pltpu.VMEM((sz.owned, sz.atot), F32),
            DMA,
            DMA,
            DMA,
            DMA,
            DMA((sz.ctx,)),
            DMA((sz.ctx,)),
            DMA,
            DMA((4,)),
        ]

    def bind(self, ins, outs, scratch):
        if ins:
            self.source = ins[0]
        self.target = outs[0]
        (
            self.got,
            self.summed,
            self.lined,
            self.taken,
            self.sum,
            self.load,
            self.r_taken,
            self.s_core,
            self.r_core,
            self.s_line,
            self.r_line,
            self.send,
            self.recv,
        ) = scratch

    def rows(self, k):
        stretch = self.sz.width // 4
        return pl.ds(pl.multiple_of((self.part * 2 + k) * stretch, 16), stretch)

    def own_rows(self, place):
        return pltpu.make_async_copy(self.source.at[self.rows(place[2])], self.summed, self.load)

    def core(self, place):
        x, y, k, z = place
        return remote(
            self.source.at[self.rows(1 - k)], self.got, self.s_core, self.r_core, at(x, y, 1 - k, z)
        )

    def own(self, ctx):
        return pl.ds(pl.multiple_of(ctx * self.sz.owned, 16), self.sz.owned)

    def line(self, place, step):
        x, y, k, z = place
        ctx = lax.rem(z + step, self.sz.ctx)
        return remote(
            self.summed.at[self.own(ctx)],
            self.lined.at[step],
            self.s_line.at[step],
            self.r_line.at[step],
            at(x, y, k, ctx),
        )

    def begin(self, place):
        self.own_rows(place).start()
        self.core(place).start()

    def middle(self, place):
        self.own_rows(place).wait()
        self.core(place).wait_recv()
        self.summed[...] = (self.summed[...].astype(F32) + self.got[...].astype(F32)).astype(BF)
        x, y, k, z = place
        n = self.sz.ctx
        for step in range(1, n):
            ctx = lax.rem(z + step, n)
            if n != RELAYED:
                self.line(place, step).start()
                continue

            @pl.when(ends(n, z, ctx))
            def _():
                remote(
                    self.summed.at[self.own(ctx)],
                    self.taken,
                    self.s_line.at[step],
                    self.r_taken,
                    at(x, y, k, jnp.where(z == 0, 1, n - 2)),
                ).start()

            @pl.when(jnp.logical_not(jnp.logical_or(ends(n, z, ctx), self.held(z, ctx))))
            def _():
                self.line(place, step).start()

    def held(self, z, ctx):
        n = self.sz.ctx
        return jnp.logical_or(
            jnp.logical_and(z == 1, ctx == n - 1), jnp.logical_and(z == n - 2, ctx == 0)
        )

    def relay(self, place):
        n = self.sz.ctx
        z = place[3]
        if n != RELAYED:
            return

        @pl.when(inner(n, z))
        def _():
            arrived(self.taken, self.r_taken)
            rows = self.own(jnp.where(z == 1, n - 1, 0))
            self.summed[rows] = (self.summed[rows].astype(F32) + self.taken[...].astype(F32)).astype(BF)
            self.line(place, 2).start()

    def homes(self, place, starting):
        x, y, k, z = place
        own = jnp.logical_and(x == self.section, y == self.part)
        target = self.target.at[2 * x + y]

        @pl.when(jnp.logical_not(own))
        def _():
            device = at(self.section, self.part, k, z)
            copy = remote(self.lined.at[0], target, self.send, self.recv.at[2 * x + y], device)
            copy.start() if starting else copy.wait_send()

        @pl.when(own)
        def _():
            copy = pltpu.make_async_copy(self.lined.at[0], target, self.send)
            copy.start() if starting else copy.wait()

    def late(self, place):
        x, y, k, z = place
        n = self.sz.ctx
        self.sum[...] = self.summed[self.own(z)].astype(F32)
        for step in range(1, n):

            @pl.when(jnp.logical_not(ends(n, z, lax.rem(z + n - step, n))))
            def _():
                self.line(place, step).wait_recv()
                self.sum[...] += self.lined[step].astype(F32)

        self.lined[0] = self.sum[...].astype(BF)
        self.homes(place, True)

    def finish(self, place):
        x, y, k, z = place
        self.core(place).wait_send()
        for step in range(1, self.sz.ctx):
            self.line(place, step).wait_send()
        self.homes(place, False)

        @pl.when(jnp.logical_and(x == self.section, y == self.part))
        def _():
            for group in range(4):

                @pl.when(group != 2 * x + y)
                def _():
                    arrived(self.target.at[group], self.recv.at[group])


class Placed:
    reach = 0

    def __init__(self, sz, first, second):
        self.ins = [(first, None), (second, None)]
        self.outs = [jax.ShapeDtypeStruct((2, sz.rows, sz.width), BF)]
        self.scratch = [DMA((2,)), DMA((2,))]

    def bind(self, ins, outs, scratch):
        self.sources, self.target = ins, outs[0]
        self.send, self.recv = scratch

    def each(self, place, starting):
        x, y, k, z = place
        for section in range(2):
            source, target = (self.sources[section], self.target.at[k])
            own = jnp.logical_and(x == section, jnp.logical_and(x == y, y == k))

            @pl.when(jnp.logical_not(own))
            def _():
                device = at(section, x, y, z)
                copy = remote(source, target, self.send.at[section], self.recv.at[k], device)
                copy.start() if starting else copy.wait_send()

            if starting:

                @pl.when(own)
                def _():
                    pltpu.make_async_copy(source, target, self.recv.at[k]).start()

    def begin(self, place):
        self.each(place, True)

    def finish(self, place):
        self.each(place, False)
        for batch in range(2):
            arrived(self.target.at[batch], self.recv.at[batch])


def begin(jobs, place, low=0.0, high=1.0):
    for job in jobs:
        job.begin(place, low, high)


def middle(jobs, place):
    for job in jobs:
        job.middle(place)


def finish(jobs, place):
    for job in jobs:
        job.finish(place)


class Gather:
    SEMS = 12

    @staticmethod
    def scratch(n):
        return [DMA((n,))] * 10 + [DMA((4, n))] * 2

    def __init__(self, n, rows, buffer, place, sems):
        self.n, self.half, self.buffer = n, rows // 2, buffer
        self.x, self.y, self.k, self.z = place
        x, y = self.x, self.y
        self.groups = (2 * x + y, 2 * x + 1 - y, 2 * (1 - x) + y, 2 * (1 - x) + 1 - y)
        (
            self.sz,
            self.rz,
            self.sy,
            self.ry,
            self.sx,
            self.rx,
            self.syd,
            self.ryd,
            self.sxd,
            self.rxd,
            self.sc,
            self.rc,
        ) = sems

    def src(self, step):
        return lax.rem(self.z + self.n - step, self.n)

    def line(self, step):
        own = self.buffer.at[self.k, self.groups[0], self.z]
        device = at(self.x, self.y, self.k, lax.rem(self.z + step, self.n))
        return remote(own, own, self.sz.at[step], self.rz.at[step], device)

    def to_y(self, step):
        part = self.buffer.at[self.k, self.groups[0], self.src(step)]
        device = at(self.x, 1 - self.y, self.k, self.z)
        return remote(part, part, self.sy.at[step], self.ry.at[step], device)

    def to_x(self, step):
        part = self.buffer.at[self.k, self.groups[0], self.src(step)]
        device = at(1 - self.x, self.y, self.k, self.z)
        return remote(part, part, self.sx.at[step], self.rx.at[step], device)

    def on_x(self, step):
        part = self.buffer.at[self.k, self.groups[1], self.src(step), pl.ds(0, self.half)]
        device = at(1 - self.x, self.y, self.k, self.z)
        return remote(part, part, self.sxd.at[step], self.rxd.at[step], device)

    def on_y(self, step):
        part = self.buffer.at[self.k, self.groups[2], self.src(step), pl.ds(self.half, self.half)]
        device = at(self.x, 1 - self.y, self.k, self.z)
        return remote(part, part, self.syd.at[step], self.ryd.at[step], device)

    def core(self, which, step):
        part = self.buffer.at[self.k, self.groups[which], self.src(step)]
        device = at(self.x, self.y, 1 - self.k, self.z)
        return remote(part, part, self.sc.at[which, step], self.rc.at[which, step], device)

    def begin(self):
        for step in range(1, self.n):
            self.line(step).start()
        self.spread(0)

    def spread(self, step):
        if step:
            arrived(self.buffer.at[self.k, self.groups[0], self.src(step)], self.rz.at[step])
        self.to_y(step).start()
        self.to_x(step).start()
        self.core(0, step).start()

    def second(self, step):
        arrived(self.buffer.at[self.k, self.groups[1], self.src(step)], self.ry.at[step])
        self.on_x(step).start()
        self.core(1, step).start()
        arrived(self.buffer.at[self.k, self.groups[2], self.src(step)], self.rx.at[step])
        self.on_y(step).start()
        self.core(2, step).start()

    def third(self, step):
        part = self.buffer.at[self.k, self.groups[3], self.src(step)]
        arrived(part.at[pl.ds(0, self.half)], self.rxd.at[step])
        arrived(part.at[pl.ds(self.half, self.half)], self.ryd.at[step])
        self.core(3, step).start()

    def other(self, which):
        for step in range(self.n):
            part = self.buffer.at[1 - self.k, self.groups[which], self.src(step)]
            arrived(part, self.rc.at[which, step])

    def finish(self):
        for step in range(self.n):
            if step:
                self.line(step).wait_send()
            self.to_y(step).wait_send()
            self.to_x(step).wait_send()
            self.on_x(step).wait_send()
            self.on_y(step).wait_send()
            for which in range(4):
                self.core(which, step).wait_send()

    def stages(self, column, nearly):
        k, steps = self.k, range(self.n)

        def spread():
            for step in range(1, self.n):
                self.spread(step)

        def second():
            for step in steps:
                self.second(step)

        def near():
            self.other(0)
            column(1 - k, 0)
            column(k, 1)
            column(k, 2)

        def third():
            for step in steps:
                self.third(step)

        def far():
            self.other(1)
            column(1 - k, 1)
            self.other(2)
            column(1 - k, 2)
            nearly()

        def last():
            column(k, 3)
            self.other(3)
            column(1 - k, 3)

        return [self.begin, spread, lambda: column(k, 0), second, near, third, far, last]


class Scatter:
    @staticmethod
    def scratch(n, rows, width):
        return [
            pltpu.VMEM((2, 4, n, rows, width), BF),
            pltpu.VMEM((4, n, rows, width), BF),
            pltpu.VMEM((2, n, rows // 2, width), BF),
            pltpu.VMEM((2, n, rows, width), BF),
            pltpu.VMEM((n, rows, width), BF),
            DMA((4,)),
            DMA((4,)),
            DMA((2, n)),
            DMA((2, n)),
            DMA((2, 2, n)),
            DMA((2, 2, n)),
            DMA((n,)),
            DMA((n,)),
        ]

    def __init__(self, n, rows, place, refs):
        self.n, self.rows, self.half = n, rows, rows // 2
        self.x, self.y, self.k, self.z = place
        x, y = self.x, self.y
        self.groups = (2 * x + y, 2 * x + 1 - y, 2 * (1 - x) + y, 2 * (1 - x) + 1 - y)
        (
            self.parts,
            self.from_core,
            self.from_diag,
            self.from_near,
            self.from_line,
            self.s_core,
            self.r_core,
            self.s_diag,
            self.r_diag,
            self.s_near,
            self.r_near,
            self.s_line,
            self.r_line,
        ) = refs
        self.near = (at(x, 1 - y, self.k, self.z), at(1 - x, y, self.k, self.z))

    def slot(self, step):
        return lax.rem(self.z + step, self.n)

    def order(self):
        return list(range(1, self.n)) + [0]

    def core(self, which):
        return remote(
            self.parts.at[1 - self.k, self.groups[which]],
            self.from_core.at[which],
            self.s_core.at[which],
            self.r_core.at[which],
            at(self.x, self.y, 1 - self.k, self.z),
        )

    def diag(self, direction, step):
        rows = pl.ds(self.half if direction == 0 else 0, self.half)
        return remote(
            self.parts.at[self.k, self.groups[3], self.slot(step), rows],
            self.from_diag.at[direction, step],
            self.s_diag.at[direction, step],
            self.r_diag.at[direction, step],
            self.near[direction],
        )

    def close(self, direction, part, step):
        rows = pl.ds(part * self.half, self.half)
        return remote(
            self.parts.at[self.k, self.groups[1 + direction], self.slot(step), rows],
            self.from_near.at[direction, step, rows],
            self.s_near.at[direction, part, step],
            self.r_near.at[direction, part, step],
            self.near[direction],
        )

    def line(self, step):
        return remote(
            self.parts.at[self.k, self.groups[0], self.slot(step)],
            self.from_line.at[step],
            self.s_line.at[step],
            self.r_line.at[step],
            at(self.x, self.y, self.k, self.slot(step)),
        )

    def add_core(self, which):
        self.core(which).wait_recv()
        group = self.groups[which]
        self.parts[self.k, group] = (
            self.parts[self.k, group].astype(F32) + self.from_core[which].astype(F32)
        ).astype(BF)

    def early(self):
        for direction, part in ((0, 1), (1, 0)):
            self.add_core(1 + direction)
            for step in self.order():
                self.close(direction, part, step).start()

    def open(self):
        self.add_core(3)
        for step in self.order():
            self.diag(1, step).start()
            self.diag(0, step).start()
        self.add_core(0)

    def late(self):
        for step in self.order():
            slot = self.slot(step)
            for direction, part in ((0, 0), (1, 1)):
                came = 1 - direction
                self.diag(came, step).wait_recv()
                rows = pl.ds(part * self.half, self.half)
                group = self.groups[1 + direction]
                self.parts[self.k, group, slot, rows] = (
                    self.parts[self.k, group, slot, rows].astype(F32)
                    + self.from_diag[came, step].astype(F32)
                ).astype(BF)
                self.close(direction, part, step).start()

    def along(self):
        group = self.groups[0]
        for step in self.order():
            slot = self.slot(step)
            for direction in range(2):
                for part in range(2):
                    self.close(direction, part, step).wait_recv()
            total = (
                self.parts[self.k, group, slot].astype(F32)
                + self.from_near[0, step].astype(F32)
                + self.from_near[1, step].astype(F32)
            )
            if step:
                self.parts[self.k, group, slot] = total.astype(BF)
                self.line(step).start()
            else:
                self.own = total

    def result(self):
        result = self.own
        for step in range(1, self.n):
            self.line(step).wait_recv()
            result = result + self.from_line[step].astype(F32)
        return result

    def stages(self):
        return [self.open, self.late, self.along]

    def finish(self):
        for which in range(4):
            self.core(which).wait_send()
        for step in range(self.n):
            for direction in range(2):
                self.diag(direction, step).wait_send()
                for part in range(2):
                    self.close(direction, part, step).wait_send()
            if step:
                self.line(step).wait_send()


CHUNKS = 2
A, B = 0, 1
TOGETHER = (
    (A, 0), (B, 0), (A, 1), (A, 2), (A, 3), (A, 4), (B, 1), (A, 5), (B, 2), (A, 6), (B, 3), (A, 7),
    (A, 8), (B, 4), (B, 5), (A, 9), (B, 6), (B, 7), (B, 8), (A, 10), (B, 9), (B, 10),
)


def run_together(first, second, after):
    for stream, number in TOGETHER:
        (first, second)[stream][number]()
        if (stream, number) in after:
            after[stream, number]()


def spread(sz, small, tokens, cotangent, qkv, out_w, gate_up, down):
    n = sz.ctx
    half = sz.plane * HB

    def body(ins, outs, scratch, jobs):
        small, tokens, cotangent, qkv, out_w, gate_up, down = ins
        small_all, tok_own, cot_own, heads_x, cols_x = outs
        s_small, r_small, s_own, r_own, s_hx, r_hx, s_cx, r_cx = scratch
        place = where_am_i()
        x, y, k, z = place
        me = x * sz.group + (y * 2 + k) * n + z
        everyone = lambda index: flat_place(index, sz.group, n)
        greet_all(me, sz.total, everyone)
        across = at(1 - x, y, k, z)

        def heads_over():
            return [
                remote(source, heads_x.at[y_to, :, cols], s_hx, r_hx, across)
                for y_to in range(2)
                for source, cols in head_columns(sz, 2 * (1 - x) + y_to, qkv, out_w)
            ]

        for copy in heads_over():
            copy.start()

        def owns(starting):
            @pl.when(x == y)
            def _():
                for batch in range(2):
                    pairs = ((tokens, tok_own, 0), (cotangent, cot_own, 1))
                    for source, target, slot in pairs:
                        own = jnp.logical_and(k == y, k == batch)

                        @pl.when(jnp.logical_not(own))
                        def _():
                            copy = remote(
                                source.at[batch],
                                target,
                                s_own.at[batch, slot],
                                r_own.at[slot],
                                at(x, k, batch, z),
                            )
                            copy.start() if starting else copy.wait_send()

                        if starting:

                            @pl.when(own)
                            def _():
                                pltpu.make_async_copy(
                                    source.at[batch], target, r_own.at[slot]
                                ).start()

        owns(True)

        @pl.loop(1, sz.total)
        def _(step):
            device = everyone(lax.rem(me + step, sz.total))
            remote(small, small_all.at[me], s_small, r_small, device).start()

        pltpu.make_async_copy(small, small_all.at[me], s_small).start()

        def columns_over(part):
            base = (sz.ff if part == 1 else 0) + (1 - x) * half
            source = (down if part == 2 else gate_up).at[:, pl.ds(pl.multiple_of(base, HB), half)]
            return remote(source, cols_x.at[part], s_cx.at[part], r_cx.at[part], across)

        heads, first = jobs
        heads.use(ins, outs)
        first.use(ins, outs)

        @pl.when(x == heads.section)
        def _():
            heads.begin(place)

        for part in range(3):
            columns_over(part).start()
        arrived(heads_x, r_hx)

        @pl.when(x != heads.section)
        def _():
            heads.begin(place)

        columns_over(0).wait_recv()
        heads.relay(place)
        first.begin(place)
        heads.middle(place)
        arrived(small_all.at[pl.ds(0, sz.total - 1)], r_small)
        arrived(small_all, s_small)
        arrived(tok_own, r_own.at[0])
        arrived(cot_own, r_own.at[1])
        owns(False)
        heads.finish(place)

        for part in range(3):
            if part:
                columns_over(part).wait_recv()
            columns_over(part).wait_send()
        arrived(heads_x, s_hx)
        first.finish(place)

    shape = jax.ShapeDtypeStruct
    outs = [
        (shape((sz.total, 16, LANES), BF), hbm()),
        (shape((sz.rows, sz.width), BF), hbm()),
        (shape((sz.rows, sz.width), BF), hbm()),
        (shape((2, sz.owned, sz.atot), BF), hbm()),
        (shape((3, sz.owned, half), BF), hbm()),
    ]
    arrays = (small, tokens, cotangent, qkv, out_w, gate_up, down)
    scratch = [DMA, DMA, DMA((2, 2)), DMA((2,)), DMA, DMA, DMA((3,)), DMA((3,))]
    jobs = [OwnHeads(sz, 0, 3, 4, 3), OwnColumns(sz, 0, 0, 5, 4)]
    return run_call(body, [(a, hbm()) for a in arrays], outs, scratch, jobs, 1, "spread_weights")


class OwnHeads(Heads):
    def __init__(self, sz, section, qkv, out_w, staged):
        super().__init__(sz, section, None, None, None)
        self.ins = []
        self.named = (qkv, out_w, staged)

    def bind(self, ins, outs, scratch):
        self.target = outs[0]
        self.send, self.recv, self.s_core, self.r_core, self.s_relay = scratch

    def use(self, ins, outs):
        qkv, out_w, staged = self.named
        self.qkv, self.out_w, self.staged = ins[qkv], ins[out_w], outs[staged]


class OwnColumns(Columns):
    def __init__(self, sz, section, part, source, staged):
        super().__init__(sz, section, part, None, None, None)
        self.ins = []
        self.named = (source, staged)

    def bind(self, ins, outs, scratch):
        self.target = outs[0]
        self.send, self.recv = scratch

    def use(self, ins, outs):
        source, staged = self.named
        self.source, self.staged = ins[source], outs[staged]


class Part:
    def __init__(self, body, ins, outs, scratch):
        self.body, self.ins, self.outs, self.scratch = body, ins, outs, scratch


def joined(sz, first, first_jobs, second, second_jobs, link, slab, collective_id, name):
    a, b, c = len(first.ins), len(first.outs), len(first.scratch)
    count = len(first_jobs)

    def body(ins, outs, scratch, jobs):
        place = where_am_i()
        x, y, k, z = place
        peers = pair_peers(x, y, k, z)
        near = list(peers) + line_peers(sz.ctx, x, y, k, z) + [at(x, y, 1 - k, z)]
        if slab:
            near += [at(x, 1 - y, 1 - k, z), at(1 - x, y, 1 - k, z), at(1 - x, 1 - y, 1 - k, z)]
        meet(sz, place, near, [peers[0], peers[2]], jobs)
        own, later = (jobs[:count], jobs[count:])
        first.body(ins[:a], outs[:b], scratch[:c], own, place)
        second.body(link(outs[:b], ins[a:], own, later), outs[b:], scratch[c:], later, place, own)

    results, extra = run_call(
        body,
        first.ins + second.ins,
        first.outs + second.outs,
        first.scratch + second.scratch,
        list(first_jobs) + list(second_jobs),
        collective_id,
        name,
    )
    return (results[:b], results[b:], extra[:count], extra[count:])


def gather_pair(buffer, place, send, recv):
    x, y, k, z = place
    own = buffer.at[2 * x + y]
    copies = [
        remote(own, own, send.at[i], recv.at[i], device)
        for i, device in enumerate(pair_peers(x, y, k, z))
    ]
    for copy in copies:
        copy.start()
    return copies


def gathered_pair(buffer, place, copies, recv):
    x, y, k, z = place
    for i, group in enumerate(pair_groups(x, y)):
        arrived(buffer.at[group], recv.at[i])


def scatter_pair(parts, landed, place, send, recv):
    x, y, k, z = place
    groups = pair_groups(x, y)
    copies = [
        remote(parts.at[groups[i]], landed.at[i], send.at[i], recv.at[i], device)
        for i, device in enumerate(pair_peers(x, y, k, z))
    ]
    for copy in copies:
        copy.start()
    return copies


def attend(sz, x_own, gain, bias, watt, tables, qpos, kpos):
    n, rows = sz.ctx, 4 * sz.rows

    def body(ins, outs, scratch, jobs, place):
        x_ref, gain, bias, watt, cosine, sine, qpos, kpos = ins
        h1_out, n1_all, q_out, kv_all, o_out, lse_out = outs
        w, parts, landed, w_sem, s_in, r_in, s_kv, r_kv, s_back, r_back = scratch
        x, y, k, z = place
        load = pltpu.make_async_copy(watt, w, w_sem)
        load.start()
        group = 2 * x + y
        values = x_ref[...].astype(F32)
        n1_all[group] = (values * row_norm(values) * gain[...]).astype(BF)
        copies = gather_pair(n1_all, place, s_in, r_in)
        begin(jobs, place, 0.0, 0.3)
        load.wait()
        gathered_pair(n1_all, place, copies, r_in)
        normed = n1_all[...].reshape(rows, sz.width)
        kv = mm(normed, w[:, sz.qcols : sz.acols]) + bias[:, sz.qcols : sz.acols]
        cos, sin = cosine[...], sine[...]
        key = kv[:, : sz.kcols]
        kv_all[z, :, : sz.kcols] = (key * cos + half_turn(key) * sin).astype(BF)
        kv_all[z, :, sz.kcols :] = kv[:, sz.kcols :].astype(BF)
        kv_copies = []
        for step, device in enumerate(line_peers(n, x, y, k, z)):
            own = kv_all.at[z]
            kv_copies.append(remote(own, own, s_kv.at[step], r_kv.at[step], device))
            kv_copies[-1].start()
        begin(jobs, place, 0.3, 1.0)
        queries = mm(normed, w[:, : sz.qcols]) + bias[:, : sz.qcols]
        for head in range(sz.per_group):
            cols = slice(head * HEAD_WIDTH_SIZE, (head + 1) * HEAD_WIDTH_SIZE)
            query = queries[:, cols]
            q_out[:, cols] = (query * cos + half_turn(query) * sin).astype(BF)
        for step in range(n - 1):
            arrived(kv_all.at[lax.rem(z + n - 1 - step, n)], r_kv.at[step])
        keys = kv_all[:, :, : sz.kcols].reshape(n * rows, sz.kcols)
        vals = kv_all[:, :, sz.kcols :].reshape(n * rows, sz.kcols)
        allowed = kpos[...] <= qpos[...]
        scale = 1.0 / math.sqrt(HEAD_WIDTH_SIZE)
        for head in range(sz.per_group):
            cols = slice(head * HEAD_WIDTH_SIZE, (head + 1) * HEAD_WIDTH_SIZE)
            scores = jnp.where(allowed, mm(q_out[:, cols], keys, NT) * scale, -1e30)
            highest = jnp.max(scores, axis=-1, keepdims=True)
            weights = jnp.exp(scores - highest)
            total = jnp.sum(weights, axis=-1, keepdims=True)
            o_out[:, cols] = mm(weights.astype(BF), vals) / total
            lse_out[head] = jnp.broadcast_to(highest + jnp.log(total), (rows, LANES))
        partial = mm(o_out[...].astype(BF), w[:, sz.acols :], NT)
        parts[...] = partial.astype(BF).reshape(4, sz.rows, sz.width)
        back = scatter_pair(parts, landed, place, s_back, r_back)
        middle(jobs, place)
        for copy in copies + kv_copies:
            copy.wait_send()
        out = values + parts[group].astype(F32)
        for i in range(3):
            back[i].wait_recv()
            out = out + landed[i].astype(F32)
        h1_out[...] = out
        for copy in back:
            copy.wait_send()

    shapes = (
        jax.ShapeDtypeStruct((sz.rows, sz.width), F32),
        jax.ShapeDtypeStruct((4, sz.rows, sz.width), BF),
        jax.ShapeDtypeStruct((rows, sz.qcols), BF),
        jax.ShapeDtypeStruct((n, rows, 2 * sz.kcols), BF),
        jax.ShapeDtypeStruct((rows, sz.qcols), F32),
        jax.ShapeDtypeStruct((sz.per_group, rows, LANES), F32),
    )
    arrays = (x_own, gain, bias, watt, *tables, qpos, kpos)
    specs = [vmem()] * 3 + [hbm()] + [vmem()] * 4
    scratch = [
        pltpu.VMEM((sz.width, sz.atot), BF),
        pltpu.VMEM((4, sz.rows, sz.width), BF),
        pltpu.VMEM((3, sz.rows, sz.width), BF),
        DMA,
        DMA((3,)),
        DMA((3,)),
        DMA((n,)),
        DMA((n,)),
        DMA((3,)),
        DMA((3,)),
    ]
    return Part(body, list(zip(arrays, specs)), [(shape, vmem()) for shape in shapes], scratch)


def attend_back(sz, dh1, x_own, gain, watt, tables, qpos, kpos, kept, plan):
    n, rows = sz.ctx, 4 * sz.rows

    def body(ins, outs, scratch, jobs, place, after=None):
        dh1, x_ref, gain, watt, cosine, sine, qpos, kpos, n1_all, q_in, kv_all, o_in, lse_in = ins
        dx_out, dw_out, gain_grad, bias_grad = outs
        w, dh_all, dkv, dkv_in, da, parts, landed, w_sem, s_in, r_in, s_kv, r_kv, s_back, r_back = scratch
        x, y, k, z = place
        load = pltpu.make_async_copy(watt, w, w_sem)
        load.start()
        group = 2 * x + y
        dh_all[group] = dh1[...].astype(BF)
        after = plan(jobs, place) if after is None else after
        copies = gather_pair(dh_all, place, s_in, r_in)
        after[0]()
        load.wait()
        gathered_pair(dh_all, place, copies, r_in)
        after[1]()
        dh = dh_all[...].reshape(rows, sz.width)
        dout = mm(dh, w[:, sz.acols :]).astype(BF)
        keys = kv_all[:, :, : sz.kcols].reshape(n * rows, sz.kcols)
        vals = kv_all[:, :, sz.kcols :].reshape(n * rows, sz.kcols)
        allowed = kpos[...] <= qpos[...]
        scale = 1.0 / math.sqrt(HEAD_WIDTH_SIZE)
        cos, sin = cosine[...], sine[...]
        dkeys, dvals = None, None
        for head in range(sz.per_group):
            cols = slice(head * HEAD_WIDTH_SIZE, (head + 1) * HEAD_WIDTH_SIZE)
            query, grad = q_in[:, cols], dout[:, cols]
            delta = jnp.sum(grad.astype(F32) * o_in[:, cols], axis=-1, keepdims=True)
            scores = mm(query, keys, NT) * scale
            probs = jnp.where(allowed, jnp.exp(scores - lse_in[head][:, :1]), 0.0)
            dscores = (probs * (mm(grad, vals, NT) - delta)).astype(BF)
            dquery = (mm(dscores, keys) * scale).astype(BF).astype(F32)
            da[:, cols] = (dquery * cos - half_turn(dquery) * sin).astype(BF)
            one_key = mm(dscores, query, TN)
            one_val = mm(probs.astype(BF), grad, TN)
            dkeys = one_key if dkeys is None else dkeys + one_key
            dvals = one_val if dvals is None else dvals + one_val
        dkv[:, :, : sz.kcols] = (dkeys * scale).astype(BF).reshape(n, rows, sz.kcols)
        dkv[:, :, sz.kcols :] = dvals.astype(BF).reshape(n, rows, sz.kcols)
        kv_copies = []
        for step, device in enumerate(line_peers(n, x, y, k, z)):
            kv_copies.append(
                remote(
                    dkv.at[lax.rem(z + 1 + step, n)],
                    dkv_in.at[step],
                    s_kv.at[step],
                    r_kv.at[step],
                    device,
                )
            )
            kv_copies[-1].start()
        after[2]()
        dw_out[:, sz.acols :] = mm(dh, o_in[...].astype(BF), TN).astype(BF)
        total = dkv[z].astype(F32)
        for step in range(n - 1):
            kv_copies[step].wait_recv()
            total = total + dkv_in[step].astype(F32)
        dkey = total[:, : sz.kcols]
        da[:, sz.qcols : sz.qcols + sz.kcols] = (dkey * cos - half_turn(dkey) * sin).astype(BF)
        da[:, sz.qcols + sz.kcols :] = total[:, sz.kcols :].astype(BF)
        parts[...] = mm(da[...], w[:, : sz.acols], NT).astype(BF).reshape(4, sz.rows, sz.width)
        back = scatter_pair(parts, landed, place, s_back, r_back)
        after[3]()
        dw_out[:, : sz.acols] = mm(n1_all[...].reshape(rows, sz.width), da[...], TN).astype(BF)
        bias_grad[...] = jnp.sum(da[...].astype(F32), axis=0, keepdims=True)
        for copy in copies + kv_copies:
            copy.wait_send()
        dn1 = parts[group].astype(F32)
        for i in range(3):
            back[i].wait_recv()
            dn1 = dn1 + landed[i].astype(F32)
        values = x_ref[...].astype(F32)
        inverse = row_norm(values)
        weighted = dn1 * gain[...]
        inner = jnp.mean(weighted * values, axis=-1, keepdims=True)
        dx = dh1[...] + inverse * weighted - values * (inverse * inverse * inverse) * inner
        dx_out[...] = dx.astype(BF)
        gain_grad[...] = jnp.sum(dn1 * values * inverse, axis=0, keepdims=True)
        for copy in back:
            copy.wait_send()

    shapes = (
        jax.ShapeDtypeStruct((sz.rows, sz.width), BF),
        jax.ShapeDtypeStruct((sz.width, sz.atot), BF),
        jax.ShapeDtypeStruct((1, sz.width), F32),
        jax.ShapeDtypeStruct((1, sz.acols), F32),
    )
    arrays = (dh1, x_own, gain, watt, *tables, qpos, kpos, *kept)
    specs = [vmem()] * 3 + [hbm()] + [vmem()] * 9
    scratch = [
        pltpu.VMEM((sz.width, sz.atot), BF),
        pltpu.VMEM((4, sz.rows, sz.width), BF),
        pltpu.VMEM((n, rows, 2 * sz.kcols), BF),
        pltpu.VMEM((n, rows, 2 * sz.kcols), BF),
        pltpu.VMEM((rows, sz.acols), BF),
        pltpu.VMEM((4, sz.rows, sz.width), BF),
        pltpu.VMEM((3, sz.rows, sz.width), BF),
        DMA,
        DMA((3,)),
        DMA((3,)),
        DMA((n,)),
        DMA((n,)),
        DMA((3,)),
        DMA((3,)),
    ]
    return Part(body, list(zip(arrays, specs)), [(shape, vmem()) for shape in shapes], scratch)


class HiddenWeights:
    def __init__(self, sz, place, sources, w, sems):
        x, y, k, z = place
        self.sz, self.sources, self.w, self.sems = sz, sources, w, sems
        self.more = has_more(sz, x * sz.group + (y * 2 + k) * sz.ctx + z)
        self.wide = sz.least * HB

    def copies(self, offset, width, kind, parts):
        cols = pl.ds(offset, width)
        return [
            pltpu.make_async_copy(
                self.sources[part].at[:, cols], self.w.at[part, :, cols], self.sems.at[kind, part]
            )
            for part in parts
        ]

    def start(self, parts=(0, 1, 2)):
        for copy in self.copies(0, self.wide, 0, parts):
            copy.start()
        if self.sz.extra:

            @pl.when(self.more)
            def _():
                for copy in self.copies(self.wide, HB, 1, parts):
                    copy.start()

            @pl.when(jnp.logical_not(self.more))
            def _():
                for part in parts:
                    self.w[part, :, self.wide :] = jnp.zeros((self.sz.width, HB), BF)

    def wait(self, parts=(0, 1, 2)):
        for copy in self.copies(0, self.wide, 0, parts):
            copy.wait()
        if self.sz.extra:

            @pl.when(self.more)
            def _():
                for copy in self.copies(self.wide, HB, 1, parts):
                    copy.wait()


def halves(n, rows, gathered, place, refs):
    count = len(Gather.scratch(n)) + len(Scatter.scratch(n, rows, 0))
    made = []
    for chunk in range(CHUNKS):
        own = refs[chunk * count : (chunk + 1) * count]
        made.append(
            (Gather(n, rows, gathered.at[chunk], place, own[:12]), Scatter(n, rows, place, own[12:]))
        )
    return made


def halves_scratch(n, rows, width):
    return (Gather.scratch(n) + Scatter.scratch(n, rows, width)) * CHUNKS


def feed(sz, gain, gate):
    n = sz.ctx
    rows = sz.rows // CHUNKS

    def body(ins, outs, scratch, jobs, place, pending):
        h1, gain, *sources = ins
        act_out, *kept_out = outs
        w, n2_all, gate_out, up_out, hm_out, w_sems, kept_sems, *refs = scratch
        x, y, k, z = place
        hidden_weights = HiddenWeights(sz, place, sources, w, w_sems)
        pairs = halves(n, rows, n2_all, place, refs)
        values = h1[...]
        normed = (values * row_norm(values) * gain[...]).astype(BF)
        for chunk in range(CHUNKS):
            n2_all[chunk, k, 2 * x + y, z] = normed[chunk * rows : (chunk + 1) * rows]

        def columns(chunk):
            gather, scatter = pairs[chunk]

            def column(core, which):
                group = gather.groups[which]
                normed = n2_all[chunk, core, group].reshape(n * rows, sz.width)
                gate = mm(normed, w[0])
                up = mm(normed, w[1])
                hidden = (gate * jax.nn.sigmoid(gate) * up).astype(BF)
                gate_out[chunk, core, group] = gate.astype(BF)
                up_out[chunk, core, group] = up.astype(BF)
                hm_out[chunk, core, group] = hidden
                scatter.parts[core, group] = (
                    mm(hidden, w[2], NT).astype(BF).reshape(n, rows, sz.width)
                )
                if core is not k:
                    scatter.core(which).start()

            return gather.stages(column, scatter.early) + scatter.stages()

        def started():
            for job in jobs[:1]:
                job.begin(place)
            begin(jobs[1:], place, 0.0, 0.75)
            finish(pending, place)
            hidden_weights.start()
            hidden_weights.wait()

        keep = [
            pltpu.make_async_copy(source, target, kept_sems.at[i])
            for i, (source, target) in enumerate(zip((n2_all, gate_out, up_out, hm_out), kept_out))
        ]

        def later():
            for copy in keep:
                copy.start()
            begin(jobs[1:], place, 0.75, 1.0)
            middle(jobs, place)

        run_together(
            columns(0),
            columns(1),
            {(B, 0): started, (A, 6): lambda: jobs[0].relay(place), (B, 8): later},
        )
        for chunk, (gather, scatter) in enumerate(pairs):
            span = slice(chunk * rows, (chunk + 1) * rows)
            act_out[span] = (values[span] + scatter.result()).astype(BF)
        for gather, scatter in pairs:
            gather.finish()
            scatter.finish()
        for copy in keep:
            copy.wait()
        finish(jobs, place)

    kept = jax.ShapeDtypeStruct((CHUNKS, 2, 4, n * rows, sz.hidden), BF)
    shapes = (
        jax.ShapeDtypeStruct((sz.rows, sz.width), BF),
        jax.ShapeDtypeStruct((CHUNKS, 2, 4, n, rows, sz.width), BF),
        kept,
        kept,
        kept,
    )
    scratch = [pltpu.VMEM((3, sz.width, sz.hidden), BF)]
    scratch += [pltpu.VMEM(shape.shape, BF) for shape in shapes[1:]]
    scratch += [DMA((2, 3)), DMA((4,))] + halves_scratch(n, rows, sz.width)
    outs = [(shape, hbm() if i else vmem()) for i, shape in enumerate(shapes)]
    return Part(body, [(gain, vmem()), (gate, hbm())], outs, scratch)


def both(sz, dy, gain, gate):
    n, rows = sz.ctx, sz.rows

    def body(ins, outs, scratch, jobs, place, pending):
        dy, h1, gain, *sources = ins
        act_out, dh1_out, dw_out, gain_grad = outs
        w, n2_all, dy_all, gate_all, up_all, hm_all, w_sems, *refs = scratch
        x, y, k, z = place
        hidden_weights = HiddenWeights(sz, place, sources, w, w_sems)
        count = len(refs) // 2
        (gather_f, scatter_f), (gather_b, scatter_b) = [
            (Gather(n, rows, buffer, place, own[:12]), Scatter(n, rows, place, own[12:]))
            for buffer, own in ((n2_all, refs[:count]), (dy_all, refs[count:]))
        ]
        values = h1[...]
        inverse = row_norm(values)
        n2_all[k, 2 * x + y, z] = (values * inverse * gain[...]).astype(BF)
        dy_all[k, 2 * x + y, z] = dy[...]

        waiting = []

        def down_product(core, which):
            group = gather_f.groups[which]
            partial = mm(hm_all[core, group], w[2], NT)
            scatter_f.parts[core, group] = partial.astype(BF).reshape(n, rows, sz.width)
            if core is not k:
                scatter_f.core(which).start()

        def down_here():
            nonlocal waiting
            finish(jobs, place)
            hidden_weights.start((2,))
            hidden_weights.wait((2,))
            for core, which in waiting:
                down_product(core, which)
            waiting = None

        def forward(core, which):
            group = gather_f.groups[which]
            normed = n2_all[core, group].reshape(n * rows, sz.width)
            gate = mm(normed, w[0])
            up = mm(normed, w[1])
            hidden = (gate * jax.nn.sigmoid(gate) * up).astype(BF)
            gate_all[core, group] = gate.astype(BF)
            up_all[core, group] = up.astype(BF)
            hm_all[core, group] = hidden
            if waiting is None:
                down_product(core, which)
            else:
                waiting.append((core, which))

        def backward(core, which):
            group = gather_b.groups[which]
            dhidden = mm(dy_all[core, group].reshape(n * rows, sz.width), w[2])
            gate = gate_all[core, group].astype(F32)
            up = up_all[core, group].astype(F32)
            sigmoid = jax.nn.sigmoid(gate)
            dgate = (dhidden * up * sigmoid * (1.0 + gate * (1.0 - sigmoid))).astype(BF)
            dup = (dhidden * gate * sigmoid).astype(BF)
            gate_all[core, group] = dgate
            up_all[core, group] = dup
            partial = mm(dgate, w[0], NT) + mm(dup, w[1], NT)
            scatter_b.parts[core, group] = partial.astype(BF).reshape(n, rows, sz.width)
            if core is not k:
                scatter_b.core(which).start()

        def weight_grad(slot, left, right):
            total = 8 * n * rows
            tile = 256 if sz.width % 256 == 0 else 128
            grads = right[...].reshape(total, sz.hidden)

            @pl.loop(0, sz.width // tile)
            def _(step):
                cols = pl.ds(pl.multiple_of(step * tile, tile), tile)
                side = left[:, :, :, :, cols].reshape(total, tile)
                dw_out[slot, cols] = mm(side, grads, TN).astype(BF)

        def result():
            act_out[...] = (h1[...] + scatter_f.result()).astype(BF)

        def started():
            finish(pending, place)
            hidden_weights.start((0, 1))
            hidden_weights.wait((0, 1))

        run_together(
            gather_f.stages(forward, scatter_f.early) + scatter_f.stages(),
            gather_b.stages(backward, scatter_b.early) + scatter_b.stages(),
            {
                (A, 0): lambda: begin(jobs, place),
                (B, 0): started,
                (A, 5): down_here,
                (B, 8): lambda: weight_grad(2, dy_all, hm_all),
                (B, 9): lambda: weight_grad(0, n2_all, gate_all),
                (B, 10): lambda: weight_grad(1, n2_all, up_all),
            },
        )
        result()
        dn2 = scatter_b.result()
        values = h1[...]
        inverse = row_norm(values)
        weighted = dn2 * gain[...]
        inner = jnp.mean(weighted * values, axis=-1, keepdims=True)
        dh1_out[...] = (
            dy[...].astype(F32) + inverse * weighted - values * (inverse * inverse * inverse) * inner
        )
        gain_grad[...] = jnp.sum(dn2 * values * inverse, axis=0, keepdims=True)
        for job in (gather_f, scatter_f, gather_b, scatter_b):
            job.finish()

    shapes = (
        jax.ShapeDtypeStruct((sz.rows, sz.width), BF),
        jax.ShapeDtypeStruct((sz.rows, sz.width), F32),
        jax.ShapeDtypeStruct((3, sz.width, sz.hidden), BF),
        jax.ShapeDtypeStruct((1, sz.width), F32),
    )
    gathered = pltpu.VMEM((2, 4, n, rows, sz.width), BF)
    inner = pltpu.VMEM((2, 4, n * rows, sz.hidden), BF)
    scratch = [
        pltpu.VMEM((3, sz.width, sz.hidden), BF),
        gathered,
        gathered,
        inner,
        inner,
        inner,
        DMA((2, 3)),
    ] + (Gather.scratch(n) + Scatter.scratch(n, rows, sz.width)) * 2
    ins = [(dy, vmem()), (gain, vmem()), (gate, hbm())]
    return Part(body, ins, [(shape, vmem()) for shape in shapes], scratch)


def feed_back(sz, h1, gain, weights, kept):
    n = sz.ctx
    rows = sz.rows // CHUNKS

    def body(ins, outs, scratch, jobs, place, pending):
        dy, h1, gain, *sources = ins[:6]
        dh1_out, dw_out, gain_grad = outs
        w, dy_all, dgate_all, dup_all, *scratch = scratch
        n2_all, gate_in, up_in, hm_in, w_sems, kept_sems, *refs = scratch
        kept = [
            pltpu.make_async_copy(source, target, kept_sems.at[i])
            for i, (source, target) in enumerate(zip(ins[6:], (n2_all, gate_in, up_in, hm_in)))
        ]
        x, y, k, z = place
        hidden_weights = HiddenWeights(sz, place, sources, w, w_sems)
        hidden_weights.start()
        for copy in kept[1:] + kept[:1]:
            copy.start()
        pairs = halves(n, rows, dy_all, place, refs)
        for chunk in range(CHUNKS):
            dy_all[chunk, k, 2 * x + y, z] = dy[chunk * rows : (chunk + 1) * rows]
        line_jobs = [job for job in jobs if isinstance(job, LineShares)]
        heads = [job for job in jobs if isinstance(job, ReturnedHeads)]

        def columns(chunk):
            gather, scatter = pairs[chunk]

            def column(core, which):
                group = gather.groups[which]
                dhidden = mm(dy_all[chunk, core, group].reshape(n * rows, sz.width), w[2])
                gate = gate_in[chunk, core, group].astype(F32)
                up = up_in[chunk, core, group].astype(F32)
                sigmoid = jax.nn.sigmoid(gate)
                dgate = (dhidden * up * sigmoid * (1.0 + gate * (1.0 - sigmoid))).astype(BF)
                dup = (dhidden * gate * sigmoid).astype(BF)
                dgate_all[chunk, core, group] = dgate
                dup_all[chunk, core, group] = dup
                partial = mm(dgate, w[0], NT) + mm(dup, w[1], NT)
                scatter.parts[core, group] = partial.astype(BF).reshape(n, rows, sz.width)
                if core is not k:
                    scatter.core(which).start()

            return gather.stages(column, scatter.early) + scatter.stages()

        total = 8 * n * sz.rows
        tile = 256 if sz.width % 256 == 0 else 128

        def weight_grad(slot, left, right):
            grads = right[...].reshape(total, sz.hidden)

            @pl.loop(0, sz.width // tile)
            def _(step):
                cols = pl.ds(pl.multiple_of(step * tile, tile), tile)
                side = left[:, :, :, :, :, cols].reshape(total, tile)
                dw_out[slot, cols] = mm(side, grads, TN).astype(BF)

        def started():
            for job in heads:
                job.begin(place)
            pending[1].begin(place, range(2, n))
            pending[1].begin(place, (0,))
            for job in line_jobs:
                job.begin(place)
            hidden_weights.wait()
            kept[1].wait()
            kept[2].wait()
            for job in heads:
                job.middle(place)

        def down_grad():
            for job in heads:
                job.relay(place)
            kept[3].wait()
            kept[0].wait()
            weight_grad(2, dy_all, hm_in)

        def last():
            weight_grad(1, n2_all, dup_all)
            for job in heads:
                job.late(place)

        run_together(
            columns(0),
            columns(1),
            {
                (B, 0): started,
                (B, 8): down_grad,
                (B, 9): lambda: weight_grad(0, n2_all, dgate_all),
                (B, 10): last,
            },
        )
        dn2 = jnp.concatenate([scatter.result() for _, scatter in pairs], axis=0)
        values = h1[...]
        inverse = row_norm(values)
        weighted = dn2 * gain[...]
        inner = jnp.mean(weighted * values, axis=-1, keepdims=True)
        dh1_out[...] = (
            dy[...].astype(F32) + inverse * weighted - values * (inverse * inverse * inverse) * inner
        )
        gain_grad[...] = jnp.sum(dn2 * values * inverse, axis=0, keepdims=True)
        for gather, scatter in pairs:
            gather.finish()
            scatter.finish()
        finish(pending, place)
        finish(jobs, place)

    shapes = (
        jax.ShapeDtypeStruct((sz.rows, sz.width), F32),
        jax.ShapeDtypeStruct((3, sz.width, sz.hidden), BF),
        jax.ShapeDtypeStruct((1, sz.width), F32),
    )
    inner = pltpu.VMEM((CHUNKS, 2, 4, n * rows, sz.hidden), BF)
    scratch = [
        pltpu.VMEM((3, sz.width, sz.hidden), BF),
        pltpu.VMEM((CHUNKS, 2, 4, n, rows, sz.width), BF),
        inner,
        inner,
        pltpu.VMEM((CHUNKS, 2, 4, n, rows, sz.width), BF),
        inner,
        inner,
        inner,
        DMA((2, 3)),
        DMA((4,)),
    ] + halves_scratch(n, rows, sz.width)
    arrays = (h1, gain, *weights, *kept)
    specs = [vmem()] * 2 + [hbm()] * 7
    return Part(body, list(zip(arrays, specs)), [(shape, vmem()) for shape in shapes], scratch)


def finale(sz, part, small, results, shares, line_jobs, head_jobs):
    n = sz.ctx
    a, count = len(part.ins), len(part.scratch)
    order = [(1, 2), (1, 0), (1, 1), (0, 2), (0, 0), (0, 1)]
    query_columns = QUERY_HEADS * HEAD_WIDTH_SIZE
    key_columns = KEY_VALUE_HEADS * HEAD_WIDTH_SIZE

    def body(ins, outs, scratch, jobs):
        small_given, grad1, *shares = ins[a:]
        small_in, grad_out, w_out = outs
        made = scratch[count : count + 4]
        small, whole_bias, s_small, r_small, s_out, r_out, *sems = scratch[count + 4 :]
        dx, dw, gain_grad, bias_grad = made
        down_line, gate_line, up_line, *heads = jobs
        place = where_am_i()
        x, y, k, z = place
        me = x * sz.group + (y * 2 + k) * n + z
        for job in heads[1:]:
            job.source = dw
        sources = [shares[2], shares[0], shares[1], down_line.target, gate_line.target, up_line.target]
        moves = {
            where: PlaneShares(sz, *where, source, w_out, [sem.at[number] for sem in sems])
            for number, (where, source) in enumerate(zip(order, sources))
        }
        greet_all(me, sz.total, lambda index: flat_place(index, sz.group, n))

        placed = Placed(sz, None, None)
        placed.bind((dx, grad1), (grad_out,), (s_out, r_out))

        def sent():
            down_line.begin(place)
            heads[0].begin(place)

        def gathered():
            moves[1, 2].begin(place)

        def shared():
            gate_line.begin(place)
            up_line.begin(place)
            down_line.finish(place)
            moves[0, 2].begin(place)

        def returned():
            moves[0, 2].cross(place)
            moves[1, 2].cross(place)

        hooks = (sent, gathered, shared, returned)
        part.body(ins[:a], made, scratch[:count], jobs, place, hooks)
        for job in heads[1:]:
            job.begin(place)
        placed.begin(place)

        small[...] = small_given[...]
        whole_bias[...] = jnp.zeros_like(whole_bias)
        starts = (
            ((2 * x + y) * sz.qcols, sz.qcols),
            (query_columns + x * sz.kcols, sz.kcols),
            (query_columns + key_columns + x * sz.kcols, sz.kcols),
        )
        offset = 0
        for start, size in starts:
            whole_bias[:, pl.ds(pl.multiple_of(start, HB), size)] = bias_grad[:, offset : offset + size]
            offset += size
        wide = (query_columns + key_columns) // sz.group
        thin = key_columns // sz.group
        for row in range(sz.group):
            small[row, 0:1, : sz.owned] = gain_grad[:, row * sz.owned : (row + 1) * sz.owned]
            small[row, 2:3, :wide] = whole_bias[:, row * wide : (row + 1) * wide]
            base = query_columns + key_columns + row * thin
            small[row, 3:4, :thin] = whole_bias[:, base : base + thin]

        @pl.loop(1, sz.total)
        def _(step):
            device = lax.rem(me + step, sz.total)
            remote(
                small.at[device], small_in.at[me], s_small, r_small, flat_place(device, sz.group, n)
            ).start()

        pltpu.make_async_copy(small.at[me], small_in.at[me], s_small).start()
        for job in heads:
            job.middle(place)
        gate_line.finish(place)
        moves[0, 0].begin(place)
        moves[1, 0].begin(place)
        moves[0, 0].cross(place)
        up_line.finish(place)
        moves[0, 1].begin(place)
        moves[1, 1].begin(place)
        moves[1, 0].cross(place)
        heads[0].relay(place)
        moves[0, 1].cross(place)
        heads[1].relay(place)
        heads[0].late(place)
        moves[1, 1].cross(place)
        heads[2].relay(place)
        for job in heads[1:]:
            job.late(place)
        placed.finish(place)
        arrived(small_in.at[pl.ds(0, sz.total - 1)], r_small)
        arrived(small_in, s_small)
        for move in moves.values():
            move.finish(place)
        for job in heads:
            job.finish(place)

    shapes = (
        jax.ShapeDtypeStruct((sz.total, 8, LANES), F32),
        jax.ShapeDtypeStruct((2, sz.rows, sz.width), BF),
        jax.ShapeDtypeStruct((2, 3, sz.owned, sz.ff), BF),
    )
    many = len(order)
    scratch = (
        part.scratch
        + [pltpu.VMEM(shape.shape, shape.dtype) for shape, _ in part.outs]
        + [
            pltpu.VMEM((sz.total, 8, LANES), F32),
            pltpu.VMEM((1, query_columns + 2 * key_columns), F32),
            DMA,
            DMA,
            DMA((2,)),
            DMA((2,)),
            DMA((many, 2)),
            DMA((many, 5)),
            DMA((many, 2)),
            DMA((many,)),
            DMA((many,)),
        ]
    )
    ins = part.ins + [(small, vmem())] + [(array, hbm()) for array in (*results, *shares)]
    return run_call(
        body,
        ins,
        [(shape, hbm()) for shape in shapes],
        scratch,
        line_jobs + head_jobs,
        6,
        "layer_last",
    )


def local_columns(
    sz,
    tokens,
    positions,
    norm1_gain,
    qkv_bias,
    qkv_weight,
    out_weight,
    norm2_gain,
    gate_up_weight,
    down_weight,
    cotangent,
):
    n, group = sz.ctx, sz.group
    x, y, k, z = where_am_i()
    mine = 2 * x + y
    bias_owned = qkv_bias.shape[1]
    qkv_weight, out_weight = (qkv_weight[0], out_weight[0])
    gate_up_weight, down_weight = (gate_up_weight[0], down_weight[0])

    def line(values):
        return jnp.pad(values, ((0, 0), (0, LANES - values.shape[1])))

    small = jnp.concatenate(
        [line(norm1_gain), line(norm2_gain), line(qkv_bias), jnp.zeros((13, LANES), BF)], axis=0
    )
    (small_all, tok_own, cot_own, heads_x, cols_x), ((att0,), (gate0,)) = spread(
        sz, small, tokens, cotangent, qkv_weight, out_weight, gate_up_weight, down_weight
    )
    per_section = small_all.reshape(2, group, 16, LANES).astype(F32)
    gain1 = per_section[:, :, 0, : sz.owned].reshape(2, 1, sz.width)
    gain2 = per_section[:, :, 1, : sz.owned].reshape(2, 1, sz.width)
    bias = per_section[:, :, 2, :bias_owned].reshape(2, 1, group * bias_owned)
    query_columns = QUERY_HEADS * HEAD_WIDTH_SIZE
    key_columns = KEY_VALUE_HEADS * HEAD_WIDTH_SIZE
    kv = mine // (4 // KEY_VALUE_HEADS)
    starts = (
        (mine * sz.qcols, sz.qcols),
        (query_columns + kv * sz.kcols, sz.kcols),
        (query_columns + key_columns + kv * sz.kcols, sz.kcols),
    )
    own_bias = jnp.concatenate(
        [lax.dynamic_slice_in_dim(bias, start, size, 2) for start, size in starts], axis=2
    )
    ordered = lax.dynamic_index_in_dim(positions, k, 0, keepdims=False)
    ordered = ordered.reshape(4, n, sz.rows).transpose(1, 0, 2)
    own_pos = lax.dynamic_index_in_dim(ordered, z, 0, keepdims=False).reshape(4 * sz.rows)
    kpos = ordered.reshape(1, sz.seq)
    qpos = own_pos[:, None]
    cosine, sine = rope_tables(own_pos, HEAD_WIDTH_SIZE)
    half = HEAD_WIDTH_SIZE // 2
    sign = jnp.where(jnp.arange(HEAD_WIDTH_SIZE) < half, -1.0, 1.0)
    tables = (cosine[:, 0], sine[:, 0] * sign)

    def columns(section, part):
        return Columns(sz, section, part, gate_up_weight, down_weight, cols_x)

    def attention(section, x_own, watt):
        return attend(sz, x_own, gain1[section], own_bias[section], watt, tables, qpos, kpos)

    (mid0, *kept_att0), (act0, *kept_feed), ((up0,), (down0,)), ((att1,), (gate1,)) = joined(
        sz,
        attention(0, tok_own, att0),
        [columns(0, 1), columns(0, 2)],
        feed(sz, gain2[0], gate0),
        [Heads(sz, 1, qkv_weight, out_weight, heads_x), columns(1, 0)],
        lambda made, given, own, later: (made[0], *given, own[0].target, own[1].target),
        False,
        3,
        "layer_forward",
    )
    (_, *kept_att1), (act1, dh1, dw1, gain2_grad1), _, _ = joined(
        sz,
        attention(1, act0, att1),
        [columns(1, 1)],
        both(sz, cot_own, gain2[1], gate1),
        [columns(1, 2)],
        lambda made, given, own, later: (given[0], made[0], *given[1:], own[0].target, later[0].target),
        False,
        4,
        "layer_turn",
    )

    def attention_back(section, dh1, x_own, watt, kept, plan=None):
        return attend_back(sz, dh1, x_own, gain1[section], watt, tables, qpos, kpos, kept, plan)

    def shares_between(jobs, place):
        return (
            lambda: jobs[0].begin(place),
            lambda: jobs[2].begin(place),
            lambda: jobs[1].begin(place, (1,)),
            lambda: None,
        )

    def heads_linked(made, given, own, later):
        later[1].source = made[1]
        return (made[0], *given)

    (
        (grad1, da1, gain1_grad1, bias_grad1),
        (dh1, dw0, gain2_grad0),
        ((down_share1,), (gate_share1,), (act_out,)),
        ((up_share1,), (heads10,)),
    ) = joined(
        sz,
        attention_back(1, dh1, act0, att1, kept_att1, shares_between),
        [LineShares(sz, 2, dw1), LineShares(sz, 0, dw1), Placed(sz, act0, act1)],
        feed_back(sz, mid0, gain2[0], (gate0, up0, down0), kept_feed),
        [LineShares(sz, 1, dw1), ReturnedHeads(sz, 1, 0, None)],
        heads_linked,
        True,
        5,
        "layer_backward",
    )
    whole_bias = jnp.zeros((1, query_columns + 2 * key_columns), F32)
    offset = 0
    for start, size in starts:
        part = bias_grad1[:, offset : offset + size]
        whole_bias = lax.dynamic_update_slice(whole_bias, part, (0, start))
        offset += size
    split = query_columns + key_columns
    rows = [gain1_grad1, gain2_grad1, whole_bias[:, :split], whole_bias[:, split:]]
    rows = [line(row.reshape(group, -1))[:, None] for row in rows]
    small1 = jnp.concatenate(rows + [jnp.zeros((group, 4, LANES), F32)], axis=1)
    small0 = jnp.pad(line(gain2_grad0.reshape(group, -1))[:, None], ((0, 0), (1, 6), (0, 0)))
    came_heads = [[None, None], [heads10, None]]
    (small_in, grad_out, w_out), more = finale(
        sz,
        attention_back(0, dh1, tok_own, att0, kept_att0),
        jnp.concatenate([small0, small1], axis=0),
        (grad1,),
        (gate_share1, up_share1, down_share1),
        [LineShares(sz, part, dw0) for part in (2, 0, 1)],
        [ReturnedHeads(sz, 1, 1, da1), ReturnedHeads(sz, 0, 0, None), ReturnedHeads(sz, 0, 1, None)],
    )
    (came_heads[1][1],), (came_heads[0][0],), (came_heads[0][1],) = more[3:]
    small_sum = jnp.sum(small_in, axis=0)
    gate_up_grad = jnp.concatenate([w_out[0, 0], w_out[0, 1]], axis=1).astype(F32)[None]
    down_grad = w_out[0, 2].astype(F32)[None]
    by_y = [jnp.where(y == 0, parts[0], parts[1]) for parts in came_heads]
    att_sum = jnp.where(x == 0, by_y[0], by_y[1]).astype(F32)
    q_grad = att_sum[:, :, : sz.qcols].transpose(1, 0, 2).reshape(sz.owned, query_columns)
    kv_grad = jnp.sum(
        att_sum[:, :, sz.qcols : sz.acols].reshape(
            KEY_VALUE_HEADS, 4 // KEY_VALUE_HEADS, sz.owned, 2, sz.kcols
        ),
        axis=1,
    )
    kv_grad = kv_grad.transpose(1, 2, 0, 3).reshape(sz.owned, 2 * key_columns)
    qkv_grad = jnp.concatenate([q_grad, kv_grad], axis=1)[None]
    out_grad = att_sum[:, :, sz.acols :].transpose(1, 0, 2).reshape(1, sz.owned, query_columns)
    return (
        act_out[None],
        grad_out[None],
        small_sum[0:1, : sz.owned],
        small_sum[2:3, : (query_columns + key_columns) // group],
        small_sum[3:4, : key_columns // group],
        qkv_grad,
        out_grad,
        small_sum[1:2, : sz.owned],
        gate_up_grad,
        down_grad,
    )


def solution(mesh):
    placed = (
        P(None, ("head", "ctx"), None),
        P(),
        P("section", ("head", "ctx")),
        P("section", ("head", "ctx")),
        P("section", ("head", "ctx"), None),
        P("section", ("head", "ctx"), None),
        P("section", ("head", "ctx")),
        P("section", ("head", "ctx"), None),
        P("section", ("head", "ctx"), None),
        P(None, ("head", "ctx"), None),
    )
    returned = (
        P("section", None, ("head", "ctx"), None),
        P("section", None, ("head", "ctx"), None),
        P("section", ("head", "ctx")),
        P("section", ("head", "ctx")),
        P("section", ("head", "ctx")),
        P("section", ("head", "ctx"), None),
        P("section", ("head", "ctx"), None),
        P("section", ("head", "ctx")),
        P("section", ("head", "ctx"), None),
        P("section", ("head", "ctx"), None),
    )

    def program(*arrays):
        sizes = Sizes(mesh, arrays[0], arrays[4], arrays[7], arrays[8])
        body = functools.partial(local_columns, sizes) if sizes.fits() else local
        return jax.shard_map(
            body, mesh=mesh, in_specs=placed, out_specs=returned, check_vma=False
        )(*arrays)

    return program
```

```python
import functools
import math

import jax
import jax.numpy as jnp
from jax import lax
from jax.experimental import pallas as pl
from jax.experimental.pallas import tpu as pltpu
from jax.sharding import PartitionSpec as P

FF = 8960
QUERY_HEADS = 12
KEY_VALUE_HEADS = 2
HEAD_WIDTH_SIZE = 128


EPSILON = 1e-06
THETA = 1000000.0


def from_behind(value, axis, steps):
    count = lax.axis_size(axis)
    first, last = (max(0, -steps), min(count, count - steps))
    return lax.ppermute(value, axis, [(source, source + steps) for source in range(first, last)])


def rope_tables(position_ids, head_width):
    frequencies = THETA ** (-(jnp.arange(head_width // 2).astype(jnp.float32) * 2.0) / head_width)
    angles = position_ids.astype(jnp.float32)[..., None] * frequencies
    angles = jnp.concatenate([angles, angles], axis=-1)
    return (jnp.cos(angles)[..., None, :], jnp.sin(angles)[..., None, :])


def rotate(values, cosine_table, sine_table):
    half_width = values.shape[-1] // 2
    turned = jnp.concatenate([-values[..., half_width:], values[..., :half_width]], axis=-1)
    return values * cosine_table + turned * sine_table


def unrotate(grad_values, cosine_table, sine_table):
    half_width = grad_values.shape[-1] // 2
    scaled = grad_values * sine_table
    return grad_values * cosine_table + jnp.concatenate(
        [scaled[..., half_width:], -scaled[..., :half_width]], axis=-1
    )


def norm_rows(values, gain_row):
    inverse = lax.rsqrt(jnp.mean(values * values, axis=-1, keepdims=True) + EPSILON)
    return (values * inverse * gain_row, inverse)


def norm_back(values, inverse, gain_row, grad_values):
    weighted = grad_values * gain_row
    inner_mean = jnp.mean(weighted * values, axis=-1, keepdims=True)
    input_grad = inverse * weighted - values * inverse**3 * inner_mean
    gain_grad = jnp.sum((grad_values * values * inverse).reshape(-1, values.shape[-1]), axis=0)
    return (input_grad, gain_grad)


def pick(flag, first_tree, second_tree):
    return jax.tree.map(
        lambda left_side, right_side: jnp.where(flag, left_side, right_side),
        first_tree,
        second_tree,
    )


def masked_scores(queries, keys_now, query_pos, key_now):
    score_scale = 1.0 / math.sqrt(queries.shape[-1])
    allowed = (key_now[:, None, :] <= query_pos[:, :, None])[:, :, None, :]
    scores = (
        jnp.einsum("grhd,gkd->grhk", queries, keys_now, preferred_element_type=jnp.float32)
        * score_scale
    )
    return (jnp.where(allowed, scores, -1e30), allowed)


def attend_forward(queries, pair_group, query_pos, key_pos):
    head_width = queries.shape[-1]
    row_shape = queries.shape[:3]
    shard_piece = lax.all_gather(pair_group, "ctx", axis=1, tiled=True)
    running = jnp.full(row_shape, -1e30, jnp.float32)
    keys_now = shard_piece[:, :, 0, :head_width]
    values_now = shard_piece[:, :, 0, head_width:]
    scores, allowed = masked_scores(queries, keys_now, query_pos, key_pos)
    highest = jnp.maximum(running, jnp.max(scores, axis=-1))
    probs_now = jnp.where(allowed, jnp.exp(scores - highest[..., None]), 0.0)
    totals = jnp.sum(probs_now, axis=-1)
    accumulated = jnp.einsum(
        "grhk,gkd->grhd",
        probs_now.astype(jnp.bfloat16),
        values_now,
        preferred_element_type=jnp.float32,
    )
    running, totals, accumulated = (highest, totals, accumulated)
    return (accumulated / totals[..., None], running + jnp.log(totals))


def attend_backward(queries, pair_group, query_pos, key_pos, out_grads, lse_rows, delta_rows):
    head_width = queries.shape[-1]
    score_scale = 1.0 / math.sqrt(head_width)
    shard_piece = lax.all_gather(pair_group, "ctx", axis=1, tiled=True)
    keys_now = shard_piece[:, :, 0, :head_width]
    values_now = shard_piece[:, :, 0, head_width:]
    scores, allowed = masked_scores(queries, keys_now, query_pos, key_pos)
    probs_now = jnp.where(allowed, jnp.exp(scores - lse_rows[..., None]), 0.0)
    prob_grads = jnp.einsum(
        "grhd,gkd->grhk", out_grads, values_now, preferred_element_type=jnp.float32
    )
    score_grads = (probs_now * (prob_grads - delta_rows[..., None])).astype(jnp.bfloat16)
    query_grads = score_scale * jnp.einsum(
        "grhk,gkd->grhd", score_grads, keys_now, preferred_element_type=jnp.float32
    )
    key_part = score_scale * jnp.einsum(
        "grhk,grhd->gkd", score_grads, queries, preferred_element_type=jnp.float32
    )
    value_part = jnp.einsum(
        "grhk,grhd->gkd",
        probs_now.astype(jnp.bfloat16),
        out_grads,
        preferred_element_type=jnp.float32,
    )
    piece_term = jnp.concatenate([key_part, value_part], axis=-1)[:, :, None, :]
    return (query_grads, piece_term)


def layer_forward(inputs, own_pos, query_pos, key_pos, weights, heads_total):
    gain_one, bias_all, w_qkv, w_out, gain_two, w_gate_up, w_down = weights
    batch_length = inputs.shape[0]
    rows_total = inputs.shape[1]
    per_device = QUERY_HEADS // heads_total
    copy_count = heads_total // KEY_VALUE_HEADS
    query_columns = QUERY_HEADS * HEAD_WIDTH_SIZE
    key_columns = KEY_VALUE_HEADS * HEAD_WIDTH_SIZE
    residual = inputs.astype(jnp.float32)
    normed_one, inverse_one = norm_rows(residual, gain_one.astype(jnp.float32))
    normed_low = normed_one.astype(jnp.bfloat16)
    projected_rows = jnp.einsum(
        "grd,dc->grc", normed_low, w_qkv, preferred_element_type=jnp.float32
    ) + bias_all.astype(jnp.float32)
    cosine_table, sine_table = rope_tables(own_pos, HEAD_WIDTH_SIZE)
    queries = rotate(
        projected_rows[..., :query_columns].reshape(
            batch_length, rows_total, QUERY_HEADS, HEAD_WIDTH_SIZE
        ),
        cosine_table,
        sine_table,
    )
    key_row_block = rotate(
        projected_rows[..., query_columns : query_columns + key_columns].reshape(
            batch_length, rows_total, KEY_VALUE_HEADS, HEAD_WIDTH_SIZE
        ),
        cosine_table,
        sine_table,
    )
    value_row_block = projected_rows[..., query_columns + key_columns :].reshape(
        batch_length, rows_total, KEY_VALUE_HEADS, HEAD_WIDTH_SIZE
    )
    pair_rows = jnp.concatenate(
        [
            jnp.repeat(key_row_block, copy_count, axis=2),
            jnp.repeat(value_row_block, copy_count, axis=2),
        ],
        axis=-1,
    ).astype(jnp.bfloat16)
    query_send = queries.astype(jnp.bfloat16).reshape(
        batch_length, rows_total, heads_total, per_device * HEAD_WIDTH_SIZE
    )
    query_group, pair_group = (
        lax.all_to_all(query_send, "head", split_axis=2, concat_axis=1, tiled=True),
        lax.all_to_all(pair_rows, "head", split_axis=2, concat_axis=1, tiled=True),
    )
    group_rows = query_group.shape[1]
    query_group = query_group.reshape(batch_length, group_rows, per_device, HEAD_WIDTH_SIZE)
    attended, lse_rows = attend_forward(query_group, pair_group, query_pos, key_pos)
    out_send = attended.astype(jnp.bfloat16).reshape(
        batch_length, group_rows, 1, per_device * HEAD_WIDTH_SIZE
    )
    out_rows = lax.all_to_all(out_send, "head", split_axis=1, concat_axis=2, tiled=True).reshape(
        batch_length, rows_total, QUERY_HEADS * HEAD_WIDTH_SIZE
    )
    middle = residual + jnp.einsum(
        "grc,dc->grd", out_rows, w_out, preferred_element_type=jnp.float32
    )
    normed_two, inverse_two = norm_rows(middle, gain_two.astype(jnp.float32))
    normed_two_low = normed_two.astype(jnp.bfloat16)
    gate_up = jnp.einsum(
        "grd,dc->grc", normed_two_low, w_gate_up, preferred_element_type=jnp.float32
    )
    hidden_low = (jax.nn.silu(gate_up[..., :FF]) * gate_up[..., FF:]).astype(jnp.bfloat16)
    output = middle + jnp.einsum(
        "grf,df->grd", hidden_low, w_down, preferred_element_type=jnp.float32
    )
    kept_now = (
        residual,
        inverse_one,
        normed_low,
        query_group,
        pair_group,
        attended,
        lse_rows,
        out_rows,
        middle,
        inverse_two,
        normed_two_low,
        gate_up,
        hidden_low,
    )
    return (output, kept_now)


def layer_backward(out_grad, kept_now, own_pos, query_pos, key_pos, weights, heads_total):
    gain_one, bias_all, w_qkv, w_out, gain_two, w_gate_up, w_down = weights
    (
        residual,
        inverse_one,
        normed_low,
        query_group,
        pair_group,
        attended,
        lse_rows,
        out_rows,
        middle,
        inverse_two,
        normed_two_low,
        gate_up,
        hidden_low,
    ) = kept_now
    batch_length = out_grad.shape[0]
    rows_total = out_grad.shape[1]
    per_device = QUERY_HEADS // heads_total
    copy_count = heads_total // KEY_VALUE_HEADS
    branch_low = out_grad.astype(jnp.bfloat16)
    hidden_grad = jnp.einsum("grd,df->grf", branch_low, w_down, preferred_element_type=jnp.float32)
    gate_values = gate_up[..., :FF]
    up_values = gate_up[..., FF:]
    sigmoid_gate = jax.nn.sigmoid(gate_values)
    gate_grad = hidden_grad * up_values * sigmoid_gate * (1.0 + gate_values * (1.0 - sigmoid_gate))
    up_grad = hidden_grad * gate_values * sigmoid_gate
    gate_up_low = jnp.concatenate([gate_grad, up_grad], axis=-1).astype(jnp.bfloat16)
    normed_two_grad = jnp.einsum(
        "grc,dc->grd", gate_up_low, w_gate_up, preferred_element_type=jnp.float32
    )
    middle_part, gain_two_grad = norm_back(
        middle, inverse_two, gain_two.astype(jnp.float32), normed_two_grad
    )
    middle_grad = out_grad + middle_part
    middle_low = middle_grad.astype(jnp.bfloat16)
    out_grad_rows = jnp.einsum(
        "grd,dc->grc", middle_low, w_out, preferred_element_type=jnp.float32
    ).astype(jnp.bfloat16)
    out_grad_rows = out_grad_rows.reshape(
        batch_length, rows_total, heads_total, per_device * HEAD_WIDTH_SIZE
    )
    out_grad_group = lax.all_to_all(out_grad_rows, "head", split_axis=2, concat_axis=1, tiled=True)
    group_rows = out_grad_group.shape[1]
    out_grad_group = out_grad_group.reshape(batch_length, group_rows, per_device, HEAD_WIDTH_SIZE)
    delta_rows = jnp.sum(out_grad_group.astype(jnp.float32) * attended, axis=-1)
    query_grads, key_grads = attend_backward(
        query_group, pair_group, query_pos, key_pos, out_grad_group, lse_rows, delta_rows
    )
    pair_own = lax.psum_scatter(
        key_grads.astype(jnp.bfloat16), "ctx", scatter_dimension=1, tiled=True
    )
    query_send = query_grads.astype(jnp.bfloat16).reshape(
        batch_length, group_rows, 1, per_device * HEAD_WIDTH_SIZE
    )
    query_back, paired_backward = (
        lax.all_to_all(query_send, "head", split_axis=1, concat_axis=2, tiled=True),
        lax.all_to_all(pair_own, "head", split_axis=1, concat_axis=2, tiled=True),
    )
    query_rows = query_back.astype(jnp.float32).reshape(
        batch_length, rows_total, QUERY_HEADS, HEAD_WIDTH_SIZE
    )
    paired_sum = jnp.sum(
        paired_backward.astype(jnp.float32).reshape(
            batch_length, rows_total, KEY_VALUE_HEADS, copy_count, 2 * HEAD_WIDTH_SIZE
        ),
        axis=3,
    )
    cosine_table, sine_table = rope_tables(own_pos, HEAD_WIDTH_SIZE)
    query_pre = unrotate(query_rows, cosine_table, sine_table).reshape(
        batch_length, rows_total, QUERY_HEADS * HEAD_WIDTH_SIZE
    )
    key_pre = unrotate(paired_sum[..., :HEAD_WIDTH_SIZE], cosine_table, sine_table).reshape(
        batch_length, rows_total, KEY_VALUE_HEADS * HEAD_WIDTH_SIZE
    )
    value_before_rotation = paired_sum[..., HEAD_WIDTH_SIZE:].reshape(
        batch_length, rows_total, KEY_VALUE_HEADS * HEAD_WIDTH_SIZE
    )
    projected_low = jnp.concatenate([query_pre, key_pre, value_before_rotation], axis=-1).astype(
        jnp.bfloat16
    )
    bias_grad = jnp.sum(
        projected_low.astype(jnp.float32).reshape(-1, projected_low.shape[-1]), axis=0
    )
    normed_grad = jnp.einsum(
        "grc,dc->grd", projected_low, w_qkv, preferred_element_type=jnp.float32
    )
    input_part, gain_one_grad = norm_back(
        residual, inverse_one, gain_one.astype(jnp.float32), normed_grad
    )
    input_grad = middle_grad + input_part
    pieces = (
        normed_low,
        projected_low,
        middle_low,
        out_rows,
        normed_two_low,
        gate_up_low,
        branch_low,
        hidden_low,
    )
    return (input_grad, pieces, (gain_one_grad, bias_grad, gain_two_grad))


def reduce_block(left_side, columns):
    block_term = jnp.einsum("rd,rc->dc", left_side, columns, preferred_element_type=jnp.float32)
    return lax.psum_scatter(block_term, ("head", "ctx"), scatter_dimension=0, tiled=True)


def local(
    tokens,
    positions,
    norm1_gain,
    qkv_bias,
    qkv_weight,
    out_weight,
    norm2_gain,
    gate_up_weight,
    down_weight,
    cotangent,
):
    heads_total = lax.axis_size("head")
    rank_count = lax.axis_size("ctx")
    batch_count = tokens.shape[0]
    rows_total = tokens.shape[1]
    seq_total = positions.shape[1]
    group_rows = heads_total * rows_total
    section_index = lax.axis_index("section")
    rank_index = lax.axis_index("ctx")
    block_index = lax.axis_index("head") * rank_count + rank_index
    ordered = (
        positions.reshape(batch_count, heads_total, rank_count, rows_total)
        .transpose(0, 2, 1, 3)
        .reshape(batch_count, seq_total)
    )
    group_count = batch_count // batch_count
    tick_count = group_count + 1

    def positions_for(group_index):
        first_row = group_index * batch_count
        own_pos = lax.dynamic_slice(
            positions, (first_row, block_index * rows_total), (batch_count, rows_total)
        )
        query_pos = lax.dynamic_slice_in_dim(ordered, rank_index * group_rows, group_rows, 1)
        return (own_pos, query_pos, ordered)

    shards = (norm1_gain, qkv_bias, qkv_weight, out_weight, norm2_gain, gate_up_weight, down_weight)
    weights = tuple(
        (
            shard_value[0]
            for shard_value in (
                lax.all_gather(shards[0], ("head", "ctx"), axis=1, tiled=True),
                lax.all_gather(shards[1], ("head", "ctx"), axis=1, tiled=True),
                lax.all_gather(shards[2], ("head", "ctx"), axis=1, tiled=True),
                lax.all_gather(shards[3], ("head", "ctx"), axis=1, tiled=True),
                lax.all_gather(shards[4], ("head", "ctx"), axis=1, tiled=True),
                lax.all_gather(shards[5], ("head", "ctx"), axis=1, tiled=True),
                lax.all_gather(shards[6], ("head", "ctx"), axis=1, tiled=True),
            )
        )
    )
    received = jnp.zeros((batch_count, rows_total, tokens.shape[2]), jnp.bfloat16)
    outputs = []
    kept_list = []
    for tick_now in range(tick_count):
        first_row = min(tick_now, group_count - 1) * batch_count
        inputs = jnp.where(section_index == 0, tokens, received)
        own_pos, query_pos, key_pos = positions_for(
            jnp.clip(tick_now - section_index, 0, group_count - 1)
        )
        result, kept_now = layer_forward(inputs, own_pos, query_pos, key_pos, weights, heads_total)
        result_low = result.astype(jnp.bfloat16)
        outputs.append(result_low)
        kept_list.append(kept_now)
        if tick_now + 1 < tick_count:
            received = from_behind(result_low, "section", 1)
    received = jnp.zeros((batch_count, rows_total, tokens.shape[2]), jnp.bfloat16)
    grads_in = []
    piece_list = []
    small_sums = None
    for tick_now in range(tick_count):
        first_row = min(tick_now, group_count - 1) * batch_count
        incoming = jnp.where(section_index == 1, cotangent, received).astype(jnp.float32)
        kept_now = pick(
            section_index == 0,
            kept_list[max(tick_now - 1, 0)],
            kept_list[min(tick_now + 1, tick_count - 1)],
        )
        group_number = tick_now - 1 + section_index
        own_pos, query_pos, key_pos = positions_for(jnp.clip(group_number, 0, group_count - 1))
        input_grad, pieces, smalls = layer_backward(
            incoming, kept_now, own_pos, query_pos, key_pos, weights, heads_total
        )
        valid_flag = jnp.logical_and(group_number >= 0, group_number < group_count)
        smalls = tuple((jnp.where(valid_flag, entry_value, 0.0) for entry_value in smalls))
        if small_sums is None:
            small_sums = smalls
        else:
            small_sums = tuple(
                (left_side + right_side for left_side, right_side in zip(small_sums, smalls))
            )
        grad_low = input_grad.astype(jnp.bfloat16)
        grads_in.append(grad_low)
        piece_list.append(pieces)
        if tick_now + 1 < tick_count:
            received = from_behind(grad_low, "section", -1)
    activations = jnp.where(section_index == 0, outputs[0], outputs[1])[None]
    input_grads = jnp.where(section_index == 0, grads_in[1], grads_in[0])[None]
    chosen = [pick(section_index == 0, piece_list[1], piece_list[0])]
    merged = tuple(
        (
            jnp.concatenate([chosen_set[slot_number] for chosen_set in chosen], axis=0).reshape(
                batch_count * rows_total, -1
            )
            for slot_number in range(8)
        )
    )
    (
        normed_all,
        projected_all,
        middle_all,
        attn_all,
        normed_two_all,
        gate_up_all,
        branch_all,
        hidden_all,
    ) = merged
    pair_list = (
        (normed_all, projected_all),
        (middle_all, attn_all),
        (normed_two_all, gate_up_all),
        (branch_all, hidden_all),
    )
    share_list = []
    for left_side, right_side in pair_list:
        width_total = right_side.shape[1]
        piece_count = width_total // 4480 if width_total % 4480 == 0 else 1
        piece_width = width_total // piece_count
        piece_shares = []
        for piece_number in range(piece_count):
            columns = right_side[:, piece_number * piece_width : (piece_number + 1) * piece_width]
            piece_shares.append(reduce_block(left_side, columns))
        share_list.append(jnp.concatenate(piece_shares, axis=1)[None])
    qkv_weight_grad, out_weight_grad, gate_up_grad, down_grad = share_list
    split_width = (QUERY_HEADS + KEY_VALUE_HEADS) * HEAD_WIDTH_SIZE
    bias_sum = small_sums[1]
    gain_one_share, query_key_share, value_share, gain_two_share = (
        lax.psum_scatter(small_sums[0][None], ("head", "ctx"), scatter_dimension=1, tiled=True),
        lax.psum_scatter(
            bias_sum[None, :split_width], ("head", "ctx"), scatter_dimension=1, tiled=True
        ),
        lax.psum_scatter(
            bias_sum[None, split_width:], ("head", "ctx"), scatter_dimension=1, tiled=True
        ),
        lax.psum_scatter(small_sums[2][None], ("head", "ctx"), scatter_dimension=1, tiled=True),
    )
    return (
        activations,
        input_grads,
        gain_one_share,
        query_key_share,
        value_share,
        qkv_weight_grad,
        out_weight_grad,
        gain_two_share,
        gate_up_grad,
        down_grad,
    )


MESH_ID = pl.DeviceIdType.MESH
BF = jnp.bfloat16
F32 = jnp.float32
LANES = 128
HB = 128
VMEM_LIMIT = 60 * 1024 * 1024
DMA = pltpu.SemaphoreType.DMA
NT = (((1,), (1,)), ((), ()))
TN = (((0,), (0,)), ((), ()))
NN = (((1,), (0,)), ((), ()))


def mm(left_side, right_side, form=NN):
    return lax.dot_general(left_side, right_side, form, preferred_element_type=F32)


def where_am_i():
    head = lax.axis_index("head")
    return (lax.axis_index("section"), head // 2, lax.rem(head, 2), lax.axis_index("ctx"))


def at(x, y, k, z):
    return (x, y * 2 + k, z)


def remote(source, target, send_sem, recv_sem, device):
    return pltpu.make_async_remote_copy(
        src_ref=source,
        dst_ref=target,
        send_sem=send_sem,
        recv_sem=recv_sem,
        device_id=device,
        device_id_type=MESH_ID,
    )


def arrived(ref, sem):
    pltpu.make_async_copy(ref, ref, sem).wait()


def greet(devices):
    barrier = pltpu.get_barrier_semaphore()
    for device in devices:
        pl.semaphore_signal(barrier, inc=1, device_id=device, device_id_type=MESH_ID)
    pl.semaphore_wait(barrier, len(devices))


def greet_all(index, total, device_of):
    barrier = pltpu.get_barrier_semaphore()

    @pl.loop(1, total)
    def _(step):
        device = device_of(lax.rem(index + step, total))
        pl.semaphore_signal(barrier, inc=1, device_id=device, device_id_type=MESH_ID)

    pl.semaphore_wait(barrier, total - 1)


def params(collective_id):
    return pltpu.CompilerParams(
        collective_id=collective_id, has_side_effects=True, vmem_limit_bytes=VMEM_LIMIT
    )


def vmem():
    return pl.BlockSpec(memory_space=pltpu.VMEM)


def hbm():
    return pl.BlockSpec(memory_space=pl.ANY)


def row_norm(values):
    return lax.rsqrt(jnp.mean(values * values, axis=-1, keepdims=True) + EPSILON)


class Sizes:
    def __init__(self, mesh, tokens, qkv_weight, gate_up, down):
        self.ctx = mesh.shape["ctx"]
        self.group = 4 * self.ctx
        self.total = 2 * self.group
        self.batches, self.seq, self.width = tokens.shape
        self.rows = self.seq // self.group
        self.ff = down.shape[2]
        self.owned = self.width // self.group
        self.blocks = self.ff // HB
        self.plane = self.blocks // 2
        self.most = -(-self.plane // self.group)
        self.least = self.plane // self.group
        self.extra = self.plane % self.group
        self.hidden = self.most * HB
        self.per_group = QUERY_HEADS // 4
        self.qcols = self.per_group * HEAD_WIDTH_SIZE
        self.kcols = HEAD_WIDTH_SIZE
        self.acols = self.qcols + 2 * self.kcols
        self.atot = self.acols + self.qcols

    def fits(self):
        gathered = self.batches * self.seq * self.width * 2
        return (
            self.batches == 2
            and gathered * 3 < VMEM_LIMIT // 2
            and self.ff % (2 * HB) == 0
            and self.ctx % 2 == 0
            and self.least >= 1
            and self.owned % 16 == 0
            and self.rows % 32 == 0
        )


def flat_place(index, group, ctx):
    inside = lax.rem(index, group)
    return (index // group, inside // ctx, lax.rem(inside, ctx))


def block_rank(sz, inside):
    head, z = (inside // sz.ctx, lax.rem(inside, sz.ctx))
    y, k = (head // 2, lax.rem(head, 2))
    turn = jnp.where(z < sz.ctx // 2, 2 * z, 2 * (sz.ctx - 1 - z) + 1)
    return turn + sz.ctx * (2 * k + lax.rem(y + z, 2))


def first_column(sz, owner):
    rank = block_rank(sz, lax.rem(owner, sz.group))
    plane = owner // sz.group * sz.plane
    return pl.multiple_of((plane + rank * sz.least + jnp.minimum(rank, sz.extra)) * HB, HB)


def has_more(sz, owner):
    return block_rank(sz, lax.rem(owner, sz.group)) < sz.extra


def extras_of_head(sz, head):
    count = 0
    for z in range(sz.ctx):
        turn = 2 * z if z < sz.ctx // 2 else 2 * (sz.ctx - 1 - z) + 1
        count += turn + sz.ctx * (2 * (head % 2) + (head // 2 + z) % 2) < sz.extra
    return count


def half_turn(values):
    return pltpu.roll(values, HEAD_WIDTH_SIZE // 2, 1)


def pair_peers(x, y, k, z):
    return (at(1 - x, y, k, z), at(x, 1 - y, k, z), at(1 - x, 1 - y, k, z))


def pair_groups(x, y):
    return (2 * (1 - x) + y, 2 * x + 1 - y, 2 * (1 - x) + 1 - y)


def line_peers(n, x, y, k, z):
    return [at(x, y, k, lax.rem(z + step, n)) for step in range(1, n)]


def tree_peers(n, x, y, k, z):
    return [at(1 - x, y, k, z), at(x, 1 - y, k, z), at(x, y, 1 - k, z)] + line_peers(n, x, y, k, z)


def meet(sz, place, near, across, jobs):
    x, y, k, z = place
    n = sz.ctx
    inside = (y * 2 + k) * n + z
    reach = max([job.reach for job in jobs], default=0)
    if reach == 2:
        greet_all(x * sz.group + inside, sz.total, lambda index: flat_place(index, sz.group, n))
    elif reach == 1:
        barrier = pltpu.get_barrier_semaphore()
        for device in across:
            pl.semaphore_signal(barrier, inc=1, device_id=device, device_id_type=MESH_ID)

        @pl.loop(1, sz.group)
        def _(step):
            device = flat_place(x * sz.group + lax.rem(inside + step, sz.group), sz.group, n)
            pl.semaphore_signal(barrier, inc=1, device_id=device, device_id_type=MESH_ID)

        pl.semaphore_wait(barrier, sz.group - 1 + len(across))
    else:
        greet(near)


def run_call(body, ins, outs, scratch, jobs, collective_id, name):
    fg_in, fg_out, fg_scratch = len(ins), len(outs), len(scratch)
    ins, outs, scratch = list(ins), list(outs), list(scratch)
    for job in jobs:
        ins += [(array, hbm() if spec is None else spec) for array, spec in job.ins]
        outs += [(shape, hbm()) for shape in job.outs]
        scratch += job.scratch

    def kernel(*refs):
        given, made, own = (
            refs[: len(ins)],
            refs[len(ins) : len(ins) + len(outs)],
            refs[len(ins) + len(outs) :],
        )
        a, b, c = fg_in, fg_out, fg_scratch
        for job in jobs:
            job.bind(
                given[a : a + len(job.ins)],
                made[b : b + len(job.outs)],
                own[c : c + len(job.scratch)],
            )
            a, b, c = a + len(job.ins), b + len(job.outs), c + len(job.scratch)
        body(given[:fg_in], made[:fg_out], own[:fg_scratch], jobs)

    results = pl.pallas_call(
        kernel,
        out_shape=tuple(shape for shape, _ in outs),
        in_specs=[spec for _, spec in ins],
        out_specs=tuple(spec for _, spec in outs),
        scratch_shapes=scratch,
        compiler_params=params(collective_id),
        name=name,
    )(*[array for array, _ in ins])
    at_out, extra = fg_out, []
    for job in jobs:
        extra.append(results[at_out : at_out + len(job.outs)])
        at_out += len(job.outs)
    return (results[:fg_out], extra)


def plane_order(n, place, index):
    x, y, k, z = place
    head = y * 2 + k
    far = 4 * (n - 1)
    if isinstance(index, int) and index == 4 * n - 1:
        return head * n + z
    rest = index - far
    head_to = lax.rem(head + jnp.where(index < far, index // (n - 1), rest + 1), 4)
    ctx_to = lax.rem(z + jnp.where(index < far, 1 + lax.rem(index, n - 1), 0), n)
    return head_to * n + ctx_to


def span_of(count, low, high):
    return (int(count * low), int(count * high))


class Columns:
    reach = 1

    def __init__(self, sz, section, part, gate_up, down, staged):
        self.sz, self.section, self.part = sz, section, part
        self.ins = [(down if part == 2 else gate_up, None), (staged, None)]
        self.outs = [jax.ShapeDtypeStruct((sz.width, sz.hidden), BF)]
        self.scratch = [DMA((2,)), DMA((2,))]

    def bind(self, ins, outs, scratch):
        self.source, self.staged = ins
        self.target = outs[0]
        self.send, self.recv = scratch

    def begin(self, place, low=0.0, high=1.0):
        sz = self.sz
        n = sz.ctx
        x, y, k, z = place
        inside = (y * 2 + k) * n + z
        me = x * sz.group + inside
        first, stop = span_of(sz.group, low, high)
        rows = pl.ds(pl.multiple_of(inside * sz.owned, 16), sz.owned)
        wide = sz.least * HB
        base = sz.ff if self.part == 1 else 0

        def pair(owner, offset, width, own):
            target = self.target.at[rows, pl.ds(offset, width)]
            if own:
                first = pl.multiple_of(base + first_column(sz, owner) + offset, HB)
                return (self.source.at[:, pl.ds(first, width)], target)
            first = first_column(sz, owner) - x * sz.plane * HB + offset
            first = pl.multiple_of(first, HB)
            return (self.staged.at[self.part, :, pl.ds(first, width)], target)

        for own in (True, False):

            @pl.when((x == self.section) == own)
            def _():
                @pl.loop(first, min(stop, sz.group - 1))
                def _(step):
                    owner = x * sz.group + plane_order(n, place, step)
                    device = flat_place(owner, sz.group, n)
                    source, target = pair(owner, 0, wide, own)
                    remote(source, target, self.send.at[0], self.recv.at[0], device).start()
                    if sz.extra:

                        @pl.when(has_more(sz, owner))
                        def _():
                            source, target = pair(owner, wide, HB, own)
                            remote(source, target, self.send.at[1], self.recv.at[1], device).start()

                if stop < sz.group:
                    return
                source, target = pair(me, 0, wide, own)
                pltpu.make_async_copy(source, target, self.send.at[0]).start()
                if sz.extra:

                    @pl.when(has_more(sz, me))
                    def _():
                        source, target = pair(me, wide, HB, own)
                        pltpu.make_async_copy(source, target, self.send.at[1]).start()

    def middle(self, place):
        pass

    def finish(self, place):
        sz = self.sz
        x, y, k, z = place
        me = x * sz.group + (y * 2 + k) * sz.ctx + z
        wide = sz.least * HB
        arrived(self.target.at[pl.ds(0, sz.width - sz.owned), pl.ds(0, wide)], self.recv.at[0])
        arrived(self.target.at[:, pl.ds(0, wide)], self.send.at[0])
        if sz.extra:
            arrived(self.target.at[pl.ds(0, sz.extra * sz.owned), pl.ds(0, HB)], self.send.at[1])

            @pl.when(has_more(sz, me))
            def _():
                arrived(
                    self.target.at[pl.ds(0, sz.width - sz.owned), pl.ds(0, HB)], self.recv.at[1]
                )


def head_columns(sz, g, qkv, out_w):
    kv = g // (4 // KEY_VALUE_HEADS)
    q0 = pl.multiple_of(g * sz.qcols, HB)
    k0 = pl.multiple_of(QUERY_HEADS * HEAD_WIDTH_SIZE + kv * sz.kcols, HB)
    v0 = pl.multiple_of((QUERY_HEADS + KEY_VALUE_HEADS) * HEAD_WIDTH_SIZE + kv * sz.kcols, HB)
    return (
        (qkv.at[:, pl.ds(q0, sz.qcols)], pl.ds(0, sz.qcols)),
        (qkv.at[:, pl.ds(k0, sz.kcols)], pl.ds(sz.qcols, sz.kcols)),
        (qkv.at[:, pl.ds(v0, sz.kcols)], pl.ds(sz.qcols + sz.kcols, sz.kcols)),
        (out_w.at[:, pl.ds(q0, sz.qcols)], pl.ds(sz.acols, sz.qcols)),
    )


RELAYED = 4


def ends(n, z, ctx):
    if n != RELAYED:
        return z < 0
    return jnp.abs(z - ctx) == n - 1


def relay_of(n, z, ctx):
    if n != RELAYED:
        return z < 0
    return jnp.logical_or(
        jnp.logical_and(z == 0, ctx == n - 2), jnp.logical_and(z == n - 1, ctx == 1)
    )


def inner(n, z):
    return jnp.logical_and(z > 0, z < n - 1)


class Heads:
    reach = 1

    def __init__(self, sz, section, qkv, out_w, staged):
        self.sz, self.section = sz, section
        self.ins = [(qkv, None), (out_w, None), (staged, None)]
        self.outs = [jax.ShapeDtypeStruct((sz.width, sz.atot), BF)]
        self.scratch = [DMA, DMA((2,)), DMA((2,)), DMA((2,)), DMA]

    def bind(self, ins, outs, scratch):
        self.qkv, self.out_w, self.staged = ins
        self.target = outs[0]
        self.send, self.recv, self.s_core, self.r_core, self.s_relay = scratch

    def begin(self, place, low=0.0, high=1.0):
        sz = self.sz
        n = sz.ctx
        x, y, k, z = place
        rows = pl.ds(pl.multiple_of(((y * 2 + k) * n + z) * sz.owned, 16), sz.owned)
        mine = y * n + z

        def pairs(y_to, own):
            if own:
                return [
                    (source, self.target.at[rows, cols])
                    for source, cols in head_columns(sz, 2 * x + y_to, self.qkv, self.out_w)
                ]
            return [(self.staged.at[y_to], self.target.at[rows])]

        for own in (True, False):

            @pl.when((x == self.section) == own)
            def _():
                @pl.loop(1, 2 * n)
                def _(step):
                    index = lax.rem(mine + step, 2 * n)
                    ctx = lax.rem(index, n)

                    @pl.when(jnp.logical_not(ends(n, z, ctx)))
                    def _():
                        recv = self.recv.at[jnp.where(relay_of(n, z, ctx), 1, 0)]
                        for source, target in pairs(index // n, own):
                            device = at(x, index // n, k, ctx)
                            remote(source, target, self.send, recv, device).start()

                for source, target in pairs(y, own):
                    pltpu.make_async_copy(source, target, self.send).start()

    def span(self, part, k):
        stretch = self.sz.width // 4
        return self.target.at[pl.ds(pl.multiple_of((part * 2 + k) * stretch, 16), stretch)]

    def relay(self, place):
        sz = self.sz
        n = sz.ctx
        x, y, k, z = place
        if n != RELAYED:
            return

        @pl.when(inner(n, z))
        def _():
            arrived(self.target.at[pl.ds(0, 2 * sz.owned)], self.recv.at[1])
            source = jnp.where(z == 1, n - 1, 0)
            for head in range(2):
                rows = ((head * 2 + k) * n + source) * sz.owned
                span = self.target.at[pl.ds(pl.multiple_of(rows, 16), sz.owned)]
                device = at(x, y, k, n - 1 - source)
                remote(span, span, self.s_relay, self.recv.at[0], device).start()

    def middle(self, place):
        sz = self.sz
        x, y, k, z = place
        half = sz.width // 2
        two = 2 * sz.owned if sz.ctx == RELAYED else 0

        @pl.when(inner(sz.ctx, z))
        def _():
            arrived(self.target.at[pl.ds(0, half - sz.owned - two)], self.recv.at[0])
            arrived(self.target.at[pl.ds(0, half)], self.send)
            if two:
                arrived(self.target.at[pl.ds(0, two)], self.s_relay)

        @pl.when(jnp.logical_not(inner(sz.ctx, z)))
        def _():
            arrived(self.target.at[pl.ds(0, half - sz.owned)], self.recv.at[0])
            arrived(self.target.at[pl.ds(0, half - two)], self.send)

        for part in range(2):
            span = self.span(part, k)
            remote(span, span, self.s_core.at[part], self.r_core.at[part], at(x, y, 1 - k, z)).start()

    def finish(self, place):
        x, y, k, z = place
        for part in range(2):
            span = self.span(part, 1 - k)
            arrived(span, self.r_core.at[part])
            arrived(span, self.s_core.at[part])


class LineShares:
    reach = 0

    def __init__(self, sz, part, grads=None):
        self.sz, self.part = sz, part
        self.ins = [] if grads is None else [(grads, None)]
        self.outs = [jax.ShapeDtypeStruct((sz.ctx, 4, sz.owned, sz.hidden), BF)]
        self.scratch = [DMA((2, sz.ctx)), DMA((2, sz.ctx))]

    def bind(self, ins, outs, scratch):
        if ins:
            self.source = ins[0]
        self.target = outs[0]
        self.send, self.recv = scratch

    def moves(self, place, step, offset, width):
        sz = self.sz
        x, y, k, z = place
        ctx = lax.rem(z + step, sz.ctx)
        for head in range(4):
            rows = pl.ds(pl.multiple_of((head * sz.ctx + ctx) * sz.owned, 16), sz.owned)
            cols = pl.ds(offset, width)
            yield (self.source.at[self.part, rows, cols], self.target.at[z, head, :, cols])

    def begin(self, place, steps=None):
        sz = self.sz
        n = sz.ctx
        x, y, k, z = place
        me = x * sz.group + (y * 2 + k) * n + z
        wide = sz.least * HB

        def go(kind, offset, width):
            for step in list(range(1, n)) + [0] if steps is None else steps:
                for source, target in self.moves(place, step, offset, width):
                    if step:
                        remote(
                            source,
                            target,
                            self.send.at[kind, step],
                            self.recv.at[kind, step],
                            at(x, y, k, lax.rem(z + step, n)),
                        ).start()
                    else:
                        pltpu.make_async_copy(source, target, self.send.at[kind, 0]).start()

        go(0, 0, wide)
        if sz.extra:

            @pl.when(has_more(sz, me))
            def _():
                go(1, wide, HB)

    def finish(self, place):
        sz = self.sz
        n = sz.ctx
        x, y, k, z = place
        first = x * sz.group + (y * 2 + k) * n
        wide = sz.least * HB
        for step in range(n):
            ctx = lax.rem(z + n - step, n)
            arrived(self.target.at[ctx, :, :, pl.ds(0, wide)], self.send.at[0, step])
            if step:
                arrived(self.target.at[ctx, :, :, pl.ds(0, wide)], self.recv.at[0, step])
            if sz.extra:

                @pl.when(has_more(sz, first + z))
                def _():
                    arrived(self.target.at[ctx, :, :, pl.ds(wide, HB)], self.send.at[1, step])

                if step:

                    @pl.when(has_more(sz, first + ctx))
                    def _():
                        arrived(self.target.at[ctx, :, :, pl.ds(wide, HB)], self.recv.at[1, step])


class PlaneShares:
    def __init__(self, sz, section, part, source, own, other, sems):
        self.sz, self.section, self.part = sz, section, part
        self.source, self.own, self.other = source, own, other
        self.send, self.recv, self.local, self.s_over, self.r_over = sems
        self.base = sz.ff if part == 1 else 0

    def begin(self, place):
        sz = self.sz
        n = sz.ctx
        x, y, k, z = place
        head = y * 2 + k
        wide = sz.least * HB

        def go(to, device, local, result):
            for ctx in range(n):
                owner = x * sz.group + head * n + ctx
                first = first_column(sz, owner)

                def one(kind, offset, width):
                    source = self.source.at[ctx, to, :, pl.ds(offset, width)]
                    cols = pl.ds(pl.multiple_of(self.base + first + offset, HB), width)
                    target = result.at[:, cols]
                    if local:
                        pltpu.make_async_copy(source, target, self.local.at[kind]).start()
                    else:
                        recv = self.recv.at[0] if kind == 0 else self.recv.at[1 + head]
                        remote(source, target, self.send.at[kind], recv, device).start()

                one(0, 0, wide)
                if sz.extra:

                    @pl.when(has_more(sz, owner))
                    def _():
                        one(1, wide, HB)

        for own in (True, False):

            @pl.when((x == self.section) == own)
            def _():
                result = self.own if own else self.other

                @pl.loop(1, 4)
                def _(step):
                    to = lax.rem(head + step, 4)
                    go(to, (x, to, z), False, result)

                go(head, None, True, result)

    def settled(self, place):
        sz = self.sz
        n = sz.ctx
        x, y, k, z = place
        head = y * 2 + k
        wide = sz.least * HB
        row = self.own
        arrived(row.at[:, pl.ds(0, 3 * n * wide)], self.recv.at[0])
        arrived(row.at[:, pl.ds(0, 3 * n * wide)], self.send.at[0])
        arrived(row.at[:, pl.ds(0, n * wide)], self.local.at[0])
        for other in range(4):
            count = extras_of_head(sz, other)
            if count:

                @pl.when(head != other)
                def _():
                    arrived(row.at[:, pl.ds(0, count * HB)], self.recv.at[1 + other])

                @pl.when(head == other)
                def _():
                    arrived(row.at[:, pl.ds(0, 3 * count * HB)], self.send.at[1])
                    arrived(row.at[:, pl.ds(0, count * HB)], self.local.at[1])

    def cross(self, place):
        self.settled(place)

        @pl.when(place[0] != self.section)
        def _():
            self.over(place).start()

    def over(self, place):
        x, y, k, z = place
        plane = 1 - self.section
        cols = pl.ds(self.base + plane * self.sz.plane * HB, self.sz.plane * HB)
        return remote(
            self.other.at[:, cols],
            self.own.at[:, cols],
            self.s_over,
            self.r_over,
            at(1 - x, y, k, z),
        )

    def finish(self, place):
        x = place[0]

        @pl.when(x != self.section)
        def _():
            self.over(place).wait_send()

        @pl.when(x == self.section)
        def _():
            self.over(place).wait_recv()


class ReturnedHeads:
    reach = 0

    def __init__(self, sz, section, part, grads):
        self.sz, self.section, self.part = sz, section, part
        stretch = sz.width // 4
        self.ins = [] if grads is None else [(grads, None)]
        self.outs = [jax.ShapeDtypeStruct((4, sz.owned, sz.atot), BF)]
        self.scratch = [
            pltpu.VMEM((stretch, sz.atot), BF),
            pltpu.VMEM((stretch, sz.atot), BF),
            pltpu.VMEM((sz.ctx, sz.owned, sz.atot), BF),
            pltpu.VMEM((sz.owned, sz.atot), BF),
            pltpu.VMEM((sz.owned, sz.atot), F32),
            DMA,
            DMA,
            DMA,
            DMA,
            DMA((sz.ctx,)),
            DMA((sz.ctx,)),
            DMA,
            DMA((4,)),
        ]

    def bind(self, ins, outs, scratch):
        if ins:
            self.source = ins[0]
        self.target = outs[0]
        (
            self.got,
            self.summed,
            self.lined,
            self.taken,
            self.sum,
            self.load,
            self.r_taken,
            self.s_core,
            self.r_core,
            self.s_line,
            self.r_line,
            self.send,
            self.recv,
        ) = scratch

    def rows(self, k):
        stretch = self.sz.width // 4
        return pl.ds(pl.multiple_of((self.part * 2 + k) * stretch, 16), stretch)

    def own_rows(self, place):
        return pltpu.make_async_copy(self.source.at[self.rows(place[2])], self.summed, self.load)

    def core(self, place):
        x, y, k, z = place
        return remote(
            self.source.at[self.rows(1 - k)], self.got, self.s_core, self.r_core, at(x, y, 1 - k, z)
        )

    def own(self, ctx):
        return pl.ds(pl.multiple_of(ctx * self.sz.owned, 16), self.sz.owned)

    def line(self, place, step):
        x, y, k, z = place
        ctx = lax.rem(z + step, self.sz.ctx)
        return remote(
            self.summed.at[self.own(ctx)],
            self.lined.at[step],
            self.s_line.at[step],
            self.r_line.at[step],
            at(x, y, k, ctx),
        )

    def begin(self, place):
        self.own_rows(place).start()
        self.core(place).start()

    def middle(self, place):
        self.own_rows(place).wait()
        self.core(place).wait_recv()
        self.summed[...] = (self.summed[...].astype(F32) + self.got[...].astype(F32)).astype(BF)
        x, y, k, z = place
        n = self.sz.ctx
        for step in range(1, n):
            ctx = lax.rem(z + step, n)
            if n != RELAYED:
                self.line(place, step).start()
                continue

            @pl.when(ends(n, z, ctx))
            def _():
                remote(
                    self.summed.at[self.own(ctx)],
                    self.taken,
                    self.s_line.at[step],
                    self.r_taken,
                    at(x, y, k, jnp.where(z == 0, 1, n - 2)),
                ).start()

            @pl.when(jnp.logical_not(jnp.logical_or(ends(n, z, ctx), self.held(z, ctx))))
            def _():
                self.line(place, step).start()

    def held(self, z, ctx):
        n = self.sz.ctx
        return jnp.logical_or(
            jnp.logical_and(z == 1, ctx == n - 1), jnp.logical_and(z == n - 2, ctx == 0)
        )

    def relay(self, place):
        n = self.sz.ctx
        z = place[3]
        if n != RELAYED:
            return

        @pl.when(inner(n, z))
        def _():
            arrived(self.taken, self.r_taken)
            rows = self.own(jnp.where(z == 1, n - 1, 0))
            self.summed[rows] = (self.summed[rows].astype(F32) + self.taken[...].astype(F32)).astype(BF)
            self.line(place, 2).start()

    def homes(self, place, starting):
        x, y, k, z = place
        own = jnp.logical_and(x == self.section, y == self.part)
        target = self.target.at[2 * x + y]

        @pl.when(jnp.logical_not(own))
        def _():
            device = at(self.section, self.part, k, z)
            copy = remote(self.lined.at[0], target, self.send, self.recv.at[2 * x + y], device)
            copy.start() if starting else copy.wait_send()

        @pl.when(own)
        def _():
            copy = pltpu.make_async_copy(self.lined.at[0], target, self.send)
            copy.start() if starting else copy.wait()

    def late(self, place):
        x, y, k, z = place
        n = self.sz.ctx
        self.sum[...] = self.summed[self.own(z)].astype(F32)
        for step in range(1, n):

            @pl.when(jnp.logical_not(ends(n, z, lax.rem(z + n - step, n))))
            def _():
                self.line(place, step).wait_recv()
                self.sum[...] += self.lined[step].astype(F32)

        self.lined[0] = self.sum[...].astype(BF)
        self.homes(place, True)

    def finish(self, place):
        x, y, k, z = place
        self.core(place).wait_send()
        for step in range(1, self.sz.ctx):
            self.line(place, step).wait_send()
        self.homes(place, False)

        @pl.when(jnp.logical_and(x == self.section, y == self.part))
        def _():
            for group in range(4):

                @pl.when(group != 2 * x + y)
                def _():
                    arrived(self.target.at[group], self.recv.at[group])


class Placed:
    reach = 0

    def __init__(self, sz, first, second):
        self.ins = [(first, None), (second, None)]
        self.outs = [jax.ShapeDtypeStruct((2, sz.rows, sz.width), BF)]
        self.scratch = [DMA((2,)), DMA((2,))]

    def bind(self, ins, outs, scratch):
        self.sources, self.target = ins, outs[0]
        self.send, self.recv = scratch

    def each(self, place, starting):
        x, y, k, z = place
        for section in range(2):
            source, target = (self.sources[section], self.target.at[k])
            own = jnp.logical_and(x == section, jnp.logical_and(x == y, y == k))

            @pl.when(jnp.logical_not(own))
            def _():
                device = at(section, x, y, z)
                copy = remote(source, target, self.send.at[section], self.recv.at[k], device)
                copy.start() if starting else copy.wait_send()

            if starting:

                @pl.when(own)
                def _():
                    pltpu.make_async_copy(source, target, self.recv.at[k]).start()

    def begin(self, place):
        self.each(place, True)

    def finish(self, place):
        self.each(place, False)
        for batch in range(2):
            arrived(self.target.at[batch], self.recv.at[batch])


def begin(jobs, place, low=0.0, high=1.0):
    for job in jobs:
        job.begin(place, low, high)


def middle(jobs, place):
    for job in jobs:
        job.middle(place)


def finish(jobs, place):
    for job in jobs:
        job.finish(place)


class Gather:
    SEMS = 12

    @staticmethod
    def scratch(n):
        return [DMA((n,))] * 10 + [DMA((4, n))] * 2

    def __init__(self, n, rows, buffer, place, sems):
        self.n, self.half, self.buffer = n, rows // 2, buffer
        self.x, self.y, self.k, self.z = place
        x, y = self.x, self.y
        self.groups = (2 * x + y, 2 * x + 1 - y, 2 * (1 - x) + y, 2 * (1 - x) + 1 - y)
        (
            self.sz,
            self.rz,
            self.sy,
            self.ry,
            self.sx,
            self.rx,
            self.syd,
            self.ryd,
            self.sxd,
            self.rxd,
            self.sc,
            self.rc,
        ) = sems

    def src(self, step):
        return lax.rem(self.z + self.n - step, self.n)

    def line(self, step):
        own = self.buffer.at[self.k, self.groups[0], self.z]
        device = at(self.x, self.y, self.k, lax.rem(self.z + step, self.n))
        return remote(own, own, self.sz.at[step], self.rz.at[step], device)

    def to_y(self, step):
        part = self.buffer.at[self.k, self.groups[0], self.src(step)]
        device = at(self.x, 1 - self.y, self.k, self.z)
        return remote(part, part, self.sy.at[step], self.ry.at[step], device)

    def to_x(self, step):
        part = self.buffer.at[self.k, self.groups[0], self.src(step)]
        device = at(1 - self.x, self.y, self.k, self.z)
        return remote(part, part, self.sx.at[step], self.rx.at[step], device)

    def on_x(self, step):
        part = self.buffer.at[self.k, self.groups[1], self.src(step), pl.ds(0, self.half)]
        device = at(1 - self.x, self.y, self.k, self.z)
        return remote(part, part, self.sxd.at[step], self.rxd.at[step], device)

    def on_y(self, step):
        part = self.buffer.at[self.k, self.groups[2], self.src(step), pl.ds(self.half, self.half)]
        device = at(self.x, 1 - self.y, self.k, self.z)
        return remote(part, part, self.syd.at[step], self.ryd.at[step], device)

    def core(self, which, step):
        part = self.buffer.at[self.k, self.groups[which], self.src(step)]
        device = at(self.x, self.y, 1 - self.k, self.z)
        return remote(part, part, self.sc.at[which, step], self.rc.at[which, step], device)

    def begin(self):
        for step in range(1, self.n):
            self.line(step).start()
        self.spread(0)

    def spread(self, step):
        if step:
            arrived(self.buffer.at[self.k, self.groups[0], self.src(step)], self.rz.at[step])
        self.to_y(step).start()
        self.to_x(step).start()
        self.core(0, step).start()

    def second(self, step):
        arrived(self.buffer.at[self.k, self.groups[1], self.src(step)], self.ry.at[step])
        self.on_x(step).start()
        self.core(1, step).start()
        arrived(self.buffer.at[self.k, self.groups[2], self.src(step)], self.rx.at[step])
        self.on_y(step).start()
        self.core(2, step).start()

    def third(self, step):
        part = self.buffer.at[self.k, self.groups[3], self.src(step)]
        arrived(part.at[pl.ds(0, self.half)], self.rxd.at[step])
        arrived(part.at[pl.ds(self.half, self.half)], self.ryd.at[step])
        self.core(3, step).start()

    def other(self, which):
        for step in range(self.n):
            part = self.buffer.at[1 - self.k, self.groups[which], self.src(step)]
            arrived(part, self.rc.at[which, step])

    def finish(self):
        for step in range(self.n):
            if step:
                self.line(step).wait_send()
            self.to_y(step).wait_send()
            self.to_x(step).wait_send()
            self.on_x(step).wait_send()
            self.on_y(step).wait_send()
            for which in range(4):
                self.core(which, step).wait_send()

    def stages(self, column, nearly):
        k, steps = self.k, range(self.n)

        def spread():
            for step in range(1, self.n):
                self.spread(step)

        def second():
            for step in steps:
                self.second(step)

        def near():
            self.other(0)
            column(1 - k, 0)
            column(k, 1)
            column(k, 2)

        def third():
            for step in steps:
                self.third(step)

        def far():
            self.other(1)
            column(1 - k, 1)
            self.other(2)
            column(1 - k, 2)
            nearly()

        def last():
            column(k, 3)
            self.other(3)
            column(1 - k, 3)

        return [self.begin, spread, lambda: column(k, 0), second, near, third, far, last]


class Scatter:
    @staticmethod
    def scratch(n, rows, width):
        return [
            pltpu.VMEM((2, 4, n, rows, width), BF),
            pltpu.VMEM((4, n, rows, width), BF),
            pltpu.VMEM((2, n, rows // 2, width), BF),
            pltpu.VMEM((2, n, rows, width), BF),
            pltpu.VMEM((n, rows, width), BF),
            DMA((4,)),
            DMA((4,)),
            DMA((2, n)),
            DMA((2, n)),
            DMA((2, 2, n)),
            DMA((2, 2, n)),
            DMA((n,)),
            DMA((n,)),
        ]

    def __init__(self, n, rows, place, refs):
        self.n, self.rows, self.half = n, rows, rows // 2
        self.x, self.y, self.k, self.z = place
        x, y = self.x, self.y
        self.groups = (2 * x + y, 2 * x + 1 - y, 2 * (1 - x) + y, 2 * (1 - x) + 1 - y)
        (
            self.parts,
            self.from_core,
            self.from_diag,
            self.from_near,
            self.from_line,
            self.s_core,
            self.r_core,
            self.s_diag,
            self.r_diag,
            self.s_near,
            self.r_near,
            self.s_line,
            self.r_line,
        ) = refs
        self.near = (at(x, 1 - y, self.k, self.z), at(1 - x, y, self.k, self.z))

    def slot(self, step):
        return lax.rem(self.z + step, self.n)

    def order(self):
        return list(range(1, self.n)) + [0]

    def core(self, which):
        return remote(
            self.parts.at[1 - self.k, self.groups[which]],
            self.from_core.at[which],
            self.s_core.at[which],
            self.r_core.at[which],
            at(self.x, self.y, 1 - self.k, self.z),
        )

    def diag(self, direction, step):
        rows = pl.ds(self.half if direction == 0 else 0, self.half)
        return remote(
            self.parts.at[self.k, self.groups[3], self.slot(step), rows],
            self.from_diag.at[direction, step],
            self.s_diag.at[direction, step],
            self.r_diag.at[direction, step],
            self.near[direction],
        )

    def close(self, direction, part, step):
        rows = pl.ds(part * self.half, self.half)
        return remote(
            self.parts.at[self.k, self.groups[1 + direction], self.slot(step), rows],
            self.from_near.at[direction, step, rows],
            self.s_near.at[direction, part, step],
            self.r_near.at[direction, part, step],
            self.near[direction],
        )

    def line(self, step):
        return remote(
            self.parts.at[self.k, self.groups[0], self.slot(step)],
            self.from_line.at[step],
            self.s_line.at[step],
            self.r_line.at[step],
            at(self.x, self.y, self.k, self.slot(step)),
        )

    def add_core(self, which):
        self.core(which).wait_recv()
        group = self.groups[which]
        self.parts[self.k, group] = (
            self.parts[self.k, group].astype(F32) + self.from_core[which].astype(F32)
        ).astype(BF)

    def early(self):
        for direction, part in ((0, 1), (1, 0)):
            self.add_core(1 + direction)
            for step in self.order():
                self.close(direction, part, step).start()

    def open(self):
        self.add_core(3)
        for step in self.order():
            self.diag(1, step).start()
            self.diag(0, step).start()
        self.add_core(0)

    def late(self):
        for step in self.order():
            slot = self.slot(step)
            for direction, part in ((0, 0), (1, 1)):
                came = 1 - direction
                self.diag(came, step).wait_recv()
                rows = pl.ds(part * self.half, self.half)
                group = self.groups[1 + direction]
                self.parts[self.k, group, slot, rows] = (
                    self.parts[self.k, group, slot, rows].astype(F32)
                    + self.from_diag[came, step].astype(F32)
                ).astype(BF)
                self.close(direction, part, step).start()

    def along(self):
        group = self.groups[0]
        for step in self.order():
            slot = self.slot(step)
            for direction in range(2):
                for part in range(2):
                    self.close(direction, part, step).wait_recv()
            total = (
                self.parts[self.k, group, slot].astype(F32)
                + self.from_near[0, step].astype(F32)
                + self.from_near[1, step].astype(F32)
            )
            if step:
                self.parts[self.k, group, slot] = total.astype(BF)
                self.line(step).start()
            else:
                self.own = total

    def result(self):
        result = self.own
        for step in range(1, self.n):
            self.line(step).wait_recv()
            result = result + self.from_line[step].astype(F32)
        return result

    def stages(self):
        return [self.open, self.late, self.along]

    def finish(self):
        for which in range(4):
            self.core(which).wait_send()
        for step in range(self.n):
            for direction in range(2):
                self.diag(direction, step).wait_send()
                for part in range(2):
                    self.close(direction, part, step).wait_send()
            if step:
                self.line(step).wait_send()


CHUNKS = 2
A, B = 0, 1
TOGETHER = (
    (A, 0), (B, 0), (A, 1), (A, 2), (A, 3), (A, 4), (B, 1), (A, 5), (B, 2), (A, 6), (B, 3), (A, 7),
    (A, 8), (B, 4), (B, 5), (A, 9), (B, 6), (B, 7), (B, 8), (A, 10), (B, 9), (B, 10),
)


def run_together(first, second, after):
    for stream, number in TOGETHER:
        (first, second)[stream][number]()
        if (stream, number) in after:
            after[stream, number]()


def spread(sz, small, tokens, cotangent, qkv, out_w, gate_up, down):
    n = sz.ctx
    half = sz.plane * HB

    def body(ins, outs, scratch, jobs):
        small, tokens, cotangent, qkv, out_w, gate_up, down = ins
        small_all, tok_own, cot_own, heads_x, cols_x = outs
        s_small, r_small, s_own, r_own, s_hx, r_hx, s_cx, r_cx = scratch
        place = where_am_i()
        x, y, k, z = place
        me = x * sz.group + (y * 2 + k) * n + z
        everyone = lambda index: flat_place(index, sz.group, n)
        greet_all(me, sz.total, everyone)
        across = at(1 - x, y, k, z)

        def heads_over():
            return [
                remote(source, heads_x.at[y_to, :, cols], s_hx, r_hx, across)
                for y_to in range(2)
                for source, cols in head_columns(sz, 2 * (1 - x) + y_to, qkv, out_w)
            ]

        for copy in heads_over():
            copy.start()

        def owns(starting):
            @pl.when(x == y)
            def _():
                for batch in range(2):
                    pairs = ((tokens, tok_own, 0), (cotangent, cot_own, 1))
                    for source, target, slot in pairs:
                        own = jnp.logical_and(k == y, k == batch)

                        @pl.when(jnp.logical_not(own))
                        def _():
                            copy = remote(
                                source.at[batch],
                                target,
                                s_own.at[batch, slot],
                                r_own.at[slot],
                                at(x, k, batch, z),
                            )
                            copy.start() if starting else copy.wait_send()

                        if starting:

                            @pl.when(own)
                            def _():
                                pltpu.make_async_copy(
                                    source.at[batch], target, r_own.at[slot]
                                ).start()

        owns(True)

        @pl.loop(1, sz.total)
        def _(step):
            device = everyone(lax.rem(me + step, sz.total))
            remote(small, small_all.at[me], s_small, r_small, device).start()

        pltpu.make_async_copy(small, small_all.at[me], s_small).start()

        def columns_over(part):
            base = (sz.ff if part == 1 else 0) + (1 - x) * half
            source = (down if part == 2 else gate_up).at[:, pl.ds(pl.multiple_of(base, HB), half)]
            return remote(source, cols_x.at[part], s_cx.at[part], r_cx.at[part], across)

        heads, first = jobs
        heads.use(ins, outs)
        first.use(ins, outs)

        @pl.when(x == heads.section)
        def _():
            heads.begin(place)

        for part in range(3):
            columns_over(part).start()
        arrived(heads_x, r_hx)

        @pl.when(x != heads.section)
        def _():
            heads.begin(place)

        columns_over(0).wait_recv()
        heads.relay(place)
        first.begin(place)
        heads.middle(place)
        arrived(small_all.at[pl.ds(0, sz.total - 1)], r_small)
        arrived(small_all, s_small)
        arrived(tok_own, r_own.at[0])
        arrived(cot_own, r_own.at[1])
        owns(False)
        heads.finish(place)

        for part in range(3):
            if part:
                columns_over(part).wait_recv()
            columns_over(part).wait_send()
        arrived(heads_x, s_hx)
        first.finish(place)

    shape = jax.ShapeDtypeStruct
    outs = [
        (shape((sz.total, 16, LANES), BF), hbm()),
        (shape((sz.rows, sz.width), BF), hbm()),
        (shape((sz.rows, sz.width), BF), hbm()),
        (shape((2, sz.owned, sz.atot), BF), hbm()),
        (shape((3, sz.owned, half), BF), hbm()),
    ]
    arrays = (small, tokens, cotangent, qkv, out_w, gate_up, down)
    scratch = [DMA, DMA, DMA((2, 2)), DMA((2,)), DMA, DMA, DMA((3,)), DMA((3,))]
    jobs = [OwnHeads(sz, 0, 3, 4, 3), OwnColumns(sz, 0, 0, 5, 4)]
    return run_call(body, [(a, hbm()) for a in arrays], outs, scratch, jobs, 1, "spread_weights")


class OwnHeads(Heads):
    def __init__(self, sz, section, qkv, out_w, staged):
        super().__init__(sz, section, None, None, None)
        self.ins = []
        self.named = (qkv, out_w, staged)

    def bind(self, ins, outs, scratch):
        self.target = outs[0]
        self.send, self.recv, self.s_core, self.r_core, self.s_relay = scratch

    def use(self, ins, outs):
        qkv, out_w, staged = self.named
        self.qkv, self.out_w, self.staged = ins[qkv], ins[out_w], outs[staged]


class OwnColumns(Columns):
    def __init__(self, sz, section, part, source, staged):
        super().__init__(sz, section, part, None, None, None)
        self.ins = []
        self.named = (source, staged)

    def bind(self, ins, outs, scratch):
        self.target = outs[0]
        self.send, self.recv = scratch

    def use(self, ins, outs):
        source, staged = self.named
        self.source, self.staged = ins[source], outs[staged]


class Part:
    def __init__(self, body, ins, outs, scratch):
        self.body, self.ins, self.outs, self.scratch = body, ins, outs, scratch


def joined(sz, first, first_jobs, second, second_jobs, link, slab, collective_id, name):
    a, b, c = len(first.ins), len(first.outs), len(first.scratch)
    count = len(first_jobs)

    def body(ins, outs, scratch, jobs):
        place = where_am_i()
        x, y, k, z = place
        peers = pair_peers(x, y, k, z)
        near = list(peers) + line_peers(sz.ctx, x, y, k, z) + [at(x, y, 1 - k, z)]
        if slab:
            near += [at(x, 1 - y, 1 - k, z), at(1 - x, y, 1 - k, z), at(1 - x, 1 - y, 1 - k, z)]
        meet(sz, place, near, [peers[0], peers[2]], jobs)
        own, later = (jobs[:count], jobs[count:])
        first.body(ins[:a], outs[:b], scratch[:c], own, place)
        second.body(link(outs[:b], ins[a:], own, later), outs[b:], scratch[c:], later, place, own)

    results, extra = run_call(
        body,
        first.ins + second.ins,
        first.outs + second.outs,
        first.scratch + second.scratch,
        list(first_jobs) + list(second_jobs),
        collective_id,
        name,
    )
    return (results[:b], results[b:], extra[:count], extra[count:])


def gather_pair(buffer, place, send, recv):
    x, y, k, z = place
    own = buffer.at[2 * x + y]
    copies = [
        remote(own, own, send.at[i], recv.at[i], device)
        for i, device in enumerate(pair_peers(x, y, k, z))
    ]
    for copy in copies:
        copy.start()
    return copies


def gathered_pair(buffer, place, copies, recv):
    x, y, k, z = place
    for i, group in enumerate(pair_groups(x, y)):
        arrived(buffer.at[group], recv.at[i])


def scatter_pair(parts, landed, place, send, recv):
    x, y, k, z = place
    groups = pair_groups(x, y)
    copies = [
        remote(parts.at[groups[i]], landed.at[i], send.at[i], recv.at[i], device)
        for i, device in enumerate(pair_peers(x, y, k, z))
    ]
    for copy in copies:
        copy.start()
    return copies


def attend(sz, section, x_own, gain, bias, watt, tables, qpos, kpos):
    n, rows = sz.ctx, 4 * sz.rows

    def body(ins, outs, scratch, jobs, place):
        x_ref, gains, biases, watt, cosine, sine, qpos, kpos = ins
        gain, bias = (gains[section : section + 1], biases[section : section + 1])
        h1_out, n1_all, q_out, kv_all, o_out, lse_out = outs
        w, parts, landed, w_sem, s_in, r_in, s_kv, r_kv, s_back, r_back = scratch
        x, y, k, z = place
        load = pltpu.make_async_copy(watt, w, w_sem)
        load.start()
        group = 2 * x + y
        values = x_ref[...].astype(F32)
        n1_all[group] = (values * row_norm(values) * gain).astype(BF)
        copies = gather_pair(n1_all, place, s_in, r_in)
        begin(jobs, place, 0.0, 0.3)
        load.wait()
        gathered_pair(n1_all, place, copies, r_in)
        normed = n1_all[...].reshape(rows, sz.width)
        kv = mm(normed, w[:, sz.qcols : sz.acols]) + bias[:, sz.qcols : sz.acols]
        cos, sin = cosine[...], sine[...]
        key = kv[:, : sz.kcols]
        kv_all[z, :, : sz.kcols] = (key * cos + half_turn(key) * sin).astype(BF)
        kv_all[z, :, sz.kcols :] = kv[:, sz.kcols :].astype(BF)
        kv_copies = []
        for step, device in enumerate(line_peers(n, x, y, k, z)):
            own = kv_all.at[z]
            kv_copies.append(remote(own, own, s_kv.at[step], r_kv.at[step], device))
            kv_copies[-1].start()
        begin(jobs, place, 0.3, 1.0)
        queries = mm(normed, w[:, : sz.qcols]) + bias[:, : sz.qcols]
        for head in range(sz.per_group):
            cols = slice(head * HEAD_WIDTH_SIZE, (head + 1) * HEAD_WIDTH_SIZE)
            query = queries[:, cols]
            q_out[:, cols] = (query * cos + half_turn(query) * sin).astype(BF)
        for step in range(n - 1):
            arrived(kv_all.at[lax.rem(z + n - 1 - step, n)], r_kv.at[step])
        keys = kv_all[:, :, : sz.kcols].reshape(n * rows, sz.kcols)
        vals = kv_all[:, :, sz.kcols :].reshape(n * rows, sz.kcols)
        allowed = kpos[...] <= qpos[...]
        scale = 1.0 / math.sqrt(HEAD_WIDTH_SIZE)
        for head in range(sz.per_group):
            cols = slice(head * HEAD_WIDTH_SIZE, (head + 1) * HEAD_WIDTH_SIZE)
            scores = jnp.where(allowed, mm(q_out[:, cols], keys, NT) * scale, -1e30)
            highest = jnp.max(scores, axis=-1, keepdims=True)
            weights = jnp.exp(scores - highest)
            total = jnp.sum(weights, axis=-1, keepdims=True)
            o_out[:, cols] = mm(weights.astype(BF), vals) / total
            lse_out[head] = jnp.broadcast_to(highest + jnp.log(total), (rows, LANES))
        partial = mm(o_out[...].astype(BF), w[:, sz.acols :], NT)
        parts[...] = partial.astype(BF).reshape(4, sz.rows, sz.width)
        back = scatter_pair(parts, landed, place, s_back, r_back)
        middle(jobs, place)
        for copy in copies + kv_copies:
            copy.wait_send()
        out = values + parts[group].astype(F32)
        for i in range(3):
            back[i].wait_recv()
            out = out + landed[i].astype(F32)
        h1_out[...] = out
        for copy in back:
            copy.wait_send()

    shapes = (
        jax.ShapeDtypeStruct((sz.rows, sz.width), F32),
        jax.ShapeDtypeStruct((4, sz.rows, sz.width), BF),
        jax.ShapeDtypeStruct((rows, sz.qcols), BF),
        jax.ShapeDtypeStruct((n, rows, 2 * sz.kcols), BF),
        jax.ShapeDtypeStruct((rows, sz.qcols), F32),
        jax.ShapeDtypeStruct((sz.per_group, rows, LANES), F32),
    )
    arrays = (x_own, gain, bias, watt, *tables, qpos, kpos)
    specs = [vmem()] * 3 + [hbm()] + [vmem()] * 4
    scratch = [
        pltpu.VMEM((sz.width, sz.atot), BF),
        pltpu.VMEM((4, sz.rows, sz.width), BF),
        pltpu.VMEM((3, sz.rows, sz.width), BF),
        DMA,
        DMA((3,)),
        DMA((3,)),
        DMA((n,)),
        DMA((n,)),
        DMA((3,)),
        DMA((3,)),
    ]
    return Part(body, list(zip(arrays, specs)), [(shape, vmem()) for shape in shapes], scratch)


def attend_back(sz, section, dh1, x_own, gain, watt, tables, qpos, kpos, kept, plan):
    n, rows = sz.ctx, 4 * sz.rows

    def body(ins, outs, scratch, jobs, place, after=None):
        dh1, x_ref, gains, watt, cosine, sine, qpos, kpos, n1_all, q_in, kv_all, o_in, lse_in = ins
        dx_out, dw_out, gain_grad, bias_grad = outs
        w, dh_all, dkv, dkv_in, da, parts, landed, w_sem, s_in, r_in, s_kv, r_kv, s_back, r_back = scratch
        x, y, k, z = place
        load = pltpu.make_async_copy(watt, w, w_sem)
        load.start()
        group = 2 * x + y
        dh_all[group] = dh1[...].astype(BF)
        after = plan(jobs, place) if after is None else after
        copies = gather_pair(dh_all, place, s_in, r_in)
        after[0]()
        load.wait()
        gathered_pair(dh_all, place, copies, r_in)
        after[1]()
        dh = dh_all[...].reshape(rows, sz.width)
        dout = mm(dh, w[:, sz.acols :]).astype(BF)
        keys = kv_all[:, :, : sz.kcols].reshape(n * rows, sz.kcols)
        vals = kv_all[:, :, sz.kcols :].reshape(n * rows, sz.kcols)
        allowed = kpos[...] <= qpos[...]
        scale = 1.0 / math.sqrt(HEAD_WIDTH_SIZE)
        cos, sin = cosine[...], sine[...]
        dkeys, dvals = None, None
        for head in range(sz.per_group):
            cols = slice(head * HEAD_WIDTH_SIZE, (head + 1) * HEAD_WIDTH_SIZE)
            query, grad = q_in[:, cols], dout[:, cols]
            delta = jnp.sum(grad.astype(F32) * o_in[:, cols], axis=-1, keepdims=True)
            scores = mm(query, keys, NT) * scale
            probs = jnp.where(allowed, jnp.exp(scores - lse_in[head][:, :1]), 0.0)
            dscores = (probs * (mm(grad, vals, NT) - delta)).astype(BF)
            dquery = (mm(dscores, keys) * scale).astype(BF).astype(F32)
            da[:, cols] = (dquery * cos - half_turn(dquery) * sin).astype(BF)
            one_key = mm(dscores, query, TN)
            one_val = mm(probs.astype(BF), grad, TN)
            dkeys = one_key if dkeys is None else dkeys + one_key
            dvals = one_val if dvals is None else dvals + one_val
        dkv[:, :, : sz.kcols] = (dkeys * scale).astype(BF).reshape(n, rows, sz.kcols)
        dkv[:, :, sz.kcols :] = dvals.astype(BF).reshape(n, rows, sz.kcols)
        kv_copies = []
        for step, device in enumerate(line_peers(n, x, y, k, z)):
            kv_copies.append(
                remote(
                    dkv.at[lax.rem(z + 1 + step, n)],
                    dkv_in.at[step],
                    s_kv.at[step],
                    r_kv.at[step],
                    device,
                )
            )
            kv_copies[-1].start()
        after[2]()
        dw_out[:, sz.acols :] = mm(dh, o_in[...].astype(BF), TN).astype(BF)
        total = dkv[z].astype(F32)
        for step in range(n - 1):
            kv_copies[step].wait_recv()
            total = total + dkv_in[step].astype(F32)
        dkey = total[:, : sz.kcols]
        da[:, sz.qcols : sz.qcols + sz.kcols] = (dkey * cos - half_turn(dkey) * sin).astype(BF)
        da[:, sz.qcols + sz.kcols :] = total[:, sz.kcols :].astype(BF)
        parts[...] = mm(da[...], w[:, : sz.acols], NT).astype(BF).reshape(4, sz.rows, sz.width)
        back = scatter_pair(parts, landed, place, s_back, r_back)
        after[3]()
        dw_out[:, : sz.acols] = mm(n1_all[...].reshape(rows, sz.width), da[...], TN).astype(BF)
        bias_grad[...] = jnp.sum(da[...].astype(F32), axis=0, keepdims=True)
        for copy in copies + kv_copies:
            copy.wait_send()
        dn1 = parts[group].astype(F32)
        for i in range(3):
            back[i].wait_recv()
            dn1 = dn1 + landed[i].astype(F32)
        values = x_ref[...].astype(F32)
        inverse = row_norm(values)
        weighted = dn1 * gains[section : section + 1]
        inner = jnp.mean(weighted * values, axis=-1, keepdims=True)
        dx = dh1[...] + inverse * weighted - values * (inverse * inverse * inverse) * inner
        dx_out[...] = dx.astype(BF)
        gain_grad[...] = jnp.sum(dn1 * values * inverse, axis=0, keepdims=True)
        for copy in back:
            copy.wait_send()

    shapes = (
        jax.ShapeDtypeStruct((sz.rows, sz.width), BF),
        jax.ShapeDtypeStruct((sz.width, sz.atot), BF),
        jax.ShapeDtypeStruct((1, sz.width), F32),
        jax.ShapeDtypeStruct((1, sz.acols), F32),
    )
    arrays = (dh1, x_own, gain, watt, *tables, qpos, kpos, *kept)
    specs = [vmem()] * 3 + [hbm()] + [vmem()] * 9
    scratch = [
        pltpu.VMEM((sz.width, sz.atot), BF),
        pltpu.VMEM((4, sz.rows, sz.width), BF),
        pltpu.VMEM((n, rows, 2 * sz.kcols), BF),
        pltpu.VMEM((n, rows, 2 * sz.kcols), BF),
        pltpu.VMEM((rows, sz.acols), BF),
        pltpu.VMEM((4, sz.rows, sz.width), BF),
        pltpu.VMEM((3, sz.rows, sz.width), BF),
        DMA,
        DMA((3,)),
        DMA((3,)),
        DMA((n,)),
        DMA((n,)),
        DMA((3,)),
        DMA((3,)),
    ]
    return Part(body, list(zip(arrays, specs)), [(shape, vmem()) for shape in shapes], scratch)


class HiddenWeights:
    def __init__(self, sz, place, sources, w, sems):
        x, y, k, z = place
        self.sz, self.sources, self.w, self.sems = sz, sources, w, sems
        self.more = has_more(sz, x * sz.group + (y * 2 + k) * sz.ctx + z)
        self.wide = sz.least * HB

    def copies(self, offset, width, kind, parts):
        cols = pl.ds(offset, width)
        return [
            pltpu.make_async_copy(
                self.sources[part].at[:, cols], self.w.at[part, :, cols], self.sems.at[kind, part]
            )
            for part in parts
        ]

    def start(self, parts=(0, 1, 2)):
        for copy in self.copies(0, self.wide, 0, parts):
            copy.start()
        if self.sz.extra:

            @pl.when(self.more)
            def _():
                for copy in self.copies(self.wide, HB, 1, parts):
                    copy.start()

            @pl.when(jnp.logical_not(self.more))
            def _():
                for part in parts:
                    self.w[part, :, self.wide :] = jnp.zeros((self.sz.width, HB), BF)

    def wait(self, parts=(0, 1, 2)):
        for copy in self.copies(0, self.wide, 0, parts):
            copy.wait()
        if self.sz.extra:

            @pl.when(self.more)
            def _():
                for copy in self.copies(self.wide, HB, 1, parts):
                    copy.wait()


def halves(n, rows, gathered, place, refs):
    count = len(Gather.scratch(n)) + len(Scatter.scratch(n, rows, 0))
    made = []
    for chunk in range(CHUNKS):
        own = refs[chunk * count : (chunk + 1) * count]
        made.append(
            (Gather(n, rows, gathered.at[chunk], place, own[:12]), Scatter(n, rows, place, own[12:]))
        )
    return made


def halves_scratch(n, rows, width):
    return (Gather.scratch(n) + Scatter.scratch(n, rows, width)) * CHUNKS


def feed(sz, gain, gate):
    n = sz.ctx
    rows = sz.rows // CHUNKS

    def body(ins, outs, scratch, jobs, place, pending):
        h1, gain, *sources = ins
        act_out, *kept_out = outs
        w, n2_all, gate_out, up_out, hm_out, w_sems, kept_sems, *refs = scratch
        x, y, k, z = place
        hidden_weights = HiddenWeights(sz, place, sources, w, w_sems)
        pairs = halves(n, rows, n2_all, place, refs)
        values = h1[...]
        normed = (values * row_norm(values) * gain[2:3]).astype(BF)
        for chunk in range(CHUNKS):
            n2_all[chunk, k, 2 * x + y, z] = normed[chunk * rows : (chunk + 1) * rows]

        def columns(chunk):
            gather, scatter = pairs[chunk]

            def column(core, which):
                group = gather.groups[which]
                normed = n2_all[chunk, core, group].reshape(n * rows, sz.width)
                gate = mm(normed, w[0])
                up = mm(normed, w[1])
                hidden = (gate * jax.nn.sigmoid(gate) * up).astype(BF)
                gate_out[chunk, core, group] = gate.astype(BF)
                up_out[chunk, core, group] = up.astype(BF)
                hm_out[chunk, core, group] = hidden
                scatter.parts[core, group] = (
                    mm(hidden, w[2], NT).astype(BF).reshape(n, rows, sz.width)
                )
                if core is not k:
                    scatter.core(which).start()

            return gather.stages(column, scatter.early) + scatter.stages()

        def started():
            for job in jobs[:1]:
                job.begin(place)
            begin(jobs[1:], place, 0.0, 0.75)
            finish(pending, place)
            hidden_weights.start()
            hidden_weights.wait()

        keep = [
            pltpu.make_async_copy(source, target, kept_sems.at[i])
            for i, (source, target) in enumerate(zip((n2_all, gate_out, up_out, hm_out), kept_out))
        ]

        def later():
            for copy in keep:
                copy.start()
            begin(jobs[1:], place, 0.75, 1.0)
            middle(jobs, place)

        run_together(
            columns(0),
            columns(1),
            {(B, 0): started, (A, 6): lambda: jobs[0].relay(place), (B, 8): later},
        )
        for chunk, (gather, scatter) in enumerate(pairs):
            span = slice(chunk * rows, (chunk + 1) * rows)
            act_out[span] = (values[span] + scatter.result()).astype(BF)
        for gather, scatter in pairs:
            gather.finish()
            scatter.finish()
        for copy in keep:
            copy.wait()
        finish(jobs, place)

    kept = jax.ShapeDtypeStruct((CHUNKS, 2, 4, n * rows, sz.hidden), BF)
    shapes = (
        jax.ShapeDtypeStruct((sz.rows, sz.width), BF),
        jax.ShapeDtypeStruct((CHUNKS, 2, 4, n, rows, sz.width), BF),
        kept,
        kept,
        kept,
    )
    scratch = [pltpu.VMEM((3, sz.width, sz.hidden), BF)]
    scratch += [pltpu.VMEM(shape.shape, BF) for shape in shapes[1:]]
    scratch += [DMA((2, 3)), DMA((4,))] + halves_scratch(n, rows, sz.width)
    outs = [(shape, hbm() if i else vmem()) for i, shape in enumerate(shapes)]
    return Part(body, [(gain, vmem()), (gate, hbm())], outs, scratch)


def both(sz, dy, gain, gate):
    n, rows = sz.ctx, sz.rows

    def body(ins, outs, scratch, jobs, place, pending):
        dy, h1, gain, *sources = ins
        act_out, dh1_out, dw_out, gain_grad = outs
        w, n2_all, dy_all, gate_all, up_all, hm_all, w_sems, *refs = scratch
        x, y, k, z = place
        hidden_weights = HiddenWeights(sz, place, sources, w, w_sems)
        count = len(refs) // 2
        (gather_f, scatter_f), (gather_b, scatter_b) = [
            (Gather(n, rows, buffer, place, own[:12]), Scatter(n, rows, place, own[12:]))
            for buffer, own in ((n2_all, refs[:count]), (dy_all, refs[count:]))
        ]
        values = h1[...]
        inverse = row_norm(values)
        n2_all[k, 2 * x + y, z] = (values * inverse * gain[3:4]).astype(BF)
        dy_all[k, 2 * x + y, z] = dy[...]

        waiting = []

        def down_product(core, which):
            group = gather_f.groups[which]
            partial = mm(hm_all[core, group], w[2], NT)
            scatter_f.parts[core, group] = partial.astype(BF).reshape(n, rows, sz.width)
            if core is not k:
                scatter_f.core(which).start()

        def down_here():
            nonlocal waiting
            finish(jobs, place)
            hidden_weights.start((2,))
            hidden_weights.wait((2,))
            for core, which in waiting:
                down_product(core, which)
            waiting = None

        def forward(core, which):
            group = gather_f.groups[which]
            normed = n2_all[core, group].reshape(n * rows, sz.width)
            gate = mm(normed, w[0])
            up = mm(normed, w[1])
            hidden = (gate * jax.nn.sigmoid(gate) * up).astype(BF)
            gate_all[core, group] = gate.astype(BF)
            up_all[core, group] = up.astype(BF)
            hm_all[core, group] = hidden
            if waiting is None:
                down_product(core, which)
            else:
                waiting.append((core, which))

        def backward(core, which):
            group = gather_b.groups[which]
            dhidden = mm(dy_all[core, group].reshape(n * rows, sz.width), w[2])
            gate = gate_all[core, group].astype(F32)
            up = up_all[core, group].astype(F32)
            sigmoid = jax.nn.sigmoid(gate)
            dgate = (dhidden * up * sigmoid * (1.0 + gate * (1.0 - sigmoid))).astype(BF)
            dup = (dhidden * gate * sigmoid).astype(BF)
            gate_all[core, group] = dgate
            up_all[core, group] = dup
            partial = mm(dgate, w[0], NT) + mm(dup, w[1], NT)
            scatter_b.parts[core, group] = partial.astype(BF).reshape(n, rows, sz.width)
            if core is not k:
                scatter_b.core(which).start()

        def weight_grad(slot, left, right):
            total = 8 * n * rows
            tile = 256 if sz.width % 256 == 0 else 128
            grads = right[...].reshape(total, sz.hidden)

            @pl.loop(0, sz.width // tile)
            def _(step):
                cols = pl.ds(pl.multiple_of(step * tile, tile), tile)
                side = left[:, :, :, :, cols].reshape(total, tile)
                dw_out[slot, cols] = mm(side, grads, TN).astype(BF)

        def result():
            act_out[...] = (h1[...] + scatter_f.result()).astype(BF)

        def started():
            finish(pending, place)
            hidden_weights.start((0, 1))
            hidden_weights.wait((0, 1))

        run_together(
            gather_f.stages(forward, scatter_f.early) + scatter_f.stages(),
            gather_b.stages(backward, scatter_b.early) + scatter_b.stages(),
            {
                (A, 0): lambda: begin(jobs, place),
                (B, 0): started,
                (A, 5): down_here,
                (B, 8): lambda: weight_grad(2, dy_all, hm_all),
                (B, 9): lambda: weight_grad(0, n2_all, gate_all),
                (B, 10): lambda: weight_grad(1, n2_all, up_all),
            },
        )
        result()
        dn2 = scatter_b.result()
        values = h1[...]
        inverse = row_norm(values)
        weighted = dn2 * gain[3:4]
        inner = jnp.mean(weighted * values, axis=-1, keepdims=True)
        dh1_out[...] = (
            dy[...].astype(F32) + inverse * weighted - values * (inverse * inverse * inverse) * inner
        )
        gain_grad[...] = jnp.sum(dn2 * values * inverse, axis=0, keepdims=True)
        for job in (gather_f, scatter_f, gather_b, scatter_b):
            job.finish()

    shapes = (
        jax.ShapeDtypeStruct((sz.rows, sz.width), BF),
        jax.ShapeDtypeStruct((sz.rows, sz.width), F32),
        jax.ShapeDtypeStruct((3, sz.width, sz.hidden), BF),
        jax.ShapeDtypeStruct((1, sz.width), F32),
    )
    gathered = pltpu.VMEM((2, 4, n, rows, sz.width), BF)
    inner = pltpu.VMEM((2, 4, n * rows, sz.hidden), BF)
    scratch = [
        pltpu.VMEM((3, sz.width, sz.hidden), BF),
        gathered,
        gathered,
        inner,
        inner,
        inner,
        DMA((2, 3)),
    ] + (Gather.scratch(n) + Scatter.scratch(n, rows, sz.width)) * 2
    ins = [(dy, vmem()), (gain, vmem()), (gate, hbm())]
    return Part(body, ins, [(shape, vmem()) for shape in shapes], scratch)


def feed_back(sz, h1, gain, weights, kept):
    n = sz.ctx
    rows = sz.rows // CHUNKS

    def body(ins, outs, scratch, jobs, place, pending):
        dy, h1, gain, *sources = ins[:6]
        dh1_out, dw_out, gain_grad = outs
        w, dy_all, dgate_all, dup_all, *scratch = scratch
        n2_all, gate_in, up_in, hm_in, w_sems, kept_sems, *refs = scratch
        kept = [
            pltpu.make_async_copy(source, target, kept_sems.at[i])
            for i, (source, target) in enumerate(zip(ins[6:], (n2_all, gate_in, up_in, hm_in)))
        ]
        x, y, k, z = place
        hidden_weights = HiddenWeights(sz, place, sources, w, w_sems)
        hidden_weights.start()
        for copy in kept[1:] + kept[:1]:
            copy.start()
        pairs = halves(n, rows, dy_all, place, refs)
        for chunk in range(CHUNKS):
            dy_all[chunk, k, 2 * x + y, z] = dy[chunk * rows : (chunk + 1) * rows]
        line_jobs = [job for job in jobs if isinstance(job, LineShares)]
        heads = [job for job in jobs if isinstance(job, ReturnedHeads)]

        def columns(chunk):
            gather, scatter = pairs[chunk]

            def column(core, which):
                group = gather.groups[which]
                dhidden = mm(dy_all[chunk, core, group].reshape(n * rows, sz.width), w[2])
                gate = gate_in[chunk, core, group].astype(F32)
                up = up_in[chunk, core, group].astype(F32)
                sigmoid = jax.nn.sigmoid(gate)
                dgate = (dhidden * up * sigmoid * (1.0 + gate * (1.0 - sigmoid))).astype(BF)
                dup = (dhidden * gate * sigmoid).astype(BF)
                dgate_all[chunk, core, group] = dgate
                dup_all[chunk, core, group] = dup
                partial = mm(dgate, w[0], NT) + mm(dup, w[1], NT)
                scatter.parts[core, group] = partial.astype(BF).reshape(n, rows, sz.width)
                if core is not k:
                    scatter.core(which).start()

            return gather.stages(column, scatter.early) + scatter.stages()

        total = 8 * n * sz.rows
        tile = 256 if sz.width % 256 == 0 else 128

        def weight_grad(slot, left, right):
            grads = right[...].reshape(total, sz.hidden)

            @pl.loop(0, sz.width // tile)
            def _(step):
                cols = pl.ds(pl.multiple_of(step * tile, tile), tile)
                side = left[:, :, :, :, :, cols].reshape(total, tile)
                dw_out[slot, cols] = mm(side, grads, TN).astype(BF)

        def started():
            for job in heads:
                job.begin(place)
            pending[1].begin(place, range(2, n))
            pending[1].begin(place, (0,))
            for job in line_jobs:
                job.begin(place)
            hidden_weights.wait()
            kept[1].wait()
            kept[2].wait()
            for job in heads:
                job.middle(place)

        def down_grad():
            for job in heads:
                job.relay(place)
            kept[3].wait()
            kept[0].wait()
            weight_grad(2, dy_all, hm_in)

        def last():
            weight_grad(1, n2_all, dup_all)
            for job in heads:
                job.late(place)

        run_together(
            columns(0),
            columns(1),
            {
                (B, 0): started,
                (B, 8): down_grad,
                (B, 9): lambda: weight_grad(0, n2_all, dgate_all),
                (B, 10): last,
            },
        )
        dn2 = jnp.concatenate([scatter.result() for _, scatter in pairs], axis=0)
        values = h1[...]
        inverse = row_norm(values)
        weighted = dn2 * gain[2:3]
        inner = jnp.mean(weighted * values, axis=-1, keepdims=True)
        dh1_out[...] = (
            dy[...].astype(F32) + inverse * weighted - values * (inverse * inverse * inverse) * inner
        )
        gain_grad[...] = jnp.sum(dn2 * values * inverse, axis=0, keepdims=True)
        for gather, scatter in pairs:
            gather.finish()
            scatter.finish()
        finish(pending, place)
        finish(jobs, place)

    shapes = (
        jax.ShapeDtypeStruct((sz.rows, sz.width), F32),
        jax.ShapeDtypeStruct((3, sz.width, sz.hidden), BF),
        jax.ShapeDtypeStruct((1, sz.width), F32),
    )
    inner = pltpu.VMEM((CHUNKS, 2, 4, n * rows, sz.hidden), BF)
    scratch = [
        pltpu.VMEM((3, sz.width, sz.hidden), BF),
        pltpu.VMEM((CHUNKS, 2, 4, n, rows, sz.width), BF),
        inner,
        inner,
        pltpu.VMEM((CHUNKS, 2, 4, n, rows, sz.width), BF),
        inner,
        inner,
        inner,
        DMA((2, 3)),
        DMA((4,)),
    ] + halves_scratch(n, rows, sz.width)
    arrays = (h1, gain, *weights, *kept)
    specs = [vmem()] * 2 + [hbm()] * 7
    return Part(body, list(zip(arrays, specs)), [(shape, vmem()) for shape in shapes], scratch)


def finale(sz, part, vectors, results, shares, line_jobs, head_jobs):
    n = sz.ctx
    a, count = len(part.ins), len(part.scratch)
    order = [(1, 2), (1, 0), (1, 1), (0, 2), (0, 0), (0, 1)]
    query_columns = QUERY_HEADS * HEAD_WIDTH_SIZE
    key_columns = KEY_VALUE_HEADS * HEAD_WIDTH_SIZE

    def body(ins, outs, scratch, jobs):
        gain1_grad1, bias_grad1, gain2_grad0, gain2_grad1, grad1, *shares = ins[a:]
        small_in, grad_out, gate_up_out, down_out, gate_up_other, down_other = outs
        made = scratch[count : count + 4]
        small, whole_bias, s_small, r_small, s_out, r_out, *sems = scratch[count + 4 :]
        dx, dw, gain_grad, bias_grad = made
        down_line, gate_line, up_line, *heads = jobs
        place = where_am_i()
        x, y, k, z = place
        me = x * sz.group + (y * 2 + k) * n + z
        for job in heads[1:]:
            job.source = dw
        sources = [shares[2], shares[0], shares[1], down_line.target, gate_line.target, up_line.target]
        moves = {
            where: PlaneShares(
                sz,
                *where,
                source,
                *((down_out, down_other) if where[1] == 2 else (gate_up_out, gate_up_other)),
                [sem.at[number] for sem in sems],
            )
            for number, (where, source) in enumerate(zip(order, sources))
        }
        greet_all(me, sz.total, lambda index: flat_place(index, sz.group, n))

        placed = Placed(sz, None, None)
        placed.bind((dx, grad1), (grad_out,), (s_out, r_out))

        def sent():
            down_line.begin(place)
            heads[0].begin(place)

        def gathered():
            moves[1, 2].begin(place)

        def shared():
            gate_line.begin(place)
            up_line.begin(place)
            down_line.finish(place)
            moves[0, 2].begin(place)

        def returned():
            moves[0, 2].cross(place)
            moves[1, 2].cross(place)

        hooks = (sent, gathered, shared, returned)
        part.body(ins[:a], made, scratch[:count], jobs, place, hooks)
        for job in heads[1:]:
            job.begin(place)
        placed.begin(place)

        starts = (
            ((2 * x + y) * sz.qcols, sz.qcols),
            (query_columns + x * sz.kcols, sz.kcols),
            (query_columns + key_columns + x * sz.kcols, sz.kcols),
        )
        wide = (query_columns + key_columns) // sz.group
        thin = key_columns // sz.group
        small[...] = jnp.zeros_like(small)
        for section, (gain1, gain2, bias) in enumerate(
            ((gain_grad, gain2_grad0, bias_grad), (gain1_grad1, gain2_grad1, bias_grad1))
        ):
            whole_bias[...] = jnp.zeros_like(whole_bias)
            offset = 0
            for start, size in starts:
                cols = pl.ds(pl.multiple_of(start, HB), size)
                whole_bias[:, cols] = bias[:, offset : offset + size]
                offset += size
            for owner in range(sz.group):
                row = section * sz.group + owner
                own = slice(owner * sz.owned, (owner + 1) * sz.owned)
                small[row, 0:1, : sz.owned] = gain1[:, own]
                small[row, 1:2, : sz.owned] = gain2[:, own]
                small[row, 2:3, :wide] = whole_bias[:, owner * wide : (owner + 1) * wide]
                base = query_columns + key_columns + owner * thin
                small[row, 3:4, :thin] = whole_bias[:, base : base + thin]

        @pl.loop(1, sz.total)
        def _(step):
            device = lax.rem(me + step, sz.total)
            remote(
                small.at[device], small_in.at[me], s_small, r_small, flat_place(device, sz.group, n)
            ).start()

        pltpu.make_async_copy(small.at[me], small_in.at[me], s_small).start()
        for job in heads:
            job.middle(place)
        gate_line.finish(place)
        moves[0, 0].begin(place)
        moves[1, 0].begin(place)
        moves[0, 0].cross(place)
        up_line.finish(place)
        moves[0, 1].begin(place)
        moves[1, 1].begin(place)
        moves[1, 0].cross(place)
        heads[0].relay(place)
        moves[0, 1].cross(place)
        heads[1].relay(place)
        heads[0].late(place)
        moves[1, 1].cross(place)
        heads[2].relay(place)
        for job in heads[1:]:
            job.late(place)
        placed.finish(place)
        arrived(small_in.at[pl.ds(0, sz.total - 1)], r_small)
        arrived(small_in, s_small)
        for move in moves.values():
            move.finish(place)
        for job in heads:
            job.finish(place)

    shapes = (
        jax.ShapeDtypeStruct((sz.total, 8, LANES), F32),
        jax.ShapeDtypeStruct((2, sz.rows, sz.width), BF),
        jax.ShapeDtypeStruct((sz.owned, 2 * sz.ff), BF),
        jax.ShapeDtypeStruct((sz.owned, sz.ff), BF),
        jax.ShapeDtypeStruct((sz.owned, 2 * sz.ff), BF),
        jax.ShapeDtypeStruct((sz.owned, sz.ff), BF),
    )
    many = len(order)
    scratch = (
        part.scratch
        + [pltpu.VMEM(shape.shape, shape.dtype) for shape, _ in part.outs]
        + [
            pltpu.VMEM((sz.total, 8, LANES), F32),
            pltpu.VMEM((1, query_columns + 2 * key_columns), F32),
            DMA,
            DMA,
            DMA((2,)),
            DMA((2,)),
            DMA((many, 2)),
            DMA((many, 5)),
            DMA((many, 2)),
            DMA((many,)),
            DMA((many,)),
        ]
    )
    ins = part.ins + [(vector, vmem()) for vector in vectors] + [(array, hbm()) for array in (*results, *shares)]
    return run_call(
        body,
        ins,
        [(shape, hbm()) for shape in shapes],
        scratch,
        line_jobs + head_jobs,
        6,
        "layer_last",
    )


def local_columns(
    sz,
    tokens,
    positions,
    norm1_gain,
    qkv_bias,
    qkv_weight,
    out_weight,
    norm2_gain,
    gate_up_weight,
    down_weight,
    cotangent,
):
    n, group = sz.ctx, sz.group
    x, y, k, z = where_am_i()
    mine = 2 * x + y
    bias_owned = qkv_bias.shape[1]
    qkv_weight, out_weight = (qkv_weight[0], out_weight[0])
    gate_up_weight, down_weight = (gate_up_weight[0], down_weight[0])

    def line(values):
        return jnp.pad(values, ((0, 0), (0, LANES - values.shape[1])))

    small = jnp.concatenate(
        [line(norm1_gain), line(norm2_gain), line(qkv_bias), jnp.zeros((13, LANES), BF)], axis=0
    )
    (small_all, tok_own, cot_own, heads_x, cols_x), ((att0,), (gate0,)) = spread(
        sz, small, tokens, cotangent, qkv_weight, out_weight, gate_up_weight, down_weight
    )
    per_section = small_all.reshape(2, group, 16, LANES).astype(F32)
    gains = per_section[:, :, :2, : sz.owned].transpose(2, 0, 1, 3).reshape(4, sz.width)
    bias = per_section[:, :, 2, :bias_owned].reshape(2, 1, group * bias_owned)
    query_columns = QUERY_HEADS * HEAD_WIDTH_SIZE
    key_columns = KEY_VALUE_HEADS * HEAD_WIDTH_SIZE
    kv = mine // (4 // KEY_VALUE_HEADS)
    starts = (
        (mine * sz.qcols, sz.qcols),
        (query_columns + kv * sz.kcols, sz.kcols),
        (query_columns + key_columns + kv * sz.kcols, sz.kcols),
    )
    own_bias = jnp.concatenate(
        [lax.dynamic_slice_in_dim(bias, start, size, 2) for start, size in starts], axis=2
    )[:, 0]
    ordered = lax.dynamic_index_in_dim(positions, k, 0, keepdims=False)
    ordered = ordered.reshape(4, n, sz.rows).transpose(1, 0, 2)
    own_pos = lax.dynamic_index_in_dim(ordered, z, 0, keepdims=False).reshape(4 * sz.rows)
    kpos = ordered.reshape(1, sz.seq)
    qpos = own_pos[:, None]
    cosine, sine = rope_tables(own_pos, HEAD_WIDTH_SIZE)
    half = HEAD_WIDTH_SIZE // 2
    sign = jnp.where(jnp.arange(HEAD_WIDTH_SIZE) < half, -1.0, 1.0)
    tables = (cosine[:, 0], sine[:, 0] * sign)

    def columns(section, part):
        return Columns(sz, section, part, gate_up_weight, down_weight, cols_x)

    def attention(section, x_own, watt):
        return attend(sz, section, x_own, gains, own_bias, watt, tables, qpos, kpos)

    (mid0, *kept_att0), (act0, *kept_feed), ((up0,), (down0,)), ((att1,), (gate1,)) = joined(
        sz,
        attention(0, tok_own, att0),
        [columns(0, 1), columns(0, 2)],
        feed(sz, gains, gate0),
        [Heads(sz, 1, qkv_weight, out_weight, heads_x), columns(1, 0)],
        lambda made, given, own, later: (made[0], *given, own[0].target, own[1].target),
        False,
        3,
        "layer_forward",
    )
    (_, *kept_att1), (act1, dh1, dw1, gain2_grad1), _, _ = joined(
        sz,
        attention(1, act0, att1),
        [columns(1, 1)],
        both(sz, cot_own, gains, gate1),
        [columns(1, 2)],
        lambda made, given, own, later: (given[0], made[0], *given[1:], own[0].target, later[0].target),
        False,
        4,
        "layer_turn",
    )

    def attention_back(section, dh1, x_own, watt, kept, plan=None):
        return attend_back(
            sz, section, dh1, x_own, gains, watt, tables, qpos, kpos, kept, plan
        )

    def shares_between(jobs, place):
        return (
            lambda: jobs[0].begin(place),
            lambda: jobs[2].begin(place),
            lambda: jobs[1].begin(place, (1,)),
            lambda: None,
        )

    def heads_linked(made, given, own, later):
        later[1].source = made[1]
        return (made[0], *given)

    (
        (grad1, da1, gain1_grad1, bias_grad1),
        (dh1, dw0, gain2_grad0),
        ((down_share1,), (gate_share1,), (act_out,)),
        ((up_share1,), (heads10,)),
    ) = joined(
        sz,
        attention_back(1, dh1, act0, att1, kept_att1, shares_between),
        [LineShares(sz, 2, dw1), LineShares(sz, 0, dw1), Placed(sz, act0, act1)],
        feed_back(sz, mid0, gains, (gate0, up0, down0), kept_feed),
        [LineShares(sz, 1, dw1), ReturnedHeads(sz, 1, 0, None)],
        heads_linked,
        True,
        5,
        "layer_backward",
    )
    came_heads = [[None, None], [heads10, None]]
    (small_in, grad_out, gate_up_out, down_out, _, _), more = finale(
        sz,
        attention_back(0, dh1, tok_own, att0, kept_att0),
        (gain1_grad1, bias_grad1, gain2_grad0, gain2_grad1),
        (grad1,),
        (gate_share1, up_share1, down_share1),
        [LineShares(sz, part, dw0) for part in (2, 0, 1)],
        [ReturnedHeads(sz, 1, 1, da1), ReturnedHeads(sz, 0, 0, None), ReturnedHeads(sz, 0, 1, None)],
    )
    (came_heads[1][1],), (came_heads[0][0],), (came_heads[0][1],) = more[3:]
    small_sum = jnp.sum(small_in, axis=0)
    gate_up_grad = gate_up_out.astype(F32)[None]
    down_grad = down_out.astype(F32)[None]
    by_y = [jnp.where(y == 0, parts[0], parts[1]) for parts in came_heads]
    att_sum = jnp.where(x == 0, by_y[0], by_y[1]).astype(F32)
    q_grad = att_sum[:, :, : sz.qcols].transpose(1, 0, 2).reshape(sz.owned, query_columns)
    kv_grad = jnp.sum(
        att_sum[:, :, sz.qcols : sz.acols].reshape(
            KEY_VALUE_HEADS, 4 // KEY_VALUE_HEADS, sz.owned, 2, sz.kcols
        ),
        axis=1,
    )
    kv_grad = kv_grad.transpose(1, 2, 0, 3).reshape(sz.owned, 2 * key_columns)
    qkv_grad = jnp.concatenate([q_grad, kv_grad], axis=1)[None]
    out_grad = att_sum[:, :, sz.acols :].transpose(1, 0, 2).reshape(1, sz.owned, query_columns)
    return (
        act_out[None],
        grad_out[None],
        small_sum[0:1, : sz.owned],
        small_sum[2:3, : (query_columns + key_columns) // group],
        small_sum[3:4, : key_columns // group],
        qkv_grad,
        out_grad,
        small_sum[1:2, : sz.owned],
        gate_up_grad,
        down_grad,
    )


def solution(mesh):
    placed = (
        P(None, ("head", "ctx"), None),
        P(),
        P("section", ("head", "ctx")),
        P("section", ("head", "ctx")),
        P("section", ("head", "ctx"), None),
        P("section", ("head", "ctx"), None),
        P("section", ("head", "ctx")),
        P("section", ("head", "ctx"), None),
        P("section", ("head", "ctx"), None),
        P(None, ("head", "ctx"), None),
    )
    returned = (
        P("section", None, ("head", "ctx"), None),
        P("section", None, ("head", "ctx"), None),
        P("section", ("head", "ctx")),
        P("section", ("head", "ctx")),
        P("section", ("head", "ctx")),
        P("section", ("head", "ctx"), None),
        P("section", ("head", "ctx"), None),
        P("section", ("head", "ctx")),
        P("section", ("head", "ctx"), None),
        P("section", ("head", "ctx"), None),
    )

    def program(*arrays):
        sizes = Sizes(mesh, arrays[0], arrays[4], arrays[7], arrays[8])
        body = functools.partial(local_columns, sizes) if sizes.fits() else local
        return jax.shard_map(
            body, mesh=mesh, in_specs=placed, out_specs=returned, check_vma=False
        )(*arrays)

    return program
```
